128 devices in a mesh: pipe: 2 (over core), dp: 64 (over y, z, x).
Axes of the slice: x: 4, y: 4, z: 4, core: 2. Of those that a mesh axis runs over, the one named last changes fastest.
Arguments:
- inputs: float32 [768, 12, 1150], P('dp'), may hold values from -1 to 1
- lower_lock: int32 [768, 1150], P('dp'), may hold values 0 or 1
- upper_lock: int32 [768, 1150], P('dp'), may hold values 0 or 1
- resets: int32 [768, 12], P('dp'), may hold values 0 or 1
- lower_input: bfloat16 [1150, 4600], P('pipe'), may hold values from -0.1875 to 0.1875
- lower_recur: bfloat16 [1150, 4600], P('pipe'), may hold values from -0.125 to 0.125
- lower_bias: bfloat16 [4600], P('pipe'), may hold values from -3 to 3
- lower_drop: int32 [1150, 230], replicated, may hold values from 0 to 1048575
- upper_input: bfloat16 [1150, 1600], P('pipe'), may hold values from -0.1875 to 0.1875
- upper_recur: bfloat16 [400, 1600], P('pipe'), may hold values from -0.21875 to 0.21875
- upper_bias: bfloat16 [1600], P('pipe'), may hold values from -3 to 3
- upper_drop: int32 [400, 80], replicated, may hold values from 0 to 1048575
- grad_out: float32 [768, 12, 400], P('dp'), may hold values from -6 to 6
Outputs:
- hidden_out: float32 [768, 12, 400], P('dp', None, 'pipe')
- grad_inputs: float32 [768, 12, 1150], P('dp', None, 'pipe')
- grad_lower_input: float32 [1150, 4600], P('pipe')
- grad_lower_recur: float32 [1150, 4600], P('pipe')
- grad_lower_bias: float32 [4600], P('pipe')
- grad_upper_input: float32 [1150, 1600], P('pipe')
- grad_upper_recur: float32 [400, 1600], P('pipe')
- grad_upper_bias: float32 [1600], P('pipe')
The draws below stay inside these ranges and needn't reach their ends.
Inputs may be any that keep to these rules, and one draw needn't show every extreme that they name: `resets`: 1 at [s, t] starts a new document at position t of stream s. `lower_lock`: 0/1 flags. `upper_lock`: 0/1 flags. `lower_drop`: bit k (0 to 19) of entry [r, j] keeps entry [r, 20 j + k] of lower_recur. `upper_drop`: bit k (0 to 19) of entry [r, j] keeps entry [r, 20 j + k] of upper_recur.
All inputs are finite; a program needn't handle non-finite values. No bound on the sum of `lower_lock` or of `upper_lock` or of `resets` on one device may be relied on, other than what follows from the above.
Results may differ from the reference program's by a relative error of at most 0.0003.
Values may be sent and summed in bfloat16 or wider, within the bound.
A program may use at most 448 MiB of HBM per device.

```python
import jax
import jax.numpy as jnp
from jax import lax

WIDTH = 1150
OUTW = 400
LENGTH = 12
STREAMS = 768


def plant(result, own_key, least, largest):
    index_at = [jax.random.randint(jax.random.fold_in(own_key, axis), (), 0, length) for axis, length in enumerate(result.shape)]
    longest = result.shape.index(max(result.shape))
    neighbour = index_at[:longest] + [(index_at[longest] + 1) % result.shape[longest]] + index_at[longest + 1:]
    return result.at[tuple(index_at)].set(least).at[tuple(neighbour)].set(largest)


def shard_levels(stream_key, shape, shards, smallest, largest):
    def one(dim, shards_of):
        steps = jax.random.uniform(jax.random.fold_in(jax.random.fold_in(stream_key, 6), dim), (shards_of,), jnp.float32, smallest / len(shards), largest / len(shards))
        return jnp.repeat(jnp.exp(steps), shape[dim] // shards_of).reshape((-1,) + (1,) * (len(shape) - dim - 1))

    gain = one(*shards[0])
    for cut in shards[1:]:
        gain = gain * one(*cut)
    return gain


def bell_draw(own_key, dims, width, limit, pieces=(), kind=jnp.bfloat16):
    drawn = jax.random.normal(own_key, dims, jnp.float32) * width
    if len(pieces) > 0:
        drawn = shard_levels(own_key, dims, pieces, -0.22, 0.18) * drawn
    return jnp.clip(drawn, min=-limit, max=limit).astype(kind)


def setup_inputs(seed: int = 0) -> dict:
    splits = jax.random.split(jax.random.key(seed), 14)
    return {
        "inputs": jnp.clip(jax.random.uniform(splits[0], (STREAMS, LENGTH, WIDTH), jnp.float32, -1.0, 1.0) * shard_levels(splits[0], (STREAMS, LENGTH, WIDTH), ((0, 64),), -0.4, 0.0), -1.0, 1.0),
        "lower_lock": plant((jax.random.randint(splits[1], (STREAMS, WIDTH), 0, 5) < 4).astype(jnp.int32), jax.random.fold_in(splits[1], 1), 0, 1),
        "upper_lock": plant((jax.random.randint(splits[2], (STREAMS, WIDTH), 0, 5) < 4).astype(jnp.int32), jax.random.fold_in(splits[2], 1), 0, 1),
        "resets": plant((jax.random.randint(splits[3], (STREAMS, LENGTH), 0, 6) < 1).astype(jnp.int32), jax.random.fold_in(splits[3], 1), 0, 1),
        "lower_input": bell_draw(splits[4], (WIDTH, 4 * WIDTH), WIDTH ** -0.5, 0.1875, ((0, 2),)),
        "lower_recur": bell_draw(splits[5], (WIDTH, 4 * WIDTH), (2 * WIDTH) ** -0.5, 0.125, ((0, 2),)),
        "lower_bias": bell_draw(splits[6], (4 * WIDTH,), 0.5, 3.0, ((0, 2),)),
        "lower_drop": plant(jax.random.randint(splits[7], (WIDTH, 4 * WIDTH // 20), 0, 1048576), jax.random.fold_in(splits[7], 1), 0, 1048575).astype(jnp.int32),
        "upper_input": bell_draw(splits[8], (WIDTH, 4 * OUTW), WIDTH ** -0.5, 0.1875, ((0, 2),)),
        "upper_recur": bell_draw(splits[9], (OUTW, 4 * OUTW), (2 * OUTW) ** -0.5, 0.21875, ((0, 2),)),
        "upper_bias": bell_draw(splits[10], (4 * OUTW,), 0.5, 3.0, ((0, 2),)),
        "upper_drop": plant(jax.random.randint(splits[11], (OUTW, 4 * OUTW // 20), 0, 1048576), jax.random.fold_in(splits[11], 1), 0, 1048575).astype(jnp.int32),
        "grad_out": bell_draw(splits[12], (STREAMS, LENGTH, OUTW), 1.0, 6.0, ((0, 64),), jnp.float32),
    }


highest = lax.Precision.HIGHEST

@jax.custom_vjp
def low(v):
    return lax.optimization_barrier(v.astype(jnp.bfloat16)).astype(jnp.float32)

@jax.custom_vjp
def low_back(v):
    return v

def low_keep(v):
    return (low(v), None)

def low_pass(kept, grad):
    return (grad,)

def back_keep(v):
    return (v, None)

def back_low(kept, grad):
    return (low(grad),)
low.defvjp(low_keep, low_pass)
low_back.defvjp(back_keep, back_low)

def unpack_keep(packed):
    shifts = jnp.arange(20, dtype=jnp.int32)
    flags = jnp.bitwise_and(jnp.right_shift(packed[:, :, None], shifts), 1)
    return flags.reshape(packed.shape[0], packed.shape[1] * 20).astype(jnp.float32)

def recurrent_layer(layer_in, weight_in, weight_rec, bias_row, keep_mask):
    units = weight_rec.shape[0]
    projected = jnp.einsum('sti,ig->tsg', layer_in, weight_in, precision=highest) + bias_row

    def advance(carried, inputs_now):
        hidden, cell_state = carried
        pre_now, keep_now = inputs_now
        hidden = hidden * keep_now[:, None]
        cell_state = cell_state * keep_now[:, None]
        gates = pre_now + jnp.dot(hidden, weight_rec, precision=highest)
        in_gate = jax.nn.sigmoid(gates[:, :units])
        forget = jax.nn.sigmoid(gates[:, units:2 * units])
        candidate = jnp.tanh(gates[:, 2 * units:3 * units])
        out_gate = jax.nn.sigmoid(gates[:, 3 * units:])
        cell_new = forget * cell_state + in_gate * candidate
        hidden_new = out_gate * jnp.tanh(cell_new)
        return ((hidden_new, cell_new), hidden_new)
    blank = jnp.zeros((layer_in.shape[0], units), jnp.float32)
    final_state, sequence = lax.scan(advance, (blank, blank), (projected, keep_mask.T))
    return jnp.transpose(sequence, (1, 0, 2))

def reference(inputs, lower_lock, upper_lock, resets, lower_input, lower_recur, lower_bias, lower_drop, upper_input, upper_recur, upper_bias, upper_drop, grad_out):
    keep_mask = (1 - resets).astype(jnp.float32)
    lock_low = lower_lock.astype(jnp.float32) * 1.25
    lock_up = upper_lock.astype(jnp.float32) * 1.25
    mask_low = unpack_keep(lower_drop) * 2.0
    mask_up = unpack_keep(upper_drop) * 2.0
    weights = (lower_input.astype(jnp.float32), lower_recur.astype(jnp.float32), lower_bias.astype(jnp.float32), upper_input.astype(jnp.float32), upper_recur.astype(jnp.float32), upper_bias.astype(jnp.float32))

    def forward(source, low_in, low_rec, low_bias, up_in, up_rec, up_bias):
        lower_hidden = recurrent_layer(source * lock_low[:, None, :], low_in, low_rec * mask_low, low_bias, keep_mask)
        return recurrent_layer(lower_hidden * lock_up[:, None, :], up_in, up_rec * mask_up, up_bias, keep_mask)
    hidden_out, pullback = jax.vjp(forward, inputs, *weights)
    grads = pullback(grad_out)
    return (hidden_out, grads[0], grads[1], grads[2], grads[3], grads[4], grads[5], grads[6])
```

```python
import functools

import jax
import jax.numpy as jnp
from jax import lax
from jax.experimental import pallas as pl
from jax.experimental.pallas import tpu as pltpu
from jax.sharding import PartitionSpec as P

BF = jnp.bfloat16
F32 = jnp.float32
MESH = pl.DeviceIdType.MESH
ROWS = 16
VMEM_LIMIT = 60 * 2**20


def ceil_to(value, multiple):
    return -(-value // multiple) * multiple


def split(value):
    high = value.astype(BF)
    low = (value - high.astype(F32)).astype(BF)
    return high, low


def fold(stacked):
    half = stacked.shape[0] // 2
    return stacked[:half] + stacked[half:]


def dot_nn(a, b):
    return jnp.dot(a, b, preferred_element_type=F32)


def dot_nt(a, b):
    return lax.dot_general(a, b, (((1,), (1,)), ((), ())), preferred_element_type=F32)


def recurrence_kernel(
    units,
    x_ref,
    keep_ref,
    lock_ref,
    gout_ref,
    wrec,
    win,
    uin,
    urec,
    blo,
    bup,
    hid_o,
    dx_o,
    x2_o,
    hk2_o,
    ux2_o,
    hku2_o,
    dal_o,
    dau_o,
    x2,
    hk2,
    ux2,
    hku2,
    dal,
    dau,
    proj,
    send_l,
    recv_l,
    send_u,
    recv_u,
    act_l,
    act_u,
    save_l,
    save_u,
    cell_l,
    cell_u,
    da_l,
    da_u,
    dstate_l,
    dstate_u,
    dx_up,
    acc,
    fs_l,
    fr_l,
    fs_u,
    fr_u,
    bs_l,
    br_l,
    bs_u,
    br_u,
    out_sem,
):
    steps = gout_ref.shape[0]
    me = lax.axis_index("pipe")
    other = 1 - me
    peer = {"pipe": other}
    wide_k = wrec.shape[1]
    wide = wrec.shape[2]
    up_wide = uin.shape[2]
    up_k = urec.shape[1]
    lane = act_l.shape[1] - wide + units

    barrier = pltpu.get_barrier_semaphore()
    pl.semaphore_signal(barrier, inc=1, device_id=peer, device_id_type=MESH)
    pl.semaphore_wait(barrier, 1)

    def remote(src, dst, send_sem, recv_sem):
        return pltpu.make_async_remote_copy(
            src_ref=src,
            dst_ref=dst,
            send_sem=send_sem,
            recv_sem=recv_sem,
            device_id=peer,
            device_id_type=MESH,
        )

    high, low = split(x_ref[...])
    rows_all = x_ref.shape[0]
    x2[0:rows_all] = high
    x2[rows_all:] = low
    chunk = 256
    for q in range(2):

        def project(index, carry, q=q):
            cols = pl.ds(pl.multiple_of(index * chunk, chunk), chunk)
            y = fold(dot_nn(x2[...], win[q, :, cols])) + blo[q, :, cols]
            proj[q, :, :, cols] = y.reshape(steps, ROWS, chunk)
            return carry

        lax.fori_loop(0, wide // chunk, project, 0)

    act_l[...] = jnp.zeros_like(act_l)
    hk2[...] = jnp.zeros_like(hk2)
    ux2[...] = jnp.zeros_like(ux2)
    hku2[...] = jnp.zeros_like(hku2)
    cell_l[...] = jnp.zeros_like(cell_l)
    cell_u[...] = jnp.zeros_like(cell_u)

    def fcopy_l(t):
        return remote(send_l, recv_l.at[t], fs_l.at[t], fr_l.at[t])

    def fcopy_u(t):
        return remote(send_u, recv_u.at[t], fs_u.at[t], fr_u.at[t])

    def lower_send(t, first):
        if first:
            send_l[...] = proj[other, t]
        else:
            send_l[...] = fold(dot_nn(hk2[t, :, :wide_k], wrec[other])) + proj[other, t]
        fcopy_l(t).start()

    def lower_own(t, first):
        if first:
            act_l[:, :wide] = proj[me, t]
        else:
            act_l[:, :wide] = fold(dot_nn(hk2[t, :, :wide_k], wrec[me])) + proj[me, t]

    def upper_part(t, q):
        y = dot_nn(ux2[t, :, :wide_k], uin[q]) + dot_nn(hku2[t, :, :up_k], urec[q])
        return fold(y) + bup[q]

    def upper_send(t):
        send_u[...] = upper_part(t, other)
        fcopy_u(t).start()

    def upper_own(t):
        act_u[...] = upper_part(t, me)

    def cell_update(a_in, a_forget, a_cand, a_out, cell, keep_now, save, t):
        gate_in = jax.nn.sigmoid(a_in)
        forget = jax.nn.sigmoid(a_forget)
        cand = jnp.tanh(a_cand)
        gate_out = jax.nn.sigmoid(a_out)
        cell_keep = cell[...] * keep_now
        cell_new = forget * cell_keep + gate_in * cand
        squashed = jnp.tanh(cell_new)
        cell[...] = cell_new
        save[t, 0] = gate_in
        save[t, 1] = forget
        save[t, 2] = cand
        save[t, 3] = gate_out
        save[t, 4] = cell_keep
        save[t, 5] = squashed
        return gate_out * squashed

    def lower_finish(t):
        fcopy_l(t).wait()
        act_l[:, :wide] += recv_l[t]
        hidden = cell_update(
            act_l[:, 0:lane],
            act_l[:, units : units + lane],
            act_l[:, 2 * units : 2 * units + lane],
            act_l[:, 3 * units : 3 * units + lane],
            cell_l,
            keep_ref[t],
            save_l,
            t,
        )
        high, low = split(hidden * keep_ref[t + 1])
        hk2[t + 1, 0:ROWS] = high
        hk2[t + 1, ROWS:] = low
        high, low = split(hidden * lock_ref[...])
        ux2[t, 0:ROWS] = high
        ux2[t, ROWS:] = low

    gate_u = up_wide // 4

    def upper_finish(t):
        fcopy_u(t).wait()
        a = act_u[...] + recv_u[t]
        hidden = cell_update(
            a[:, 0:gate_u],
            a[:, gate_u : 2 * gate_u],
            a[:, 2 * gate_u : 3 * gate_u],
            a[:, 3 * gate_u :],
            cell_u,
            keep_ref[t],
            save_u,
            t,
        )
        hid_o[t] = hidden
        high, low = split(hidden * keep_ref[t + 1])
        hku2[t + 1, 0:ROWS] = high
        hku2[t + 1, ROWS:] = low

    lower_send(0, True)
    lower_own(0, True)
    lower_finish(0)

    def forward_round(r, carry):
        lower_send(r, False)
        upper_send(r - 1)
        lower_own(r, False)
        upper_own(r - 1)
        lower_finish(r)
        upper_finish(r - 1)
        return carry

    lax.fori_loop(1, steps, forward_round, 0)
    upper_send(steps - 1)
    upper_own(steps - 1)
    upper_finish(steps - 1)

    dstate_l[...] = jnp.zeros_like(dstate_l)
    dstate_u[...] = jnp.zeros_like(dstate_u)
    da_l[...] = jnp.zeros_like(da_l)

    def bcopy_l(t):
        return remote(dal.at[me, t], dal.at[me, t], bs_l.at[t], br_l.at[t])

    def bcopy_u(t):
        return remote(dau.at[me, t], dau.at[me, t], bs_u.at[t], br_u.at[t])

    def gate_grads(dy, dstate, save, keep_now, t):
        gate_in, forget, cand, gate_out = save[t, 0], save[t, 1], save[t, 2], save[t, 3]
        cell_keep, squashed = save[t, 4], save[t, 5]
        dh = dstate[0] + dy
        dc = dstate[1] + dh * gate_out * (1.0 - squashed * squashed)
        dstate[1] = dc * forget * keep_now
        return (
            dc * cand * gate_in * (1.0 - gate_in),
            dc * cell_keep * forget * (1.0 - forget),
            dc * gate_in * (1.0 - cand * cand),
            dh * squashed * gate_out * (1.0 - gate_out),
        )

    def lower_back_start(t):
        grads = gate_grads(dx_up[...] * lock_ref[...], dstate_l, save_l, keep_ref[t], t)
        for g in range(4):
            da_l[:, g * units : (g + 1) * units] = grads[g][:, :units]
        high, low = split(da_l[...])
        dal[me, t, 0:ROWS] = high
        dal[me, t, ROWS:] = low
        bcopy_l(t).start()

    def upper_back_start(t):
        grads = gate_grads(gout_ref[t], dstate_u, save_u, keep_ref[t], t)
        for g in range(4):
            high, low = split(grads[g])
            dau[me, t, 0:ROWS, g * gate_u : (g + 1) * gate_u] = high
            dau[me, t, ROWS:, g * gate_u : (g + 1) * gate_u] = low
        bcopy_u(t).start()

    def lower_back_part(t, q):
        return fold(dot_nt(dal[q, t], wrec[q]))

    def upper_back_part(t, q):
        grad = dau[q, t]
        return fold(dot_nt(grad, uin[q])), fold(dot_nt(grad, urec[q]))

    def lower_back_own(t):
        acc[:, :wide_k] = lower_back_part(t, me)

    def lower_back_finish(t):
        bcopy_l(t).wait()
        dstate_l[0, :, :wide_k] = keep_ref[t] * (acc[:, :wide_k] + lower_back_part(t, other))

    def upper_back_own(t):
        into_x, into_h = upper_back_part(t, me)
        dx_up[:, :wide_k] = into_x
        dstate_u[0, :, :up_k] = into_h

    def upper_back_finish(t):
        bcopy_u(t).wait()
        into_x, into_h = upper_back_part(t, other)
        dx_up[:, :wide_k] += into_x
        dstate_u[0, :, :up_k] = keep_ref[t] * (dstate_u[0, :, :up_k] + into_h)

    dx_up[...] = jnp.zeros_like(dx_up)
    upper_back_start(steps - 1)
    upper_back_own(steps - 1)
    upper_back_finish(steps - 1)

    def backward_round(r, carry):
        t = steps - r
        lower_back_start(t)
        upper_back_start(t - 1)
        lower_back_own(t)
        upper_back_own(t - 1)
        lower_back_finish(t)
        upper_back_finish(t - 1)
        return carry

    lax.fori_loop(1, steps, backward_round, 0)
    lower_back_start(0)
    bcopy_l(0).wait()

    dx_o[...] = jnp.zeros_like(dx_o)
    for q in range(2):

        def input_grad(index, carry, q=q):
            cols = pl.ds(pl.multiple_of(index * chunk, chunk), chunk)
            grad = dal[q, :, :, cols].reshape(steps * 2 * ROWS, chunk)
            y = dot_nt(grad, win[q, :, cols]).reshape(steps, 2 * ROWS, wide_k)
            dx_o[...] += y[:, :ROWS] + y[:, ROWS:]
            return carry

        lax.fori_loop(0, wide // chunk, input_grad, 0)

    copies = [
        pltpu.make_async_copy(x2, x2_o, out_sem.at[0]),
        pltpu.make_async_copy(hk2, hk2_o, out_sem.at[1]),
        pltpu.make_async_copy(ux2, ux2_o, out_sem.at[2]),
        pltpu.make_async_copy(hku2, hku2_o, out_sem.at[3]),
        pltpu.make_async_copy(dal, dal_o, out_sem.at[4]),
        pltpu.make_async_copy(dau, dau_o, out_sem.at[5]),
    ]
    for copy in copies:
        copy.start()
    for copy in copies:
        copy.wait()


def recurrence(x, keep, lock, gout, wrec, win, uin, urec, blo, bup, units):
    steps = gout.shape[0]
    wide_k, wide = wrec.shape[1:]
    up_k, up_wide = urec.shape[1:]
    lane = ceil_to(units, 128)
    gate_u = up_wide // 4
    vm = pl.BlockSpec(memory_space=pltpu.VMEM)
    hbm = pl.BlockSpec(memory_space=pl.ANY)
    sds = jax.ShapeDtypeStruct
    shapes = dict(
        x2=((2 * steps * ROWS, wide_k), BF),
        hk2=((steps + 1, 2 * ROWS, lane), BF),
        ux2=((steps, 2 * ROWS, lane), BF),
        hku2=((steps + 1, 2 * ROWS, gate_u), BF),
        dal=((2, steps, 2 * ROWS, wide), BF),
        dau=((2, steps, 2 * ROWS, up_wide), BF),
    )
    dma = pltpu.SemaphoreType.DMA
    return pl.pallas_call(
        functools.partial(recurrence_kernel, units),
        out_shape=(
            sds((steps, ROWS, gate_u), F32),
            sds((steps, ROWS, wide_k), F32),
        )
        + tuple(sds(*s) for s in shapes.values()),
        in_specs=[vm] * 10,
        out_specs=(vm, vm) + (hbm,) * len(shapes),
        scratch_shapes=[pltpu.VMEM(*s) for s in shapes.values()]
        + [
            pltpu.VMEM((2, steps, ROWS, wide), F32),
            pltpu.VMEM((ROWS, wide), F32),
            pltpu.VMEM((steps, ROWS, wide), F32),
            pltpu.VMEM((ROWS, up_wide), F32),
            pltpu.VMEM((steps, ROWS, up_wide), F32),
            pltpu.VMEM((ROWS, wide + lane - units), F32),
            pltpu.VMEM((ROWS, up_wide), F32),
            pltpu.VMEM((steps, 6, ROWS, lane), F32),
            pltpu.VMEM((steps, 6, ROWS, gate_u), F32),
            pltpu.VMEM((ROWS, lane), F32),
            pltpu.VMEM((ROWS, gate_u), F32),
            pltpu.VMEM((ROWS, wide), F32),
            pltpu.VMEM((ROWS, up_wide), F32),
            pltpu.VMEM((2, ROWS, lane), F32),
            pltpu.VMEM((2, ROWS, gate_u), F32),
            pltpu.VMEM((ROWS, lane), F32),
            pltpu.VMEM((ROWS, lane), F32),
        ]
        + [dma((steps,))] * 8
        + [dma((6,))],
        compiler_params=pltpu.CompilerParams(
            vmem_limit_bytes=VMEM_LIMIT, collective_id=0, has_side_effects=True
        ),
    )(x, keep, lock, gout, wrec, win, uin, urec, blo, bup)


def unpack_keep(packed):
    shifts = jnp.arange(20, dtype=jnp.int32)
    flags = jnp.bitwise_and(jnp.right_shift(packed[:, :, None], shifts), 1)
    return flags.reshape(packed.shape[0], packed.shape[1] * 20)


def by_half(weight, units, gate, rows, wide):
    held = weight.shape[0]
    parts = jnp.transpose(weight.reshape(held, 4, 2, units), (2, 0, 1, 3))
    parts = jnp.pad(parts, ((0, 0), (0, rows - held), (0, 0), (0, gate - units)))
    parts = parts.reshape(2, rows, 4 * gate)
    return jnp.pad(parts, ((0, 0), (0, 0), (0, wide - 4 * gate)))


def body(
    inputs,
    lower_lock,
    upper_lock,
    resets,
    lower_input,
    lower_recur,
    lower_bias,
    lower_drop,
    upper_input,
    upper_recur,
    upper_bias,
    upper_drop,
    grad_out,
):
    me = lax.axis_index("pipe")
    streams, steps, width = inputs.shape
    units, outs = lower_recur.shape[0], upper_recur.shape[0]
    wide_k = ceil_to(units, 16)
    wide = ceil_to(4 * units, 256)
    lane = ceil_to(units, 128)
    gate_u = ceil_to(outs, 128)
    up_k = ceil_to(outs, 16)
    pad_rows = ROWS - streams

    def own(array, axis, size):
        return lax.dynamic_slice_in_dim(array, me * size, size, axis)

    mask_low = unpack_keep(own(lower_drop, 0, units)) * 2
    mask_up = unpack_keep(own(upper_drop, 0, outs)) * 2
    wrec = by_half(lower_recur * mask_low.astype(BF), units, units, wide_k, wide)
    win = by_half(lower_input, units, units, wide_k, wide)
    uin = by_half(upper_input, outs, gate_u, wide_k, 4 * gate_u)
    urec = by_half(upper_recur * mask_up.astype(BF), outs, gate_u, up_k, 4 * gate_u)

    def bias_part(bias, half_units, gate, wide_to):
        full = jnp.zeros((2, bias.shape[0]), F32)
        full = lax.dynamic_update_slice(full, bias.astype(F32)[None], (me, 0))
        return by_half(full.reshape(1, -1), half_units, gate, 1, wide_to)

    blo = bias_part(lower_bias, units, units, wide)
    bup = bias_part(upper_bias, outs, gate_u, 4 * gate_u)

    keep = (1 - resets).astype(F32).T
    keep = jnp.pad(keep, ((0, 1), (0, pad_rows)))[:, :, None]
    lock_low = own(lower_lock.astype(F32) * 1.25, 1, units)
    lock_up = own(upper_lock.astype(F32) * 1.25, 1, units)
    x = jnp.transpose(own(inputs, 2, units) * lock_low[:, None, :], (1, 0, 2))
    x = jnp.pad(x, ((0, 0), (0, pad_rows), (0, wide_k - units))).reshape(steps * ROWS, wide_k)
    lock = jnp.pad(lock_up, ((0, pad_rows), (0, lane - units)))
    gout = jnp.transpose(own(grad_out, 2, outs), (1, 0, 2))
    gout = jnp.pad(gout, ((0, 0), (0, pad_rows), (0, gate_u - outs)))

    hid, dx, x2, hk2, ux2, hku2, dal, dau = recurrence(
        x, keep, lock, gout, wrec, win, uin, urec, blo, bup, units
    )
    hidden_out = jnp.transpose(hid[:, :streams, :outs], (1, 0, 2))
    grad_inputs = jnp.transpose(dx[:, :streams, :units], (1, 0, 2)) * lock_low[:, None, :]

    def in_order(grads, half_units, gate):
        parts = grads[..., : 4 * gate].reshape(2, steps, 2, ROWS, 4, gate)[..., :half_units]
        parts = jnp.transpose(parts, (1, 2, 3, 4, 0, 5))
        return parts.reshape(steps, 2, ROWS, 8 * half_units)

    da_low = in_order(dal, units, units)
    da_up = in_order(dau, outs, gate_u)

    def weight_grad(stack, da, held):
        left = stack.reshape(steps, 2, ROWS, -1)[..., :held]
        parts = [
            lax.dot_general(
                left[:, i],
                da[:, j],
                (((0, 1), (0, 1)), ((), ())),
                preferred_element_type=F32,
            )
            for i, j in ((0, 0), (1, 0), (0, 1))
        ]
        return parts[0] + parts[1] + parts[2]

    x2 = jnp.transpose(x2.reshape(2, steps, ROWS, wide_k), (1, 0, 2, 3))
    grads = (
        weight_grad(x2, da_low, units),
        weight_grad(hk2[:steps], da_low, units) * mask_low.astype(F32),
        own(jnp.sum(da_low.astype(F32), axis=(0, 1, 2)), 0, 4 * units),
        weight_grad(ux2, da_up, units),
        weight_grad(hku2[:steps], da_up, outs) * mask_up.astype(F32),
        own(jnp.sum(da_up.astype(F32), axis=(0, 1, 2)), 0, 4 * outs),
    )
    grads = lax.psum(grads, "dp")
    return (hidden_out, grad_inputs) + grads


def solution(mesh):
    return jax.shard_map(
        body,
        mesh=mesh,
        in_specs=(
            P("dp", None, None),
            P("dp", None),
            P("dp", None),
            P("dp", None),
            P("pipe", None),
            P("pipe", None),
            P("pipe"),
            P(),
            P("pipe", None),
            P("pipe", None),
            P("pipe"),
            P(),
            P("dp", None, None),
        ),
        out_specs=(
            P("dp", None, "pipe"),
            P("dp", None, "pipe"),
            P("pipe", None),
            P("pipe", None),
            P("pipe"),
            P("pipe", None),
            P("pipe", None),
            P("pipe"),
        ),
        check_vma=False,
    )
```

```python
import functools

import jax
import jax.numpy as jnp
from jax import lax
from jax.experimental import pallas as pl
from jax.experimental.pallas import tpu as pltpu
from jax.sharding import PartitionSpec as P

BF = jnp.bfloat16
F32 = jnp.float32
MESH = pl.DeviceIdType.MESH
ROWS = 16
VMEM_LIMIT = 60 * 2**20
TAIL_ROWS = 368


def ceil_to(value, multiple):
    return -(-value // multiple) * multiple


def split(value):
    high = value.astype(BF)
    low = (value - high.astype(F32)).astype(BF)
    return high, low


def fold(stacked):
    half = stacked.shape[0] // 2
    return stacked[:half] + stacked[half:]


def dot_nn(a, b):
    return jnp.dot(a, b, preferred_element_type=F32)


def dot_nt(a, b):
    return lax.dot_general(a, b, (((1,), (1,)), ((), ())), preferred_element_type=F32)


def drop_bits(words, start):
    column = lax.broadcasted_iota(jnp.int32, (1, 128), 1) + start
    index = (column * 52429) >> 20
    bit = column - index * 20
    first = start // 2560 * 128
    held = words[:, first : first + 128]
    index = jnp.broadcast_to(index - first, held.shape)
    found = jnp.take_along_axis(held, index, axis=1, mode="promise_in_bounds")
    return (found >> bit) & 2


def recurrence_kernel(
    units,
    x_ref,
    keep_ref,
    lock_ref,
    gout_ref,
    wrec_raw,
    win_raw,
    uin_raw,
    urec_raw,
    words_l,
    words_u,
    blo,
    bup,
    hid_o,
    dx_o,
    da_o,
    du_o,
    xh_o,
    lr_o,
    wrec,
    uin,
    urec,
    praw,
    da_all,
    du_all,
    xh,
    lr,
    x2,
    hk2,
    ux2,
    hku2,
    dal,
    dau,
    proj,
    send_l,
    recv_l,
    send_u,
    recv_u,
    act_l,
    act_u,
    save_l,
    save_u,
    cell_l,
    cell_u,
    da_l,
    da_u,
    dstate_l,
    dstate_u,
    dx_up,
    acc,
    fs_l,
    fr_l,
    fs_u,
    fr_u,
    bs_l,
    br_l,
    bs_u,
    br_u,
    out_sem,
):
    steps = gout_ref.shape[0]
    me = lax.axis_index("pipe")
    other = 1 - me
    peer = {"pipe": other}
    wide_k = wrec.shape[1]
    wide = wrec.shape[2]
    up_wide = uin.shape[2]
    up_k = urec.shape[1]
    lane = act_l.shape[1] - wide + units

    barrier = pltpu.get_barrier_semaphore()
    pl.semaphore_signal(barrier, inc=1, device_id=peer, device_id_type=MESH)
    pl.semaphore_wait(barrier, 1)

    def remote(src, dst, send_sem, recv_sem):
        return pltpu.make_async_remote_copy(
            src_ref=src,
            dst_ref=dst,
            send_sem=send_sem,
            recv_sem=recv_sem,
            device_id=peer,
            device_id_type=MESH,
        )

    full = wrec_raw.shape[1]
    held = wrec_raw.shape[0]
    held_u = urec_raw.shape[0]
    full_u = urec_raw.shape[1]
    unit_u = full_u // 8
    gate_u = up_wide // 4
    wrec[:, :, wide - 128 :] = jnp.zeros((2, wide_k, 128), BF)
    wrec[:, wide_k - ROWS :, :] = jnp.zeros((2, ROWS, wide), BF)
    uin[...] = jnp.zeros_like(uin)
    urec[...] = jnp.zeros_like(urec)

    def prepare_lower(row, count):
        words = words_l[pl.ds(row, ROWS), :] * 2
        parts = [drop_bits(words, 128 * n) for n in range(ceil_to(full, 128) // 128)]
        scale = jnp.concatenate(parts, axis=1)[:count, :full].astype(F32)
        weight = (wrec_raw[pl.ds(row, count), :].astype(F32) * scale).astype(BF)
        for q in range(2):
            for g in range(4):
                start = (2 * g + q) * units
                wrec[q, pl.ds(row, count), g * units : (g + 1) * units] = weight[
                    :, start : start + units
                ]

    def prepare_block(index, carry):
        prepare_lower(pl.multiple_of(index * ROWS, ROWS), ROWS)
        return carry

    lax.fori_loop(0, held // ROWS, prepare_block, 0)
    if held % ROWS:
        prepare_lower(held // ROWS * ROWS, held % ROWS)

    def place_upper(target, row, count, weight):
        for q in range(2):
            for g in range(4):
                start = (2 * g + q) * unit_u
                target[q, pl.ds(row, count), g * gate_u : g * gate_u + unit_u] = weight[
                    :, start : start + unit_u
                ]

    def upper_in_block(index, carry):
        row = pl.multiple_of(index * ROWS, ROWS)
        place_upper(uin, row, ROWS, uin_raw[pl.ds(row, ROWS), :])
        return carry

    lax.fori_loop(0, held // ROWS, upper_in_block, 0)
    if held % ROWS:
        row = held // ROWS * ROWS
        place_upper(uin, row, held % ROWS, uin_raw[row:held, :])

    def upper_rec_block(row, count):
        words = words_u[pl.ds(row, ROWS), :] * 2
        parts = [drop_bits(words, 128 * n) for n in range(ceil_to(full_u, 128) // 128)]
        scale = jnp.concatenate(parts, axis=1)[:count, :full_u].astype(F32)
        weight = (urec_raw[pl.ds(row, count), :].astype(F32) * scale).astype(BF)
        place_upper(urec, row, count, weight)

    def upper_rec_step(index, carry):
        upper_rec_block(pl.multiple_of(index * ROWS, ROWS), ROWS)
        return carry

    lax.fori_loop(0, held_u // ROWS, upper_rec_step, 0)
    if held_u % ROWS:
        upper_rec_block(held_u // ROWS * ROWS, held_u % ROWS)

    rows_all = x_ref.shape[0]
    high, low = split(x_ref[...])
    x2[0:rows_all] = high
    x2[rows_all:] = low
    praw[...] = jnp.zeros_like(praw)
    chunk = 512
    for start in range(0, full, chunk):
        stop = min(start + chunk, full)
        y = fold(dot_nn(x2[:, :held], win_raw[:, start:stop]))
        praw[:, :, start:stop] = y.reshape(steps, ROWS, stop - start)

    proj[...] = jnp.zeros_like(proj)

    def reorder(t, carry):
        for q in range(2):
            for g in range(4):
                start = (2 * g + q) * units
                proj[q, t, :, g * units : (g + 1) * units] = praw[t, :, start : start + units]
            proj[q, t] = proj[q, t] + blo[q]
        return carry

    lax.fori_loop(0, steps, reorder, 0)

    act_l[...] = jnp.zeros_like(act_l)
    hk2[...] = jnp.zeros_like(hk2)
    ux2[...] = jnp.zeros_like(ux2)
    hku2[...] = jnp.zeros_like(hku2)
    cell_l[...] = jnp.zeros_like(cell_l)
    cell_u[...] = jnp.zeros_like(cell_u)

    def fcopy_l(t):
        return remote(send_l, recv_l.at[t], fs_l.at[t], fr_l.at[t])

    def fcopy_u(t):
        return remote(send_u, recv_u.at[t], fs_u.at[t], fr_u.at[t])

    def lower_send(t, first):
        if first:
            send_l[...] = proj[other, t]
        else:
            send_l[...] = fold(dot_nn(hk2[t, :, :wide_k], wrec[other])) + proj[other, t]
        fcopy_l(t).start()

    def lower_own(t, first):
        if first:
            act_l[:, :wide] = proj[me, t]
        else:
            act_l[:, :wide] = fold(dot_nn(hk2[t, :, :wide_k], wrec[me])) + proj[me, t]

    def upper_part(t, q):
        y = dot_nn(ux2[t, :, :wide_k], uin[q]) + dot_nn(hku2[t, :, :up_k], urec[q])
        return fold(y) + bup[q]

    def upper_send(t):
        send_u[...] = upper_part(t, other)
        fcopy_u(t).start()

    def upper_own(t):
        act_u[...] = upper_part(t, me)

    def cell_update(a_in, a_forget, a_cand, a_out, cell, keep_now, save, t):
        gate_in = jax.nn.sigmoid(a_in)
        forget = jax.nn.sigmoid(a_forget)
        cand = jnp.tanh(a_cand)
        gate_out = jax.nn.sigmoid(a_out)
        cell_keep = cell[...] * keep_now
        cell_new = forget * cell_keep + gate_in * cand
        squashed = jnp.tanh(cell_new)
        cell[...] = cell_new
        save[t, 0] = gate_in
        save[t, 1] = forget
        save[t, 2] = cand
        save[t, 3] = gate_out
        save[t, 4] = cell_keep
        save[t, 5] = squashed
        return gate_out * squashed

    def lower_finish(t):
        fcopy_l(t).wait()
        act_l[:, :wide] += recv_l[t]
        hidden = cell_update(
            act_l[:, 0:lane],
            act_l[:, units : units + lane],
            act_l[:, 2 * units : 2 * units + lane],
            act_l[:, 3 * units : 3 * units + lane],
            cell_l,
            keep_ref[t],
            save_l,
            t,
        )
        high, low = split(hidden * keep_ref[t + 1])
        hk2[t + 1, 0:ROWS] = high
        hk2[t + 1, ROWS:] = low
        ones_at = lax.broadcasted_iota(jnp.int32, (ROWS, lane), 1) == units
        high, low = split(jnp.where(ones_at, 1.0, hidden * lock_ref[...]))
        ux2[t, 0:ROWS] = high
        ux2[t, ROWS:] = low

    def upper_finish(t):
        fcopy_u(t).wait()
        a = act_u[...] + recv_u[t]
        hidden = cell_update(
            a[:, 0:gate_u],
            a[:, gate_u : 2 * gate_u],
            a[:, 2 * gate_u : 3 * gate_u],
            a[:, 3 * gate_u :],
            cell_u,
            keep_ref[t],
            save_u,
            t,
        )
        hid_o[t] = hidden
        high, low = split(hidden * keep_ref[t + 1])
        hku2[t + 1, 0:ROWS] = high
        hku2[t + 1, ROWS:] = low

    lower_send(0, True)
    lower_own(0, True)
    lower_finish(0)

    def forward_round(r, carry):
        lower_send(r, False)
        upper_send(r - 1)
        lower_own(r, False)
        upper_own(r - 1)
        lower_finish(r)
        upper_finish(r - 1)
        return carry

    lax.fori_loop(1, steps, forward_round, 0)
    upper_send(steps - 1)
    upper_own(steps - 1)
    upper_finish(steps - 1)

    dstate_l[...] = jnp.zeros_like(dstate_l)
    dstate_u[...] = jnp.zeros_like(dstate_u)
    da_l[...] = jnp.zeros_like(da_l)

    def bcopy_l(t):
        return remote(dal.at[me, t], dal.at[me, t], bs_l.at[t], br_l.at[t])

    def bcopy_u(t):
        return remote(dau.at[me, t], dau.at[me, t], bs_u.at[t], br_u.at[t])

    def gate_grads(dy, dstate, save, keep_now, t):
        gate_in, forget, cand, gate_out = save[t, 0], save[t, 1], save[t, 2], save[t, 3]
        cell_keep, squashed = save[t, 4], save[t, 5]
        dh = dstate[0] + dy
        dc = dstate[1] + dh * gate_out * (1.0 - squashed * squashed)
        dstate[1] = dc * forget * keep_now
        return (
            dc * cand * gate_in * (1.0 - gate_in),
            dc * cell_keep * forget * (1.0 - forget),
            dc * gate_in * (1.0 - cand * cand),
            dh * squashed * gate_out * (1.0 - gate_out),
        )

    def lower_back_start(t):
        grads = gate_grads(dx_up[...] * lock_ref[...], dstate_l, save_l, keep_ref[t], t)
        for g in range(4):
            da_l[:, g * units : (g + 1) * units] = grads[g][:, :units]
        high, low = split(da_l[...])
        dal[me, t, 0:ROWS] = high
        dal[me, t, ROWS:] = low
        bcopy_l(t).start()

    def upper_back_start(t):
        grads = gate_grads(gout_ref[t], dstate_u, save_u, keep_ref[t], t)
        for g in range(4):
            high, low = split(grads[g])
            dau[me, t, 0:ROWS, g * gate_u : (g + 1) * gate_u] = high
            dau[me, t, ROWS:, g * gate_u : (g + 1) * gate_u] = low
        bcopy_u(t).start()

    def lower_back_part(t, q):
        return fold(dot_nt(dal[q, t], wrec[q]))

    def upper_back_part(t, q):
        grad = dau[q, t]
        return fold(dot_nt(grad, uin[q])), fold(dot_nt(grad, urec[q]))

    def lower_back_own(t):
        acc[:, :wide_k] = lower_back_part(t, me)

    def lower_back_finish(t):
        bcopy_l(t).wait()
        dstate_l[0, :, :wide_k] = keep_ref[t] * (acc[:, :wide_k] + lower_back_part(t, other))

    def upper_back_own(t):
        into_x, into_h = upper_back_part(t, me)
        dx_up[:, :wide_k] = into_x
        dstate_u[0, :, :up_k] = into_h

    def upper_back_finish(t):
        bcopy_u(t).wait()
        into_x, into_h = upper_back_part(t, other)
        dx_up[:, :wide_k] += into_x
        dstate_u[0, :, :up_k] = keep_ref[t] * (dstate_u[0, :, :up_k] + into_h)

    dx_up[...] = jnp.zeros_like(dx_up)
    upper_back_start(steps - 1)
    upper_back_own(steps - 1)
    upper_back_finish(steps - 1)

    def backward_round(r, carry):
        t = steps - r
        lower_back_start(t)
        upper_back_start(t - 1)
        lower_back_own(t)
        upper_back_own(t - 1)
        lower_back_finish(t)
        upper_back_finish(t - 1)
        return carry

    lax.fori_loop(1, steps, backward_round, 0)
    lower_back_start(0)
    bcopy_l(0).wait()

    da_all[...] = jnp.zeros_like(da_all)
    du_all[...] = jnp.zeros_like(du_all)

    def own_order(t, carry):
        for part in range(2):
            rows = slice(part * ROWS, (part + 1) * ROWS)
            for q in range(2):
                for g in range(4):
                    start = (2 * g + q) * units
                    da_all[part, t, :, start : start + units] = dal[
                        q, t, rows, g * units : (g + 1) * units
                    ]
                    start = (2 * g + q) * unit_u
                    du_all[part, t, :, start : start + unit_u] = dau[
                        q, t, rows, g * gate_u : g * gate_u + unit_u
                    ]
        return carry

    lax.fori_loop(0, steps, own_order, 0)

    def place_left(target, row, count, high, low):
        high, low = jnp.transpose(high)[:count], jnp.transpose(low)[:count]
        target[row : row + count, 0:rows_all] = high
        target[row : row + count, rows_all : 2 * rows_all] = low
        target[row : row + count, 2 * rows_all : 3 * rows_all] = high

    def parts_of(stack):
        width = stack.shape[2]
        return [
            stack[0:steps, i * ROWS : (i + 1) * ROWS, :].reshape(rows_all, width) for i in (0, 1)
        ]

    place_left(xh, 0, wide_k, x2[0:rows_all], x2[rows_all:])
    place_left(xh, wide_k, wide_k, *parts_of(hk2))
    lr[...] = jnp.zeros_like(lr)
    place_left(lr, 0, wide_k, *parts_of(ux2))
    place_left(lr, wide_k, up_k, *parts_of(hku2))

    copies = [
        pltpu.make_async_copy(da_all, da_o, out_sem.at[0]),
        pltpu.make_async_copy(du_all, du_o, out_sem.at[1]),
        pltpu.make_async_copy(xh, xh_o, out_sem.at[2]),
        pltpu.make_async_copy(lr, lr_o, out_sem.at[3]),
    ]
    for copy in copies:
        copy.start()

    dx_o[...] = jnp.zeros_like(dx_o)

    def input_grad(cols, width):
        grad = da_all[:, :, :, cols].reshape(2 * rows_all, width)
        y = fold(dot_nt(grad, win_raw[:, cols])).reshape(steps, ROWS, held)
        dx_o[:, :, :held] += y

    def input_grad_step(index, carry):
        input_grad(pl.ds(pl.multiple_of(index * chunk, chunk), chunk), chunk)
        return carry

    lax.fori_loop(0, full // chunk, input_grad_step, 0)
    if full % chunk:
        input_grad(slice(full // chunk * chunk, full), full % chunk)
    for copy in copies:
        copy.wait()


def recurrence(x, keep, lock, gout, wrec, win, uin, urec, words_l, words_u, blo, bup):
    steps = gout.shape[0]
    units, full = wrec.shape
    outs, full_u = urec.shape
    wide_k = ceil_to(units, 16)
    wide = ceil_to(full // 2, 256)
    up_k = ceil_to(outs, 16)
    gate_u = ceil_to(outs, 128)
    up_wide = 4 * gate_u
    lane = ceil_to(units, 128)
    rows_all = steps * ROWS
    vm = pl.BlockSpec(memory_space=pltpu.VMEM)
    hbm = pl.BlockSpec(memory_space=pl.ANY)
    sds = jax.ShapeDtypeStruct
    shared = [
        ((2, steps, ROWS, ceil_to(full, 256)), BF),
        ((2, steps, ROWS, ceil_to(full_u, 256)), BF),
        ((2 * wide_k, 3 * rows_all), BF),
        ((6 * TAIL_ROWS, 3 * rows_all), BF),
    ]
    dma = pltpu.SemaphoreType.DMA
    return pl.pallas_call(
        functools.partial(recurrence_kernel, units),
        out_shape=(sds((steps, ROWS, gate_u), F32), sds((steps, ROWS, wide_k), F32))
        + tuple(sds(*s) for s in shared),
        in_specs=[vm] * 12,
        out_specs=(vm, vm) + (hbm,) * len(shared),
        scratch_shapes=[
            pltpu.VMEM((2, wide_k, wide), BF),
            pltpu.VMEM((2, wide_k, up_wide), BF),
            pltpu.VMEM((2, up_k, up_wide), BF),
            pltpu.VMEM((steps, ROWS, ceil_to(full, 128)), F32),
        ]
        + [pltpu.VMEM(*s) for s in shared]
        + [
            pltpu.VMEM((2 * rows_all, lane), BF),
            pltpu.VMEM((steps + 1, 2 * ROWS, lane), BF),
            pltpu.VMEM((steps, 2 * ROWS, lane), BF),
            pltpu.VMEM((steps + 1, 2 * ROWS, gate_u), BF),
            pltpu.VMEM((2, steps, 2 * ROWS, wide), BF),
            pltpu.VMEM((2, steps, 2 * ROWS, up_wide), BF),
            pltpu.VMEM((2, steps, ROWS, wide), F32),
            pltpu.VMEM((ROWS, wide), F32),
            pltpu.VMEM((steps, ROWS, wide), F32),
            pltpu.VMEM((ROWS, up_wide), F32),
            pltpu.VMEM((steps, ROWS, up_wide), F32),
            pltpu.VMEM((ROWS, wide + lane - units), F32),
            pltpu.VMEM((ROWS, up_wide), F32),
            pltpu.VMEM((steps, 6, ROWS, lane), F32),
            pltpu.VMEM((steps, 6, ROWS, gate_u), F32),
            pltpu.VMEM((ROWS, lane), F32),
            pltpu.VMEM((ROWS, gate_u), F32),
            pltpu.VMEM((ROWS, wide), F32),
            pltpu.VMEM((ROWS, up_wide), F32),
            pltpu.VMEM((2, ROWS, lane), F32),
            pltpu.VMEM((2, ROWS, gate_u), F32),
            pltpu.VMEM((ROWS, lane), F32),
            pltpu.VMEM((ROWS, lane), F32),
        ]
        + [dma((steps,))] * 8
        + [dma((4,))],
        compiler_params=pltpu.CompilerParams(
            vmem_limit_bytes=VMEM_LIMIT, collective_id=0, has_side_effects=True
        ),
    )(x, keep, lock, gout, wrec, win, uin, urec, words_l, words_u, blo, bup)


PANEL = 576
GROUP = 144
HALF = 2 * GROUP
FULL = PANEL + 8
PAIRS = 24
LOWER_PAIRS = 18
SMALLEST = 2.0**-111


def code(group):
    largest = jnp.maximum(jnp.max(jnp.abs(group), axis=0, keepdims=True), SMALLEST)
    step = jnp.floor(jnp.log2(largest) * 64.0).astype(jnp.int32) + 2
    return step, 32767.0 * jnp.exp2(step.astype(F32) * (-1.0 / 64.0))


def factor(step):
    return jnp.exp2(step.astype(F32) * (1.0 / 64.0)) * (1.0 / 32767.0)


def encode(a, b):
    step_a, up_a = code(a)
    step_b, up_b = code(b)
    word_a = jnp.round(a * up_a).astype(jnp.int32)
    word_b = jnp.round(b * up_b).astype(jnp.int32)
    return (word_a << 16) | (word_b & 0xFFFF), step_a, step_b


def decode(words, step_a, step_b):
    a = (words >> 16).astype(F32) * factor(step_a)
    b = ((words << 16) >> 16).astype(F32) * factor(step_b)
    return a, b


def sum_kernel(
    xh,
    lr,
    da,
    du,
    out,
    grads,
    mine,
    send1,
    recv1,
    send2,
    recv2,
    send3,
    recv3,
    shard,
    scales,
    panel,
    send_sem,
    recv_sem,
    copy_sem,
):
    dp = lax.axis_index("dp")
    pipe = lax.axis_index("pipe")
    place = [lax.rem(dp, 4), lax.rem(lax.div(dp, 4), 4), lax.div(dp, 16)]
    stride = [1, 4, 16]

    def peer(axis, distance):
        moved = lax.rem(place[axis] + (distance + 4), 4)
        return {"pipe": pipe, "dp": dp + (moved - place[axis]) * stride[axis]}

    barrier = pltpu.get_barrier_semaphore()
    for axis in range(3):
        for distance in (1, 2, 3):
            pl.semaphore_signal(
                barrier, inc=1, device_id=peer(axis, distance), device_id_type=MESH
            )
    pl.semaphore_wait(barrier, 9)

    def remote(src, dst, number, axis, distance):
        return pltpu.make_async_remote_copy(
            src_ref=src,
            dst_ref=dst,
            send_sem=send_sem.at[number],
            recv_sem=recv_sem.at[number],
            device_id=peer(axis, distance),
            device_id_type=MESH,
        )

    third = xh.shape[1] // 3

    def right(source, cols):
        high = source[0, :, cols]
        return jnp.concatenate([high, high, source[1, :, cols]], axis=0)

    def compute(pair):
        @pl.when(pair < LOWER_PAIRS)
        def _():
            cols = pl.ds(pl.multiple_of(pair * 256, 256), 256)
            y = dot_nn(xh[...], right(da, cols))
            for n in range(2):
                for ab in range(2):
                    grads[ab, n] = y[ab * PANEL : (ab + 1) * PANEL, n * 128 : (n + 1) * 128]

        @pl.when(pair >= LOWER_PAIRS)
        def _():
            index = pair - LOWER_PAIRS
            cols = pl.ds(pl.multiple_of(index * 256, 256), 256)
            middle = right(du, cols)
            y = dot_nn(lr[0:PANEL], middle)
            top = dot_nn(lr[PANEL : 2 * PANEL - TAIL_ROWS], middle)
            tail = right(du, pl.ds(6 * 256, 256))
            rows = pl.ds(pl.multiple_of(index * TAIL_ROWS, 16), TAIL_ROWS)
            bottom = dot_nn(lr[rows], tail)
            for n in range(2):
                grads[0, n] = y[:, n * 128 : (n + 1) * 128]
                grads[1, n, 0 : PANEL - TAIL_ROWS] = top[:, n * 128 : (n + 1) * 128]
                grads[1, n, PANEL - TAIL_ROWS :] = bottom[:, n * 128 : (n + 1) * 128]

    def rows_of(group):
        return pl.ds(pl.multiple_of(group * GROUP, 8), GROUP)

    def steps_at(ref, base, group):
        return ref[pl.ds(base + 2 * group, 1), :], ref[pl.ds(base + 2 * group + 1, 1), :]

    def store_code(ref, base, group, words, step_a, step_b):
        ref[rows_of(group), :] = words
        ref[pl.ds(base + 2 * group, 1), :] = step_a
        ref[pl.ds(base + 2 * group + 1, 1), :] = step_b

    def arrived(ref, base, group):
        return decode(ref[rows_of(group), :], *steps_at(ref, base, group))

    def stage1(k, way, kind):
        number = (k * 2 + way) * 3 + kind
        return remote(
            send1.at[k, way, kind], recv1.at[k, way, kind], number, k, 1 if way == 0 else -1
        )

    def pair_at(k, offset, half):
        return k * 8 + lax.rem(place[k] + (offset + 4), 4) * 2 + half

    def pack_pair(target, added):
        def group_step(index, carry):
            n, group = lax.div(index, 4), lax.rem(index, 4)
            a, b = grads[0, n, rows_of(group), :], grads[1, n, rows_of(group), :]
            if added is not None:
                more_a, more_b = arrived(added.at[n], PANEL, group)
                a, b = a + more_a, b + more_b
            store_code(target.at[n], PANEL, group, *encode(a, b))
            return carry

        lax.fori_loop(0, 8, group_step, 0)

    ways = ((0, 1), (1, -1))
    for k in range(3):
        for way, sign in ways:
            compute(pair_at(k, 2, way))
            pack_pair(send1.at[k, way, 0], None)
            stage1(k, way, 0).start()
    for k in range(3):
        for way, sign in ways:
            compute(pair_at(k, sign, 1 - way))
            pack_pair(send1.at[k, way, 1], None)
            stage1(k, way, 1).start()
    for k in range(3):
        for way, sign in ways:
            compute(pair_at(k, sign, way))
            stage1(k, way, 0).wait_recv()
            pack_pair(send1.at[k, way, 2], recv1.at[k, way, 0])
            stage1(k, way, 2).start()
    for k in range(3):
        for half in range(2):
            compute(pair_at(k, 0, half))
            for ab in range(2):
                mine[k, ab, 2 * half : 2 * half + 2] = grads[ab]

    def add_pair(k, half, first, second):
        def group_step(index, carry):
            n, group = lax.div(index, 4), lax.rem(index, 4)
            a1, b1 = arrived(first.at[n], PANEL, group)
            a2, b2 = arrived(second.at[n], PANEL, group)
            mine[k, 0, 2 * half + n, rows_of(group), :] += a1 + a2
            mine[k, 1, 2 * half + n, rows_of(group), :] += b1 + b2
            return carry

        lax.fori_loop(0, 8, group_step, 0)

    def stage2(k, way, kind):
        number = 18 + (k * 2 + way) * 3 + kind
        axis = (k + 1) % 3
        return remote(
            send2.at[k, way, kind], recv2.at[k, way, kind], number, axis, 1 if way == 0 else -1
        )

    def pack_half(k, offset, half, target, added):
        block = lax.rem(place[(k + 1) % 3] + (offset + 4), 4)
        for group in range(2):
            rows = slice(half * HALF + group * GROUP, half * HALF + (group + 1) * GROUP)
            a, b = mine[k, 0, block, rows, :], mine[k, 1, block, rows, :]
            if added is not None:
                more_a, more_b = arrived(added, HALF, group)
                a, b = a + more_a, b + more_b
            store_code(target, HALF, group, *encode(a, b))

    for k in range(3):
        stage1(k, 0, 1).wait_recv()
        stage1(k, 1, 1).wait_recv()
        stage1(k, 0, 2).wait_recv()
        stage1(k, 1, 2).wait_recv()
        add_pair(k, 0, recv1.at[k, 0, 2], recv1.at[k, 1, 1])
        add_pair(k, 1, recv1.at[k, 0, 1], recv1.at[k, 1, 2])
        for way, sign in ways:
            pack_half(k, 2, way, send2.at[k, way, 0], None)
            stage2(k, way, 0).start()
        for way, sign in ways:
            pack_half(k, sign, 1 - way, send2.at[k, way, 1], None)
            stage2(k, way, 1).start()
    for k in range(3):
        for way, sign in ways:
            stage2(k, way, 0).wait_recv()
            pack_half(k, sign, way, send2.at[k, way, 2], recv2.at[k, way, 0])
            stage2(k, way, 2).start()

    def stage3(k, d):
        number = 36 + k * 3 + d - 1
        return remote(send3.at[k, d - 1], recv3.at[k, d - 1], number, (k + 2) % 3, d)

    for k in range(3):
        block = place[(k + 1) % 3]
        stage2(k, 0, 1).wait_recv()
        stage2(k, 1, 1).wait_recv()
        stage2(k, 0, 2).wait_recv()
        stage2(k, 1, 2).wait_recv()
        for group in range(4):
            half, inner = group // 2, group % 2
            first = recv2.at[k, 0, 2 - half]
            second = recv2.at[k, 1, 1 + half]
            a1, b1 = arrived(first, HALF, inner)
            a2, b2 = arrived(second, HALF, inner)
            rows = slice(group * GROUP, (group + 1) * GROUP)
            mine[k, 0, block, rows, :] += a1 + a2
            mine[k, 1, block, rows, :] += b1 + b2
        for d in (1, 2, 3):
            group = lax.rem(place[(k + 2) % 3] + d, 4)
            a, b = mine[k, 0, block, rows_of(group), :], mine[k, 1, block, rows_of(group), :]
            store_code(send3.at[k, d - 1], GROUP, 0, *encode(a, b))
            stage3(k, d).start()

    def spread3(k, d):
        group = place[(k + 2) % 3]
        number = 45 + (k * 3 + d - 1) * 2
        data = remote(
            shard.at[k, 0:GROUP], panel.at[k, rows_of(group)], number, (k + 2) % 3, d
        )
        scale = remote(
            shard.at[k, GROUP : GROUP + 8], scales.at[k, d - 1], number + 1, (k + 2) % 3, d
        )
        return data, scale

    def spread3_from(k, d):
        group = lax.rem(place[(k + 2) % 3] + (4 - d), 4)
        number = 45 + (k * 3 + d - 1) * 2
        data = remote(
            shard.at[k, 0:GROUP], panel.at[k, rows_of(group)], number, (k + 2) % 3, d
        )
        scale = remote(
            shard.at[k, GROUP : GROUP + 8], scales.at[k, d - 1], number + 1, (k + 2) % 3, d
        )
        return group, data, scale

    for k in range(3):
        block = place[(k + 1) % 3]
        own = place[(k + 2) % 3]
        a, b = mine[k, 0, block, rows_of(own), :], mine[k, 1, block, rows_of(own), :]
        for d in (1, 2, 3):
            stage3(k, d).wait_recv()
            more_a, more_b = arrived(recv3.at[k, d - 1], GROUP, 0)
            a, b = a + more_a, b + more_b
        store_code(shard.at[k], GROUP, 0, *encode(a, b))
        for d in (1, 2, 3):
            for copy in spread3(k, d):
                copy.start()
        panel[k, rows_of(own), :] = shard[k, 0:GROUP, :]

    def at(k, first, second):
        return out.at[k * 16 + first * 4 + second]

    def turned(axis, distance):
        return lax.rem(place[axis] + (distance + 4), 4)

    def spread2(k, way, src, first, second):
        return remote(src, at(k, first, second), 63 + k * 4 + way, (k + 1) % 3, 1 - 2 * way)

    def pass2(k, way, first, second):
        rows = slice(0, HALF) if way == 0 else slice(HALF, FULL)
        ref = at(k, first, second).at[rows]
        return remote(ref, ref, 63 + k * 4 + 2 + way, (k + 1) % 3, 1 - 2 * way)

    def spread1(k, way, order, src, first, second):
        return remote(src, at(k, first, second), 75 + (k * 2 + way) * 6 + order, k, 1 - 2 * way)

    offsets = (0, -1, 1, 2)
    for k in range(3):
        merged = shard[k, GROUP : GROUP + 8, :]
        row = lax.broadcasted_iota(jnp.int32, (8, 128), 0)
        own = place[(k + 2) % 3]
        total = jnp.zeros((8, 128), jnp.int32)
        for d in (0, 1, 2, 3):
            if d == 0:
                group, tile = own, merged
            else:
                group, data, scale = spread3_from(k, d)
                data.wait_recv()
                scale.wait_recv()
                tile = scales[k, d - 1]
            total = jnp.where(row == 2 * group, tile[0:1], total)
            total = jnp.where(row == 2 * group + 1, tile[1:2], total)
        panel[k, PANEL:FULL, :] = total
        first, second = place[k], place[(k + 1) % 3]
        for way in range(2):
            spread2(k, way, panel.at[k], first, second).start()
        pltpu.make_async_copy(panel.at[k], at(k, first, second), copy_sem.at[k]).start()
        for way in range(2):
            spread1(k, way, 0, panel.at[k], first, second).start()
    for k in range(3):
        first = place[k]
        for way in range(2):
            second = turned((k + 1) % 3, 2 * way - 1)
            spread2(k, way, panel.at[k], first, second).wait_recv()
            pass2(k, way, first, second).start()
            for way1 in range(2):
                src = at(k, first, second)
                spread1(k, way1, 1 + way, src, first, second).start()
    for k in range(3):
        first, second = place[k], turned((k + 1) % 3, 2)
        for way in range(2):
            pass2(k, way, first, second).wait_recv()
        for way1 in range(2):
            src = at(k, first, second)
            spread1(k, way1, 3, src, first, second).start()

    def pass1(k, way, order, first):
        ref = at(k, first, turned((k + 1) % 3, offsets[order]))
        return remote(ref, ref, 75 + (k * 2 + way) * 6 + 4 + order % 2, k, 1 - 2 * way)

    passed = ((0, 0), (1, 2), (0, 1), (1, 3))
    seen = set()
    for way, order in passed:
        for k in range(3):
            first = turned(k, 2 * way - 1)
            second = turned((k + 1) % 3, offsets[order])
            spread1(k, way, order, panel.at[k], first, second).wait_recv()
            seen.add((k, way, order))
            pass1(k, way, order, first).start()
    for k in range(3):
        for way in range(2):
            for order in range(4):
                if (k, way, order) not in seen:
                    first = turned(k, 2 * way - 1)
                    second = turned((k + 1) % 3, offsets[order])
                    spread1(k, way, order, panel.at[k], first, second).wait_recv()
    for way, order in passed:
        for k in range(3):
            pass1(k, way, order, turned(k, 2)).wait_recv()

    for k in range(3):
        for way in range(2):
            for kind in range(3):
                stage1(k, way, kind).wait_send()
                stage2(k, way, kind).wait_send()
        for d in (1, 2, 3):
            stage3(k, d).wait_send()
            for copy in spread3(k, d):
                copy.wait_send()
        first, second = place[k], place[(k + 1) % 3]
        pltpu.make_async_copy(panel.at[k], at(k, first, second), copy_sem.at[k]).wait()
        for way in range(2):
            spread2(k, way, panel.at[k], first, second).wait_send()
            pass2(k, way, first, turned((k + 1) % 3, 2 * way - 1)).wait_send()
            for order in range(4):
                second_now = turned((k + 1) % 3, offsets[order])
                src = panel.at[k] if order == 0 else at(k, first, second_now)
                spread1(k, way, order, src, first, second_now).wait_send()
        for way, order in passed:
            pass1(k, way, order, turned(k, 2 * way - 1)).wait_send()


def summed_panels(xh, lr, da, du):
    vm = pl.BlockSpec(memory_space=pltpu.VMEM)
    i32 = jnp.int32
    messages = 75 + 36
    dma = pltpu.SemaphoreType.DMA
    return pl.pallas_call(
        sum_kernel,
        out_shape=jax.ShapeDtypeStruct((2 * PAIRS, FULL, 128), i32),
        in_specs=[vm] * 4,
        out_specs=pl.BlockSpec(memory_space=pl.ANY),
        scratch_shapes=[
            pltpu.VMEM((2, 2, PANEL, 128), F32),
            pltpu.VMEM((3, 2, 4, PANEL, 128), F32),
            pltpu.VMEM((3, 2, 3, 2, FULL, 128), i32),
            pltpu.VMEM((3, 2, 3, 2, FULL, 128), i32),
            pltpu.VMEM((3, 2, 3, HALF + 8, 128), i32),
            pltpu.VMEM((3, 2, 3, HALF + 8, 128), i32),
            pltpu.VMEM((3, 3, GROUP + 8, 128), i32),
            pltpu.VMEM((3, 3, GROUP + 8, 128), i32),
            pltpu.VMEM((3, GROUP + 8, 128), i32),
            pltpu.VMEM((3, 3, 8, 128), i32),
            pltpu.VMEM((3, FULL, 128), i32),
            dma((messages,)),
            dma((messages,)),
            dma((3,)),
        ],
        compiler_params=pltpu.CompilerParams(
            vmem_limit_bytes=VMEM_LIMIT, collective_id=1, has_side_effects=True
        ),
    )(xh, lr, da, du)


def unpack_kernel(panels, words_l, words_u, low_in, low_rec, low_bias, up_in, up_rec, up_bias, tail):
    step = pl.program_id(0)
    units, outs = low_in.shape[0], up_rec.shape[0]

    def values(n, ab):
        parts = []
        for group in range(4):
            words = panels[n, group * GROUP : (group + 1) * GROUP, :]
            scale = factor(panels[n, PANEL + 2 * group + ab : PANEL + 2 * group + ab + 1, :])
            half = (words >> 16) if ab == 0 else ((words << 16) >> 16)
            parts.append(half.astype(F32) * scale)
        return jnp.concatenate(parts, axis=0)

    def keep_bits(words_ref, block, n, rows):
        part = lax.div(block, 10)
        held = words_ref[:, pl.ds(pl.multiple_of(part * 128, 128), 128)] * 2
        column = lax.broadcasted_iota(jnp.int32, (1, 128), 1) + (block * 256 + n * 128)
        index = (column * 52429) >> 20
        bit = column - index * 20
        index = jnp.clip(index - part * 128, 0, 127)
        index = jnp.broadcast_to(index, held.shape)
        found = jnp.take_along_axis(held, index, axis=1, mode="promise_in_bounds")
        return ((found >> bit) & 2).astype(F32)[:rows]

    for n in range(2):
        cols = slice(n * 128, (n + 1) * 128)

        @pl.when(step < LOWER_PAIRS)
        def _():
            a = values(n, 0)
            low_in[:, cols] = a[:units]
            low_bias[:, cols] = a[units : units + 1]
            b = values(n, 1)[:units]
            low_rec[:, cols] = b * keep_bits(words_l, step, n, units)

        @pl.when((step >= LOWER_PAIRS) & (step < PAIRS))
        def _():
            index = step - LOWER_PAIRS
            a = values(n, 0)
            up_in[:, cols] = a[:units]
            up_bias[:, cols] = a[units : units + 1]
            b = values(n, 1)
            up_rec[:, cols] = b[:outs] * keep_bits(words_u, index, n, outs)
            if n == 0:
                rows = pl.ds(pl.multiple_of(index * TAIL_ROWS, 8), TAIL_ROWS)
                tail[rows, :] = b[PANEL - TAIL_ROWS :]

    @pl.when(step == PAIRS)
    def _():
        up_in[:, :128] = tail[:units]
        up_bias[:, :128] = tail[units : units + 1]
        index = jnp.int32(PAIRS - LOWER_PAIRS)
        up_rec[:, :128] = tail[PANEL : PANEL + outs] * keep_bits(words_u, index, 0, outs)


def unpack(panels, words_l, words_u, units, full, outs, full_u):
    sds = jax.ShapeDtypeStruct
    lower = lambda i: (0, jnp.minimum(i, LOWER_PAIRS - 1))
    upper = lambda i: (0, jnp.maximum(i - LOWER_PAIRS, 0))
    whole = lambda i: (0, 0)
    return pl.pallas_call(
        unpack_kernel,
        grid=(PAIRS + 1,),
        out_shape=(
            sds((units, full), F32),
            sds((units, full), F32),
            sds((1, full), F32),
            sds((units, full_u), F32),
            sds((outs, full_u), F32),
            sds((1, full_u), F32),
        ),
        in_specs=[
            pl.BlockSpec((2, FULL, 128), lambda i: (jnp.minimum(i, PAIRS - 1), 0, 0)),
            pl.BlockSpec(words_l.shape, whole),
            pl.BlockSpec(words_u.shape, whole),
        ],
        out_specs=(
            pl.BlockSpec((units, 256), lower),
            pl.BlockSpec((units, 256), lower),
            pl.BlockSpec((1, 256), lower),
            pl.BlockSpec((units, 256), upper),
            pl.BlockSpec((outs, 256), upper),
            pl.BlockSpec((1, 256), upper),
        ),
        scratch_shapes=[pltpu.VMEM((6 * TAIL_ROWS, 128), F32)],
        compiler_params=pltpu.CompilerParams(vmem_limit_bytes=VMEM_LIMIT),
    )(panels, words_l, words_u)


def by_half(weight, units, gate, wide):
    parts = jnp.transpose(weight.reshape(1, 4, 2, units), (2, 0, 1, 3))
    parts = jnp.pad(parts, ((0, 0), (0, 0), (0, 0), (0, gate - units))).reshape(2, 1, 4 * gate)
    return jnp.pad(parts, ((0, 0), (0, 0), (0, wide - 4 * gate)))


def body(
    inputs,
    lower_lock,
    upper_lock,
    resets,
    lower_input,
    lower_recur,
    lower_bias,
    lower_drop,
    upper_input,
    upper_recur,
    upper_bias,
    upper_drop,
    grad_out,
):
    me = lax.axis_index("pipe")
    streams, steps, width = inputs.shape
    units, full = lower_recur.shape
    outs, full_u = upper_recur.shape
    wide = ceil_to(full // 2, 256)
    lane = ceil_to(units, 128)
    gate_u = ceil_to(outs, 128)
    pad_rows = ROWS - streams

    def own(array, axis, size):
        return lax.dynamic_slice_in_dim(array, me * size, size, axis)

    def padded(array, rows, lanes):
        return jnp.pad(array, ((0, rows - array.shape[0]), (0, lanes - array.shape[1])))

    words_l = padded(own(lower_drop, 0, units), ceil_to(units, 16), 256)
    words_u = padded(own(upper_drop, 0, outs), ceil_to(outs, 16), 128)

    def bias_part(bias, half_units, gate, wide_to):
        placed = jnp.zeros((2 * bias.shape[0],), F32)
        placed = lax.dynamic_update_slice(placed, bias.astype(F32), (me * bias.shape[0],))
        return by_half(placed, half_units, gate, wide_to)

    blo = bias_part(lower_bias, units, units, wide)
    bup = bias_part(upper_bias, outs, gate_u, 4 * gate_u)

    keep = (1 - resets).astype(F32).T
    keep = jnp.pad(keep, ((0, 1), (0, pad_rows)))[:, :, None]
    lock_low = own(lower_lock.astype(F32) * 1.25, 1, units)
    lock_up = own(upper_lock.astype(F32) * 1.25, 1, units)
    x = jnp.transpose(own(inputs, 2, units) * lock_low[:, None, :], (1, 0, 2))
    x = jnp.pad(x, ((0, 0), (0, pad_rows), (0, 1)), constant_values=1.0)
    x = jnp.pad(x, ((0, 0), (0, 0), (0, lane - units - 1))).reshape(steps * ROWS, lane)
    lock = jnp.pad(lock_up, ((0, pad_rows), (0, lane - units)))
    gout = jnp.transpose(own(grad_out, 2, outs), (1, 0, 2))
    gout = jnp.pad(gout, ((0, 0), (0, pad_rows), (0, gate_u - outs)))

    hid, dx, da, du, xh, lr = recurrence(
        x,
        keep,
        lock,
        gout,
        lower_recur,
        lower_input,
        upper_input,
        upper_recur,
        words_l,
        words_u,
        blo,
        bup,
    )
    hidden_out = jnp.transpose(hid[:, :streams, :outs], (1, 0, 2))
    grad_inputs = jnp.transpose(dx[:, :streams, :units], (1, 0, 2)) * lock_low[:, None, :]

    rows_all = steps * ROWS
    panels = summed_panels(
        xh, lr, da.reshape(2, rows_all, da.shape[3]), du.reshape(2, rows_all, du.shape[3])
    )
    low_in, low_rec, low_bias, up_in, up_rec, up_bias = unpack(
        panels, words_l, words_u, units, full, outs, full_u
    )
    return (
        hidden_out,
        grad_inputs,
        low_in,
        low_rec,
        own(low_bias[0], 0, full // 2),
        up_in,
        up_rec,
        own(up_bias[0], 0, full_u // 2),
    )


def solution(mesh):
    return jax.shard_map(
        body,
        mesh=mesh,
        in_specs=(
            P("dp", None, None),
            P("dp", None),
            P("dp", None),
            P("dp", None),
            P("pipe", None),
            P("pipe", None),
            P("pipe"),
            P(),
            P("pipe", None),
            P("pipe", None),
            P("pipe"),
            P(),
            P("dp", None, None),
        ),
        out_specs=(
            P("dp", None, "pipe"),
            P("dp", None, "pipe"),
            P("pipe", None),
            P("pipe", None),
            P("pipe"),
            P("pipe", None),
            P("pipe", None),
            P("pipe"),
        ),
        check_vma=False,
    )
```

```python
import functools

import jax
import jax.numpy as jnp
from jax import lax
from jax.experimental import pallas as pl
from jax.experimental.pallas import tpu as pltpu
from jax.sharding import PartitionSpec as P

BF = jnp.bfloat16
F32 = jnp.float32
MESH = pl.DeviceIdType.MESH
ROWS = 16
VMEM_LIMIT = 62 * 2**20
TAIL_ROWS = 368
SUM_VMEM = 47 * 2**20
UNPACK_VMEM = 24 * 2**20


def ceil_to(value, multiple):
    return -(-value // multiple) * multiple


def split(value):
    high = value.astype(BF)
    low = (value - high.astype(F32)).astype(BF)
    return high, low


def fold(stacked):
    half = stacked.shape[0] // 2
    return stacked[:half] + stacked[half:]


def dot_nn(a, b):
    return jnp.dot(a, b, preferred_element_type=F32)


def dot_nt(a, b):
    return lax.dot_general(a, b, (((1,), (1,)), ((), ())), preferred_element_type=F32)


def drop_bits(words, start):
    column = lax.broadcasted_iota(jnp.int32, (1, 128), 1) + start
    index = (column * 52429) >> 20
    bit = column - index * 20
    first = start // 2560 * 128
    held = words[:, first : first + 128]
    index = jnp.broadcast_to(index - first, held.shape)
    found = jnp.take_along_axis(held, index, axis=1, mode="promise_in_bounds")
    return (found >> bit) & 2


def recurrence_kernel(
    units,
    inputs,
    lower_lock,
    upper_lock,
    resets,
    grad_out,
    lower_drop,
    upper_drop,
    lower_bias,
    upper_bias,
    wrec_in,
    win_in,
    uin_in,
    urec_in,
    hid_o,
    dx_o,
    da_o,
    du_o,
    xh_o,
    lr_o,
    flags_o,
    flags_u_o,
    wrec_raw,
    win_raw,
    uin_raw,
    urec_raw,
    flag_rows,
    words_l,
    words_u,
    keep_ref,
    lock_low,
    lock_ref,
    gout_ref,
    blo,
    bup,
    wrec_t,
    uin_t,
    urec_t,
    wrec,
    uin,
    urec,
    da_all,
    du_all,
    xh,
    lr,
    x2,
    hk2,
    ux2,
    hku2,
    dal,
    dau,
    proj,
    send_l,
    recv_l,
    send_u,
    recv_u,
    act_l,
    act_u,
    save_l,
    save_u,
    cell_l,
    cell_u,
    da_l,
    da_u,
    dstate_l,
    dstate_u,
    dx_up,
    acc,
    dx,
    fs_l,
    fr_l,
    fs_u,
    fr_u,
    bs_l,
    br_l,
    bs_u,
    br_u,
    in_sem,
    out_sem,
    flag_sem,
):
    streams, steps = resets.shape
    me = lax.axis_index("pipe")
    other = 1 - me
    peer = {"pipe": other}
    wide_k = wrec.shape[1]
    wide = wrec.shape[2]
    up_wide = uin.shape[2]
    up_k = urec.shape[1]
    lane = act_l.shape[1] - wide + units

    barrier = pltpu.get_barrier_semaphore()
    pl.semaphore_signal(barrier, inc=1, device_id=peer, device_id_type=MESH)
    loads = [
        pltpu.make_async_copy(win_in, win_raw, in_sem.at[0]),
        pltpu.make_async_copy(wrec_in, wrec_raw, in_sem.at[1]),
        pltpu.make_async_copy(uin_in, uin_raw, in_sem.at[2]),
        pltpu.make_async_copy(urec_in, urec_raw, in_sem.at[3]),
    ]
    for load in loads:
        load.start()
    pl.semaphore_wait(barrier, 1)

    def remote(src, dst, send_sem, recv_sem):
        return pltpu.make_async_remote_copy(
            src_ref=src,
            dst_ref=dst,
            send_sem=send_sem,
            recv_sem=recv_sem,
            device_id=peer,
            device_id_type=MESH,
        )

    full = wrec_raw.shape[1]
    held = wrec_raw.shape[0]
    held_u = urec_raw.shape[0]
    full_u = urec_raw.shape[1]
    unit_u = full_u // 8
    gate_u = up_wide // 4
    rows_all = steps * ROWS

    def to_rows(value, lanes, filler=0.0):
        more = lanes - value.shape[1]
        if more:
            value = jnp.concatenate([value, jnp.full((streams, more), filler, F32)], axis=1)
        return jnp.concatenate([value, jnp.zeros((ROWS - streams, lanes), F32)], axis=0)

    keep_ref[...] = jnp.zeros_like(keep_ref)
    for t in range(steps):
        now = 1.0 - resets[:, t : t + 1].astype(F32)
        keep_ref[t] = to_rows(jnp.broadcast_to(now, (streams, 128)), 128)
    blo[...] = jnp.zeros_like(blo)
    bup[...] = jnp.zeros_like(bup)
    def place_words(target, packed):
        rows, lanes = packed.shape
        more = ceil_to(lanes, 128) - lanes
        packed = jnp.concatenate([packed, jnp.zeros((rows, more), jnp.int32)], axis=1)
        more = ceil_to(rows, 128) - rows
        packed = jnp.concatenate([packed, jnp.zeros((more, packed.shape[1]), jnp.int32)], axis=0)
        target[...] = jnp.transpose(packed)[: target.shape[0]]

    for half in range(2):

        @pl.when(me == half)
        def _(half=half):
            mine = slice(half * units, (half + 1) * units)
            lock_low[...] = to_rows(lower_lock[:, mine].astype(F32) * 1.25, lane)
            lock_ref[...] = to_rows(upper_lock[:, mine].astype(F32) * 1.25, lane)
            one = jnp.full((streams, 1), 1.0, F32)
            for t in range(steps):
                now = inputs[:, t, mine] * lock_low[0:streams, 0:units]
                now = to_rows(jnp.concatenate([now, one], axis=1), lane)
                high, low = split(now)
                x2[t * ROWS : (t + 1) * ROWS] = high
                x2[rows_all + t * ROWS : rows_all + (t + 1) * ROWS] = low
                out = grad_out[:, t, half * unit_u : (half + 1) * unit_u]
                gout_ref[t] = to_rows(out, gate_u)
            place_words(words_l, lower_drop[:, mine])
            place_words(words_u, upper_drop[:, half * held_u : (half + 1) * held_u])
            bias = lower_bias[...].astype(F32)
            bias_u = upper_bias[...].astype(F32)
            for q in range(2):
                for i in range(2):
                    g = 2 * half + i
                    start = (2 * i + q) * units
                    blo[q, :, g * units : (g + 1) * units] = bias[:, start : start + units]
                    start = (2 * i + q) * unit_u
                    bup[q, :, g * gate_u : g * gate_u + unit_u] = bias_u[
                        :, start : start + unit_u
                    ]

    loads[0].wait()
    proj[:, :, :, wide - 128 :] = jnp.zeros((2, steps, ROWS, 128), F32)
    for q in range(2):
        for g in range(4):
            start, stop = (2 * g + q) * units, (2 * g + q + 1) * units
            first, last = start // 128 * 128, min(ceil_to(stop, 128), full)
            y = fold(dot_nn(x2[:, :held], win_raw[:, first:last]))
            y = y[:, start - first : stop - first] + blo[q, :, g * units : (g + 1) * units]
            proj[q, :, :, g * units : (g + 1) * units] = y.reshape(steps, ROWS, units)

    for load in loads[1:]:
        load.wait()
    wrec[:, :, wide - 128 :] = jnp.zeros((2, wide_k, 128), BF)
    wrec[:, wide_k - ROWS :, :] = jnp.zeros((2, ROWS, wide), BF)
    uin[...] = jnp.zeros_like(uin)
    urec[...] = jnp.zeros_like(urec)

    def flag_copy(row, slot):
        rows = pl.ds(row, ROWS)
        return pltpu.make_async_copy(flag_rows.at[slot], flags_o.at[rows], flag_sem.at[slot])

    def prepare_lower(row, count, slot):
        words = words_l[pl.ds(row, ROWS), :] * 2
        parts = [drop_bits(words, 128 * n) for n in range(ceil_to(full, 128) // 128)]
        scale = jnp.concatenate(parts, axis=1).astype(F32)
        flag_rows[slot] = scale.astype(BF)
        flag_copy(row, slot).start()
        weight = wrec_raw[pl.ds(row, count), :].astype(F32) * scale[:count, :full]
        weight = weight.astype(BF)
        for q in range(2):
            for g in range(4):
                start = (2 * g + q) * units
                wrec[q, pl.ds(row, count), g * units : (g + 1) * units] = weight[
                    :, start : start + units
                ]

    def prepare_block(index, carry):
        row = pl.multiple_of(index * ROWS, ROWS)
        slot = lax.rem(index, 2)

        @pl.when(index >= 2)
        def _():
            flag_copy(row - 2 * ROWS, slot).wait()

        prepare_lower(row, ROWS, slot)
        return carry

    blocks = held // ROWS
    lax.fori_loop(0, blocks, prepare_block, 0)
    flag_copy((blocks - 2) * ROWS, blocks % 2).wait()
    prepare_lower(blocks * ROWS, held % ROWS, blocks % 2)
    flag_copy((blocks - 1) * ROWS, (blocks - 1) % 2).wait()
    flag_copy(blocks * ROWS, blocks % 2).wait()

    def place_upper(target, row, count, weight):
        for q in range(2):
            for g in range(4):
                start = (2 * g + q) * unit_u
                target[q, pl.ds(row, count), g * gate_u : g * gate_u + unit_u] = weight[
                    :, start : start + unit_u
                ]

    def upper_in_block(index, carry):
        row = pl.multiple_of(index * ROWS, ROWS)
        place_upper(uin, row, ROWS, uin_raw[pl.ds(row, ROWS), :])
        return carry

    lax.fori_loop(0, held // ROWS, upper_in_block, 0)
    if held % ROWS:
        row = held // ROWS * ROWS
        place_upper(uin, row, held % ROWS, uin_raw[row:held, :])

    def upper_rec_block(row, count):
        words = words_u[pl.ds(row, ROWS), :] * 2
        parts = [drop_bits(words, 128 * n) for n in range(ceil_to(full_u, 128) // 128)]
        scale = jnp.concatenate(parts, axis=1)[:count, :full_u].astype(F32)
        weight = (urec_raw[pl.ds(row, count), :].astype(F32) * scale).astype(BF)
        urec_raw[pl.ds(row, count), :] = scale.astype(BF)
        place_upper(urec, row, count, weight)

    def upper_rec_step(index, carry):
        upper_rec_block(pl.multiple_of(index * ROWS, ROWS), ROWS)
        return carry

    lax.fori_loop(0, held_u // ROWS, upper_rec_step, 0)
    if held_u % ROWS:
        upper_rec_block(held_u // ROWS * ROWS, held_u % ROWS)

    copies = [
        pltpu.make_async_copy(urec_raw, flags_u_o, out_sem.at[4]),
    ]
    for copy in copies:
        copy.start()
    for q in range(2):
        wrec_t[q] = jnp.transpose(wrec[q])
        uin_t[q] = jnp.transpose(uin[q])
        urec_t[q] = jnp.transpose(urec[q])

    act_l[...] = jnp.zeros_like(act_l)
    hk2[...] = jnp.zeros_like(hk2)
    ux2[...] = jnp.zeros_like(ux2)
    hku2[...] = jnp.zeros_like(hku2)
    cell_l[...] = jnp.zeros_like(cell_l)
    cell_u[...] = jnp.zeros_like(cell_u)

    def fcopy_l(t):
        return remote(send_l, recv_l.at[t], fs_l.at[t], fr_l.at[t])

    def fcopy_u(t):
        return remote(send_u, recv_u.at[t], fs_u.at[t], fr_u.at[t])

    def lower_send(t, first):
        if first:
            send_l[...] = proj[other, t]
        else:
            send_l[...] = fold(dot_nn(hk2[t, :, :wide_k], wrec[other])) + proj[other, t]
        fcopy_l(t).start()

    def lower_own(t, first):
        if first:
            act_l[:, :wide] = proj[me, t]
        else:
            act_l[:, :wide] = fold(dot_nn(hk2[t, :, :wide_k], wrec[me])) + proj[me, t]

    def upper_part(t, q):
        y = dot_nn(ux2[t, :, :wide_k], uin[q]) + dot_nn(hku2[t, :, :up_k], urec[q])
        return fold(y) + bup[q]

    def upper_send(t):
        send_u[...] = upper_part(t, other)
        fcopy_u(t).start()

    def upper_own(t):
        act_u[...] = upper_part(t, me)

    def keep_at(t, lanes):
        return jnp.concatenate([keep_ref[t]] * (ceil_to(lanes, 128) // 128), axis=1)[
            :, :lanes
        ]

    def cell_update(a_in, a_forget, a_cand, a_out, cell, keep_now, save, t):
        gate_in = jax.nn.sigmoid(a_in)
        forget = jax.nn.sigmoid(a_forget)
        cand = jnp.tanh(a_cand)
        gate_out = jax.nn.sigmoid(a_out)
        cell_keep = cell[...] * keep_now
        cell_new = forget * cell_keep + gate_in * cand
        squashed = jnp.tanh(cell_new)
        cell[...] = cell_new
        save[t, 0] = gate_in
        save[t, 1] = forget
        save[t, 2] = cand
        save[t, 3] = gate_out
        save[t, 4] = cell_keep
        save[t, 5] = squashed
        return gate_out * squashed

    def lower_finish(t):
        fcopy_l(t).wait()
        act_l[:, :wide] += recv_l[t]
        hidden = cell_update(
            act_l[:, 0:lane],
            act_l[:, units : units + lane],
            act_l[:, 2 * units : 2 * units + lane],
            act_l[:, 3 * units : 3 * units + lane],
            cell_l,
            keep_at(t, lane),
            save_l,
            t,
        )
        high, low = split(hidden * keep_at(t + 1, lane))
        hk2[t + 1, 0:ROWS] = high
        hk2[t + 1, ROWS:] = low
        ones_at = lax.broadcasted_iota(jnp.int32, (ROWS, lane), 1) == units
        high, low = split(jnp.where(ones_at, 1.0, hidden * lock_ref[...]))
        ux2[t, 0:ROWS] = high
        ux2[t, ROWS:] = low

    def upper_finish(t):
        fcopy_u(t).wait()
        a = act_u[...] + recv_u[t]
        hidden = cell_update(
            a[:, 0:gate_u],
            a[:, gate_u : 2 * gate_u],
            a[:, 2 * gate_u : 3 * gate_u],
            a[:, 3 * gate_u :],
            cell_u,
            keep_at(t, gate_u),
            save_u,
            t,
        )
        hid_o[:, pl.ds(t, 1), :] = hidden[:streams, :unit_u].reshape(streams, 1, unit_u)
        high, low = split(hidden * keep_at(t + 1, gate_u))
        hku2[t + 1, 0:ROWS] = high
        hku2[t + 1, ROWS:] = low

    lower_send(0, True)
    lower_own(0, True)
    lower_finish(0)

    def forward_round(r, carry):
        lower_send(r, False)
        upper_send(r - 1)
        lower_own(r, False)
        upper_own(r - 1)
        lower_finish(r)
        upper_finish(r - 1)
        return carry

    lax.fori_loop(1, steps, forward_round, 0)
    upper_send(steps - 1)
    upper_own(steps - 1)
    upper_finish(steps - 1)

    dstate_l[...] = jnp.zeros_like(dstate_l)
    dstate_u[...] = jnp.zeros_like(dstate_u)
    da_l[...] = jnp.zeros_like(da_l)

    def bcopy_l(t):
        return remote(dal.at[me, t], dal.at[me, t], bs_l.at[t], br_l.at[t])

    def bcopy_u(t):
        return remote(dau.at[me, t], dau.at[me, t], bs_u.at[t], br_u.at[t])

    def gate_grads(dy, dstate, save, keep_now, t):
        gate_in, forget, cand, gate_out = save[t, 0], save[t, 1], save[t, 2], save[t, 3]
        cell_keep, squashed = save[t, 4], save[t, 5]
        dh = dstate[0] + dy
        dc = dstate[1] + dh * gate_out * (1.0 - squashed * squashed)
        dstate[1] = dc * forget * keep_now
        return (
            dc * cand * gate_in * (1.0 - gate_in),
            dc * cell_keep * forget * (1.0 - forget),
            dc * gate_in * (1.0 - cand * cand),
            dh * squashed * gate_out * (1.0 - gate_out),
        )

    def lower_back_start(t):
        grads = gate_grads(dx_up[...] * lock_ref[...], dstate_l, save_l, keep_at(t, lane), t)
        for g in range(4):
            da_l[:, g * units : (g + 1) * units] = grads[g][:, :units]
        high, low = split(da_l[...])
        dal[me, t, 0:ROWS] = high
        dal[me, t, ROWS:] = low
        bcopy_l(t).start()

    def upper_back_start(t):
        grads = gate_grads(gout_ref[t], dstate_u, save_u, keep_at(t, gate_u), t)
        for g in range(4):
            high, low = split(grads[g])
            dau[me, t, 0:ROWS, g * gate_u : (g + 1) * gate_u] = high
            dau[me, t, ROWS:, g * gate_u : (g + 1) * gate_u] = low
        bcopy_u(t).start()

    def lower_back_part(t, q):
        return fold(dot_nn(dal[q, t], wrec_t[q]))

    def upper_back_part(t, q):
        grad = dau[q, t]
        return fold(dot_nn(grad, uin_t[q])), fold(dot_nn(grad, urec_t[q]))

    def lower_back_own(t):
        acc[:, :wide_k] = lower_back_part(t, me)

    def lower_back_finish(t):
        bcopy_l(t).wait()
        total = acc[:, :wide_k] + lower_back_part(t, other)
        dstate_l[0, :, :wide_k] = keep_at(t, wide_k) * total

    def upper_back_own(t):
        into_x, into_h = upper_back_part(t, me)
        dx_up[:, :wide_k] = into_x
        dstate_u[0, :, :up_k] = into_h

    def upper_back_finish(t):
        bcopy_u(t).wait()
        into_x, into_h = upper_back_part(t, other)
        dx_up[:, :wide_k] += into_x
        dstate_u[0, :, :up_k] = keep_at(t, up_k) * (dstate_u[0, :, :up_k] + into_h)

    dx_up[...] = jnp.zeros_like(dx_up)
    upper_back_start(steps - 1)
    upper_back_own(steps - 1)
    upper_back_finish(steps - 1)

    def backward_round(r, carry):
        t = steps - r
        lower_back_start(t)
        upper_back_start(t - 1)
        lower_back_own(t)
        upper_back_own(t - 1)
        lower_back_finish(t)
        upper_back_finish(t - 1)
        return carry

    lax.fori_loop(1, steps, backward_round, 0)
    lower_back_start(0)
    bcopy_l(0).wait()

    da_all[...] = jnp.zeros_like(da_all)
    du_all[...] = jnp.zeros_like(du_all)

    def own_order(t, carry):
        for part in range(2):
            rows = slice(part * ROWS, (part + 1) * ROWS)
            for q in range(2):
                for g in range(4):
                    start = (2 * g + q) * units
                    da_all[part, t, :, start : start + units] = dal[
                        q, t, rows, g * units : (g + 1) * units
                    ]
                    start = (2 * g + q) * unit_u
                    du_all[part, t, :, start : start + unit_u] = dau[
                        q, t, rows, g * gate_u : g * gate_u + unit_u
                    ]
        return carry

    lax.fori_loop(0, steps, own_order, 0)

    def place_left(target, row, count, high, low):
        high, low = jnp.transpose(high)[:count], jnp.transpose(low)[:count]
        target[row : row + count, 0:rows_all] = high
        target[row : row + count, rows_all : 2 * rows_all] = low
        target[row : row + count, 2 * rows_all : 3 * rows_all] = high

    def parts_of(stack):
        width = stack.shape[2]
        return [
            stack[0:steps, i * ROWS : (i + 1) * ROWS, :].reshape(rows_all, width) for i in (0, 1)
        ]

    place_left(xh, 0, wide_k, x2[0:rows_all], x2[rows_all:])
    place_left(xh, wide_k, wide_k, *parts_of(hk2))
    lr[...] = jnp.zeros_like(lr)
    place_left(lr, 0, wide_k, *parts_of(ux2))
    place_left(lr, wide_k, up_k, *parts_of(hku2))

    copies += [
        pltpu.make_async_copy(da_all, da_o, out_sem.at[0]),
        pltpu.make_async_copy(du_all, du_o, out_sem.at[1]),
        pltpu.make_async_copy(xh, xh_o, out_sem.at[2]),
        pltpu.make_async_copy(lr, lr_o, out_sem.at[3]),
    ]
    for copy in copies[1:]:
        copy.start()

    chunk = 512

    def input_grad(cols, width):
        grad = da_all[:, :, :, cols].reshape(2 * rows_all, width)
        return fold(dot_nt(grad, win_raw[:, cols]))

    tail = full // chunk * chunk
    dx[:, :held] = input_grad(slice(tail, full), full % chunk) if full % chunk else 0.0

    def input_grad_step(index, carry):
        dx[:, :held] += input_grad(pl.ds(pl.multiple_of(index * chunk, chunk), chunk), chunk)
        return carry

    lax.fori_loop(0, full // chunk, input_grad_step, 0)
    for t in range(steps):
        now = dx[t * ROWS : t * ROWS + streams, :held] * lock_low[0:streams, :held]
        dx_o[:, t, :] = now
    for copy in copies:
        copy.wait()


def recurrence(
    inputs,
    lower_lock,
    upper_lock,
    resets,
    grad_out,
    lower_drop,
    upper_drop,
    lower_bias,
    upper_bias,
    wrec,
    win,
    uin,
    urec,
):
    streams, steps = resets.shape
    units, full = wrec.shape
    outs, full_u = urec.shape
    wide_k = ceil_to(units, 16)
    wide = ceil_to(full // 2, 256)
    up_k = ceil_to(outs, 16)
    gate_u = ceil_to(outs, 128)
    up_wide = 4 * gate_u
    lane = ceil_to(units, 128)
    rows_all = steps * ROWS
    vm = pl.BlockSpec(memory_space=pltpu.VMEM)
    hbm = pl.BlockSpec(memory_space=pl.ANY)
    sds = jax.ShapeDtypeStruct
    i32 = jnp.int32
    shared = [
        ((2, steps, ROWS, ceil_to(full, 256)), BF),
        ((2, steps, ROWS, ceil_to(full_u, 256)), BF),
        ((2 * wide_k, 3 * rows_all), BF),
        ((6 * TAIL_ROWS, 3 * rows_all), BF),
    ]
    raw = [(w.shape, BF) for w in (wrec, win, uin, urec)]
    dma = pltpu.SemaphoreType.DMA
    return pl.pallas_call(
        functools.partial(recurrence_kernel, units),
        out_shape=(sds((streams, steps, outs), F32), sds((streams, steps, units), F32))
        + tuple(sds(*s) for s in shared)
        + (sds((wide_k, ceil_to(full, 128)), BF), sds(urec.shape, BF)),
        in_specs=[vm] * 9 + [hbm] * 4,
        out_specs=(vm, vm) + (hbm,) * (len(shared) + 2),
        scratch_shapes=[pltpu.VMEM(*s) for s in raw]
        + [
            pltpu.VMEM((2, ROWS, ceil_to(full, 128)), BF),
            pltpu.VMEM((wide_k, 256), i32),
            pltpu.VMEM((up_k, 128), i32),
            pltpu.VMEM((steps + 1, ROWS, 128), F32),
            pltpu.VMEM((ROWS, lane), F32),
            pltpu.VMEM((ROWS, lane), F32),
            pltpu.VMEM((steps, ROWS, gate_u), F32),
            pltpu.VMEM((2, 1, wide), F32),
            pltpu.VMEM((2, 1, up_wide), F32),
            pltpu.VMEM((2, wide, wide_k), BF),
            pltpu.VMEM((2, up_wide, wide_k), BF),
            pltpu.VMEM((2, up_wide, up_k), BF),
            pltpu.VMEM((2, wide_k, wide), BF),
            pltpu.VMEM((2, wide_k, up_wide), BF),
            pltpu.VMEM((2, up_k, up_wide), BF),
        ]
        + [pltpu.VMEM(*s) for s in shared]
        + [
            pltpu.VMEM((2 * rows_all, lane), BF),
            pltpu.VMEM((steps + 1, 2 * ROWS, lane), BF),
            pltpu.VMEM((steps, 2 * ROWS, lane), BF),
            pltpu.VMEM((steps + 1, 2 * ROWS, gate_u), BF),
            pltpu.VMEM((2, steps, 2 * ROWS, wide), BF),
            pltpu.VMEM((2, steps, 2 * ROWS, up_wide), BF),
            pltpu.VMEM((2, steps, ROWS, wide), F32),
            pltpu.VMEM((ROWS, wide), F32),
            pltpu.VMEM((steps, ROWS, wide), F32),
            pltpu.VMEM((ROWS, up_wide), F32),
            pltpu.VMEM((steps, ROWS, up_wide), F32),
            pltpu.VMEM((ROWS, wide + lane - units), F32),
            pltpu.VMEM((ROWS, up_wide), F32),
            pltpu.VMEM((steps, 6, ROWS, lane), F32),
            pltpu.VMEM((steps, 6, ROWS, gate_u), F32),
            pltpu.VMEM((ROWS, lane), F32),
            pltpu.VMEM((ROWS, gate_u), F32),
            pltpu.VMEM((ROWS, wide), F32),
            pltpu.VMEM((ROWS, up_wide), F32),
            pltpu.VMEM((2, ROWS, lane), F32),
            pltpu.VMEM((2, ROWS, gate_u), F32),
            pltpu.VMEM((ROWS, lane), F32),
            pltpu.VMEM((ROWS, lane), F32),
            pltpu.VMEM((rows_all, lane), F32),
        ]
        + [dma((steps,))] * 8
        + [dma((4,)), dma((5,)), dma((2,))],
        compiler_params=pltpu.CompilerParams(
            vmem_limit_bytes=VMEM_LIMIT, collective_id=0, has_side_effects=True
        ),
    )(
        inputs,
        lower_lock,
        upper_lock,
        resets,
        grad_out,
        lower_drop,
        upper_drop,
        lower_bias,
        upper_bias,
        wrec,
        win,
        uin,
        urec,
    )


PANEL = 576
GROUP = 144
HALF = 2 * GROUP
FULL = PANEL + 8
PAIRS = 24
LOWER_PAIRS = 18
SMALLEST = 2.0**-111
WIDTH = 4


def code(group):
    largest = jnp.maximum(jnp.max(jnp.abs(group), axis=0, keepdims=True), SMALLEST)
    step = jnp.floor(jnp.log2(largest) * 64.0).astype(jnp.int32) + 2
    return step, 32767.0 * jnp.exp2(step.astype(F32) * (-1.0 / 64.0))


def factor(step):
    return jnp.exp2(step.astype(F32) * (1.0 / 64.0)) * (1.0 / 32767.0)


def encode(a, b):
    step_a, up_a = code(a)
    step_b, up_b = code(b)
    word_a = jnp.round(a * up_a).astype(jnp.int32)
    word_b = jnp.round(b * up_b).astype(jnp.int32)
    return (word_a << 16) | (word_b & 0xFFFF), step_a, step_b


def decode(words, step_a, step_b):
    a = (words >> 16).astype(F32) * factor(step_a)
    b = ((words << 16) >> 16).astype(F32) * factor(step_b)
    return a, b


def sum_kernel(
    xh,
    lr,
    da,
    du,
    flags,
    out,
    kept,
    grads,
    mine,
    send1,
    recv1,
    send2,
    recv2,
    send3,
    recv3,
    shard,
    scales,
    panel,
    send_sem,
    recv_sem,
    copy_sem,
    kept_sem,
):
    dp = lax.axis_index("dp")
    pipe = lax.axis_index("pipe")
    place = [lax.rem(dp, 4), lax.rem(lax.div(dp, 4), 4), lax.div(dp, 16)]
    stride = [1, 4, 16]

    def peer(axis, distance):
        moved = lax.rem(place[axis] + (distance + 4), 4)
        return {"pipe": pipe, "dp": dp + (moved - place[axis]) * stride[axis]}

    barrier = pltpu.get_barrier_semaphore()
    for axis in range(3):
        for distance in (1, 2, 3):
            pl.semaphore_signal(
                barrier, inc=1, device_id=peer(axis, distance), device_id_type=MESH
            )
    pl.semaphore_wait(barrier, 9)

    def kept_copy(k):
        number = k * 16 + place[k] * 4 + place[(k + 1) % 3]
        rows = pl.ds(pl.multiple_of(place[(k + 2) % 3] * GROUP, GROUP), GROUP)
        cols = pl.ds(pl.multiple_of(number * 128, 128), 128)
        copy = pltpu.make_async_copy(flags.at[rows, cols], kept.at[k], kept_sem.at[k])
        return number < 2 * LOWER_PAIRS, copy

    for k in range(3):
        kept[k] = jnp.ones((GROUP, 128), BF)
        is_lower, copy = kept_copy(k)
        pl.when(is_lower)(copy.start)

    def remote(src, dst, number, axis, distance):
        return pltpu.make_async_remote_copy(
            src_ref=src,
            dst_ref=dst,
            send_sem=send_sem.at[number],
            recv_sem=recv_sem.at[number],
            device_id=peer(axis, distance),
            device_id_type=MESH,
        )

    third = xh.shape[1] // 3

    def right(source, cols):
        high = source[0, :, cols]
        return jnp.concatenate([high, high, source[1, :, cols]], axis=0)

    def compute(pair):
        @pl.when(pair < LOWER_PAIRS)
        def _():
            cols = pl.ds(pl.multiple_of(pair * 256, 256), 256)
            y = dot_nn(xh[...], right(da, cols))
            for n in range(2):
                for ab in range(2):
                    grads[ab, n] = y[ab * PANEL : (ab + 1) * PANEL, n * 128 : (n + 1) * 128]

        @pl.when(pair >= LOWER_PAIRS)
        def _():
            index = pair - LOWER_PAIRS
            cols = pl.ds(pl.multiple_of(index * 256, 256), 256)
            middle = right(du, cols)
            y = dot_nn(lr[0:PANEL], middle)
            top = dot_nn(lr[PANEL : 2 * PANEL - TAIL_ROWS], middle)
            tail = right(du, pl.ds(6 * 256, 256))
            rows = pl.ds(pl.multiple_of(index * TAIL_ROWS, 16), TAIL_ROWS)
            bottom = dot_nn(lr[rows], tail)
            for n in range(2):
                grads[0, n] = y[:, n * 128 : (n + 1) * 128]
                grads[1, n, 0 : PANEL - TAIL_ROWS] = top[:, n * 128 : (n + 1) * 128]
                grads[1, n, PANEL - TAIL_ROWS :] = bottom[:, n * 128 : (n + 1) * 128]

    def rows_of(group):
        return pl.ds(pl.multiple_of(group * GROUP, 8), GROUP)

    def steps_at(ref, base, group):
        return ref[pl.ds(base + 2 * group, 1), :], ref[pl.ds(base + 2 * group + 1, 1), :]

    def store_code(ref, base, group, words, step_a, step_b):
        ref[rows_of(group), :] = words
        ref[pl.ds(base + 2 * group, 1), :] = step_a
        ref[pl.ds(base + 2 * group + 1, 1), :] = step_b

    def arrived(ref, base, group):
        return decode(ref[rows_of(group), :], *steps_at(ref, base, group))

    def stage1(k, way, kind):
        number = (k * 2 + way) * 3 + kind
        return remote(
            send1.at[k, way, kind % 2], recv1.at[k, way, kind], number, k, 1 if way == 0 else -1
        )

    def pair_at(k, offset, half):
        return k * 8 + lax.rem(place[k] + (offset + 4), 4) * 2 + half

    def pack_pair(target, added):
        def group_step(index, carry):
            n, group = lax.div(index, 4), lax.rem(index, 4)
            a, b = grads[0, n, rows_of(group), :], grads[1, n, rows_of(group), :]
            if added is not None:
                more_a, more_b = arrived(added.at[n], PANEL, group)
                a, b = a + more_a, b + more_b
            store_code(target.at[n], PANEL, group, *encode(a, b))
            return carry

        lax.fori_loop(0, 8, group_step, 0)

    ways = ((0, 1), (1, -1))
    for k in range(3):
        for way, sign in ways:
            compute(pair_at(k, 2, way))
            pack_pair(send1.at[k, way, 0], None)
            stage1(k, way, 0).start()
    for k in range(3):
        for way, sign in ways:
            compute(pair_at(k, sign, 1 - way))
            pack_pair(send1.at[k, way, 1], None)
            stage1(k, way, 1).start()
    for k in range(3):
        for way, sign in ways:
            compute(pair_at(k, sign, way))
            stage1(k, way, 0).wait()
            pack_pair(send1.at[k, way, 0], recv1.at[k, way, 0])
            stage1(k, way, 2).start()
    for k in range(3):
        for half in range(2):
            compute(pair_at(k, 0, half))
            for ab in range(2):
                mine[k, ab, 2 * half : 2 * half + 2] = grads[ab]

    def add_pair(k, half, first, second):
        def group_step(index, carry):
            n, group = lax.div(index, 4), lax.rem(index, 4)
            a1, b1 = arrived(first.at[n], PANEL, group)
            a2, b2 = arrived(second.at[n], PANEL, group)
            mine[k, 0, 2 * half + n, rows_of(group), :] += a1 + a2
            mine[k, 1, 2 * half + n, rows_of(group), :] += b1 + b2
            return carry

        lax.fori_loop(0, 8, group_step, 0)

    def stage2(k, way, kind):
        number = 18 + (k * 2 + way) * 3 + kind
        axis = (k + 1) % 3
        return remote(
            send2.at[k, way, kind], recv2.at[k, way, kind], number, axis, 1 if way == 0 else -1
        )

    def pack_half(k, offset, half, target, added):
        block = lax.rem(place[(k + 1) % 3] + (offset + 4), 4)
        for group in range(2):
            rows = slice(half * HALF + group * GROUP, half * HALF + (group + 1) * GROUP)
            a, b = mine[k, 0, block, rows, :], mine[k, 1, block, rows, :]
            if added is not None:
                more_a, more_b = arrived(added, HALF, group)
                a, b = a + more_a, b + more_b
            store_code(target, HALF, group, *encode(a, b))

    for k in range(3):
        stage1(k, 0, 1).wait_recv()
        stage1(k, 1, 1).wait_recv()
        stage1(k, 0, 2).wait_recv()
        stage1(k, 1, 2).wait_recv()
        add_pair(k, 0, recv1.at[k, 0, 2], recv1.at[k, 1, 1])
        add_pair(k, 1, recv1.at[k, 0, 1], recv1.at[k, 1, 2])
        for way, sign in ways:
            pack_half(k, 2, way, send2.at[k, way, 0], None)
            stage2(k, way, 0).start()
        for way, sign in ways:
            pack_half(k, sign, 1 - way, send2.at[k, way, 1], None)
            stage2(k, way, 1).start()
    for k in range(3):
        for way, sign in ways:
            stage2(k, way, 0).wait_recv()
            pack_half(k, sign, way, send2.at[k, way, 2], recv2.at[k, way, 0])
            stage2(k, way, 2).start()

    def stage3(k, d):
        number = 36 + k * 3 + d - 1
        return remote(send3.at[k, d - 1], recv3.at[k, d - 1], number, (k + 2) % 3, d)

    for k in range(3):
        block = place[(k + 1) % 3]
        stage2(k, 0, 1).wait_recv()
        stage2(k, 1, 1).wait_recv()
        stage2(k, 0, 2).wait_recv()
        stage2(k, 1, 2).wait_recv()
        for group in range(4):
            half, inner = group // 2, group % 2
            first = recv2.at[k, 0, 2 - half]
            second = recv2.at[k, 1, 1 + half]
            a1, b1 = arrived(first, HALF, inner)
            a2, b2 = arrived(second, HALF, inner)
            rows = slice(group * GROUP, (group + 1) * GROUP)
            mine[k, 0, block, rows, :] += a1 + a2
            mine[k, 1, block, rows, :] += b1 + b2
        for d in (1, 2, 3):
            group = lax.rem(place[(k + 2) % 3] + d, 4)
            a, b = mine[k, 0, block, rows_of(group), :], mine[k, 1, block, rows_of(group), :]
            store_code(send3.at[k, d - 1], GROUP, 0, *encode(a, b))
            stage3(k, d).start()

    def spread3(k, d):
        group = place[(k + 2) % 3]
        number = 45 + (k * 3 + d - 1) * 2
        data = remote(
            shard.at[k, 0:GROUP], panel.at[k, rows_of(group)], number, (k + 2) % 3, d
        )
        scale = remote(
            shard.at[k, GROUP : GROUP + 8], scales.at[k, d - 1], number + 1, (k + 2) % 3, d
        )
        return data, scale

    def spread3_from(k, d):
        group = lax.rem(place[(k + 2) % 3] + (4 - d), 4)
        number = 45 + (k * 3 + d - 1) * 2
        data = remote(
            shard.at[k, 0:GROUP], panel.at[k, rows_of(group)], number, (k + 2) % 3, d
        )
        scale = remote(
            shard.at[k, GROUP : GROUP + 8], scales.at[k, d - 1], number + 1, (k + 2) % 3, d
        )
        return group, data, scale

    for k in range(3):
        block = place[(k + 1) % 3]
        own = place[(k + 2) % 3]
        a, b = mine[k, 0, block, rows_of(own), :], mine[k, 1, block, rows_of(own), :]
        for d in (1, 2, 3):
            stage3(k, d).wait_recv()
            more_a, more_b = arrived(recv3.at[k, d - 1], GROUP, 0)
            a, b = a + more_a, b + more_b
        is_lower, copy = kept_copy(k)
        pl.when(is_lower)(copy.wait)
        store_code(shard.at[k], GROUP, 0, *encode(a, b * kept[k].astype(F32)))
        for d in (1, 2, 3):
            for copy in spread3(k, d):
                copy.start()
        panel[k, rows_of(own), :] = shard[k, 0:GROUP, :]

    def at(k, first, second):
        return out.at[k * 16 + first * 4 + second]

    def turned(axis, distance):
        return lax.rem(place[axis] + (distance + 4), 4)

    def spread2(k, way, src, first, second):
        return remote(src, at(k, first, second), 63 + k * 4 + way, (k + 1) % 3, 1 - 2 * way)

    def pass2(k, way, first, second):
        rows = slice(0, HALF) if way == 0 else slice(HALF, FULL)
        ref = at(k, first, second).at[rows]
        return remote(ref, ref, 63 + k * 4 + 2 + way, (k + 1) % 3, 1 - 2 * way)

    def spread1(k, way, order, src, first, second):
        return remote(src, at(k, first, second), 75 + (k * 2 + way) * 6 + order, k, 1 - 2 * way)

    offsets = (0, -1, 1, 2)
    for k in range(3):
        merged = shard[k, GROUP : GROUP + 8, :]
        row = lax.broadcasted_iota(jnp.int32, (8, 128), 0)
        own = place[(k + 2) % 3]
        total = jnp.zeros((8, 128), jnp.int32)
        for d in (0, 1, 2, 3):
            if d == 0:
                group, tile = own, merged
            else:
                group, data, scale = spread3_from(k, d)
                data.wait_recv()
                scale.wait_recv()
                tile = scales[k, d - 1]
            total = jnp.where(row == 2 * group, tile[0:1], total)
            total = jnp.where(row == 2 * group + 1, tile[1:2], total)
        panel[k, PANEL:FULL, :] = total
        first, second = place[k], place[(k + 1) % 3]
        for way in range(2):
            spread2(k, way, panel.at[k], first, second).start()
        pltpu.make_async_copy(panel.at[k], at(k, first, second), copy_sem.at[k]).start()
        for way in range(2):
            spread1(k, way, 0, panel.at[k], first, second).start()
    for k in range(3):
        first = place[k]
        for way in range(2):
            second = turned((k + 1) % 3, 2 * way - 1)
            spread2(k, way, panel.at[k], first, second).wait_recv()
            pass2(k, way, first, second).start()
            for way1 in range(2):
                src = at(k, first, second)
                spread1(k, way1, 1 + way, src, first, second).start()
    for k in range(3):
        first, second = place[k], turned((k + 1) % 3, 2)
        for way in range(2):
            pass2(k, way, first, second).wait_recv()
        for way1 in range(2):
            src = at(k, first, second)
            spread1(k, way1, 3, src, first, second).start()

    def pass1(k, way, order, first):
        ref = at(k, first, turned((k + 1) % 3, offsets[order]))
        return remote(ref, ref, 75 + (k * 2 + way) * 6 + 4 + order % 2, k, 1 - 2 * way)

    passed = ((0, 0), (1, 2), (0, 1), (1, 3))
    seen = set()
    for way, order in passed:
        for k in range(3):
            first = turned(k, 2 * way - 1)
            second = turned((k + 1) % 3, offsets[order])
            spread1(k, way, order, panel.at[k], first, second).wait_recv()
            seen.add((k, way, order))
            pass1(k, way, order, first).start()
    for k in range(3):
        for way in range(2):
            for order in range(4):
                if (k, way, order) not in seen:
                    first = turned(k, 2 * way - 1)
                    second = turned((k + 1) % 3, offsets[order])
                    spread1(k, way, order, panel.at[k], first, second).wait_recv()
    for way, order in passed:
        for k in range(3):
            pass1(k, way, order, turned(k, 2)).wait_recv()

    for k in range(3):
        for way in range(2):
            for kind in range(3):
                if kind > 0:
                    stage1(k, way, kind).wait_send()
                stage2(k, way, kind).wait_send()
        for d in (1, 2, 3):
            stage3(k, d).wait_send()
            for copy in spread3(k, d):
                copy.wait_send()
        first, second = place[k], place[(k + 1) % 3]
        pltpu.make_async_copy(panel.at[k], at(k, first, second), copy_sem.at[k]).wait()
        for way in range(2):
            spread2(k, way, panel.at[k], first, second).wait_send()
            pass2(k, way, first, turned((k + 1) % 3, 2 * way - 1)).wait_send()
            for order in range(4):
                second_now = turned((k + 1) % 3, offsets[order])
                src = panel.at[k] if order == 0 else at(k, first, second_now)
                spread1(k, way, order, src, first, second_now).wait_send()
        for way, order in passed:
            pass1(k, way, order, turned(k, 2 * way - 1)).wait_send()


def summed_panels(xh, lr, da, du, flags):
    vm = pl.BlockSpec(memory_space=pltpu.VMEM)
    i32 = jnp.int32
    messages = 75 + 36
    dma = pltpu.SemaphoreType.DMA
    return pl.pallas_call(
        sum_kernel,
        out_shape=pltpu.VMEM((2 * PAIRS, FULL, 128), i32),
        in_specs=[vm] * 4 + [pl.BlockSpec(memory_space=pl.ANY)],
        out_specs=pl.BlockSpec(memory_space=pl.ANY),
        scratch_shapes=[
            pltpu.VMEM((3, GROUP, 128), BF),
            pltpu.VMEM((2, 2, PANEL, 128), F32),
            pltpu.VMEM((3, 2, 4, PANEL, 128), F32),
            pltpu.VMEM((3, 2, 2, 2, FULL, 128), i32),
            pltpu.VMEM((3, 2, 3, 2, FULL, 128), i32),
            pltpu.VMEM((3, 2, 3, HALF + 8, 128), i32),
            pltpu.VMEM((3, 2, 3, HALF + 8, 128), i32),
            pltpu.VMEM((3, 3, GROUP + 8, 128), i32),
            pltpu.VMEM((3, 3, GROUP + 8, 128), i32),
            pltpu.VMEM((3, GROUP + 8, 128), i32),
            pltpu.VMEM((3, 3, 8, 128), i32),
            pltpu.VMEM((3, FULL, 128), i32),
            dma((messages,)),
            dma((messages,)),
            dma((3,)),
            dma((3,)),
        ],
        compiler_params=pltpu.CompilerParams(
            vmem_limit_bytes=SUM_VMEM, collective_id=1, has_side_effects=True
        ),
    )(xh, lr, da, du, flags)


def unpack_kernel(panels, flags_u, low_in, low_rec, low_bias, up_in, up_rec, up_bias, tail):
    step = pl.program_id(0)
    units, outs = low_in.shape[0], up_rec.shape[0]
    lower_steps, all_steps = 2 * LOWER_PAIRS // WIDTH, 2 * PAIRS // WIDTH

    def values(n, ab):
        parts = []
        n = jnp.minimum(step, all_steps - 1) * WIDTH + n
        for group in range(4):
            words = panels[n, group * GROUP : (group + 1) * GROUP, :]
            scale = factor(panels[n, PANEL + 2 * group + ab : PANEL + 2 * group + ab + 1, :])
            half = (words >> 16) if ab == 0 else ((words << 16) >> 16)
            parts.append(half.astype(F32) * scale)
        return jnp.concatenate(parts, axis=0)

    for n in range(WIDTH):
        cols = slice(n * 128, (n + 1) * 128)

        @pl.when(step < lower_steps)
        def _():
            a = values(n, 0)
            low_in[:, cols] = a[:units]
            low_bias[:, cols] = a[units : units + 1]
            b = values(n, 1)[:units]
            low_rec[:, cols] = b

        @pl.when((step >= lower_steps) & (step < all_steps))
        def _():
            a = values(n, 0)
            up_in[:, cols] = a[:units]
            up_bias[:, cols] = a[units : units + 1]
            b = values(n, 1)
            up_rec[:, cols] = b[:outs] * flags_u[:, cols].astype(F32)
            if n % 2 == 0:
                index = (step - lower_steps) * (WIDTH // 2) + n // 2
                rows = pl.ds(pl.multiple_of(index * TAIL_ROWS, 8), TAIL_ROWS)
                tail[rows, :] = b[PANEL - TAIL_ROWS :]

    @pl.when(step == all_steps)
    def _():
        up_in[:, :128] = tail[:units]
        up_bias[:, :128] = tail[units : units + 1]
        up_rec[:, :128] = tail[PANEL : PANEL + outs] * flags_u[:, :128].astype(F32)


def unpack(panels, flags_u, units, full):
    outs, full_u = flags_u.shape
    sds = jax.ShapeDtypeStruct
    lower_steps, all_steps = 2 * LOWER_PAIRS // WIDTH, 2 * PAIRS // WIDTH
    wide = 128 * WIDTH
    lower = lambda i: (0, jnp.minimum(i, lower_steps - 1))
    upper = lambda i: (0, jnp.maximum(i - lower_steps, 0))
    return pl.pallas_call(
        unpack_kernel,
        grid=(all_steps + 1,),
        out_shape=(
            sds((units, full), F32),
            sds((units, full), F32),
            sds((1, full), F32),
            sds((units, full_u), F32),
            sds((outs, full_u), F32),
            sds((1, full_u), F32),
        ),
        in_specs=[
            pl.BlockSpec(memory_space=pltpu.VMEM),
            pl.BlockSpec((outs, wide), upper),
        ],
        out_specs=(
            pl.BlockSpec((units, wide), lower),
            pl.BlockSpec((units, wide), lower),
            pl.BlockSpec((1, wide), lower),
            pl.BlockSpec((units, wide), upper),
            pl.BlockSpec((outs, wide), upper),
            pl.BlockSpec((1, wide), upper),
        ),
        scratch_shapes=[pltpu.VMEM((6 * TAIL_ROWS, 128), F32)],
        compiler_params=pltpu.CompilerParams(vmem_limit_bytes=UNPACK_VMEM),
    )(panels, flags_u)


def body(
    inputs,
    lower_lock,
    upper_lock,
    resets,
    lower_input,
    lower_recur,
    lower_bias,
    lower_drop,
    upper_input,
    upper_recur,
    upper_bias,
    upper_drop,
    grad_out,
):
    me = lax.axis_index("pipe")
    streams, steps, width = inputs.shape
    hidden_out, grad_inputs, da, du, xh, lr, flags, flags_u = recurrence(
        inputs,
        lower_lock,
        upper_lock,
        resets,
        grad_out,
        lower_drop.T,
        upper_drop.T,
        lower_bias.reshape(1, -1),
        upper_bias.reshape(1, -1),
        lower_recur,
        lower_input,
        upper_input,
        upper_recur,
    )
    rows_all = steps * ROWS
    panels = summed_panels(
        xh, lr, da.reshape(2, rows_all, da.shape[3]), du.reshape(2, rows_all, du.shape[3]), flags
    )
    low_in, low_rec, low_bias, up_in, up_rec, up_bias = unpack(
        panels, flags_u, *lower_recur.shape
    )

    def own(row):
        half = row.shape[1] // 2
        return lax.dynamic_slice_in_dim(row[0], me * half, half, 0)

    return (
        hidden_out,
        grad_inputs,
        low_in,
        low_rec,
        own(low_bias),
        up_in,
        up_rec,
        own(up_bias),
    )


def solution(mesh):
    return jax.shard_map(
        body,
        mesh=mesh,
        in_specs=(
            P("dp", None, None),
            P("dp", None),
            P("dp", None),
            P("dp", None),
            P("pipe", None),
            P("pipe", None),
            P("pipe"),
            P(),
            P("pipe", None),
            P("pipe", None),
            P("pipe"),
            P(),
            P("dp", None, None),
        ),
        out_specs=(
            P("dp", None, "pipe"),
            P("dp", None, "pipe"),
            P("pipe", None),
            P("pipe", None),
            P("pipe"),
            P("pipe", None),
            P("pipe", None),
            P("pipe"),
        ),
        check_vma=False,
    )
```

```python
import functools

import jax
import jax.numpy as jnp
from jax import lax
from jax.experimental import pallas as pl
from jax.experimental.pallas import tpu as pltpu
from jax.sharding import PartitionSpec as P

BF = jnp.bfloat16
F32 = jnp.float32
MESH = pl.DeviceIdType.MESH
ROWS = 16
VMEM_LIMIT = 62 * 2**20
TAIL_ROWS = 368
SUM_VMEM = 47 * 2**20
UNPACK_VMEM = 24 * 2**20


def ceil_to(value, multiple):
    return -(-value // multiple) * multiple


def split(value):
    high = value.astype(BF)
    low = (value - high.astype(F32)).astype(BF)
    return high, low


def fold(stacked):
    half = stacked.shape[0] // 2
    return stacked[:half] + stacked[half:]


def dot_nn(a, b):
    return jnp.dot(a, b, preferred_element_type=F32)


def dot_nt(a, b):
    return lax.dot_general(a, b, (((1,), (1,)), ((), ())), preferred_element_type=F32)


def flags_at(words, column):
    column = lax.broadcasted_iota(jnp.int32, (1, 128), 1) + column
    index = (column * 52429) >> 20
    bit = column - index * 20
    index = jnp.broadcast_to(index & 127, words.shape)
    found = jnp.take_along_axis(words, index, axis=1, mode="promise_in_bounds")
    return (found >> bit) & 1


def recurrence_kernel(
    units,
    inputs,
    lower_lock,
    upper_lock,
    resets,
    grad_out,
    lower_drop,
    upper_drop,
    lower_bias,
    upper_bias,
    wrec_in,
    win_in,
    uin_in,
    urec_in,
    hid_o,
    dx_o,
    da_o,
    du_o,
    xh_o,
    lr_o,
    rows_l_o,
    rows_u_o,
    wrec_raw,
    win_raw,
    uin_raw,
    urec_raw,
    words_l,
    words_u,
    slab,
    keep_ref,
    lock_low,
    lock_ref,
    gout_ref,
    blo,
    bup,
    wrec_t,
    uin_t,
    urec_t,
    wrec,
    uin,
    urec,
    da_all,
    du_all,
    xh,
    lr,
    x2,
    hk2,
    ux2,
    hku2,
    dal,
    dau,
    proj,
    send_l,
    recv_l,
    send_u,
    recv_u,
    act_l,
    act_u,
    save_l,
    save_u,
    cell_l,
    cell_u,
    da_l,
    da_u,
    dstate_l,
    dstate_u,
    dx_up,
    acc,
    dx,
    fs_l,
    fr_l,
    fs_u,
    fr_u,
    bs_l,
    br_l,
    bs_u,
    br_u,
    in_sem,
    out_sem,
):
    streams, steps = resets.shape
    me = lax.axis_index("pipe")
    other = 1 - me
    peer = {"pipe": other}
    wide_k = wrec.shape[1]
    wide = wrec.shape[2]
    up_wide = uin.shape[2]
    up_k = urec.shape[1]
    lane = act_l.shape[1] - wide + units

    barrier = pltpu.get_barrier_semaphore()
    pl.semaphore_signal(barrier, inc=1, device_id=peer, device_id_type=MESH)
    loads = [
        pltpu.make_async_copy(win_in, win_raw, in_sem.at[0]),
        pltpu.make_async_copy(wrec_in, wrec_raw, in_sem.at[1]),
        pltpu.make_async_copy(uin_in, uin_raw, in_sem.at[2]),
        pltpu.make_async_copy(urec_in, urec_raw, in_sem.at[3]),
    ]
    for load in loads:
        load.start()
    pl.semaphore_wait(barrier, 1)

    def remote(src, dst, send_sem, recv_sem):
        return pltpu.make_async_remote_copy(
            src_ref=src,
            dst_ref=dst,
            send_sem=send_sem,
            recv_sem=recv_sem,
            device_id=peer,
            device_id_type=MESH,
        )

    full = wrec_raw.shape[1]
    held = wrec_raw.shape[0]
    held_u = urec_raw.shape[0]
    full_u = urec_raw.shape[1]
    unit_u = full_u // 8
    gate_u = up_wide // 4
    rows_all = steps * ROWS

    def to_rows(value, lanes, filler=0.0):
        more = lanes - value.shape[1]
        if more:
            value = jnp.concatenate([value, jnp.full((streams, more), filler, F32)], axis=1)
        return jnp.concatenate([value, jnp.zeros((ROWS - streams, lanes), F32)], axis=0)

    keep_ref[...] = jnp.zeros_like(keep_ref)
    for t in range(steps):
        now = 1.0 - resets[:, t : t + 1].astype(F32)
        keep_ref[t] = to_rows(jnp.broadcast_to(now, (streams, 128)), 128)
    blo[...] = jnp.zeros_like(blo)
    bup[...] = jnp.zeros_like(bup)
    def place_words(target, packed):
        rows, lanes = packed.shape
        more = target.shape[1] - lanes
        packed = jnp.concatenate([packed, jnp.zeros((rows, more), jnp.int32)], axis=1)
        target[0:rows, :] = packed

    words_l[...] = jnp.zeros_like(words_l)
    words_u[...] = jnp.zeros_like(words_u)
    for half in range(2):

        @pl.when(me == half)
        def _(half=half):
            mine = slice(half * units, (half + 1) * units)
            lock_low[...] = to_rows(lower_lock[:, mine].astype(F32) * 1.25, lane)
            lock_ref[...] = to_rows(upper_lock[:, mine].astype(F32) * 1.25, lane)
            one = jnp.full((streams, 1), 1.0, F32)
            for t in range(steps):
                now = inputs[:, t, mine] * lock_low[0:streams, 0:units]
                now = to_rows(jnp.concatenate([now, one], axis=1), lane)
                high, low = split(now)
                x2[t * ROWS : (t + 1) * ROWS] = high
                x2[rows_all + t * ROWS : rows_all + (t + 1) * ROWS] = low
                out = grad_out[:, t, half * unit_u : (half + 1) * unit_u]
                gout_ref[t] = to_rows(out, gate_u)
            place_words(words_l, lower_drop[:, mine])
            place_words(words_u, upper_drop[:, half * held_u : (half + 1) * held_u])
            bias = lower_bias[...].astype(F32)
            bias_u = upper_bias[...].astype(F32)
            for q in range(2):
                for i in range(2):
                    g = 2 * half + i
                    start = (2 * i + q) * units
                    blo[q, :, g * units : (g + 1) * units] = bias[:, start : start + units]
                    start = (2 * i + q) * unit_u
                    bup[q, :, g * gate_u : g * gate_u + unit_u] = bias_u[
                        :, start : start + unit_u
                    ]

    loads[0].wait()
    proj[:, :, :, wide - 128 :] = jnp.zeros((2, steps, ROWS, 128), F32)
    for q in range(2):
        for g in range(4):
            start, stop = (2 * g + q) * units, (2 * g + q + 1) * units
            first, last = start // 128 * 128, min(ceil_to(stop, 128), full)
            y = fold(dot_nn(x2[:, :held], win_raw[:, first:last]))
            y = y[:, start - first : stop - first] + blo[q, :, g * units : (g + 1) * units]
            proj[q, :, :, g * units : (g + 1) * units] = y.reshape(steps, ROWS, units)

    for load in loads[1:]:
        load.wait()
    sub = lax.broadcasted_iota(jnp.int32, (8, 128), 0)

    def flags_of(held, i):
        left, right = 8 * i // 20, (8 * i + 7) // 20
        now = jnp.broadcast_to(held[left : left + 1], (8, 128))
        if right != left:
            later = jnp.broadcast_to(held[right : right + 1], (8, 128))
            now = jnp.where(sub < 20 * right - 8 * i, now, later)
        bit = sub + 8 * i % 20
        bit = jnp.where(bit >= 20, bit - 20, bit)
        return (now >> bit) & 1

    def masked_columns(weight, words, first, lanes):
        rows, columns = weight.shape
        words = words[pl.ds(first, ceil_to(ceil_to(columns, 20) // 20, 8)), lanes]
        turned = jnp.transpose(weight.astype(F32))
        if rows < 128:
            turned = jnp.concatenate([turned, jnp.zeros((columns, 128 - rows), F32)], axis=1)
        out = []
        for i in range(columns // 8):
            now = turned[8 * i : 8 * i + 8]
            out.append(jnp.where(flags_of(words, i) != 0, now + now, 0.0))
        return jnp.concatenate(out, axis=0)

    block = 640
    row16 = lax.broadcasted_iota(jnp.int32, (ROWS, 128), 0)

    def lower_slab(rows, start):
        lanes = pl.ds(start, 128)
        many = min(128, wide_k - start) if isinstance(start, int) else 128

        def fill(index, carry):
            cols = pl.ds(pl.multiple_of(index * block, block), block)
            first = pl.multiple_of(index * (block // 20), block // 20)
            part = masked_columns(wrec_raw[rows, cols], words_l, first, lanes)
            slab[cols, :] = part
            return carry

        lax.fori_loop(0, full // block, fill, 0)
        last = full // block * block
        slab[last:full, :] = masked_columns(
            wrec_raw[rows, last:full], words_l, last // 20, lanes
        )
        target = pl.ds(start, many)
        tiles = units // ROWS
        for q in range(2):
            for g in range(4):
                shift = units * (g + q)
                base = (tiles + 1) * ROWS * g

                def move(index, carry, q=q, shift=shift, base=base):
                    for i in range(7):
                        row = pl.multiple_of(base + (index * 7 + i) * ROWS, ROWS)
                        now = slab[pl.ds(row + shift, ROWS), :]
                        wrec_t[q, pl.ds(row, ROWS), target] = now.astype(BF)[:, :many]
                    return carry

                lax.fori_loop(0, tiles // 7, move, 0)
                row = base + tiles * ROWS
                now = slab[row + shift : row + shift + ROWS, :]
                if g < 3:
                    later = slab[row + shift + units : row + shift + units + ROWS, :]
                else:
                    later = jnp.zeros((ROWS, 128), F32)
                now = jnp.where(row16 < units * (g + 1) - row, now, later)
                wrec_t[q, row : row + ROWS, target] = now.astype(BF)[:, :many]

    def lower_slab_step(index, carry):
        start = pl.multiple_of(index * 128, 128)
        lower_slab(pl.ds(start, 128), start)
        return carry

    lax.fori_loop(0, held // 128, lower_slab_step, 0)
    lower_slab(slice(held // 128 * 128, held), held // 128 * 128)

    def place_upper(target, turned, start, many):
        for q in range(2):
            for g in range(4):
                first = (2 * g + q) * unit_u
                part = turned[first : first + unit_u]
                part = jnp.concatenate([part, jnp.zeros((gate_u - unit_u, 128), F32)], axis=0)
                rows = slice(g * gate_u, (g + 1) * gate_u)
                target[q, rows, pl.ds(start, many)] = part.astype(BF)[:, :many]

    def upper_slab(index, carry):
        start = pl.multiple_of(index * 128, 128)
        turned = jnp.transpose(uin_raw[pl.ds(start, 128), :].astype(F32))
        place_upper(uin_t, turned, start, 128)
        return carry

    lax.fori_loop(0, held // 128, upper_slab, 0)
    start = held // 128 * 128
    turned = jnp.transpose(uin_raw[start:held, :].astype(F32))
    turned = jnp.concatenate([turned, jnp.zeros((full_u, 128 - held % 128), F32)], axis=1)
    place_upper(uin_t, turned, start, wide_k - start)
    for start in range(0, held_u, 128):
        stop = min(start + 128, held_u)
        lanes = pl.ds(start, 128)
        turned = [
            masked_columns(
                urec_raw[start:stop, i : min(i + block, full_u)], words_u, i // 20, lanes
            )
            for i in range(0, full_u, block)
        ]
        many = min(128, up_k - start)
        place_upper(urec_t, jnp.concatenate(turned, axis=0), start, many)
    for q in range(2):
        wrec[q] = jnp.transpose(wrec_t[q])
        uin[q] = jnp.transpose(uin_t[q])
        urec[q] = jnp.transpose(urec_t[q])
    rows_l_o[...] = jnp.transpose(words_l[...])
    rows_u_o[...] = jnp.transpose(words_u[...])

    act_l[...] = jnp.zeros_like(act_l)
    hk2[...] = jnp.zeros_like(hk2)
    ux2[...] = jnp.zeros_like(ux2)
    hku2[...] = jnp.zeros_like(hku2)
    cell_l[...] = jnp.zeros_like(cell_l)
    cell_u[...] = jnp.zeros_like(cell_u)

    def fcopy_l(t):
        return remote(send_l, recv_l.at[lax.rem(t, 2)], fs_l.at[t], fr_l.at[t])

    def fcopy_u(t):
        return remote(send_u, recv_u.at[lax.rem(t, 2)], fs_u.at[t], fr_u.at[t])

    def lower_send(t, first):
        if first:
            send_l[...] = proj[other, t]
        else:
            send_l[...] = fold(dot_nn(hk2[t, :, :wide_k], wrec[other])) + proj[other, t]
        fcopy_l(t).start()

    def lower_own(t, first):
        if first:
            act_l[:, :wide] = proj[me, t]
        else:
            act_l[:, :wide] = fold(dot_nn(hk2[t, :, :wide_k], wrec[me])) + proj[me, t]

    def upper_part(t, q):
        y = dot_nn(ux2[t, :, :wide_k], uin[q]) + dot_nn(hku2[t, :, :up_k], urec[q])
        return fold(y) + bup[q]

    def upper_send(t):
        send_u[...] = upper_part(t, other)
        fcopy_u(t).start()

    def upper_own(t):
        act_u[...] = upper_part(t, me)

    def keep_at(t, lanes):
        return jnp.concatenate([keep_ref[t]] * (ceil_to(lanes, 128) // 128), axis=1)[
            :, :lanes
        ]

    def cell_update(a_in, a_forget, a_cand, a_out, cell, keep_now, save, t):
        gate_in = jax.nn.sigmoid(a_in)
        forget = jax.nn.sigmoid(a_forget)
        cand = jnp.tanh(a_cand)
        gate_out = jax.nn.sigmoid(a_out)
        cell_keep = cell[...] * keep_now
        cell_new = forget * cell_keep + gate_in * cand
        squashed = jnp.tanh(cell_new)
        cell[...] = cell_new
        save[t, 0] = gate_in
        save[t, 1] = forget
        save[t, 2] = cand
        save[t, 3] = gate_out
        save[t, 4] = cell_keep
        save[t, 5] = squashed
        return gate_out * squashed

    def lower_finish(t):
        fcopy_l(t).wait()
        act_l[:, :wide] += recv_l[lax.rem(t, 2)]
        hidden = cell_update(
            act_l[:, 0:lane],
            act_l[:, units : units + lane],
            act_l[:, 2 * units : 2 * units + lane],
            act_l[:, 3 * units : 3 * units + lane],
            cell_l,
            keep_at(t, lane),
            save_l,
            t,
        )
        high, low = split(hidden * keep_at(t + 1, lane))
        hk2[t + 1, 0:ROWS] = high
        hk2[t + 1, ROWS:] = low
        ones_at = lax.broadcasted_iota(jnp.int32, (ROWS, lane), 1) == units
        high, low = split(jnp.where(ones_at, 1.0, hidden * lock_ref[...]))
        ux2[t, 0:ROWS] = high
        ux2[t, ROWS:] = low

    def upper_finish(t):
        fcopy_u(t).wait()
        a = act_u[...] + recv_u[lax.rem(t, 2)]
        hidden = cell_update(
            a[:, 0:gate_u],
            a[:, gate_u : 2 * gate_u],
            a[:, 2 * gate_u : 3 * gate_u],
            a[:, 3 * gate_u :],
            cell_u,
            keep_at(t, gate_u),
            save_u,
            t,
        )
        hid_o[:, pl.ds(t, 1), :] = hidden[:streams, :unit_u].reshape(streams, 1, unit_u)
        high, low = split(hidden * keep_at(t + 1, gate_u))
        hku2[t + 1, 0:ROWS] = high
        hku2[t + 1, ROWS:] = low

    lower_send(0, True)
    lower_own(0, True)
    lower_finish(0)

    def forward_round(r, carry):
        lower_send(r, False)
        upper_send(r - 1)
        lower_own(r, False)
        upper_own(r - 1)
        lower_finish(r)
        upper_finish(r - 1)
        return carry

    lax.fori_loop(1, steps, forward_round, 0)
    upper_send(steps - 1)
    upper_own(steps - 1)
    upper_finish(steps - 1)

    dstate_l[...] = jnp.zeros_like(dstate_l)
    dstate_u[...] = jnp.zeros_like(dstate_u)
    da_l[...] = jnp.zeros_like(da_l)

    def bcopy_l(t):
        return remote(dal.at[me, t], dal.at[me, t], bs_l.at[t], br_l.at[t])

    def bcopy_u(t):
        return remote(dau.at[me, t], dau.at[me, t], bs_u.at[t], br_u.at[t])

    def gate_grads(dy, dstate, save, keep_now, t):
        gate_in, forget, cand, gate_out = save[t, 0], save[t, 1], save[t, 2], save[t, 3]
        cell_keep, squashed = save[t, 4], save[t, 5]
        dh = dstate[0] + dy
        dc = dstate[1] + dh * gate_out * (1.0 - squashed * squashed)
        dstate[1] = dc * forget * keep_now
        return (
            dc * cand * gate_in * (1.0 - gate_in),
            dc * cell_keep * forget * (1.0 - forget),
            dc * gate_in * (1.0 - cand * cand),
            dh * squashed * gate_out * (1.0 - gate_out),
        )

    def lower_back_start(t):
        grads = gate_grads(dx_up[...] * lock_ref[...], dstate_l, save_l, keep_at(t, lane), t)
        for g in range(4):
            da_l[:, g * units : (g + 1) * units] = grads[g][:, :units]
        high, low = split(da_l[...])
        dal[me, t, 0:ROWS] = high
        dal[me, t, ROWS:] = low
        bcopy_l(t).start()

    def upper_back_start(t):
        grads = gate_grads(gout_ref[t], dstate_u, save_u, keep_at(t, gate_u), t)
        for g in range(4):
            high, low = split(grads[g])
            dau[me, t, 0:ROWS, g * gate_u : (g + 1) * gate_u] = high
            dau[me, t, ROWS:, g * gate_u : (g + 1) * gate_u] = low
        bcopy_u(t).start()

    def lower_back_part(t, q):
        return fold(dot_nn(dal[q, t], wrec_t[q]))

    def upper_back_part(t, q):
        grad = dau[q, t]
        return fold(dot_nn(grad, uin_t[q])), fold(dot_nn(grad, urec_t[q]))

    def lower_back_own(t):
        acc[:, :wide_k] = lower_back_part(t, me)

    def lower_back_finish(t):
        bcopy_l(t).wait()
        total = acc[:, :wide_k] + lower_back_part(t, other)
        dstate_l[0, :, :wide_k] = keep_at(t, wide_k) * total

    def upper_back_own(t):
        into_x, into_h = upper_back_part(t, me)
        dx_up[:, :wide_k] = into_x
        dstate_u[0, :, :up_k] = into_h

    def upper_back_finish(t):
        bcopy_u(t).wait()
        into_x, into_h = upper_back_part(t, other)
        dx_up[:, :wide_k] += into_x
        dstate_u[0, :, :up_k] = keep_at(t, up_k) * (dstate_u[0, :, :up_k] + into_h)

    dx_up[...] = jnp.zeros_like(dx_up)
    upper_back_start(steps - 1)
    upper_back_own(steps - 1)
    upper_back_finish(steps - 1)

    def backward_round(r, carry):
        t = steps - r
        lower_back_start(t)
        upper_back_start(t - 1)
        lower_back_own(t)
        upper_back_own(t - 1)
        lower_back_finish(t)
        upper_back_finish(t - 1)
        return carry

    lax.fori_loop(1, steps, backward_round, 0)
    lower_back_start(0)
    bcopy_l(0).wait()

    da_all[...] = jnp.zeros_like(da_all)
    du_all[...] = jnp.zeros_like(du_all)

    def own_order(t, carry):
        for part in range(2):
            rows = slice(part * ROWS, (part + 1) * ROWS)
            for q in range(2):
                for g in range(4):
                    start = (2 * g + q) * units
                    da_all[part, t, :, start : start + units] = dal[
                        q, t, rows, g * units : (g + 1) * units
                    ]
                    start = (2 * g + q) * unit_u
                    du_all[part, t, :, start : start + unit_u] = dau[
                        q, t, rows, g * gate_u : g * gate_u + unit_u
                    ]
        return carry

    lax.fori_loop(0, steps, own_order, 0)

    def place_left(target, row, count, high, low):
        high, low = jnp.transpose(high)[:count], jnp.transpose(low)[:count]
        target[row : row + count, 0:rows_all] = high
        target[row : row + count, rows_all : 2 * rows_all] = low
        target[row : row + count, 2 * rows_all : 3 * rows_all] = high

    def parts_of(stack):
        width = stack.shape[2]
        return [
            stack[0:steps, i * ROWS : (i + 1) * ROWS, :].reshape(rows_all, width) for i in (0, 1)
        ]

    place_left(xh, 0, wide_k, x2[0:rows_all], x2[rows_all:])
    place_left(xh, wide_k, wide_k, *parts_of(hk2))
    lr[...] = jnp.zeros_like(lr)
    place_left(lr, 0, wide_k, *parts_of(ux2))
    place_left(lr, wide_k, up_k, *parts_of(hku2))

    copies = [
        pltpu.make_async_copy(da_all, da_o, out_sem.at[0]),
        pltpu.make_async_copy(du_all, du_o, out_sem.at[1]),
        pltpu.make_async_copy(xh, xh_o, out_sem.at[2]),
        pltpu.make_async_copy(lr, lr_o, out_sem.at[3]),
    ]
    for copy in copies:
        copy.start()

    chunk = 512

    def input_grad(cols, width):
        grad = da_all[:, :, :, cols].reshape(2 * rows_all, width)
        return fold(dot_nt(grad, win_raw[:, cols]))

    tail = full // chunk * chunk
    dx[:, :held] = input_grad(slice(tail, full), full % chunk) if full % chunk else 0.0

    def input_grad_step(index, carry):
        dx[:, :held] += input_grad(pl.ds(pl.multiple_of(index * chunk, chunk), chunk), chunk)
        return carry

    lax.fori_loop(0, full // chunk, input_grad_step, 0)
    for t in range(steps):
        now = dx[t * ROWS : t * ROWS + streams, :held] * lock_low[0:streams, :held]
        dx_o[:, t, :] = now
    for copy in copies:
        copy.wait()


def recurrence(
    inputs,
    lower_lock,
    upper_lock,
    resets,
    grad_out,
    lower_drop,
    upper_drop,
    lower_bias,
    upper_bias,
    wrec,
    win,
    uin,
    urec,
):
    streams, steps = resets.shape
    units, full = wrec.shape
    outs, full_u = urec.shape
    wide_k = ceil_to(units, 16)
    wide = ceil_to(full // 2, 256)
    up_k = ceil_to(outs, 16)
    gate_u = ceil_to(outs, 128)
    up_wide = 4 * gate_u
    lane = ceil_to(units, 128)
    rows_all = steps * ROWS
    vm = pl.BlockSpec(memory_space=pltpu.VMEM)
    hbm = pl.BlockSpec(memory_space=pl.ANY)
    sds = jax.ShapeDtypeStruct
    i32 = jnp.int32
    shared = [
        ((2, steps, ROWS, ceil_to(full, 256)), BF),
        ((2, steps, ROWS, ceil_to(full_u, 256)), BF),
        ((2 * wide_k, 3 * rows_all), BF),
        ((4 * TAIL_ROWS, 3 * rows_all), BF),
    ]
    raw = [(w.shape, BF) for w in (wrec, win, uin, urec)]
    dma = pltpu.SemaphoreType.DMA
    return pl.pallas_call(
        functools.partial(recurrence_kernel, units),
        out_shape=(sds((streams, steps, outs), F32), sds((streams, steps, units), F32))
        + tuple(sds(*s) for s in shared)
        + (sds((lane, 256), i32), sds((ceil_to(outs, 128), 128), i32)),
        in_specs=[vm] * 9 + [hbm] * 4,
        out_specs=(vm, vm) + (hbm,) * len(shared) + (vm, vm),
        scratch_shapes=[pltpu.VMEM(*s) for s in raw]
        + [
            pltpu.VMEM((256, lane), i32),
            pltpu.VMEM((128, ceil_to(outs, 128)), i32),
            pltpu.VMEM((ceil_to(full, 16), 128), F32),
            pltpu.VMEM((steps + 1, ROWS, 128), F32),
            pltpu.VMEM((ROWS, lane), F32),
            pltpu.VMEM((ROWS, lane), F32),
            pltpu.VMEM((steps, ROWS, gate_u), F32),
            pltpu.VMEM((2, 1, wide), F32),
            pltpu.VMEM((2, 1, up_wide), F32),
            pltpu.VMEM((2, wide, wide_k), BF),
            pltpu.VMEM((2, up_wide, wide_k), BF),
            pltpu.VMEM((2, up_wide, up_k), BF),
            pltpu.VMEM((2, wide_k, wide), BF),
            pltpu.VMEM((2, wide_k, up_wide), BF),
            pltpu.VMEM((2, up_k, up_wide), BF),
        ]
        + [pltpu.VMEM(*s) for s in shared]
        + [
            pltpu.VMEM((2 * rows_all, lane), BF),
            pltpu.VMEM((steps + 1, 2 * ROWS, lane), BF),
            pltpu.VMEM((steps, 2 * ROWS, lane), BF),
            pltpu.VMEM((steps + 1, 2 * ROWS, gate_u), BF),
            pltpu.VMEM((2, steps, 2 * ROWS, wide), BF),
            pltpu.VMEM((2, steps, 2 * ROWS, up_wide), BF),
            pltpu.VMEM((2, steps, ROWS, wide), F32),
            pltpu.VMEM((ROWS, wide), F32),
            pltpu.VMEM((2, ROWS, wide), F32),
            pltpu.VMEM((ROWS, up_wide), F32),
            pltpu.VMEM((2, ROWS, up_wide), F32),
            pltpu.VMEM((ROWS, wide + lane - units), F32),
            pltpu.VMEM((ROWS, up_wide), F32),
            pltpu.VMEM((steps, 6, ROWS, lane), F32),
            pltpu.VMEM((steps, 6, ROWS, gate_u), F32),
            pltpu.VMEM((ROWS, lane), F32),
            pltpu.VMEM((ROWS, gate_u), F32),
            pltpu.VMEM((ROWS, wide), F32),
            pltpu.VMEM((ROWS, up_wide), F32),
            pltpu.VMEM((2, ROWS, lane), F32),
            pltpu.VMEM((2, ROWS, gate_u), F32),
            pltpu.VMEM((ROWS, lane), F32),
            pltpu.VMEM((ROWS, lane), F32),
            pltpu.VMEM((rows_all, lane), F32),
        ]
        + [dma((steps,))] * 8
        + [dma((4,)), dma((4,))],
        compiler_params=pltpu.CompilerParams(
            vmem_limit_bytes=VMEM_LIMIT, collective_id=0, has_side_effects=True
        ),
    )(
        inputs,
        lower_lock,
        upper_lock,
        resets,
        grad_out,
        lower_drop,
        upper_drop,
        lower_bias,
        upper_bias,
        wrec,
        win,
        uin,
        urec,
    )


PANEL = 576
GROUP = 144
HALF = 2 * GROUP
FULL = PANEL + 8
PAIRS = 24
LOWER_PAIRS = 18
SMALLEST = 2.0**-111
WIDTH = 4


def code(group):
    largest = jnp.maximum(jnp.max(jnp.abs(group), axis=0, keepdims=True), SMALLEST)
    step = jnp.floor(jnp.log2(largest) * 64.0).astype(jnp.int32) + 2
    return step, 32767.0 * jnp.exp2(step.astype(F32) * (-1.0 / 64.0))


def factor(step):
    return jnp.exp2(step.astype(F32) * (1.0 / 64.0)) * (1.0 / 32767.0)


def encode(a, b):
    step_a, up_a = code(a)
    step_b, up_b = code(b)
    word_a = jnp.round(a * up_a).astype(jnp.int32)
    word_b = jnp.round(b * up_b).astype(jnp.int32)
    return (word_a << 16) | (word_b & 0xFFFF), step_a, step_b


def decode(words, step_a, step_b):
    a = (words >> 16).astype(F32) * factor(step_a)
    b = ((words << 16) >> 16).astype(F32) * factor(step_b)
    return a, b


def sum_kernel(
    xh,
    lr,
    da,
    du,
    words,
    out,
    kept,
    grads,
    mine,
    send1,
    recv1,
    send2,
    recv2,
    send3,
    recv3,
    shard,
    scales,
    panel,
    send_sem,
    recv_sem,
    copy_sem,
    kept_sem,
):
    dp = lax.axis_index("dp")
    pipe = lax.axis_index("pipe")
    place = [lax.rem(dp, 4), lax.rem(lax.div(dp, 4), 4), lax.div(dp, 16)]
    stride = [1, 4, 16]

    def peer(axis, distance):
        moved = lax.rem(place[axis] + (distance + 4), 4)
        return {"pipe": pipe, "dp": dp + (moved - place[axis]) * stride[axis]}

    barrier = pltpu.get_barrier_semaphore()
    for axis in range(3):
        for distance in (1, 2, 3):
            pl.semaphore_signal(
                barrier, inc=1, device_id=peer(axis, distance), device_id_type=MESH
            )
    pl.semaphore_wait(barrier, 9)

    def kept_copy(k):
        number = k * 16 + place[k] * 4 + place[(k + 1) % 3]
        rows = pl.ds(pl.multiple_of(place[(k + 2) % 3] * GROUP, GROUP), GROUP)
        part = jnp.minimum(lax.div(number, 20), 1)
        lanes = pl.ds(pl.multiple_of(part * 128, 128), 128)
        return number, pltpu.make_async_copy(words.at[rows, lanes], kept.at[k], kept_sem.at[k])

    for k in range(3):
        kept_copy(k)[1].start()

    def remote(src, dst, number, axis, distance):
        return pltpu.make_async_remote_copy(
            src_ref=src,
            dst_ref=dst,
            send_sem=send_sem.at[number],
            recv_sem=recv_sem.at[number],
            device_id=peer(axis, distance),
            device_id_type=MESH,
        )

    third = xh.shape[1] // 3

    def right(source, cols):
        high = source[0, :, cols]
        return jnp.concatenate([high, high, source[1, :, cols]], axis=0)

    def compute(pair):
        @pl.when(pair < LOWER_PAIRS)
        def _():
            cols = pl.ds(pl.multiple_of(pair * 256, 256), 256)
            y = dot_nn(xh[...], right(da, cols))
            for n in range(2):
                for ab in range(2):
                    grads[ab, n] = y[ab * PANEL : (ab + 1) * PANEL, n * 128 : (n + 1) * 128]

        @pl.when(pair >= LOWER_PAIRS)
        def _():
            index = pair - LOWER_PAIRS
            cols = pl.ds(pl.multiple_of(index * 256, 256), 256)
            middle = right(du, cols)
            y = dot_nn(lr[0:PANEL], middle)
            top = dot_nn(lr[PANEL : 2 * PANEL - TAIL_ROWS], middle)
            tail = right(du, pl.ds(6 * 256, 256))
            rows = pl.ds(pl.multiple_of(jnp.minimum(index, 3) * TAIL_ROWS, 16), TAIL_ROWS)
            bottom = dot_nn(lr[rows], tail)
            for n in range(2):
                grads[0, n] = y[:, n * 128 : (n + 1) * 128]
                grads[1, n, 0 : PANEL - TAIL_ROWS] = top[:, n * 128 : (n + 1) * 128]
                grads[1, n, PANEL - TAIL_ROWS :] = bottom[:, n * 128 : (n + 1) * 128]

    def rows_of(group):
        return pl.ds(pl.multiple_of(group * GROUP, 8), GROUP)

    def steps_at(ref, base, group):
        return ref[pl.ds(base + 2 * group, 1), :], ref[pl.ds(base + 2 * group + 1, 1), :]

    def store_code(ref, base, group, words, step_a, step_b):
        ref[rows_of(group), :] = words
        ref[pl.ds(base + 2 * group, 1), :] = step_a
        ref[pl.ds(base + 2 * group + 1, 1), :] = step_b

    def arrived(ref, base, group):
        return decode(ref[rows_of(group), :], *steps_at(ref, base, group))

    def stage1(k, way, kind):
        number = (k * 2 + way) * 3 + kind
        return remote(
            send1.at[k, way, kind % 2], recv1.at[k, way, kind], number, k, 1 if way == 0 else -1
        )

    def pair_at(k, offset, half):
        return k * 8 + lax.rem(place[k] + (offset + 4), 4) * 2 + half

    def pack_pair(target, added):
        def group_step(index, carry):
            n, group = lax.div(index, 4), lax.rem(index, 4)
            a, b = grads[0, n, rows_of(group), :], grads[1, n, rows_of(group), :]
            if added is not None:
                more_a, more_b = arrived(added.at[n], PANEL, group)
                a, b = a + more_a, b + more_b
            store_code(target.at[n], PANEL, group, *encode(a, b))
            return carry

        lax.fori_loop(0, 8, group_step, 0)

    ways = ((0, 1), (1, -1))
    for k in range(3):
        for way, sign in ways:
            compute(pair_at(k, 2, way))
            pack_pair(send1.at[k, way, 0], None)
            stage1(k, way, 0).start()
    for k in range(3):
        for way, sign in ways:
            compute(pair_at(k, sign, 1 - way))
            pack_pair(send1.at[k, way, 1], None)
            stage1(k, way, 1).start()
    for k in range(3):
        for way, sign in ways:
            compute(pair_at(k, sign, way))
            stage1(k, way, 0).wait()
            pack_pair(send1.at[k, way, 0], recv1.at[k, way, 0])
            stage1(k, way, 2).start()
    for k in range(3):
        for half in range(2):
            compute(pair_at(k, 0, half))
            for ab in range(2):
                mine[k, ab, 2 * half : 2 * half + 2] = grads[ab]

    def add_pair(k, half, first, second):
        def group_step(index, carry):
            n, group = lax.div(index, 4), lax.rem(index, 4)
            a1, b1 = arrived(first.at[n], PANEL, group)
            a2, b2 = arrived(second.at[n], PANEL, group)
            mine[k, 0, 2 * half + n, rows_of(group), :] += a1 + a2
            mine[k, 1, 2 * half + n, rows_of(group), :] += b1 + b2
            return carry

        lax.fori_loop(0, 8, group_step, 0)

    def stage2(k, way, kind):
        number = 18 + (k * 2 + way) * 3 + kind
        axis = (k + 1) % 3
        return remote(
            send2.at[k, way, kind], recv2.at[k, way, kind], number, axis, 1 if way == 0 else -1
        )

    def pack_half(k, offset, half, target, added):
        block = lax.rem(place[(k + 1) % 3] + (offset + 4), 4)
        for group in range(2):
            rows = slice(half * HALF + group * GROUP, half * HALF + (group + 1) * GROUP)
            a, b = mine[k, 0, block, rows, :], mine[k, 1, block, rows, :]
            if added is not None:
                more_a, more_b = arrived(added, HALF, group)
                a, b = a + more_a, b + more_b
            store_code(target, HALF, group, *encode(a, b))

    for k in range(3):
        stage1(k, 0, 1).wait_recv()
        stage1(k, 1, 1).wait_recv()
        stage1(k, 0, 2).wait_recv()
        stage1(k, 1, 2).wait_recv()
        add_pair(k, 0, recv1.at[k, 0, 2], recv1.at[k, 1, 1])
        add_pair(k, 1, recv1.at[k, 0, 1], recv1.at[k, 1, 2])
        for way, sign in ways:
            pack_half(k, 2, way, send2.at[k, way, 0], None)
            stage2(k, way, 0).start()
        for way, sign in ways:
            pack_half(k, sign, 1 - way, send2.at[k, way, 1], None)
            stage2(k, way, 1).start()
    for k in range(3):
        for way, sign in ways:
            stage2(k, way, 0).wait_recv()
            pack_half(k, sign, way, send2.at[k, way, 2], recv2.at[k, way, 0])
            stage2(k, way, 2).start()

    def stage3(k, d):
        number = 36 + k * 3 + d - 1
        return remote(send3.at[k, d - 1], recv3.at[k, d - 1], number, (k + 2) % 3, d)

    for k in range(3):
        block = place[(k + 1) % 3]
        stage2(k, 0, 1).wait_recv()
        stage2(k, 1, 1).wait_recv()
        stage2(k, 0, 2).wait_recv()
        stage2(k, 1, 2).wait_recv()
        for group in range(4):
            half, inner = group // 2, group % 2
            first = recv2.at[k, 0, 2 - half]
            second = recv2.at[k, 1, 1 + half]
            a1, b1 = arrived(first, HALF, inner)
            a2, b2 = arrived(second, HALF, inner)
            rows = slice(group * GROUP, (group + 1) * GROUP)
            mine[k, 0, block, rows, :] += a1 + a2
            mine[k, 1, block, rows, :] += b1 + b2
        for d in (1, 2, 3):
            group = lax.rem(place[(k + 2) % 3] + d, 4)
            a, b = mine[k, 0, block, rows_of(group), :], mine[k, 1, block, rows_of(group), :]
            store_code(send3.at[k, d - 1], GROUP, 0, *encode(a, b))
            stage3(k, d).start()

    def spread3(k, d):
        group = place[(k + 2) % 3]
        number = 45 + (k * 3 + d - 1) * 2
        data = remote(
            shard.at[k, 0:GROUP], panel.at[k, rows_of(group)], number, (k + 2) % 3, d
        )
        scale = remote(
            shard.at[k, GROUP : GROUP + 8], scales.at[k, d - 1], number + 1, (k + 2) % 3, d
        )
        return data, scale

    def spread3_from(k, d):
        group = lax.rem(place[(k + 2) % 3] + (4 - d), 4)
        number = 45 + (k * 3 + d - 1) * 2
        data = remote(
            shard.at[k, 0:GROUP], panel.at[k, rows_of(group)], number, (k + 2) % 3, d
        )
        scale = remote(
            shard.at[k, GROUP : GROUP + 8], scales.at[k, d - 1], number + 1, (k + 2) % 3, d
        )
        return group, data, scale

    for k in range(3):
        block = place[(k + 1) % 3]
        own = place[(k + 2) % 3]
        a, b = mine[k, 0, block, rows_of(own), :], mine[k, 1, block, rows_of(own), :]
        for d in (1, 2, 3):
            stage3(k, d).wait_recv()
            more_a, more_b = arrived(recv3.at[k, d - 1], GROUP, 0)
            a, b = a + more_a, b + more_b
        number, copy = kept_copy(k)
        copy.wait()
        flags = jnp.where(number < 2 * LOWER_PAIRS, flags_at(kept[k], number * 128) * 2, 1)
        store_code(shard.at[k], GROUP, 0, *encode(a, b * flags.astype(F32)))
        for d in (1, 2, 3):
            for copy in spread3(k, d):
                copy.start()
        panel[k, rows_of(own), :] = shard[k, 0:GROUP, :]

    def at(k, first, second):
        return out.at[k * 16 + first * 4 + second]

    def turned(axis, distance):
        return lax.rem(place[axis] + (distance + 4), 4)

    def spread2(k, way, src, first, second):
        return remote(src, at(k, first, second), 63 + k * 4 + way, (k + 1) % 3, 1 - 2 * way)

    def pass2(k, way, first, second):
        rows = slice(0, HALF) if way == 0 else slice(HALF, FULL)
        ref = at(k, first, second).at[rows]
        return remote(ref, ref, 63 + k * 4 + 2 + way, (k + 1) % 3, 1 - 2 * way)

    def spread1(k, way, order, src, first, second):
        return remote(src, at(k, first, second), 75 + (k * 2 + way) * 6 + order, k, 1 - 2 * way)

    offsets = (0, -1, 1, 2)
    for k in range(3):
        merged = shard[k, GROUP : GROUP + 8, :]
        row = lax.broadcasted_iota(jnp.int32, (8, 128), 0)
        own = place[(k + 2) % 3]
        total = jnp.zeros((8, 128), jnp.int32)
        for d in (0, 1, 2, 3):
            if d == 0:
                group, tile = own, merged
            else:
                group, data, scale = spread3_from(k, d)
                data.wait_recv()
                scale.wait_recv()
                tile = scales[k, d - 1]
            total = jnp.where(row == 2 * group, tile[0:1], total)
            total = jnp.where(row == 2 * group + 1, tile[1:2], total)
        panel[k, PANEL:FULL, :] = total
        first, second = place[k], place[(k + 1) % 3]
        for way in range(2):
            spread2(k, way, panel.at[k], first, second).start()
        pltpu.make_async_copy(panel.at[k], at(k, first, second), copy_sem.at[k]).start()
        for way in range(2):
            spread1(k, way, 0, panel.at[k], first, second).start()
    for k in range(3):
        first = place[k]
        for way in range(2):
            second = turned((k + 1) % 3, 2 * way - 1)
            spread2(k, way, panel.at[k], first, second).wait_recv()
            pass2(k, way, first, second).start()
            for way1 in range(2):
                src = at(k, first, second)
                spread1(k, way1, 1 + way, src, first, second).start()
    for k in range(3):
        first, second = place[k], turned((k + 1) % 3, 2)
        for way in range(2):
            pass2(k, way, first, second).wait_recv()
        for way1 in range(2):
            src = at(k, first, second)
            spread1(k, way1, 3, src, first, second).start()

    def pass1(k, way, order, first):
        ref = at(k, first, turned((k + 1) % 3, offsets[order]))
        return remote(ref, ref, 75 + (k * 2 + way) * 6 + 4 + order % 2, k, 1 - 2 * way)

    passed = ((0, 0), (1, 2), (0, 1), (1, 3))
    seen = set()
    for way, order in passed:
        for k in range(3):
            first = turned(k, 2 * way - 1)
            second = turned((k + 1) % 3, offsets[order])
            spread1(k, way, order, panel.at[k], first, second).wait_recv()
            seen.add((k, way, order))
            pass1(k, way, order, first).start()
    for k in range(3):
        for way in range(2):
            for order in range(4):
                if (k, way, order) not in seen:
                    first = turned(k, 2 * way - 1)
                    second = turned((k + 1) % 3, offsets[order])
                    spread1(k, way, order, panel.at[k], first, second).wait_recv()
    for way, order in passed:
        for k in range(3):
            pass1(k, way, order, turned(k, 2)).wait_recv()

    for k in range(3):
        for way in range(2):
            for kind in range(3):
                if kind > 0:
                    stage1(k, way, kind).wait_send()
                stage2(k, way, kind).wait_send()
        for d in (1, 2, 3):
            stage3(k, d).wait_send()
            for copy in spread3(k, d):
                copy.wait_send()
        first, second = place[k], place[(k + 1) % 3]
        pltpu.make_async_copy(panel.at[k], at(k, first, second), copy_sem.at[k]).wait()
        for way in range(2):
            spread2(k, way, panel.at[k], first, second).wait_send()
            pass2(k, way, first, turned((k + 1) % 3, 2 * way - 1)).wait_send()
            for order in range(4):
                second_now = turned((k + 1) % 3, offsets[order])
                src = panel.at[k] if order == 0 else at(k, first, second_now)
                spread1(k, way, order, src, first, second_now).wait_send()
        for way, order in passed:
            pass1(k, way, order, turned(k, 2 * way - 1)).wait_send()


def summed_panels(xh, lr, da, du, words):
    vm = pl.BlockSpec(memory_space=pltpu.VMEM)
    i32 = jnp.int32
    messages = 75 + 36
    dma = pltpu.SemaphoreType.DMA
    return pl.pallas_call(
        sum_kernel,
        out_shape=pltpu.VMEM((2 * PAIRS, FULL, 128), i32),
        in_specs=[vm] * 4 + [pl.BlockSpec(memory_space=pl.ANY)],
        out_specs=pl.BlockSpec(memory_space=pl.ANY),
        scratch_shapes=[
            pltpu.VMEM((3, GROUP, 128), i32),
            pltpu.VMEM((2, 2, PANEL, 128), F32),
            pltpu.VMEM((3, 2, 4, PANEL, 128), F32),
            pltpu.VMEM((3, 2, 2, 2, FULL, 128), i32),
            pltpu.VMEM((3, 2, 3, 2, FULL, 128), i32),
            pltpu.VMEM((3, 2, 3, HALF + 8, 128), i32),
            pltpu.VMEM((3, 2, 3, HALF + 8, 128), i32),
            pltpu.VMEM((3, 3, GROUP + 8, 128), i32),
            pltpu.VMEM((3, 3, GROUP + 8, 128), i32),
            pltpu.VMEM((3, GROUP + 8, 128), i32),
            pltpu.VMEM((3, 3, 8, 128), i32),
            pltpu.VMEM((3, FULL, 128), i32),
            dma((messages,)),
            dma((messages,)),
            dma((3,)),
            dma((3,)),
        ],
        compiler_params=pltpu.CompilerParams(
            vmem_limit_bytes=SUM_VMEM, collective_id=1, has_side_effects=True
        ),
    )(xh, lr, da, du, words)


def unpack_kernel(panels, words_u, low_in, low_rec, low_bias, up_in, up_rec, up_bias, tail):
    step = pl.program_id(0)
    units, outs = low_in.shape[0], up_rec.shape[0]
    lower_steps, all_steps = 2 * LOWER_PAIRS // WIDTH, 2 * PAIRS // WIDTH

    def values(n, ab):
        parts = []
        n = jnp.minimum(step, all_steps - 1) * WIDTH + n
        for group in range(4):
            words = panels[n, group * GROUP : (group + 1) * GROUP, :]
            scale = factor(panels[n, PANEL + 2 * group + ab : PANEL + 2 * group + ab + 1, :])
            half = (words >> 16) if ab == 0 else ((words << 16) >> 16)
            parts.append(half.astype(F32) * scale)
        return jnp.concatenate(parts, axis=0)

    for n in range(WIDTH):
        cols = slice(n * 128, (n + 1) * 128)

        @pl.when(step < lower_steps)
        def _():
            a = values(n, 0)
            low_in[:, cols] = a[:units]
            low_bias[:, cols] = a[units : units + 1]
            b = values(n, 1)[:units]
            low_rec[:, cols] = b

        @pl.when((step >= lower_steps) & (step < all_steps))
        def _():
            a = values(n, 0)
            up_in[:, cols] = a[:units]
            up_bias[:, cols] = a[units : units + 1]
            b = values(n, 1)
            flags = flags_at(words_u[...], (step - lower_steps) * WIDTH * 128 + n * 128)
            up_rec[:, cols] = b[:outs] * (flags * 2).astype(F32)[:outs]
            if n % 2 == 0:
                index = (step - lower_steps) * (WIDTH // 2) + n // 2
                rows = pl.ds(pl.multiple_of(index * TAIL_ROWS, 8), TAIL_ROWS)
                tail[rows, :] = b[PANEL - TAIL_ROWS :]

    @pl.when(step == all_steps)
    def _():
        up_in[:, :128] = tail[:units]
        up_bias[:, :128] = tail[units : units + 1]
        flags = flags_at(words_u[...], 2 * (PAIRS - LOWER_PAIRS) * 128)
        up_rec[:, :128] = tail[PANEL : PANEL + outs] * (flags * 2).astype(F32)[:outs]


def unpack(panels, words_u, units, full, outs, full_u):
    sds = jax.ShapeDtypeStruct
    lower_steps, all_steps = 2 * LOWER_PAIRS // WIDTH, 2 * PAIRS // WIDTH
    wide = 128 * WIDTH
    lower = lambda i: (0, jnp.minimum(i, lower_steps - 1))
    upper = lambda i: (0, jnp.maximum(i - lower_steps, 0))
    return pl.pallas_call(
        unpack_kernel,
        grid=(all_steps + 1,),
        out_shape=(
            sds((units, full), F32),
            sds((units, full), F32),
            sds((1, full), F32),
            sds((units, full_u), F32),
            sds((outs, full_u), F32),
            sds((1, full_u), F32),
        ),
        in_specs=[
            pl.BlockSpec(memory_space=pltpu.VMEM),
            pl.BlockSpec(memory_space=pltpu.VMEM),
        ],
        out_specs=(
            pl.BlockSpec((units, wide), lower),
            pl.BlockSpec((units, wide), lower),
            pl.BlockSpec((1, wide), lower),
            pl.BlockSpec((units, wide), upper),
            pl.BlockSpec((outs, wide), upper),
            pl.BlockSpec((1, wide), upper),
        ),
        scratch_shapes=[pltpu.VMEM((6 * TAIL_ROWS, 128), F32)],
        compiler_params=pltpu.CompilerParams(vmem_limit_bytes=UNPACK_VMEM),
    )(panels, words_u)


def body(
    inputs,
    lower_lock,
    upper_lock,
    resets,
    lower_input,
    lower_recur,
    lower_bias,
    lower_drop,
    upper_input,
    upper_recur,
    upper_bias,
    upper_drop,
    grad_out,
):
    me = lax.axis_index("pipe")
    streams, steps, width = inputs.shape
    hidden_out, grad_inputs, da, du, xh, lr, words_l, words_u = recurrence(
        inputs,
        lower_lock,
        upper_lock,
        resets,
        grad_out,
        lower_drop.T,
        upper_drop.T,
        lower_bias.reshape(1, -1),
        upper_bias.reshape(1, -1),
        lower_recur,
        lower_input,
        upper_input,
        upper_recur,
    )
    rows_all = steps * ROWS
    panels = summed_panels(
        xh, lr, da.reshape(2, rows_all, da.shape[3]), du.reshape(2, rows_all, du.shape[3]), words_l
    )
    low_in, low_rec, low_bias, up_in, up_rec, up_bias = unpack(
        panels, words_u, *lower_recur.shape, *upper_recur.shape
    )

    def own(row):
        half = row.shape[1] // 2
        return lax.dynamic_slice_in_dim(row[0], me * half, half, 0)

    return (
        hidden_out,
        grad_inputs,
        low_in,
        low_rec,
        own(low_bias),
        up_in,
        up_rec,
        own(up_bias),
    )


def solution(mesh):
    return jax.shard_map(
        body,
        mesh=mesh,
        in_specs=(
            P("dp", None, None),
            P("dp", None),
            P("dp", None),
            P("dp", None),
            P("pipe", None),
            P("pipe", None),
            P("pipe"),
            P(),
            P("pipe", None),
            P("pipe", None),
            P("pipe"),
            P(),
            P("dp", None, None),
        ),
        out_specs=(
            P("dp", None, "pipe"),
            P("dp", None, "pipe"),
            P("pipe", None),
            P("pipe", None),
            P("pipe"),
            P("pipe", None),
            P("pipe", None),
            P("pipe"),
        ),
        check_vma=False,
    )
```

```python
import functools

import jax
import jax.numpy as jnp
from jax import lax
from jax.experimental import pallas as pl
from jax.experimental.pallas import tpu as pltpu
from jax.sharding import PartitionSpec as P

BF = jnp.bfloat16
F32 = jnp.float32
MESH = pl.DeviceIdType.MESH
ROWS = 16
VMEM_LIMIT = 62 * 2**20
TAIL_ROWS = 368
EARLY = 8
SUM_VMEM = 47 * 2**20
UNPACK_VMEM = 24 * 2**20


def ceil_to(value, multiple):
    return -(-value // multiple) * multiple


def split(value):
    high = value.astype(BF)
    low = (value - high.astype(F32)).astype(BF)
    return high, low


def fold(stacked):
    half = stacked.shape[0] // 2
    return stacked[:half] + stacked[half:]


def dot_nn(a, b):
    return jnp.dot(a, b, preferred_element_type=F32)


def dot_nt(a, b):
    return lax.dot_general(a, b, (((1,), (1,)), ((), ())), preferred_element_type=F32)


def torus():
    dp = lax.axis_index("dp")
    place = [lax.rem(dp, 4), lax.rem(lax.div(dp, 4), 4), lax.div(dp, 16)]
    stride = [1, 4, 16]

    def across(axis, distance):
        moved = lax.rem(place[axis] + (distance + 4), 4)
        return {"dp": dp + (moved - place[axis]) * stride[axis]}

    return place, across


def flags_at(words, column):
    column = lax.broadcasted_iota(jnp.int32, (1, 128), 1) + column
    index = (column * 52429) >> 20
    bit = column - index * 20
    index = jnp.broadcast_to(index & 127, words.shape)
    found = jnp.take_along_axis(words, index, axis=1, mode="promise_in_bounds")
    return (found >> bit) & 1


def recurrence_kernel(
    units,
    inputs,
    lower_lock,
    upper_lock,
    resets,
    grad_out,
    lower_drop,
    upper_drop,
    lower_bias,
    upper_bias,
    wrec_in,
    win_in,
    uin_in,
    urec_in,
    hid_o,
    dx_o,
    da_o,
    du_o,
    xh_o,
    lr_o,
    left_o,
    right_o,
    rows_l_o,
    rows_u_o,
    wrec_raw,
    win_raw,
    uin_raw,
    urec_raw,
    words_l,
    words_u,
    slab,
    keep_ref,
    lock_low,
    lock_ref,
    gout_ref,
    blo,
    bup,
    wrec_t,
    uin_t,
    urec_t,
    wrec,
    uin,
    urec,
    da_all,
    du_all,
    xh,
    lr,
    x2,
    hk2,
    ux2,
    hku2,
    dal,
    dau,
    proj,
    send_l,
    recv_l,
    send_u,
    recv_u,
    act_l,
    act_u,
    save_l,
    save_u,
    cell_l,
    cell_u,
    da_l,
    da_u,
    dstate_l,
    dstate_u,
    dx_up,
    acc,
    dx,
    fs_l,
    fr_l,
    fs_u,
    fr_u,
    bs_l,
    br_l,
    bs_u,
    br_u,
    far_s,
    far_r,
    in_sem,
    out_sem,
):
    streams, steps = resets.shape
    me = lax.axis_index("pipe")
    other = 1 - me
    peer = {"pipe": other}
    wide_k = wrec.shape[1]
    wide = wrec.shape[2]
    up_wide = uin.shape[2]
    up_k = urec.shape[1]
    lane = act_l.shape[1] - wide + units

    barrier = pltpu.get_barrier_semaphore()
    pl.semaphore_signal(barrier, inc=1, device_id=peer, device_id_type=MESH)
    place, across = torus()
    for axis in range(3):
        for d in (1, 2, 3):
            pl.semaphore_signal(barrier, inc=1, device_id=across(axis, d), device_id_type=MESH)
    loads = [
        pltpu.make_async_copy(win_in, win_raw, in_sem.at[0]),
        pltpu.make_async_copy(wrec_in, wrec_raw, in_sem.at[1]),
        pltpu.make_async_copy(uin_in, uin_raw, in_sem.at[2]),
        pltpu.make_async_copy(urec_in, urec_raw, in_sem.at[3]),
    ]
    for load in loads:
        load.start()
    pl.semaphore_wait(barrier, 10)

    def remote(src, dst, send_sem, recv_sem):
        return pltpu.make_async_remote_copy(
            src_ref=src,
            dst_ref=dst,
            send_sem=send_sem,
            recv_sem=recv_sem,
            device_id=peer,
            device_id_type=MESH,
        )

    full = wrec_raw.shape[1]
    held = wrec_raw.shape[0]
    held_u = urec_raw.shape[0]
    full_u = urec_raw.shape[1]
    unit_u = full_u // 8
    gate_u = up_wide // 4
    rows_all = steps * ROWS

    def to_rows(value, lanes, filler=0.0):
        more = lanes - value.shape[1]
        if more:
            value = jnp.concatenate([value, jnp.full((streams, more), filler, F32)], axis=1)
        return jnp.concatenate([value, jnp.zeros((ROWS - streams, lanes), F32)], axis=0)

    keep_ref[...] = jnp.zeros_like(keep_ref)
    for t in range(steps):
        now = 1.0 - resets[:, t : t + 1].astype(F32)
        keep_ref[t] = to_rows(jnp.broadcast_to(now, (streams, 128)), 128)
    blo[...] = jnp.zeros_like(blo)
    bup[...] = jnp.zeros_like(bup)
    def place_words(target, packed):
        rows, lanes = packed.shape
        more = target.shape[1] - lanes
        packed = jnp.concatenate([packed, jnp.zeros((rows, more), jnp.int32)], axis=1)
        target[0:rows, :] = packed

    words_l[...] = jnp.zeros_like(words_l)
    words_u[...] = jnp.zeros_like(words_u)
    for half in range(2):

        @pl.when(me == half)
        def _(half=half):
            mine = slice(half * units, (half + 1) * units)
            lock_low[...] = to_rows(lower_lock[:, mine].astype(F32) * 1.25, lane)
            lock_ref[...] = to_rows(upper_lock[:, mine].astype(F32) * 1.25, lane)
            one = jnp.full((streams, 1), 1.0, F32)
            for t in range(steps):
                now = inputs[:, t, mine] * lock_low[0:streams, 0:units]
                now = to_rows(jnp.concatenate([now, one], axis=1), lane)
                high, low = split(now)
                x2[t * ROWS : (t + 1) * ROWS] = high
                x2[rows_all + t * ROWS : rows_all + (t + 1) * ROWS] = low
                out = grad_out[:, t, half * unit_u : (half + 1) * unit_u]
                gout_ref[t] = to_rows(out, gate_u)
            place_words(words_l, lower_drop[:, mine])
            place_words(words_u, upper_drop[:, half * held_u : (half + 1) * held_u])
            bias = lower_bias[...].astype(F32)
            bias_u = upper_bias[...].astype(F32)
            for q in range(2):
                for i in range(2):
                    g = 2 * half + i
                    start = (2 * i + q) * units
                    blo[q, :, g * units : (g + 1) * units] = bias[:, start : start + units]
                    start = (2 * i + q) * unit_u
                    bup[q, :, g * gate_u : g * gate_u + unit_u] = bias_u[
                        :, start : start + unit_u
                    ]

    loads[0].wait()
    proj[:, :, :, wide - 128 :] = jnp.zeros((2, steps, ROWS, 128), F32)
    for q in range(2):
        for g in range(4):
            start, stop = (2 * g + q) * units, (2 * g + q + 1) * units
            first, last = start // 128 * 128, min(ceil_to(stop, 128), full)
            y = fold(dot_nn(x2[:, :held], win_raw[:, first:last]))
            y = y[:, start - first : stop - first] + blo[q, :, g * units : (g + 1) * units]
            proj[q, :, :, g * units : (g + 1) * units] = y.reshape(steps, ROWS, units)

    for load in loads[1:]:
        load.wait()
    sub = lax.broadcasted_iota(jnp.int32, (8, 128), 0)

    def flags_of(held, i):
        left, right = 8 * i // 20, (8 * i + 7) // 20
        now = jnp.broadcast_to(held[left : left + 1], (8, 128))
        if right != left:
            later = jnp.broadcast_to(held[right : right + 1], (8, 128))
            now = jnp.where(sub < 20 * right - 8 * i, now, later)
        bit = sub + 8 * i % 20
        bit = jnp.where(bit >= 20, bit - 20, bit)
        return (now >> bit) & 1

    def masked_columns(weight, words, first, lanes):
        rows, columns = weight.shape
        words = words[pl.ds(first, ceil_to(ceil_to(columns, 20) // 20, 8)), lanes]
        turned = jnp.transpose(weight.astype(F32))
        if rows < 128:
            turned = jnp.concatenate([turned, jnp.zeros((columns, 128 - rows), F32)], axis=1)
        out = []
        for i in range(columns // 8):
            now = turned[8 * i : 8 * i + 8]
            out.append(jnp.where(flags_of(words, i) != 0, now + now, 0.0))
        return jnp.concatenate(out, axis=0)

    block = 640
    row16 = lax.broadcasted_iota(jnp.int32, (ROWS, 128), 0)

    def lower_slab(rows, start):
        lanes = pl.ds(start, 128)
        many = min(128, wide_k - start) if isinstance(start, int) else 128

        def fill(index, carry):
            cols = pl.ds(pl.multiple_of(index * block, block), block)
            first = pl.multiple_of(index * (block // 20), block // 20)
            part = masked_columns(wrec_raw[rows, cols], words_l, first, lanes)
            slab[cols, :] = part
            return carry

        lax.fori_loop(0, full // block, fill, 0)
        last = full // block * block
        slab[last:full, :] = masked_columns(
            wrec_raw[rows, last:full], words_l, last // 20, lanes
        )
        target = pl.ds(start, many)
        tiles = units // ROWS
        for q in range(2):
            for g in range(4):
                shift = units * (g + q)
                base = (tiles + 1) * ROWS * g

                def move(index, carry, q=q, shift=shift, base=base):
                    for i in range(7):
                        row = pl.multiple_of(base + (index * 7 + i) * ROWS, ROWS)
                        now = slab[pl.ds(row + shift, ROWS), :]
                        wrec_t[q, pl.ds(row, ROWS), target] = now.astype(BF)[:, :many]
                    return carry

                lax.fori_loop(0, tiles // 7, move, 0)
                row = base + tiles * ROWS
                now = slab[row + shift : row + shift + ROWS, :]
                if g < 3:
                    later = slab[row + shift + units : row + shift + units + ROWS, :]
                else:
                    later = jnp.zeros((ROWS, 128), F32)
                now = jnp.where(row16 < units * (g + 1) - row, now, later)
                wrec_t[q, row : row + ROWS, target] = now.astype(BF)[:, :many]

    def lower_slab_step(index, carry):
        start = pl.multiple_of(index * 128, 128)
        lower_slab(pl.ds(start, 128), start)
        return carry

    lax.fori_loop(0, held // 128, lower_slab_step, 0)
    lower_slab(slice(held // 128 * 128, held), held // 128 * 128)

    def place_upper(target, turned, start, many):
        for q in range(2):
            for g in range(4):
                first = (2 * g + q) * unit_u
                part = turned[first : first + unit_u]
                part = jnp.concatenate([part, jnp.zeros((gate_u - unit_u, 128), F32)], axis=0)
                rows = slice(g * gate_u, (g + 1) * gate_u)
                target[q, rows, pl.ds(start, many)] = part.astype(BF)[:, :many]

    def upper_slab(index, carry):
        start = pl.multiple_of(index * 128, 128)
        turned = jnp.transpose(uin_raw[pl.ds(start, 128), :].astype(F32))
        place_upper(uin_t, turned, start, 128)
        return carry

    lax.fori_loop(0, held // 128, upper_slab, 0)
    start = held // 128 * 128
    turned = jnp.transpose(uin_raw[start:held, :].astype(F32))
    turned = jnp.concatenate([turned, jnp.zeros((full_u, 128 - held % 128), F32)], axis=1)
    place_upper(uin_t, turned, start, wide_k - start)
    for start in range(0, held_u, 128):
        stop = min(start + 128, held_u)
        lanes = pl.ds(start, 128)
        turned = [
            masked_columns(
                urec_raw[start:stop, i : min(i + block, full_u)], words_u, i // 20, lanes
            )
            for i in range(0, full_u, block)
        ]
        many = min(128, up_k - start)
        place_upper(urec_t, jnp.concatenate(turned, axis=0), start, many)
    for q in range(2):
        wrec[q] = jnp.transpose(wrec_t[q])
        uin[q] = jnp.transpose(uin_t[q])
        urec[q] = jnp.transpose(urec_t[q])
    rows_l_o[...] = jnp.transpose(words_l[...])
    rows_u_o[...] = jnp.transpose(words_u[...])

    early = EARLY * ROWS

    def place_left(target, row, count, high, low, first):
        steps_rows = high.shape[0]
        start = 2 * early if first else 0
        high, low = jnp.transpose(high)[:count], jnp.transpose(low)[:count]
        target[row : row + count, start : start + steps_rows] = high
        target[row : row + count, start + steps_rows : start + 2 * steps_rows] = low

    def place_steps(target, row, count, stack, first, last):
        width = stack.shape[2]
        high, low = [
            stack[first:last, i * ROWS : (i + 1) * ROWS, :].reshape((last - first) * ROWS, width)
            for i in (0, 1)
        ]
        place_left(target, row, count, high, low, first)

    place_left(xh, 0, wide_k, x2[0:early], x2[rows_all : rows_all + early], 0)
    place_left(xh, 0, wide_k, x2[early:rows_all], x2[rows_all + early :], EARLY)

    def far_copy(src, dst, number, axis, d):
        return pltpu.make_async_remote_copy(
            src_ref=src,
            dst_ref=dst,
            send_sem=far_s.at[number],
            recv_sem=far_r.at[number],
            device_id=across(axis, d),
            device_id_type=MESH,
        )

    lr_rows = lr.shape[0]

    def left_copy(k, d, kind, upper):
        lanes = slice(2 * early if kind == 2 else 0, 2 * early if kind == 1 else 2 * rows_all)
        if upper:
            src, rows = lr.at[:, lanes], slice(0, lr_rows)
        else:
            rows = slice(0, wide_k) if kind == 0 else slice(wide_k, 2 * wide_k)
            src = xh.at[rows, lanes]
        return far_copy(src, left_o.at[k, d - 1, rows, lanes], (k * 3 + d - 1) * 3 + kind, k, d)

    def for_left(kind, act, target):
        for k in range(3):
            for d in (1, 2, 3):
                lower_copy = left_copy(k, d, kind, False)
                if k < 2:
                    act(lower_copy)
                    continue
                is_lower = target(k, d) == 0

                @pl.when(is_lower)
                def _(copy=lower_copy):
                    act(copy)

                if kind > 0:
                    upper_copy = left_copy(k, d, kind, True)

                    @pl.when(jnp.logical_not(is_lower))
                    def _(copy=upper_copy):
                        act(copy)

    def at_peer(k, d):
        return lax.rem(place[k] + d, 4)

    def at_home(k, d):
        return place[k]

    for_left(0, lambda copy: copy.start(), at_peer)

    def right_copies(k, d, chunk, row, count, upper, target):
        rows = pl.ds(row, count)
        dst = right_o.at[k, d - 1, :, rows, 0:512]
        number = 27 + (k * 3 + d - 1) * 4 + chunk
        if not upper:
            col = (4 * k + (target if k < 2 else 0)) * 512
            src = da_all.at[:, rows, pl.ds(pl.multiple_of(col, 512), 512)]
            return [far_copy(src, dst, number, k, d)]
        col = pl.multiple_of(jnp.maximum(target - 1, 0) * 512, 512)
        tail_dst = right_o.at[k, d - 1, :, rows, 512:640]
        return [
            far_copy(du_all.at[:, rows, pl.ds(col, 512)], dst, number, k, d),
            far_copy(du_all.at[:, rows, 1536:1664], tail_dst, 63 + (d - 1) * 4 + chunk, k, d),
        ]

    def for_right(chunk, row, count, act, target):
        for k in range(3):
            for d in (1, 2, 3):
                goes = target(k, d)
                if k < 2:
                    for copy in right_copies(k, d, chunk, row, count, False, goes):
                        act(copy)
                    continue

                @pl.when(goes == 0)
                def _(k=k, d=d, goes=goes):
                    for copy in right_copies(k, d, chunk, row, count, False, goes):
                        act(copy)

                @pl.when(goes != 0)
                def _(k=k, d=d, goes=goes):
                    for copy in right_copies(k, d, chunk, row, count, True, goes):
                        act(copy)

    chunks = ((8, 4), (4, 4), (2, 2), (0, 2))

    act_l[...] = jnp.zeros_like(act_l)
    hk2[...] = jnp.zeros_like(hk2)
    ux2[...] = jnp.zeros_like(ux2)
    hku2[...] = jnp.zeros_like(hku2)
    cell_l[...] = jnp.zeros_like(cell_l)
    cell_u[...] = jnp.zeros_like(cell_u)

    def fcopy_l(t):
        return remote(send_l, recv_l.at[lax.rem(t, 2)], fs_l.at[t], fr_l.at[t])

    def fcopy_u(t):
        return remote(send_u, recv_u.at[lax.rem(t, 2)], fs_u.at[t], fr_u.at[t])

    def lower_send(t, first):
        if first:
            send_l[...] = proj[other, t]
        else:
            send_l[...] = fold(dot_nn(hk2[t, :, :wide_k], wrec[other])) + proj[other, t]
        fcopy_l(t).start()

    def lower_own(t, first):
        if first:
            act_l[:, :wide] = proj[me, t]
        else:
            act_l[:, :wide] = fold(dot_nn(hk2[t, :, :wide_k], wrec[me])) + proj[me, t]

    def upper_part(t, q):
        y = dot_nn(ux2[t, :, :wide_k], uin[q]) + dot_nn(hku2[t, :, :up_k], urec[q])
        return fold(y) + bup[q]

    def upper_send(t):
        send_u[...] = upper_part(t, other)
        fcopy_u(t).start()

    def upper_own(t):
        act_u[...] = upper_part(t, me)

    def keep_at(t, lanes):
        return jnp.concatenate([keep_ref[t]] * (ceil_to(lanes, 128) // 128), axis=1)[
            :, :lanes
        ]

    def cell_update(a_in, a_forget, a_cand, a_out, cell, keep_now, save, t):
        gate_in = jax.nn.sigmoid(a_in)
        forget = jax.nn.sigmoid(a_forget)
        cand = jnp.tanh(a_cand)
        gate_out = jax.nn.sigmoid(a_out)
        cell_keep = cell[...] * keep_now
        cell_new = forget * cell_keep + gate_in * cand
        squashed = jnp.tanh(cell_new)
        cell[...] = cell_new
        save[t, 0] = gate_in
        save[t, 1] = forget
        save[t, 2] = cand
        save[t, 3] = gate_out
        save[t, 4] = cell_keep
        save[t, 5] = squashed
        return gate_out * squashed

    def lower_finish(t):
        fcopy_l(t).wait()
        act_l[:, :wide] += recv_l[lax.rem(t, 2)]
        hidden = cell_update(
            act_l[:, 0:lane],
            act_l[:, units : units + lane],
            act_l[:, 2 * units : 2 * units + lane],
            act_l[:, 3 * units : 3 * units + lane],
            cell_l,
            keep_at(t, lane),
            save_l,
            t,
        )
        high, low = split(hidden * keep_at(t + 1, lane))
        hk2[t + 1, 0:ROWS] = high
        hk2[t + 1, ROWS:] = low
        ones_at = lax.broadcasted_iota(jnp.int32, (ROWS, lane), 1) == units
        high, low = split(jnp.where(ones_at, 1.0, hidden * lock_ref[...]))
        ux2[t, 0:ROWS] = high
        ux2[t, ROWS:] = low

    def upper_finish(t):
        fcopy_u(t).wait()
        a = act_u[...] + recv_u[lax.rem(t, 2)]
        hidden = cell_update(
            a[:, 0:gate_u],
            a[:, gate_u : 2 * gate_u],
            a[:, 2 * gate_u : 3 * gate_u],
            a[:, 3 * gate_u :],
            cell_u,
            keep_at(t, gate_u),
            save_u,
            t,
        )
        hid_o[:, pl.ds(t, 1), :] = hidden[:streams, :unit_u].reshape(streams, 1, unit_u)
        high, low = split(hidden * keep_at(t + 1, gate_u))
        hku2[t + 1, 0:ROWS] = high
        hku2[t + 1, ROWS:] = low

    lower_send(0, True)
    lower_own(0, True)
    lower_finish(0)

    def forward_round(r, carry):
        lower_send(r, False)
        upper_send(r - 1)
        lower_own(r, False)
        upper_own(r - 1)
        lower_finish(r)
        upper_finish(r - 1)

        @pl.when(r == EARLY - 1)
        def _():
            place_steps(xh, wide_k, wide_k, hk2, 0, EARLY)
            place_steps(lr, 0, wide_k, ux2, 0, EARLY)
            place_steps(lr, wide_k, up_k, hku2, 0, EARLY)
            for_left(1, lambda copy: copy.start(), at_peer)

        return carry

    lax.fori_loop(1, steps, forward_round, 0)
    upper_send(steps - 1)
    upper_own(steps - 1)
    upper_finish(steps - 1)

    place_steps(xh, wide_k, wide_k, hk2, EARLY, steps)
    place_steps(lr, 0, wide_k, ux2, EARLY, steps)
    place_steps(lr, wide_k, up_k, hku2, EARLY, steps)
    for_left(2, lambda copy: copy.start(), at_peer)

    da_all[...] = jnp.zeros_like(da_all)
    du_all[...] = jnp.zeros_like(du_all)

    def own_order(t, carry):
        to = pl.ds(pl.multiple_of(t * ROWS, ROWS), ROWS)
        for part in range(2):
            rows = slice(part * ROWS, (part + 1) * ROWS)
            for q in range(2):
                for g in range(4):
                    start = (2 * g + q) * units
                    da_all[part, to, start : start + units] = dal[
                        q, t, rows, g * units : (g + 1) * units
                    ]
                    start = (2 * g + q) * unit_u
                    du_all[part, to, start : start + unit_u] = dau[
                        q, t, rows, g * gate_u : g * gate_u + unit_u
                    ]
        return carry

    def send_right(chunk):
        first, count = chunks[chunk]
        lax.fori_loop(first, first + count, own_order, 0)
        for_right(chunk, first * ROWS, count * ROWS, lambda copy: copy.start(), at_peer)

    dstate_l[...] = jnp.zeros_like(dstate_l)
    dstate_u[...] = jnp.zeros_like(dstate_u)
    da_l[...] = jnp.zeros_like(da_l)

    def bcopy_l(t):
        return remote(dal.at[me, t], dal.at[me, t], bs_l.at[t], br_l.at[t])

    def bcopy_u(t):
        return remote(dau.at[me, t], dau.at[me, t], bs_u.at[t], br_u.at[t])

    def gate_grads(dy, dstate, save, keep_now, t):
        gate_in, forget, cand, gate_out = save[t, 0], save[t, 1], save[t, 2], save[t, 3]
        cell_keep, squashed = save[t, 4], save[t, 5]
        dh = dstate[0] + dy
        dc = dstate[1] + dh * gate_out * (1.0 - squashed * squashed)
        dstate[1] = dc * forget * keep_now
        return (
            dc * cand * gate_in * (1.0 - gate_in),
            dc * cell_keep * forget * (1.0 - forget),
            dc * gate_in * (1.0 - cand * cand),
            dh * squashed * gate_out * (1.0 - gate_out),
        )

    def lower_back_start(t):
        grads = gate_grads(dx_up[...] * lock_ref[...], dstate_l, save_l, keep_at(t, lane), t)
        for g in range(4):
            da_l[:, g * units : (g + 1) * units] = grads[g][:, :units]
        high, low = split(da_l[...])
        dal[me, t, 0:ROWS] = high
        dal[me, t, ROWS:] = low
        bcopy_l(t).start()

    def upper_back_start(t):
        grads = gate_grads(gout_ref[t], dstate_u, save_u, keep_at(t, gate_u), t)
        for g in range(4):
            high, low = split(grads[g])
            dau[me, t, 0:ROWS, g * gate_u : (g + 1) * gate_u] = high
            dau[me, t, ROWS:, g * gate_u : (g + 1) * gate_u] = low
        bcopy_u(t).start()

    def lower_back_part(t, q):
        return fold(dot_nn(dal[q, t], wrec_t[q]))

    def upper_back_part(t, q):
        grad = dau[q, t]
        return fold(dot_nn(grad, uin_t[q])), fold(dot_nn(grad, urec_t[q]))

    def lower_back_own(t):
        acc[:, :wide_k] = lower_back_part(t, me)

    def lower_back_finish(t):
        bcopy_l(t).wait()
        total = acc[:, :wide_k] + lower_back_part(t, other)
        dstate_l[0, :, :wide_k] = keep_at(t, wide_k) * total

    def upper_back_own(t):
        into_x, into_h = upper_back_part(t, me)
        dx_up[:, :wide_k] = into_x
        dstate_u[0, :, :up_k] = into_h

    def upper_back_finish(t):
        bcopy_u(t).wait()
        into_x, into_h = upper_back_part(t, other)
        dx_up[:, :wide_k] += into_x
        dstate_u[0, :, :up_k] = keep_at(t, up_k) * (dstate_u[0, :, :up_k] + into_h)

    dx_up[...] = jnp.zeros_like(dx_up)
    upper_back_start(steps - 1)
    upper_back_own(steps - 1)
    upper_back_finish(steps - 1)

    def backward_round(r, carry):
        t = steps - r
        lower_back_start(t)
        upper_back_start(t - 1)
        lower_back_own(t)
        upper_back_own(t - 1)
        lower_back_finish(t)
        upper_back_finish(t - 1)
        for chunk in range(3):

            @pl.when(t == chunks[chunk][0])
            def _(chunk=chunk):
                send_right(chunk)

        return carry

    lax.fori_loop(1, steps, backward_round, 0)
    lower_back_start(0)
    bcopy_l(0).wait()

    send_right(3)

    copies = [
        pltpu.make_async_copy(da_all, da_o, out_sem.at[0]),
        pltpu.make_async_copy(du_all, du_o, out_sem.at[1]),
        pltpu.make_async_copy(xh, xh_o, out_sem.at[2]),
        pltpu.make_async_copy(lr, lr_o, out_sem.at[3]),
    ]
    for copy in copies:
        copy.start()

    chunk = 512

    def input_grad(cols, width):
        grad = da_all[:, :, cols].reshape(2 * rows_all, width)
        return fold(dot_nt(grad, win_raw[:, cols]))

    tail = full // chunk * chunk
    dx[:, :held] = input_grad(slice(tail, full), full % chunk) if full % chunk else 0.0

    def input_grad_step(index, carry):
        dx[:, :held] += input_grad(pl.ds(pl.multiple_of(index * chunk, chunk), chunk), chunk)
        return carry

    lax.fori_loop(0, full // chunk, input_grad_step, 0)
    for t in range(steps):
        now = dx[t * ROWS : t * ROWS + streams, :held] * lock_low[0:streams, :held]
        dx_o[:, t, :] = now
    for copy in copies:
        copy.wait()
    for kind in range(3):
        for_left(kind, lambda copy: copy.wait_send(), at_peer)
        for_left(kind, lambda copy: copy.wait_recv(), at_home)
    for chunk in range(4):
        row, count = chunks[chunk][0] * ROWS, chunks[chunk][1] * ROWS
        for_right(chunk, row, count, lambda copy: copy.wait_send(), at_peer)
        for_right(chunk, row, count, lambda copy: copy.wait_recv(), at_home)


def recurrence(
    inputs,
    lower_lock,
    upper_lock,
    resets,
    grad_out,
    lower_drop,
    upper_drop,
    lower_bias,
    upper_bias,
    wrec,
    win,
    uin,
    urec,
):
    streams, steps = resets.shape
    units, full = wrec.shape
    outs, full_u = urec.shape
    wide_k = ceil_to(units, 16)
    wide = ceil_to(full // 2, 256)
    up_k = ceil_to(outs, 16)
    gate_u = ceil_to(outs, 128)
    up_wide = 4 * gate_u
    lane = ceil_to(units, 128)
    rows_all = steps * ROWS
    vm = pl.BlockSpec(memory_space=pltpu.VMEM)
    hbm = pl.BlockSpec(memory_space=pl.ANY)
    sds = jax.ShapeDtypeStruct
    i32 = jnp.int32
    shared = [
        ((2, rows_all, ceil_to(full, 512)), BF),
        ((2, rows_all, ceil_to(full_u, 128)), BF),
        ((2 * wide_k, 2 * rows_all), BF),
        ((wide_k + up_k, 2 * rows_all), BF),
    ]
    landed = [
        ((3, 3, 2 * wide_k, 2 * rows_all), BF),
        ((3, 3, 2, rows_all, 640), BF),
    ]
    raw = [(w.shape, BF) for w in (wrec, win, uin, urec)]
    dma = pltpu.SemaphoreType.DMA
    return pl.pallas_call(
        functools.partial(recurrence_kernel, units),
        out_shape=(sds((streams, steps, outs), F32), sds((streams, steps, units), F32))
        + tuple(sds(*s) for s in shared + landed)
        + (sds((lane, 256), i32), sds((ceil_to(outs, 128), 128), i32)),
        in_specs=[vm] * 9 + [hbm] * 4,
        out_specs=(vm, vm) + (hbm,) * len(shared + landed) + (vm, vm),
        scratch_shapes=[pltpu.VMEM(*s) for s in raw]
        + [
            pltpu.VMEM((256, lane), i32),
            pltpu.VMEM((128, ceil_to(outs, 128)), i32),
            pltpu.VMEM((ceil_to(full, 16), 128), F32),
            pltpu.VMEM((steps + 1, ROWS, 128), F32),
            pltpu.VMEM((ROWS, lane), F32),
            pltpu.VMEM((ROWS, lane), F32),
            pltpu.VMEM((steps, ROWS, gate_u), F32),
            pltpu.VMEM((2, 1, wide), F32),
            pltpu.VMEM((2, 1, up_wide), F32),
            pltpu.VMEM((2, wide, wide_k), BF),
            pltpu.VMEM((2, up_wide, wide_k), BF),
            pltpu.VMEM((2, up_wide, up_k), BF),
            pltpu.VMEM((2, wide_k, wide), BF),
            pltpu.VMEM((2, wide_k, up_wide), BF),
            pltpu.VMEM((2, up_k, up_wide), BF),
        ]
        + [pltpu.VMEM(*s) for s in shared]
        + [
            pltpu.VMEM((2 * rows_all, lane), BF),
            pltpu.VMEM((steps + 1, 2 * ROWS, lane), BF),
            pltpu.VMEM((steps, 2 * ROWS, lane), BF),
            pltpu.VMEM((steps + 1, 2 * ROWS, gate_u), BF),
            pltpu.VMEM((2, steps, 2 * ROWS, wide), BF),
            pltpu.VMEM((2, steps, 2 * ROWS, up_wide), BF),
            pltpu.VMEM((2, steps, ROWS, wide), F32),
            pltpu.VMEM((ROWS, wide), F32),
            pltpu.VMEM((2, ROWS, wide), F32),
            pltpu.VMEM((ROWS, up_wide), F32),
            pltpu.VMEM((2, ROWS, up_wide), F32),
            pltpu.VMEM((ROWS, wide + lane - units), F32),
            pltpu.VMEM((ROWS, up_wide), F32),
            pltpu.VMEM((steps, 6, ROWS, lane), F32),
            pltpu.VMEM((steps, 6, ROWS, gate_u), F32),
            pltpu.VMEM((ROWS, lane), F32),
            pltpu.VMEM((ROWS, gate_u), F32),
            pltpu.VMEM((ROWS, wide), F32),
            pltpu.VMEM((ROWS, up_wide), F32),
            pltpu.VMEM((2, ROWS, lane), F32),
            pltpu.VMEM((2, ROWS, gate_u), F32),
            pltpu.VMEM((ROWS, lane), F32),
            pltpu.VMEM((ROWS, lane), F32),
            pltpu.VMEM((rows_all, lane), F32),
        ]
        + [dma((steps,))] * 8
        + [dma((75,)), dma((75,)), dma((4,)), dma((4,))],
        compiler_params=pltpu.CompilerParams(
            vmem_limit_bytes=VMEM_LIMIT, collective_id=0, has_side_effects=True
        ),
    )(
        inputs,
        lower_lock,
        upper_lock,
        resets,
        grad_out,
        lower_drop,
        upper_drop,
        lower_bias,
        upper_bias,
        wrec,
        win,
        uin,
        urec,
    )


PANEL = 576
GROUP = 144
HALF = 2 * GROUP
FULL = PANEL + 8
PAIRS = 24
LOWER_PAIRS = 18
SMALLEST = 2.0**-111
WIDTH = 4


def code(group):
    largest = jnp.maximum(jnp.max(jnp.abs(group), axis=0, keepdims=True), SMALLEST)
    step = jnp.floor(jnp.log2(largest) * 64.0).astype(jnp.int32) + 2
    return step, 32767.0 * jnp.exp2(step.astype(F32) * (-1.0 / 64.0))


def factor(step):
    return jnp.exp2(step.astype(F32) * (1.0 / 64.0)) * (1.0 / 32767.0)


def encode(a, b):
    step_a, up_a = code(a)
    step_b, up_b = code(b)
    word_a = jnp.round(a * up_a).astype(jnp.int32)
    word_b = jnp.round(b * up_b).astype(jnp.int32)
    return (word_a << 16) | (word_b & 0xFFFF), step_a, step_b


def decode(words, step_a, step_b):
    a = (words >> 16).astype(F32) * factor(step_a)
    b = ((words << 16) >> 16).astype(F32) * factor(step_b)
    return a, b


def sum_kernel(
    xh,
    lr,
    da,
    du,
    far_left,
    far_right,
    words,
    out,
    kept,
    lhs,
    rhs,
    mine,
    send2,
    recv2,
    send3,
    recv3,
    shard,
    scales,
    panel,
    send_sem,
    recv_sem,
    copy_sem,
    kept_sem,
    left_sem,
    right_sem,
):
    place, peer = torus()
    barrier = pltpu.get_barrier_semaphore()
    for axis in range(3):
        for distance in (1, 2, 3):
            pl.semaphore_signal(
                barrier, inc=1, device_id=peer(axis, distance), device_id_type=MESH
            )
    pl.semaphore_wait(barrier, 9)

    def kept_copy(k):
        number = k * 16 + place[k] * 4 + place[(k + 1) % 3]
        rows = pl.ds(pl.multiple_of(place[(k + 2) % 3] * GROUP, GROUP), GROUP)
        part = jnp.minimum(lax.div(number, 20), 1)
        lanes = pl.ds(pl.multiple_of(part * 128, 128), 128)
        return number, pltpu.make_async_copy(words.at[rows, lanes], kept.at[k], kept_sem.at[k])

    for k in range(3):
        kept_copy(k)[1].start()

    def remote(src, dst, number, axis, distance):
        return pltpu.make_async_remote_copy(
            src_ref=src,
            dst_ref=dst,
            send_sem=send_sem.at[number],
            recv_sem=recv_sem.at[number],
            device_id=peer(axis, distance),
            device_id_type=MESH,
        )

    upper_here = place[2] != 0
    rows_all = da.shape[1]
    lr_rows = lr.shape[0]
    early = EARLY * ROWS

    def operand_copies(k, upper):
        copies = []
        for s in range(4):
            rows = slice(0, lr_rows if upper else 2 * PANEL)
            src = (lr if upper else xh) if s == 0 else far_left.at[k, s - 1]
            at = s * 640
            for i, (first, last) in enumerate(((0, 384), (0, 128), (256, 384))):
                to = lhs.at[k, rows, at : at + last - first]
                copies.append(
                    pltpu.make_async_copy(
                        src.at[rows, first:last], to, left_sem.at[(k * 4 + s) * 3 + i]
                    )
                )
                at += last - first
            sems = [right_sem.at[(k * 4 + s) * 2 + i] for i in (0, 1)]
            to = rhs.at[k, s, :, :, 0:512]
            if s > 0:
                src = far_right.at[k, s - 1, :, :, 0:512]
            elif upper:
                col = pl.multiple_of(jnp.maximum(place[k] - 1, 0) * 512, 512)
                src = du.at[:, :, pl.ds(col, 512)]
            else:
                col = pl.multiple_of((4 * k + (place[k] if k < 2 else 0)) * 512, 512)
                src = da.at[:, :, pl.ds(col, 512)]
            copies.append(pltpu.make_async_copy(src, to, sems[0]))
            if upper:
                src = far_right.at[k, s - 1, :, :, 512:640] if s > 0 else du.at[:, :, 1536:1664]
                copies.append(pltpu.make_async_copy(src, rhs.at[k, s, :, :, 512:640], sems[1]))
        return copies

    def for_operands(k, act):
        if k < 2:
            for copy in operand_copies(k, False):
                act(copy)
            return

        @pl.when(jnp.logical_not(upper_here))
        def _():
            for copy in operand_copies(k, False):
                act(copy)

        @pl.when(upper_here)
        def _():
            for copy in operand_copies(k, True):
                act(copy)

    for k in range(3):
        for_operands(k, lambda copy: copy.start())

    def right(k, cols, width):
        parts = []
        for s in range(4):
            high, low = rhs[k, s, 0, :, cols], rhs[k, s, 1, :, cols]
            parts += [high[:early], high[:early], high[early:], high[early:]]
            parts += [low[:early], low[early:], jnp.zeros((640 - 3 * rows_all, width), BF)]
        return jnp.concatenate(parts, axis=0)

    def compute(k, half):
        def lower():
            cols = pl.ds(pl.multiple_of(half * 256, 256), 256)
            y = dot_nn(lhs[k], right(k, cols, 256))
            for n in range(2):
                for ab in range(2):
                    now = y[ab * PANEL : (ab + 1) * PANEL, n * 128 : (n + 1) * 128]
                    mine[k, ab, 2 * half + n] = now

        def upper():
            cols = pl.ds(pl.multiple_of(half * 256, 256), 256)
            y = dot_nn(lhs[k, 0:lr_rows], right(k, cols, 256))
            index = 2 * (place[k] - 1) + half
            start = pl.multiple_of(jnp.clip(index, 0, 2) * TAIL_ROWS, 16)
            tail = right(k, slice(512, 640), 128)
            bottom = dot_nn(lhs[k, pl.ds(start, TAIL_ROWS)], tail)
            bottom = jnp.where(index < 3, bottom, 0.0)
            top = PANEL - TAIL_ROWS
            for n in range(2):
                cols = slice(n * 128, (n + 1) * 128)
                mine[k, 0, 2 * half + n] = y[:PANEL, cols]
                mine[k, 1, 2 * half + n, 0:top] = y[PANEL : PANEL + top, cols]
                mine[k, 1, 2 * half + n, top:] = bottom if n == 0 else jnp.zeros_like(bottom)

        if k < 2:
            lower()
        else:
            pl.when(jnp.logical_not(upper_here))(lower)
            pl.when(upper_here)(upper)

    def compute_part(k):
        for_operands(k, lambda copy: copy.wait())

        def step(half, carry):
            compute(k, half)
            return carry

        lax.fori_loop(0, 2, step, 0)

    @pl.when(upper_here)
    def _():
        lhs[2, lr_rows:, :] = jnp.zeros((2 * PANEL - lr_rows, lhs.shape[2]), BF)

    def rows_of(group):
        return pl.ds(pl.multiple_of(group * GROUP, 8), GROUP)

    def steps_at(ref, base, group):
        return ref[pl.ds(base + 2 * group, 1), :], ref[pl.ds(base + 2 * group + 1, 1), :]

    def store_code(ref, base, group, words, step_a, step_b):
        ref[rows_of(group), :] = words
        ref[pl.ds(base + 2 * group, 1), :] = step_a
        ref[pl.ds(base + 2 * group + 1, 1), :] = step_b

    def arrived(ref, base, group):
        return decode(ref[rows_of(group), :], *steps_at(ref, base, group))

    ways = ((0, 1), (1, -1))

    def stage2(k, way, kind):
        number = (k * 2 + way) * 3 + kind
        axis = (k + 1) % 3
        return remote(
            send2.at[k, way, kind], recv2.at[k, way, kind], number, axis, 1 if way == 0 else -1
        )

    def pack_half(k, offset, half, target, added):
        block = lax.rem(place[(k + 1) % 3] + (offset + 4), 4)
        for group in range(2):
            rows = slice(half * HALF + group * GROUP, half * HALF + (group + 1) * GROUP)
            a, b = mine[k, 0, block, rows, :], mine[k, 1, block, rows, :]
            if added is not None:
                more_a, more_b = arrived(added, HALF, group)
                a, b = a + more_a, b + more_b
            store_code(target, HALF, group, *encode(a, b))

    for k in range(3):
        compute_part(k)
        for way, sign in ways:
            pack_half(k, 2, way, send2.at[k, way, 0], None)
            stage2(k, way, 0).start()
        for way, sign in ways:
            pack_half(k, sign, 1 - way, send2.at[k, way, 1], None)
            stage2(k, way, 1).start()
    for k in range(3):
        for way, sign in ways:
            stage2(k, way, 0).wait_recv()
            pack_half(k, sign, way, send2.at[k, way, 2], recv2.at[k, way, 0])
            stage2(k, way, 2).start()

    def stage3(k, d):
        number = 18 + k * 3 + d - 1
        return remote(send3.at[k, d - 1], recv3.at[k, d - 1], number, (k + 2) % 3, d)

    for k in range(3):
        block = place[(k + 1) % 3]
        stage2(k, 0, 1).wait_recv()
        stage2(k, 1, 1).wait_recv()
        stage2(k, 0, 2).wait_recv()
        stage2(k, 1, 2).wait_recv()
        for group in range(4):
            half, inner = group // 2, group % 2
            first = recv2.at[k, 0, 2 - half]
            second = recv2.at[k, 1, 1 + half]
            a1, b1 = arrived(first, HALF, inner)
            a2, b2 = arrived(second, HALF, inner)
            rows = slice(group * GROUP, (group + 1) * GROUP)
            mine[k, 0, block, rows, :] += a1 + a2
            mine[k, 1, block, rows, :] += b1 + b2
        for d in (1, 2, 3):
            group = lax.rem(place[(k + 2) % 3] + d, 4)
            a, b = mine[k, 0, block, rows_of(group), :], mine[k, 1, block, rows_of(group), :]
            store_code(send3.at[k, d - 1], GROUP, 0, *encode(a, b))
            stage3(k, d).start()

    def spread3(k, d):
        group = place[(k + 2) % 3]
        number = 27 + (k * 3 + d - 1) * 2
        data = remote(
            shard.at[k, 0:GROUP], panel.at[k, rows_of(group)], number, (k + 2) % 3, d
        )
        scale = remote(
            shard.at[k, GROUP : GROUP + 8], scales.at[k, d - 1], number + 1, (k + 2) % 3, d
        )
        return data, scale

    def spread3_from(k, d):
        group = lax.rem(place[(k + 2) % 3] + (4 - d), 4)
        number = 27 + (k * 3 + d - 1) * 2
        data = remote(
            shard.at[k, 0:GROUP], panel.at[k, rows_of(group)], number, (k + 2) % 3, d
        )
        scale = remote(
            shard.at[k, GROUP : GROUP + 8], scales.at[k, d - 1], number + 1, (k + 2) % 3, d
        )
        return group, data, scale

    for k in range(3):
        block = place[(k + 1) % 3]
        own = place[(k + 2) % 3]
        a, b = mine[k, 0, block, rows_of(own), :], mine[k, 1, block, rows_of(own), :]
        for d in (1, 2, 3):
            stage3(k, d).wait_recv()
            more_a, more_b = arrived(recv3.at[k, d - 1], GROUP, 0)
            a, b = a + more_a, b + more_b
        number, copy = kept_copy(k)
        copy.wait()
        flags = jnp.where(number < 2 * LOWER_PAIRS, flags_at(kept[k], number * 128) * 2, 1)
        store_code(shard.at[k], GROUP, 0, *encode(a, b * flags.astype(F32)))
        for d in (1, 2, 3):
            for copy in spread3(k, d):
                copy.start()
        panel[k, rows_of(own), :] = shard[k, 0:GROUP, :]

    def at(k, first, second):
        return out.at[k * 16 + first * 4 + second]

    def turned(axis, distance):
        return lax.rem(place[axis] + (distance + 4), 4)

    def spread2(k, way, src, first, second):
        return remote(src, at(k, first, second), 45 + k * 4 + way, (k + 1) % 3, 1 - 2 * way)

    def pass2(k, way, first, second):
        rows = slice(0, HALF) if way == 0 else slice(HALF, FULL)
        ref = at(k, first, second).at[rows]
        return remote(ref, ref, 45 + k * 4 + 2 + way, (k + 1) % 3, 1 - 2 * way)

    def spread1(k, way, order, src, first, second):
        return remote(src, at(k, first, second), 57 + (k * 2 + way) * 6 + order, k, 1 - 2 * way)

    offsets = (0, -1, 1, 2)
    for k in range(3):
        merged = shard[k, GROUP : GROUP + 8, :]
        row = lax.broadcasted_iota(jnp.int32, (8, 128), 0)
        own = place[(k + 2) % 3]
        total = jnp.zeros((8, 128), jnp.int32)
        for d in (0, 1, 2, 3):
            if d == 0:
                group, tile = own, merged
            else:
                group, data, scale = spread3_from(k, d)
                data.wait_recv()
                scale.wait_recv()
                tile = scales[k, d - 1]
            total = jnp.where(row == 2 * group, tile[0:1], total)
            total = jnp.where(row == 2 * group + 1, tile[1:2], total)
        panel[k, PANEL:FULL, :] = total
        first, second = place[k], place[(k + 1) % 3]
        for way in range(2):
            spread2(k, way, panel.at[k], first, second).start()
        pltpu.make_async_copy(panel.at[k], at(k, first, second), copy_sem.at[k]).start()
        for way in range(2):
            spread1(k, way, 0, panel.at[k], first, second).start()
    for k in range(3):
        first = place[k]
        for way in range(2):
            second = turned((k + 1) % 3, 2 * way - 1)
            spread2(k, way, panel.at[k], first, second).wait_recv()
            pass2(k, way, first, second).start()
            for way1 in range(2):
                src = at(k, first, second)
                spread1(k, way1, 1 + way, src, first, second).start()
    for k in range(3):
        first, second = place[k], turned((k + 1) % 3, 2)
        for way in range(2):
            pass2(k, way, first, second).wait_recv()
        for way1 in range(2):
            src = at(k, first, second)
            spread1(k, way1, 3, src, first, second).start()

    def pass1(k, way, order, first):
        ref = at(k, first, turned((k + 1) % 3, offsets[order]))
        return remote(ref, ref, 57 + (k * 2 + way) * 6 + 4 + order % 2, k, 1 - 2 * way)

    passed = ((0, 0), (1, 2), (0, 1), (1, 3))
    seen = set()
    for way, order in passed:
        for k in range(3):
            first = turned(k, 2 * way - 1)
            second = turned((k + 1) % 3, offsets[order])
            spread1(k, way, order, panel.at[k], first, second).wait_recv()
            seen.add((k, way, order))
            pass1(k, way, order, first).start()
    for k in range(3):
        for way in range(2):
            for order in range(4):
                if (k, way, order) not in seen:
                    first = turned(k, 2 * way - 1)
                    second = turned((k + 1) % 3, offsets[order])
                    spread1(k, way, order, panel.at[k], first, second).wait_recv()
    for way, order in passed:
        for k in range(3):
            pass1(k, way, order, turned(k, 2)).wait_recv()

    for k in range(3):
        for way in range(2):
            for kind in range(3):
                stage2(k, way, kind).wait_send()
        for d in (1, 2, 3):
            stage3(k, d).wait_send()
            for copy in spread3(k, d):
                copy.wait_send()
        first, second = place[k], place[(k + 1) % 3]
        pltpu.make_async_copy(panel.at[k], at(k, first, second), copy_sem.at[k]).wait()
        for way in range(2):
            spread2(k, way, panel.at[k], first, second).wait_send()
            pass2(k, way, first, turned((k + 1) % 3, 2 * way - 1)).wait_send()
            for order in range(4):
                second_now = turned((k + 1) % 3, offsets[order])
                src = panel.at[k] if order == 0 else at(k, first, second_now)
                spread1(k, way, order, src, first, second_now).wait_send()
        for way, order in passed:
            pass1(k, way, order, turned(k, 2 * way - 1)).wait_send()


def summed_panels(xh, lr, da, du, left, right, words):
    i32 = jnp.int32
    messages = 57 + 36
    rows_all = da.shape[1]
    dma = pltpu.SemaphoreType.DMA
    return pl.pallas_call(
        sum_kernel,
        out_shape=pltpu.VMEM((2 * PAIRS, FULL, 128), i32),
        in_specs=[pl.BlockSpec(memory_space=pl.ANY)] * 7,
        out_specs=pl.BlockSpec(memory_space=pl.ANY),
        scratch_shapes=[
            pltpu.VMEM((3, GROUP, 128), i32),
            pltpu.VMEM((3, 2 * PANEL, 4 * 640), BF),
            pltpu.VMEM((3, 4, 2, rows_all, 640), BF),
            pltpu.VMEM((3, 2, 4, PANEL, 128), F32),
            pltpu.VMEM((3, 2, 3, HALF + 8, 128), i32),
            pltpu.VMEM((3, 2, 3, HALF + 8, 128), i32),
            pltpu.VMEM((3, 3, GROUP + 8, 128), i32),
            pltpu.VMEM((3, 3, GROUP + 8, 128), i32),
            pltpu.VMEM((3, GROUP + 8, 128), i32),
            pltpu.VMEM((3, 3, 8, 128), i32),
            pltpu.VMEM((3, FULL, 128), i32),
            dma((messages,)),
            dma((messages,)),
            dma((3,)),
            dma((3,)),
            dma((36,)),
            dma((24,)),
        ],
        compiler_params=pltpu.CompilerParams(
            vmem_limit_bytes=SUM_VMEM, collective_id=1, has_side_effects=True
        ),
    )(xh, lr, da, du, left, right, words)


def unpack_kernel(panels, words_u, low_in, low_rec, low_bias, up_in, up_rec, up_bias, tail):
    step = pl.program_id(0)
    units, outs = low_in.shape[0], up_rec.shape[0]
    lower_steps, all_steps = 2 * LOWER_PAIRS // WIDTH, 2 * PAIRS // WIDTH

    def values(n, ab):
        parts = []
        n = jnp.minimum(step, all_steps - 1) * WIDTH + n
        for group in range(4):
            words = panels[n, group * GROUP : (group + 1) * GROUP, :]
            scale = factor(panels[n, PANEL + 2 * group + ab : PANEL + 2 * group + ab + 1, :])
            half = (words >> 16) if ab == 0 else ((words << 16) >> 16)
            parts.append(half.astype(F32) * scale)
        return jnp.concatenate(parts, axis=0)

    for n in range(WIDTH):
        cols = slice(n * 128, (n + 1) * 128)

        @pl.when(step < lower_steps)
        def _():
            a = values(n, 0)
            low_in[:, cols] = a[:units]
            low_bias[:, cols] = a[units : units + 1]
            b = values(n, 1)[:units]
            low_rec[:, cols] = b

        @pl.when((step >= lower_steps) & (step < all_steps))
        def _():
            a = values(n, 0)
            up_in[:, cols] = a[:units]
            up_bias[:, cols] = a[units : units + 1]
            b = values(n, 1)
            flags = flags_at(words_u[...], (step - lower_steps) * WIDTH * 128 + n * 128)
            up_rec[:, cols] = b[:outs] * (flags * 2).astype(F32)[:outs]
            if n % 2 == 0:
                index = (step - lower_steps) * (WIDTH // 2) + n // 2
                rows = pl.ds(pl.multiple_of(index * TAIL_ROWS, 8), TAIL_ROWS)
                tail[rows, :] = b[PANEL - TAIL_ROWS :]

    @pl.when(step == all_steps)
    def _():
        up_in[:, :128] = tail[:units]
        up_bias[:, :128] = tail[units : units + 1]
        flags = flags_at(words_u[...], 2 * (PAIRS - LOWER_PAIRS) * 128)
        up_rec[:, :128] = tail[PANEL : PANEL + outs] * (flags * 2).astype(F32)[:outs]


def unpack(panels, words_u, units, full, outs, full_u):
    sds = jax.ShapeDtypeStruct
    lower_steps, all_steps = 2 * LOWER_PAIRS // WIDTH, 2 * PAIRS // WIDTH
    wide = 128 * WIDTH
    lower = lambda i: (0, jnp.minimum(i, lower_steps - 1))
    upper = lambda i: (0, jnp.maximum(i - lower_steps, 0))
    return pl.pallas_call(
        unpack_kernel,
        grid=(all_steps + 1,),
        out_shape=(
            sds((units, full), F32),
            sds((units, full), F32),
            sds((1, full), F32),
            sds((units, full_u), F32),
            sds((outs, full_u), F32),
            sds((1, full_u), F32),
        ),
        in_specs=[
            pl.BlockSpec(memory_space=pltpu.VMEM),
            pl.BlockSpec(memory_space=pltpu.VMEM),
        ],
        out_specs=(
            pl.BlockSpec((units, wide), lower),
            pl.BlockSpec((units, wide), lower),
            pl.BlockSpec((1, wide), lower),
            pl.BlockSpec((units, wide), upper),
            pl.BlockSpec((outs, wide), upper),
            pl.BlockSpec((1, wide), upper),
        ),
        scratch_shapes=[pltpu.VMEM((6 * TAIL_ROWS, 128), F32)],
        compiler_params=pltpu.CompilerParams(vmem_limit_bytes=UNPACK_VMEM),
    )(panels, words_u)


def body(
    inputs,
    lower_lock,
    upper_lock,
    resets,
    lower_input,
    lower_recur,
    lower_bias,
    lower_drop,
    upper_input,
    upper_recur,
    upper_bias,
    upper_drop,
    grad_out,
):
    me = lax.axis_index("pipe")
    streams, steps, width = inputs.shape
    hidden_out, grad_inputs, da, du, xh, lr, left, right, words_l, words_u = recurrence(
        inputs,
        lower_lock,
        upper_lock,
        resets,
        grad_out,
        lower_drop.T,
        upper_drop.T,
        lower_bias.reshape(1, -1),
        upper_bias.reshape(1, -1),
        lower_recur,
        lower_input,
        upper_input,
        upper_recur,
    )
    panels = summed_panels(xh, lr, da, du, left, right, words_l)
    low_in, low_rec, low_bias, up_in, up_rec, up_bias = unpack(
        panels, words_u, *lower_recur.shape, *upper_recur.shape
    )

    def own(row):
        half = row.shape[1] // 2
        return lax.dynamic_slice_in_dim(row[0], me * half, half, 0)

    return (
        hidden_out,
        grad_inputs,
        low_in,
        low_rec,
        own(low_bias),
        up_in,
        up_rec,
        own(up_bias),
    )


def solution(mesh):
    return jax.shard_map(
        body,
        mesh=mesh,
        in_specs=(
            P("dp", None, None),
            P("dp", None),
            P("dp", None),
            P("dp", None),
            P("pipe", None),
            P("pipe", None),
            P("pipe"),
            P(),
            P("pipe", None),
            P("pipe", None),
            P("pipe"),
            P(),
            P("dp", None, None),
        ),
        out_specs=(
            P("dp", None, "pipe"),
            P("dp", None, "pipe"),
            P("pipe", None),
            P("pipe", None),
            P("pipe"),
            P("pipe", None),
            P("pipe", None),
            P("pipe"),
        ),
        check_vma=False,
    )
```

```python
import functools

import jax
import jax.numpy as jnp
from jax import lax
from jax.experimental import pallas as pl
from jax.experimental.pallas import tpu as pltpu
from jax.sharding import PartitionSpec as P

BF = jnp.bfloat16
F32 = jnp.float32
MESH = pl.DeviceIdType.MESH
ROWS = 16
VMEM_LIMIT = 62 * 2**20
TAIL_ROWS = 368
EARLY = 8
SUM_VMEM = 47 * 2**20
UNPACK_VMEM = 24 * 2**20


def ceil_to(value, multiple):
    return -(-value // multiple) * multiple


def split(value):
    high = value.astype(BF)
    low = (value - high.astype(F32)).astype(BF)
    return high, low


def fold(stacked):
    half = stacked.shape[0] // 2
    return stacked[:half] + stacked[half:]


def dot_nn(a, b):
    return jnp.dot(a, b, preferred_element_type=F32)


def dot_nt(a, b):
    return lax.dot_general(a, b, (((1,), (1,)), ((), ())), preferred_element_type=F32)


def torus():
    dp = lax.axis_index("dp")
    place = [lax.rem(dp, 4), lax.rem(lax.div(dp, 4), 4), lax.div(dp, 16)]
    stride = [1, 4, 16]

    def across(axis, distance):
        moved = lax.rem(place[axis] + (distance + 4), 4)
        return {"dp": dp + (moved - place[axis]) * stride[axis]}

    return place, across


def flags_at(words, column):
    column = lax.broadcasted_iota(jnp.int32, (1, 128), 1) + column
    index = (column * 52429) >> 20
    bit = column - index * 20
    index = jnp.broadcast_to(index & 127, words.shape)
    found = jnp.take_along_axis(words, index, axis=1, mode="promise_in_bounds")
    return (found >> bit) & 1


def recurrence_kernel(
    units,
    inputs,
    lower_lock,
    upper_lock,
    resets,
    grad_out,
    lower_drop,
    upper_drop,
    lower_bias,
    upper_bias,
    wrec_in,
    win_in,
    uin_in,
    urec_in,
    hid_o,
    dx_o,
    da_o,
    du_o,
    xh_o,
    lr_o,
    left_o,
    right_o,
    rows_l_o,
    rows_u_o,
    wrec_raw,
    win_raw,
    uin_raw,
    urec_raw,
    words_l,
    words_u,
    slab,
    keep_ref,
    lock_low,
    lock_ref,
    gout_ref,
    blo,
    bup,
    wrec_t,
    uin_t,
    urec_t,
    wrec,
    uin,
    urec,
    da_all,
    du_all,
    xh,
    lr,
    x2,
    hk2,
    ux2,
    hku2,
    dal,
    dau,
    proj,
    send_l,
    recv_l,
    send_u,
    recv_u,
    act_l,
    act_u,
    save_l,
    save_u,
    cell_l,
    cell_u,
    da_l,
    da_u,
    dstate_l,
    dstate_u,
    dx_up,
    acc,
    dx,
    fs_l,
    fr_l,
    fs_u,
    fr_u,
    bs_l,
    br_l,
    bs_u,
    br_u,
    far_s,
    far_r,
    in_sem,
    out_sem,
):
    streams, steps = resets.shape
    me = lax.axis_index("pipe")
    other = 1 - me
    peer = {"pipe": other}
    wide_k = wrec.shape[1]
    wide = wrec.shape[2]
    up_wide = uin.shape[2]
    up_k = urec.shape[1]
    lane = act_l.shape[1] - wide + units

    barrier = pltpu.get_barrier_semaphore()
    pl.semaphore_signal(barrier, inc=1, device_id=peer, device_id_type=MESH)
    place, across = torus()
    for axis in range(3):
        for d in (1, 2, 3):
            pl.semaphore_signal(barrier, inc=1, device_id=across(axis, d), device_id_type=MESH)
    loads = [
        pltpu.make_async_copy(win_in, win_raw, in_sem.at[0]),
        pltpu.make_async_copy(wrec_in, wrec_raw, in_sem.at[1]),
        pltpu.make_async_copy(uin_in, uin_raw, in_sem.at[2]),
        pltpu.make_async_copy(urec_in, urec_raw, in_sem.at[3]),
    ]
    for load in loads:
        load.start()
    pl.semaphore_wait(barrier, 10)

    def remote(src, dst, send_sem, recv_sem):
        return pltpu.make_async_remote_copy(
            src_ref=src,
            dst_ref=dst,
            send_sem=send_sem,
            recv_sem=recv_sem,
            device_id=peer,
            device_id_type=MESH,
        )

    full = wrec_raw.shape[1]
    held = wrec_raw.shape[0]
    held_u = urec_raw.shape[0]
    full_u = urec_raw.shape[1]
    unit_u = full_u // 8
    gate_u = up_wide // 4
    rows_all = steps * ROWS

    def to_rows(value, lanes, filler=0.0):
        more = lanes - value.shape[1]
        if more:
            value = jnp.concatenate([value, jnp.full((streams, more), filler, F32)], axis=1)
        return jnp.concatenate([value, jnp.zeros((ROWS - streams, lanes), F32)], axis=0)

    keep_ref[...] = jnp.zeros_like(keep_ref)
    for t in range(steps):
        now = 1.0 - resets[:, t : t + 1].astype(F32)
        keep_ref[t] = to_rows(jnp.broadcast_to(now, (streams, 128)), 128)
    blo[...] = jnp.zeros_like(blo)
    bup[...] = jnp.zeros_like(bup)
    def place_words(target, packed):
        rows, lanes = packed.shape
        more = target.shape[1] - lanes
        packed = jnp.concatenate([packed, jnp.zeros((rows, more), jnp.int32)], axis=1)
        target[0:rows, :] = packed

    words_l[...] = jnp.zeros_like(words_l)
    words_u[...] = jnp.zeros_like(words_u)
    for half in range(2):

        @pl.when(me == half)
        def _(half=half):
            mine = slice(half * units, (half + 1) * units)
            lock_low[...] = to_rows(lower_lock[:, mine].astype(F32) * 1.25, lane)
            lock_ref[...] = to_rows(upper_lock[:, mine].astype(F32) * 1.25, lane)
            one = jnp.full((streams, 1), 1.0, F32)
            for t in range(steps):
                now = inputs[:, t, mine] * lock_low[0:streams, 0:units]
                now = to_rows(jnp.concatenate([now, one], axis=1), lane)
                high, low = split(now)
                x2[t * ROWS : (t + 1) * ROWS] = high
                x2[rows_all + t * ROWS : rows_all + (t + 1) * ROWS] = low
                out = grad_out[:, t, half * unit_u : (half + 1) * unit_u]
                gout_ref[t] = to_rows(out, gate_u)
            place_words(words_l, lower_drop[:, mine])
            place_words(words_u, upper_drop[:, half * held_u : (half + 1) * held_u])
            bias = lower_bias[...].astype(F32)
            bias_u = upper_bias[...].astype(F32)
            for q in range(2):
                for i in range(2):
                    g = 2 * half + i
                    start = (2 * i + q) * units
                    blo[q, :, g * units : (g + 1) * units] = bias[:, start : start + units]
                    start = (2 * i + q) * unit_u
                    bup[q, :, g * gate_u : g * gate_u + unit_u] = bias_u[
                        :, start : start + unit_u
                    ]

    loads[0].wait()
    proj[:, :, :, wide - 128 :] = jnp.zeros((2, steps, ROWS, 128), F32)
    for q in range(2):
        for g in range(4):
            start, stop = (2 * g + q) * units, (2 * g + q + 1) * units
            first, last = start // 128 * 128, min(ceil_to(stop, 128), full)
            y = fold(dot_nn(x2[:, :held], win_raw[:, first:last]))
            y = y[:, start - first : stop - first] + blo[q, :, g * units : (g + 1) * units]
            proj[q, :, :, g * units : (g + 1) * units] = y.reshape(steps, ROWS, units)

    for load in loads[1:]:
        load.wait()
    sub = lax.broadcasted_iota(jnp.int32, (8, 128), 0)

    def flags_of(held, i):
        left, right = 8 * i // 20, (8 * i + 7) // 20
        now = jnp.broadcast_to(held[left : left + 1], (8, 128))
        if right != left:
            later = jnp.broadcast_to(held[right : right + 1], (8, 128))
            now = jnp.where(sub < 20 * right - 8 * i, now, later)
        bit = sub + 8 * i % 20
        bit = jnp.where(bit >= 20, bit - 20, bit)
        return (now >> bit) & 1

    def masked_columns(weight, words, first, lanes):
        rows, columns = weight.shape
        words = words[pl.ds(first, ceil_to(ceil_to(columns, 20) // 20, 8)), lanes]
        turned = jnp.transpose(weight.astype(F32))
        if rows < 128:
            turned = jnp.concatenate([turned, jnp.zeros((columns, 128 - rows), F32)], axis=1)
        out = []
        for i in range(columns // 8):
            now = turned[8 * i : 8 * i + 8]
            out.append(jnp.where(flags_of(words, i) != 0, now + now, 0.0))
        return jnp.concatenate(out, axis=0)

    block = 640
    row16 = lax.broadcasted_iota(jnp.int32, (ROWS, 128), 0)

    def lower_slab(rows, start):
        lanes = pl.ds(start, 128)
        many = min(128, wide_k - start) if isinstance(start, int) else 128

        def fill(index, carry):
            cols = pl.ds(pl.multiple_of(index * block, block), block)
            first = pl.multiple_of(index * (block // 20), block // 20)
            part = masked_columns(wrec_raw[rows, cols], words_l, first, lanes)
            slab[cols, :] = part
            return carry

        lax.fori_loop(0, full // block, fill, 0)
        last = full // block * block
        slab[last:full, :] = masked_columns(
            wrec_raw[rows, last:full], words_l, last // 20, lanes
        )
        target = pl.ds(start, many)
        tiles = units // ROWS
        for q in range(2):
            for g in range(4):
                shift = units * (g + q)
                base = (tiles + 1) * ROWS * g

                def move(index, carry, q=q, shift=shift, base=base):
                    for i in range(7):
                        row = pl.multiple_of(base + (index * 7 + i) * ROWS, ROWS)
                        now = slab[pl.ds(row + shift, ROWS), :]
                        wrec_t[q, pl.ds(row, ROWS), target] = now.astype(BF)[:, :many]
                    return carry

                lax.fori_loop(0, tiles // 7, move, 0)
                row = base + tiles * ROWS
                now = slab[row + shift : row + shift + ROWS, :]
                if g < 3:
                    later = slab[row + shift + units : row + shift + units + ROWS, :]
                else:
                    later = jnp.zeros((ROWS, 128), F32)
                now = jnp.where(row16 < units * (g + 1) - row, now, later)
                wrec_t[q, row : row + ROWS, target] = now.astype(BF)[:, :many]

    def lower_slab_step(index, carry):
        start = pl.multiple_of(index * 128, 128)
        lower_slab(pl.ds(start, 128), start)
        return carry

    lax.fori_loop(0, held // 128, lower_slab_step, 0)
    lower_slab(slice(held // 128 * 128, held), held // 128 * 128)

    def place_upper(target, turned, start, many):
        for q in range(2):
            for g in range(4):
                first = (2 * g + q) * unit_u
                part = turned[first : first + unit_u]
                part = jnp.concatenate([part, jnp.zeros((gate_u - unit_u, 128), F32)], axis=0)
                rows = slice(g * gate_u, (g + 1) * gate_u)
                target[q, rows, pl.ds(start, many)] = part.astype(BF)[:, :many]

    def upper_slab(index, carry):
        start = pl.multiple_of(index * 128, 128)
        turned = jnp.transpose(uin_raw[pl.ds(start, 128), :].astype(F32))
        place_upper(uin_t, turned, start, 128)
        return carry

    lax.fori_loop(0, held // 128, upper_slab, 0)
    start = held // 128 * 128
    turned = jnp.transpose(uin_raw[start:held, :].astype(F32))
    turned = jnp.concatenate([turned, jnp.zeros((full_u, 128 - held % 128), F32)], axis=1)
    place_upper(uin_t, turned, start, wide_k - start)
    for start in range(0, held_u, 128):
        stop = min(start + 128, held_u)
        lanes = pl.ds(start, 128)
        turned = [
            masked_columns(
                urec_raw[start:stop, i : min(i + block, full_u)], words_u, i // 20, lanes
            )
            for i in range(0, full_u, block)
        ]
        many = min(128, up_k - start)
        place_upper(urec_t, jnp.concatenate(turned, axis=0), start, many)
    for q in range(2):
        wrec[q] = jnp.transpose(wrec_t[q])
        uin[q] = jnp.transpose(uin_t[q])
        urec[q] = jnp.transpose(urec_t[q])
    rows_l_o[...] = jnp.transpose(words_l[...])
    rows_u_o[...] = jnp.transpose(words_u[...])

    early = EARLY * ROWS

    def place_left(target, row, count, high, low, first):
        steps_rows = high.shape[0]
        start = 2 * early if first else 0
        high, low = jnp.transpose(high)[:count], jnp.transpose(low)[:count]
        target[row : row + count, start : start + steps_rows] = high
        target[row : row + count, start + steps_rows : start + 2 * steps_rows] = low

    def place_steps(target, row, count, stack, first, last):
        width = stack.shape[2]
        high, low = [
            stack[first:last, i * ROWS : (i + 1) * ROWS, :].reshape((last - first) * ROWS, width)
            for i in (0, 1)
        ]
        place_left(target, row, count, high, low, first)

    place_left(xh, 0, wide_k, x2[0:early], x2[rows_all : rows_all + early], 0)
    place_left(xh, 0, wide_k, x2[early:rows_all], x2[rows_all + early :], EARLY)

    def far_copy(src, dst, number, axis, d):
        return pltpu.make_async_remote_copy(
            src_ref=src,
            dst_ref=dst,
            send_sem=far_s.at[number],
            recv_sem=far_r.at[number],
            device_id=across(axis, d),
            device_id_type=MESH,
        )

    lr_rows = lr.shape[0]

    def left_copy(k, d, kind, upper):
        lanes = slice(2 * early if kind == 2 else 0, 2 * early if kind == 1 else 2 * rows_all)
        if upper:
            src, rows = lr.at[:, lanes], slice(0, lr_rows)
        else:
            rows = slice(0, wide_k) if kind == 0 else slice(wide_k, 2 * wide_k)
            src = xh.at[rows, lanes]
        return far_copy(src, left_o.at[k, d - 1, rows, lanes], (k * 3 + d - 1) * 3 + kind, k, d)

    def for_left(kind, act, target):
        for k in range(3):
            for d in (1, 2, 3):
                lower_copy = left_copy(k, d, kind, False)
                if k < 2:
                    act(lower_copy)
                    continue
                is_lower = target(k, d) == 0

                @pl.when(is_lower)
                def _(copy=lower_copy):
                    act(copy)

                if kind > 0:
                    upper_copy = left_copy(k, d, kind, True)

                    @pl.when(jnp.logical_not(is_lower))
                    def _(copy=upper_copy):
                        act(copy)

    def at_peer(k, d):
        return lax.rem(place[k] + d, 4)

    def at_home(k, d):
        return place[k]

    for_left(0, lambda copy: copy.start(), at_peer)

    def right_copies(k, d, chunk, row, count, upper, target):
        rows = pl.ds(row, count)
        dst = right_o.at[k, d - 1, :, rows, 0:512]
        number = 27 + (k * 3 + d - 1) * 4 + chunk
        if not upper:
            col = (4 * k + (target if k < 2 else 0)) * 512
            src = da_all.at[:, rows, pl.ds(pl.multiple_of(col, 512), 512)]
            return [far_copy(src, dst, number, k, d)]
        col = pl.multiple_of(jnp.maximum(target - 1, 0) * 512, 512)
        tail_dst = right_o.at[k, d - 1, :, rows, 512:640]
        return [
            far_copy(du_all.at[:, rows, pl.ds(col, 512)], dst, number, k, d),
            far_copy(du_all.at[:, rows, 1536:1664], tail_dst, 63 + (d - 1) * 4 + chunk, k, d),
        ]

    def for_right(chunk, row, count, act, target):
        for k in range(3):
            for d in (1, 2, 3):
                goes = target(k, d)
                if k < 2:
                    for copy in right_copies(k, d, chunk, row, count, False, goes):
                        act(copy)
                    continue

                @pl.when(goes == 0)
                def _(k=k, d=d, goes=goes):
                    for copy in right_copies(k, d, chunk, row, count, False, goes):
                        act(copy)

                @pl.when(goes != 0)
                def _(k=k, d=d, goes=goes):
                    for copy in right_copies(k, d, chunk, row, count, True, goes):
                        act(copy)

    chunks = ((8, 4), (4, 4), (2, 2), (0, 2))

    act_l[...] = jnp.zeros_like(act_l)
    hk2[...] = jnp.zeros_like(hk2)
    ux2[...] = jnp.zeros_like(ux2)
    hku2[...] = jnp.zeros_like(hku2)
    cell_l[...] = jnp.zeros_like(cell_l)
    cell_u[...] = jnp.zeros_like(cell_u)

    def fcopy_l(t):
        return remote(send_l, recv_l.at[lax.rem(t, 2)], fs_l.at[t], fr_l.at[t])

    def fcopy_u(t):
        return remote(send_u, recv_u.at[lax.rem(t, 2)], fs_u.at[t], fr_u.at[t])

    def lower_send(t, first):
        if first:
            send_l[...] = proj[other, t]
        else:
            send_l[...] = fold(dot_nn(hk2[t, :, :wide_k], wrec[other])) + proj[other, t]
        fcopy_l(t).start()

    def lower_own(t, first):
        if first:
            act_l[:, :wide] = proj[me, t]
        else:
            act_l[:, :wide] = fold(dot_nn(hk2[t, :, :wide_k], wrec[me])) + proj[me, t]

    def upper_part(t, q):
        y = dot_nn(ux2[t, :, :wide_k], uin[q]) + dot_nn(hku2[t, :, :up_k], urec[q])
        return fold(y) + bup[q]

    def upper_send(t):
        send_u[...] = upper_part(t, other)
        fcopy_u(t).start()

    def upper_own(t):
        act_u[...] = upper_part(t, me)

    def keep_at(t, lanes):
        return jnp.concatenate([keep_ref[t]] * (ceil_to(lanes, 128) // 128), axis=1)[
            :, :lanes
        ]

    def cell_update(a_in, a_forget, a_cand, a_out, cell, keep_now, save, t):
        gate_in = jax.nn.sigmoid(a_in)
        forget = jax.nn.sigmoid(a_forget)
        cand = jnp.tanh(a_cand)
        gate_out = jax.nn.sigmoid(a_out)
        cell_keep = cell[...] * keep_now
        cell_new = forget * cell_keep + gate_in * cand
        squashed = jnp.tanh(cell_new)
        cell[...] = cell_new
        save[t, 0] = gate_in
        save[t, 1] = forget
        save[t, 2] = cand
        save[t, 3] = gate_out
        save[t, 4] = cell_keep
        save[t, 5] = squashed
        return gate_out * squashed

    def lower_finish(t):
        fcopy_l(t).wait()
        act_l[:, :wide] += recv_l[lax.rem(t, 2)]
        hidden = cell_update(
            act_l[:, 0:lane],
            act_l[:, units : units + lane],
            act_l[:, 2 * units : 2 * units + lane],
            act_l[:, 3 * units : 3 * units + lane],
            cell_l,
            keep_at(t, lane),
            save_l,
            t,
        )
        high, low = split(hidden * keep_at(t + 1, lane))
        hk2[t + 1, 0:ROWS] = high
        hk2[t + 1, ROWS:] = low
        ones_at = lax.broadcasted_iota(jnp.int32, (ROWS, lane), 1) == units
        high, low = split(jnp.where(ones_at, 1.0, hidden * lock_ref[...]))
        ux2[t, 0:ROWS] = high
        ux2[t, ROWS:] = low

    def upper_finish(t):
        fcopy_u(t).wait()
        a = act_u[...] + recv_u[lax.rem(t, 2)]
        hidden = cell_update(
            a[:, 0:gate_u],
            a[:, gate_u : 2 * gate_u],
            a[:, 2 * gate_u : 3 * gate_u],
            a[:, 3 * gate_u :],
            cell_u,
            keep_at(t, gate_u),
            save_u,
            t,
        )
        hid_o[:, pl.ds(t, 1), :] = hidden[:streams, :unit_u].reshape(streams, 1, unit_u)
        high, low = split(hidden * keep_at(t + 1, gate_u))
        hku2[t + 1, 0:ROWS] = high
        hku2[t + 1, ROWS:] = low

    lower_send(0, True)
    lower_own(0, True)
    lower_finish(0)

    def forward_round(r, carry):
        lower_send(r, False)
        upper_send(r - 1)
        lower_own(r, False)
        upper_own(r - 1)
        lower_finish(r)
        upper_finish(r - 1)

        @pl.when(r == EARLY - 1)
        def _():
            place_steps(xh, wide_k, wide_k, hk2, 0, EARLY)
            place_steps(lr, 0, wide_k, ux2, 0, EARLY)
            place_steps(lr, wide_k, up_k, hku2, 0, EARLY)
            for_left(1, lambda copy: copy.start(), at_peer)

        return carry

    lax.fori_loop(1, steps, forward_round, 0)
    upper_send(steps - 1)
    upper_own(steps - 1)
    upper_finish(steps - 1)

    place_steps(xh, wide_k, wide_k, hk2, EARLY, steps)
    place_steps(lr, 0, wide_k, ux2, EARLY, steps)
    place_steps(lr, wide_k, up_k, hku2, EARLY, steps)
    for_left(2, lambda copy: copy.start(), at_peer)

    da_all[...] = jnp.zeros_like(da_all)
    du_all[...] = jnp.zeros_like(du_all)

    def own_order(t, carry):
        to = pl.ds(pl.multiple_of(t * ROWS, ROWS), ROWS)
        for part in range(2):
            rows = slice(part * ROWS, (part + 1) * ROWS)
            for q in range(2):
                for g in range(4):
                    start = (2 * g + q) * units
                    da_all[part, to, start : start + units] = dal[
                        q, t, rows, g * units : (g + 1) * units
                    ]
                    start = (2 * g + q) * unit_u
                    du_all[part, to, start : start + unit_u] = dau[
                        q, t, rows, g * gate_u : g * gate_u + unit_u
                    ]
        return carry

    def send_right(chunk):
        first, count = chunks[chunk]
        lax.fori_loop(first, first + count, own_order, 0)
        for_right(chunk, first * ROWS, count * ROWS, lambda copy: copy.start(), at_peer)

    dstate_l[...] = jnp.zeros_like(dstate_l)
    dstate_u[...] = jnp.zeros_like(dstate_u)
    da_l[...] = jnp.zeros_like(da_l)

    def bcopy_l(t):
        return remote(dal.at[me, t], dal.at[me, t], bs_l.at[t], br_l.at[t])

    def bcopy_u(t):
        return remote(dau.at[me, t], dau.at[me, t], bs_u.at[t], br_u.at[t])

    def gate_grads(dy, dstate, save, keep_now, t):
        gate_in, forget, cand, gate_out = save[t, 0], save[t, 1], save[t, 2], save[t, 3]
        cell_keep, squashed = save[t, 4], save[t, 5]
        dh = dstate[0] + dy
        dc = dstate[1] + dh * gate_out * (1.0 - squashed * squashed)
        dstate[1] = dc * forget * keep_now
        return (
            dc * cand * gate_in * (1.0 - gate_in),
            dc * cell_keep * forget * (1.0 - forget),
            dc * gate_in * (1.0 - cand * cand),
            dh * squashed * gate_out * (1.0 - gate_out),
        )

    def lower_back_start(t):
        grads = gate_grads(dx_up[...] * lock_ref[...], dstate_l, save_l, keep_at(t, lane), t)
        for g in range(4):
            da_l[:, g * units : (g + 1) * units] = grads[g][:, :units]
        high, low = split(da_l[...])
        dal[me, t, 0:ROWS] = high
        dal[me, t, ROWS:] = low
        bcopy_l(t).start()

    def upper_back_start(t):
        grads = gate_grads(gout_ref[t], dstate_u, save_u, keep_at(t, gate_u), t)
        for g in range(4):
            high, low = split(grads[g])
            dau[me, t, 0:ROWS, g * gate_u : (g + 1) * gate_u] = high
            dau[me, t, ROWS:, g * gate_u : (g + 1) * gate_u] = low
        bcopy_u(t).start()

    def lower_back_part(t, q):
        return fold(dot_nn(dal[q, t], wrec_t[q]))

    def upper_back_part(t, q):
        grad = dau[q, t]
        return fold(dot_nn(grad, uin_t[q])), fold(dot_nn(grad, urec_t[q]))

    def lower_back_own(t):
        acc[:, :wide_k] = lower_back_part(t, me)

    def lower_back_finish(t):
        bcopy_l(t).wait()
        total = acc[:, :wide_k] + lower_back_part(t, other)
        dstate_l[0, :, :wide_k] = keep_at(t, wide_k) * total

    def upper_back_own(t):
        into_x, into_h = upper_back_part(t, me)
        dx_up[:, :wide_k] = into_x
        dstate_u[0, :, :up_k] = into_h

    def upper_back_finish(t):
        bcopy_u(t).wait()
        into_x, into_h = upper_back_part(t, other)
        dx_up[:, :wide_k] += into_x
        dstate_u[0, :, :up_k] = keep_at(t, up_k) * (dstate_u[0, :, :up_k] + into_h)

    dx_up[...] = jnp.zeros_like(dx_up)
    upper_back_start(steps - 1)
    upper_back_own(steps - 1)
    upper_back_finish(steps - 1)

    def backward_round(r, carry):
        t = steps - r
        lower_back_start(t)
        upper_back_start(t - 1)
        lower_back_own(t)
        upper_back_own(t - 1)
        lower_back_finish(t)
        upper_back_finish(t - 1)
        for chunk in range(3):

            @pl.when(t == chunks[chunk][0])
            def _(chunk=chunk):
                send_right(chunk)

        return carry

    lax.fori_loop(1, steps, backward_round, 0)
    lower_back_start(0)
    bcopy_l(0).wait()

    send_right(3)

    copies = [
        pltpu.make_async_copy(da_all, da_o, out_sem.at[0]),
        pltpu.make_async_copy(du_all, du_o, out_sem.at[1]),
        pltpu.make_async_copy(xh, xh_o, out_sem.at[2]),
        pltpu.make_async_copy(lr, lr_o, out_sem.at[3]),
    ]
    for copy in copies:
        copy.start()

    chunk = 512

    def input_grad(cols, width):
        grad = da_all[:, :, cols].reshape(2 * rows_all, width)
        return fold(dot_nt(grad, win_raw[:, cols]))

    tail = full // chunk * chunk
    dx[:, :held] = input_grad(slice(tail, full), full % chunk) if full % chunk else 0.0

    def input_grad_step(index, carry):
        dx[:, :held] += input_grad(pl.ds(pl.multiple_of(index * chunk, chunk), chunk), chunk)
        return carry

    lax.fori_loop(0, full // chunk, input_grad_step, 0)
    for t in range(steps):
        now = dx[t * ROWS : t * ROWS + streams, :held] * lock_low[0:streams, :held]
        dx_o[:, t, :] = now
    for copy in copies:
        copy.wait()
    for kind in range(3):
        for_left(kind, lambda copy: copy.wait_send(), at_peer)
        for_left(kind, lambda copy: copy.wait_recv(), at_home)
    for chunk in range(4):
        row, count = chunks[chunk][0] * ROWS, chunks[chunk][1] * ROWS
        for_right(chunk, row, count, lambda copy: copy.wait_send(), at_peer)
        for_right(chunk, row, count, lambda copy: copy.wait_recv(), at_home)


def recurrence(
    inputs,
    lower_lock,
    upper_lock,
    resets,
    grad_out,
    lower_drop,
    upper_drop,
    lower_bias,
    upper_bias,
    wrec,
    win,
    uin,
    urec,
):
    streams, steps = resets.shape
    units, full = wrec.shape
    outs, full_u = urec.shape
    wide_k = ceil_to(units, 16)
    wide = ceil_to(full // 2, 256)
    up_k = ceil_to(outs, 16)
    gate_u = ceil_to(outs, 128)
    up_wide = 4 * gate_u
    lane = ceil_to(units, 128)
    rows_all = steps * ROWS
    vm = pl.BlockSpec(memory_space=pltpu.VMEM)
    hbm = pl.BlockSpec(memory_space=pl.ANY)
    sds = jax.ShapeDtypeStruct
    i32 = jnp.int32
    shared = [
        ((2, rows_all, ceil_to(full, 512)), BF),
        ((2, rows_all, ceil_to(full_u, 128)), BF),
        ((2 * wide_k, 2 * rows_all), BF),
        ((wide_k + up_k, 2 * rows_all), BF),
    ]
    landed = [
        ((3, 3, 2 * wide_k, 2 * rows_all), BF),
        ((3, 3, 2, rows_all, 640), BF),
    ]
    raw = [(w.shape, BF) for w in (wrec, win, uin, urec)]
    dma = pltpu.SemaphoreType.DMA
    return pl.pallas_call(
        functools.partial(recurrence_kernel, units),
        out_shape=(sds((streams, steps, outs), F32), sds((streams, steps, units), F32))
        + tuple(sds(*s) for s in shared + landed)
        + (sds((lane, 256), i32), sds((ceil_to(outs, 128), 128), i32)),
        in_specs=[vm] * 9 + [hbm] * 4,
        out_specs=(vm, vm) + (hbm,) * len(shared + landed) + (vm, vm),
        scratch_shapes=[pltpu.VMEM(*s) for s in raw]
        + [
            pltpu.VMEM((256, lane), i32),
            pltpu.VMEM((128, ceil_to(outs, 128)), i32),
            pltpu.VMEM((ceil_to(full, 16), 128), F32),
            pltpu.VMEM((steps + 1, ROWS, 128), F32),
            pltpu.VMEM((ROWS, lane), F32),
            pltpu.VMEM((ROWS, lane), F32),
            pltpu.VMEM((steps, ROWS, gate_u), F32),
            pltpu.VMEM((2, 1, wide), F32),
            pltpu.VMEM((2, 1, up_wide), F32),
            pltpu.VMEM((2, wide, wide_k), BF),
            pltpu.VMEM((2, up_wide, wide_k), BF),
            pltpu.VMEM((2, up_wide, up_k), BF),
            pltpu.VMEM((2, wide_k, wide), BF),
            pltpu.VMEM((2, wide_k, up_wide), BF),
            pltpu.VMEM((2, up_k, up_wide), BF),
        ]
        + [pltpu.VMEM(*s) for s in shared]
        + [
            pltpu.VMEM((2 * rows_all, lane), BF),
            pltpu.VMEM((steps + 1, 2 * ROWS, lane), BF),
            pltpu.VMEM((steps, 2 * ROWS, lane), BF),
            pltpu.VMEM((steps + 1, 2 * ROWS, gate_u), BF),
            pltpu.VMEM((2, steps, 2 * ROWS, wide), BF),
            pltpu.VMEM((2, steps, 2 * ROWS, up_wide), BF),
            pltpu.VMEM((2, steps, ROWS, wide), F32),
            pltpu.VMEM((ROWS, wide), F32),
            pltpu.VMEM((2, ROWS, wide), F32),
            pltpu.VMEM((ROWS, up_wide), F32),
            pltpu.VMEM((2, ROWS, up_wide), F32),
            pltpu.VMEM((ROWS, wide + lane - units), F32),
            pltpu.VMEM((ROWS, up_wide), F32),
            pltpu.VMEM((steps, 6, ROWS, lane), F32),
            pltpu.VMEM((steps, 6, ROWS, gate_u), F32),
            pltpu.VMEM((ROWS, lane), F32),
            pltpu.VMEM((ROWS, gate_u), F32),
            pltpu.VMEM((ROWS, wide), F32),
            pltpu.VMEM((ROWS, up_wide), F32),
            pltpu.VMEM((2, ROWS, lane), F32),
            pltpu.VMEM((2, ROWS, gate_u), F32),
            pltpu.VMEM((ROWS, lane), F32),
            pltpu.VMEM((ROWS, lane), F32),
            pltpu.VMEM((rows_all, lane), F32),
        ]
        + [dma((steps,))] * 8
        + [dma((75,)), dma((75,)), dma((4,)), dma((4,))],
        compiler_params=pltpu.CompilerParams(
            vmem_limit_bytes=VMEM_LIMIT, collective_id=0, has_side_effects=True
        ),
    )(
        inputs,
        lower_lock,
        upper_lock,
        resets,
        grad_out,
        lower_drop,
        upper_drop,
        lower_bias,
        upper_bias,
        wrec,
        win,
        uin,
        urec,
    )


PANEL = 576
STRIP = 288
GROUP = 72
HALF = 2 * GROUP
FULL = STRIP + 8
PAIRS = 24
LOWER_PAIRS = 18
SMALLEST = 2.0**-111
WIDTH = 4


def code(group):
    largest = jnp.maximum(jnp.max(jnp.abs(group), axis=0, keepdims=True), SMALLEST)
    step = jnp.floor(jnp.log2(largest) * 64.0).astype(jnp.int32) + 2
    return step, 32767.0 * jnp.exp2(step.astype(F32) * (-1.0 / 64.0))


def factor(step):
    return jnp.exp2(step.astype(F32) * (1.0 / 64.0)) * (1.0 / 32767.0)


def encode(a, b):
    step_a, up_a = code(a)
    step_b, up_b = code(b)
    word_a = jnp.round(a * up_a).astype(jnp.int32)
    word_b = jnp.round(b * up_b).astype(jnp.int32)
    return (word_a << 16) | (word_b & 0xFFFF), step_a, step_b


def decode(words, step_a, step_b):
    a = (words >> 16).astype(F32) * factor(step_a)
    b = ((words << 16) >> 16).astype(F32) * factor(step_b)
    return a, b


def sum_kernel(
    xh,
    lr,
    da,
    du,
    far_left,
    far_right,
    words,
    out,
    kept,
    lhs,
    rhs,
    mine,
    send2,
    recv2,
    send3,
    recv3,
    shard,
    scales,
    panel,
    send_sem,
    recv_sem,
    copy_sem,
    kept_sem,
    left_sem,
    right_sem,
):
    place, peer = torus()
    barrier = pltpu.get_barrier_semaphore()
    for axis in range(3):
        for distance in (1, 2, 3):
            pl.semaphore_signal(
                barrier, inc=1, device_id=peer(axis, distance), device_id_type=MESH
            )

    parts = tuple(range(6))

    def axes(m):
        return m % 3, (m + 1) % 3, (m + 2) % 3

    def kept_copy(m):
        first, second, third = axes(m)
        number = first * 16 + place[first] * 4 + place[second]
        start = pl.multiple_of(m // 3 * STRIP + place[third] * GROUP, 8)
        part = jnp.minimum(lax.div(number, 20), 1)
        lanes = pl.ds(pl.multiple_of(part * 128, 128), 128)
        src = words.at[pl.ds(start, GROUP), lanes]
        return number, pltpu.make_async_copy(src, kept.at[m], kept_sem.at[m])

    for m in parts:
        kept_copy(m)[1].start()

    def remote(src, dst, number, axis, distance):
        return pltpu.make_async_remote_copy(
            src_ref=src,
            dst_ref=dst,
            send_sem=send_sem.at[number],
            recv_sem=recv_sem.at[number],
            device_id=peer(axis, distance),
            device_id_type=MESH,
        )

    upper_here = place[2] != 0
    rows_all = da.shape[1]
    lr_rows = lr.shape[0]
    early = EARLY * ROWS

    def operand_copies(k, upper):
        copies = []
        for s in range(4):
            rows = slice(0, lr_rows if upper else 2 * PANEL)
            src = (lr if upper else xh) if s == 0 else far_left.at[k, s - 1]
            at = s * 640
            for i, (first, last) in enumerate(((0, 384), (0, 128), (256, 384))):
                to = lhs.at[k, rows, at : at + last - first]
                copies.append(
                    pltpu.make_async_copy(
                        src.at[rows, first:last], to, left_sem.at[(k * 4 + s) * 3 + i]
                    )
                )
                at += last - first
            sems = [right_sem.at[(k * 4 + s) * 2 + i] for i in (0, 1)]
            to = rhs.at[k, s, :, :, 0:512]
            if s > 0:
                src = far_right.at[k, s - 1, :, :, 0:512]
            elif upper:
                col = pl.multiple_of(jnp.maximum(place[k] - 1, 0) * 512, 512)
                src = du.at[:, :, pl.ds(col, 512)]
            else:
                col = pl.multiple_of((4 * k + (place[k] if k < 2 else 0)) * 512, 512)
                src = da.at[:, :, pl.ds(col, 512)]
            copies.append(pltpu.make_async_copy(src, to, sems[0]))
            if upper:
                src = far_right.at[k, s - 1, :, :, 512:640] if s > 0 else du.at[:, :, 1536:1664]
                copies.append(pltpu.make_async_copy(src, rhs.at[k, s, :, :, 512:640], sems[1]))
        return copies

    def for_operands(k, act):
        if k < 2:
            for copy in operand_copies(k, False):
                act(copy)
            return

        @pl.when(jnp.logical_not(upper_here))
        def _():
            for copy in operand_copies(k, False):
                act(copy)

        @pl.when(upper_here)
        def _():
            for copy in operand_copies(k, True):
                act(copy)

    def right(k, cols, width):
        parts = []
        for s in range(4):
            high, low = rhs[k, s, 0, :, cols], rhs[k, s, 1, :, cols]
            parts += [high[:early], high[:early], high[early:], high[early:]]
            parts += [low[:early], low[early:], jnp.zeros((640 - 3 * rows_all, width), BF)]
        return jnp.concatenate(parts, axis=0)

    def compute(m, half):
        k, row = m % 3, m // 3 * STRIP
        cols = pl.ds(pl.multiple_of(half * 256, 256), 256)

        def put(ab, n, rows, value):
            mine[m, ab, 2 * half + n, rows, :] = value[:, n * 128 : (n + 1) * 128]

        def lower():
            operand = right(k, cols, 256)
            for ab in range(2):
                y = dot_nn(lhs[k, ab * PANEL + row : ab * PANEL + row + STRIP], operand)
                for n in range(2):
                    put(ab, n, slice(0, STRIP), y)

        def upper():
            operand = right(k, cols, 256)
            y = dot_nn(lhs[k, row : row + STRIP], operand)
            top = PANEL - TAIL_ROWS if row == 0 else 0
            index = 2 * (place[k] - 1) + half
            start = jnp.clip(index, 0, 2) * TAIL_ROWS + (STRIP - PANEL + TAIL_ROWS if row else 0)
            rows = pl.ds(pl.multiple_of(start, 16), STRIP - top)
            bottom = dot_nn(lhs[k, rows], right(k, slice(512, 640), 128))
            bottom = jnp.where(index < 3, bottom, 0.0)
            for n in range(2):
                put(0, n, slice(0, STRIP), y)
            if top:
                y = dot_nn(lhs[k, PANEL : PANEL + top], operand)
                for n in range(2):
                    put(1, n, slice(0, top), y)
            mine[m, 1, 2 * half, top:, :] = bottom
            mine[m, 1, 2 * half + 1, top:, :] = jnp.zeros_like(bottom)

        if k < 2:
            lower()
        else:
            pl.when(jnp.logical_not(upper_here))(lower)
            pl.when(upper_here)(upper)

    def compute_part(m):
        def step(half, carry):
            compute(m, half)
            return carry

        lax.fori_loop(0, 2, step, 0)

    @pl.when(upper_here)
    def _():
        lhs[2, lr_rows:, :] = jnp.zeros((2 * PANEL - lr_rows, lhs.shape[2]), BF)

    def rows_of(group):
        return pl.ds(pl.multiple_of(group * GROUP, 8), GROUP)

    def steps_at(ref, base, group):
        return ref[pl.ds(base + 2 * group, 1), :], ref[pl.ds(base + 2 * group + 1, 1), :]

    def store_code(ref, base, group, words, step_a, step_b):
        ref[rows_of(group), :] = words
        ref[pl.ds(base + 2 * group, 1), :] = step_a
        ref[pl.ds(base + 2 * group + 1, 1), :] = step_b

    def arrived(ref, base, group):
        return decode(ref[rows_of(group), :], *steps_at(ref, base, group))

    ways = ((0, 1), (1, -1))

    def stage2(m, way, kind):
        number = (m * 2 + way) * 3 + kind
        return remote(
            send2.at[m, way, kind], recv2.at[m, way, kind], number, axes(m)[1], 1 - 2 * way
        )

    def pack_half(m, offset, half, target, added):
        block = lax.rem(place[axes(m)[1]] + (offset + 4), 4)
        for group in range(2):
            rows = slice(half * HALF + group * GROUP, half * HALF + (group + 1) * GROUP)
            a, b = mine[m, 0, block, rows, :], mine[m, 1, block, rows, :]
            if added is not None:
                more_a, more_b = arrived(added, HALF, group)
                a, b = a + more_a, b + more_b
            store_code(target, HALF, group, *encode(a, b))

    def reduce2_first(m):
        for way, sign in ways:
            pack_half(m, 2, way, send2.at[m, way, 0], None)
            stage2(m, way, 0).start()
        for way, sign in ways:
            pack_half(m, sign, 1 - way, send2.at[m, way, 1], None)
            stage2(m, way, 1).start()

    def reduce2_second(m):
        for way, sign in ways:
            stage2(m, way, 0).wait_recv()
            pack_half(m, sign, way, send2.at[m, way, 2], recv2.at[m, way, 0])
            stage2(m, way, 2).start()

    def stage3(m, d):
        number = 36 + m * 3 + d - 1
        return remote(send3.at[m, d - 1], recv3.at[m, d - 1], number, axes(m)[2], d)

    def reduce3(m):
        block = place[axes(m)[1]]
        for kind in (1, 2):
            for way in range(2):
                stage2(m, way, kind).wait_recv()
        for group in range(4):
            half, inner = group // 2, group % 2
            a1, b1 = arrived(recv2.at[m, 0, 2 - half], HALF, inner)
            a2, b2 = arrived(recv2.at[m, 1, 1 + half], HALF, inner)
            rows = slice(group * GROUP, (group + 1) * GROUP)
            mine[m, 0, block, rows, :] += a1 + a2
            mine[m, 1, block, rows, :] += b1 + b2
        for d in (1, 2, 3):
            group = lax.rem(place[axes(m)[2]] + d, 4)
            a, b = mine[m, 0, block, rows_of(group), :], mine[m, 1, block, rows_of(group), :]
            store_code(send3.at[m, d - 1], GROUP, 0, *encode(a, b))
            stage3(m, d).start()

    def spread3(m, d, group):
        number = 54 + (m * 3 + d - 1) * 2
        axis = axes(m)[2]
        data = remote(shard.at[m, 0:GROUP], panel.at[m, rows_of(group)], number, axis, d)
        scale = remote(
            shard.at[m, GROUP : GROUP + 8], scales.at[m, d - 1], number + 1, axis, d
        )
        return data, scale

    def finish(m):
        first, second, third = axes(m)
        block, own = place[second], place[third]
        a, b = mine[m, 0, block, rows_of(own), :], mine[m, 1, block, rows_of(own), :]
        for d in (1, 2, 3):
            stage3(m, d).wait_recv()
            more_a, more_b = arrived(recv3.at[m, d - 1], GROUP, 0)
            a, b = a + more_a, b + more_b
        number, copy = kept_copy(m)
        copy.wait()
        flags = jnp.where(number < 2 * LOWER_PAIRS, flags_at(kept[m], number * 128) * 2, 1)
        store_code(shard.at[m], GROUP, 0, *encode(a, b * flags.astype(F32)))
        for d in (1, 2, 3):
            for copy in spread3(m, d, own):
                copy.start()
        panel[m, rows_of(own), :] = shard[m, 0:GROUP, :]

    def at(m, first, second):
        return out.at[m * 16 + first * 4 + second]

    def turned(axis, distance):
        return lax.rem(place[axis] + (distance + 4), 4)

    def spread2(m, way, src, first, second):
        return remote(src, at(m, first, second), 90 + m * 4 + way, axes(m)[1], 1 - 2 * way)

    def pass2(m, way, first, second):
        rows = slice(0, HALF) if way == 0 else slice(HALF, FULL)
        ref = at(m, first, second).at[rows]
        return remote(ref, ref, 90 + m * 4 + 2 + way, axes(m)[1], 1 - 2 * way)

    def spread1(m, way, order, src, first, second):
        number = 114 + (m * 2 + way) * 6 + order
        return remote(src, at(m, first, second), number, axes(m)[0], 1 - 2 * way)

    offsets = (0, -1, 1, 2)

    def own_copy(m):
        first, second, third = axes(m)
        return pltpu.make_async_copy(
            panel.at[m], at(m, place[first], place[second]), copy_sem.at[m]
        )

    def gather_own(m):
        first, second, third = axes(m)
        row = lax.broadcasted_iota(jnp.int32, (8, 128), 0)
        total = jnp.zeros((8, 128), jnp.int32)
        for d in (0, 1, 2, 3):
            group = lax.rem(place[third] + (4 - d), 4)
            if d == 0:
                tile = shard[m, GROUP : GROUP + 8, :]
            else:
                for copy in spread3(m, d, group):
                    copy.wait_recv()
                tile = scales[m, d - 1]
            total = jnp.where(row == 2 * group, tile[0:1], total)
            total = jnp.where(row == 2 * group + 1, tile[1:2], total)
        panel[m, STRIP:FULL, :] = total
        for way in range(2):
            spread2(m, way, panel.at[m], place[first], place[second]).start()
        own_copy(m).start()
        for way in range(2):
            spread1(m, way, 0, panel.at[m], place[first], place[second]).start()

    def gather_near(m):
        first = place[axes(m)[0]]
        for way in range(2):
            second = turned(axes(m)[1], 2 * way - 1)
            spread2(m, way, panel.at[m], first, second).wait_recv()
            pass2(m, way, first, second).start()
            for way1 in range(2):
                spread1(m, way1, 1 + way, at(m, first, second), first, second).start()

    def gather_far(m):
        first, second = place[axes(m)[0]], turned(axes(m)[1], 2)
        for way in range(2):
            pass2(m, way, first, second).wait_recv()
        for way1 in range(2):
            spread1(m, way1, 3, at(m, first, second), first, second).start()

    passed = ((0, 0), (1, 2), (0, 1), (1, 3))

    def pass1(m, way, order, first):
        ref = at(m, first, turned(axes(m)[1], offsets[order]))
        number = 114 + (m * 2 + way) * 6 + 4 + order % 2
        return remote(ref, ref, number, axes(m)[0], 1 - 2 * way)

    def spread1_arrived(m, way, order):
        first = turned(axes(m)[0], 2 * way - 1)
        second = turned(axes(m)[1], offsets[order])
        spread1(m, way, order, panel.at[m], first, second).wait_recv()

    def pass_on(m, which):
        for way, order in passed[which]:
            spread1_arrived(m, way, order)
            pass1(m, way, order, turned(axes(m)[0], 2 * way - 1)).start()

    one, two = parts[:3], parts[3:]
    early_half, late_half = slice(0, 2), slice(2, 4)
    for_operands(0, lambda copy: copy.start())
    for_operands(1, lambda copy: copy.start())
    pl.semaphore_wait(barrier, 9)
    for m in one:
        for_operands(m, lambda copy: copy.wait())
        if m == 0:
            for_operands(2, lambda copy: copy.start())
        compute_part(m)
        reduce2_first(m)
    for m in two:
        compute_part(m)
        reduce2_first(m)
        reduce2_second(m - 3)
    for step in (
        (reduce3, one),
        (reduce2_second, two),
        (finish, one),
        (reduce3, two),
        (gather_own, one),
        (finish, two),
        (gather_near, one),
        (gather_own, two),
        (gather_far, one),
        (gather_near, two),
        (lambda m: pass_on(m, early_half), one),
        (gather_far, two),
        (lambda m: pass_on(m, late_half), one),
        (lambda m: pass_on(m, early_half), two),
        (lambda m: pass_on(m, late_half), two),
    ):
        for m in step[1]:
            step[0](m)
    for m in parts:
        for way in range(2):
            for order in range(4):
                if (way, order) not in passed:
                    spread1_arrived(m, way, order)
        for way, order in passed:
            pass1(m, way, order, turned(axes(m)[0], 2)).wait_recv()

    for m in parts:
        for way in range(2):
            for kind in range(3):
                stage2(m, way, kind).wait_send()
        for d in (1, 2, 3):
            stage3(m, d).wait_send()
            for copy in spread3(m, d, place[axes(m)[2]]):
                copy.wait_send()
        first, second = place[axes(m)[0]], place[axes(m)[1]]
        own_copy(m).wait()
        for way in range(2):
            spread2(m, way, panel.at[m], first, second).wait_send()
            pass2(m, way, first, turned(axes(m)[1], 2 * way - 1)).wait_send()
            for order in range(4):
                second_now = turned(axes(m)[1], offsets[order])
                src = panel.at[m] if order == 0 else at(m, first, second_now)
                spread1(m, way, order, src, first, second_now).wait_send()
        for way, order in passed:
            pass1(m, way, order, turned(axes(m)[0], 2 * way - 1)).wait_send()


def summed_panels(xh, lr, da, du, left, right, words):
    i32 = jnp.int32
    messages = 114 + 72
    rows_all = da.shape[1]
    dma = pltpu.SemaphoreType.DMA
    return pl.pallas_call(
        sum_kernel,
        out_shape=pltpu.VMEM((4 * PAIRS, FULL, 128), i32),
        in_specs=[pl.BlockSpec(memory_space=pl.ANY)] * 7,
        out_specs=pl.BlockSpec(memory_space=pl.ANY),
        scratch_shapes=[
            pltpu.VMEM((6, GROUP, 128), i32),
            pltpu.VMEM((3, 2 * PANEL, 4 * 640), BF),
            pltpu.VMEM((3, 4, 2, rows_all, 640), BF),
            pltpu.VMEM((6, 2, 4, STRIP, 128), F32),
            pltpu.VMEM((6, 2, 3, HALF + 8, 128), i32),
            pltpu.VMEM((6, 2, 3, HALF + 8, 128), i32),
            pltpu.VMEM((6, 3, GROUP + 8, 128), i32),
            pltpu.VMEM((6, 3, GROUP + 8, 128), i32),
            pltpu.VMEM((6, GROUP + 8, 128), i32),
            pltpu.VMEM((6, 3, 8, 128), i32),
            pltpu.VMEM((6, FULL, 128), i32),
            dma((messages,)),
            dma((messages,)),
            dma((6,)),
            dma((6,)),
            dma((36,)),
            dma((24,)),
        ],
        compiler_params=pltpu.CompilerParams(
            vmem_limit_bytes=SUM_VMEM, collective_id=1, has_side_effects=True
        ),
    )(xh, lr, da, du, left, right, words)


def unpack_kernel(panels, words_u, low_in, low_rec, low_bias, up_in, up_rec, up_bias, tail):
    step = pl.program_id(0)
    units, outs = low_in.shape[0], up_rec.shape[0]
    lower_steps, all_steps = 2 * LOWER_PAIRS // WIDTH, 2 * PAIRS // WIDTH

    def values(n, ab):
        parts = []
        n = jnp.minimum(step, all_steps - 1) * WIDTH + n
        for strip in range(2):
            at = strip * 2 * PAIRS + n
            for group in range(4):
                words = panels[at, group * GROUP : (group + 1) * GROUP, :]
                row = STRIP + 2 * group + ab
                scale = factor(panels[at, row : row + 1, :])
                half = (words >> 16) if ab == 0 else ((words << 16) >> 16)
                parts.append(half.astype(F32) * scale)
        return jnp.concatenate(parts, axis=0)

    for n in range(WIDTH):
        cols = slice(n * 128, (n + 1) * 128)

        @pl.when(step < lower_steps)
        def _():
            a = values(n, 0)
            low_in[:, cols] = a[:units]
            low_bias[:, cols] = a[units : units + 1]
            b = values(n, 1)[:units]
            low_rec[:, cols] = b

        @pl.when((step >= lower_steps) & (step < all_steps))
        def _():
            a = values(n, 0)
            up_in[:, cols] = a[:units]
            up_bias[:, cols] = a[units : units + 1]
            b = values(n, 1)
            flags = flags_at(words_u[...], (step - lower_steps) * WIDTH * 128 + n * 128)
            up_rec[:, cols] = b[:outs] * (flags * 2).astype(F32)[:outs]
            if n % 2 == 0:
                index = (step - lower_steps) * (WIDTH // 2) + n // 2
                rows = pl.ds(pl.multiple_of(index * TAIL_ROWS, 8), TAIL_ROWS)
                tail[rows, :] = b[PANEL - TAIL_ROWS :]

    @pl.when(step == all_steps)
    def _():
        up_in[:, :128] = tail[:units]
        up_bias[:, :128] = tail[units : units + 1]
        flags = flags_at(words_u[...], 2 * (PAIRS - LOWER_PAIRS) * 128)
        up_rec[:, :128] = tail[PANEL : PANEL + outs] * (flags * 2).astype(F32)[:outs]


def unpack(panels, words_u, units, full, outs, full_u):
    sds = jax.ShapeDtypeStruct
    lower_steps, all_steps = 2 * LOWER_PAIRS // WIDTH, 2 * PAIRS // WIDTH
    wide = 128 * WIDTH
    lower = lambda i: (0, jnp.minimum(i, lower_steps - 1))
    upper = lambda i: (0, jnp.maximum(i - lower_steps, 0))
    return pl.pallas_call(
        unpack_kernel,
        grid=(all_steps + 1,),
        out_shape=(
            sds((units, full), F32),
            sds((units, full), F32),
            sds((1, full), F32),
            sds((units, full_u), F32),
            sds((outs, full_u), F32),
            sds((1, full_u), F32),
        ),
        in_specs=[
            pl.BlockSpec(memory_space=pltpu.VMEM),
            pl.BlockSpec(memory_space=pltpu.VMEM),
        ],
        out_specs=(
            pl.BlockSpec((units, wide), lower),
            pl.BlockSpec((units, wide), lower),
            pl.BlockSpec((1, wide), lower),
            pl.BlockSpec((units, wide), upper),
            pl.BlockSpec((outs, wide), upper),
            pl.BlockSpec((1, wide), upper),
        ),
        scratch_shapes=[pltpu.VMEM((6 * TAIL_ROWS, 128), F32)],
        compiler_params=pltpu.CompilerParams(vmem_limit_bytes=UNPACK_VMEM),
    )(panels, words_u)


def body(
    inputs,
    lower_lock,
    upper_lock,
    resets,
    lower_input,
    lower_recur,
    lower_bias,
    lower_drop,
    upper_input,
    upper_recur,
    upper_bias,
    upper_drop,
    grad_out,
):
    me = lax.axis_index("pipe")
    streams, steps, width = inputs.shape
    hidden_out, grad_inputs, da, du, xh, lr, left, right, words_l, words_u = recurrence(
        inputs,
        lower_lock,
        upper_lock,
        resets,
        grad_out,
        lower_drop.T,
        upper_drop.T,
        lower_bias.reshape(1, -1),
        upper_bias.reshape(1, -1),
        lower_recur,
        lower_input,
        upper_input,
        upper_recur,
    )
    panels = summed_panels(xh, lr, da, du, left, right, words_l)
    low_in, low_rec, low_bias, up_in, up_rec, up_bias = unpack(
        panels, words_u, *lower_recur.shape, *upper_recur.shape
    )

    def own(row):
        half = row.shape[1] // 2
        return lax.dynamic_slice_in_dim(row[0], me * half, half, 0)

    return (
        hidden_out,
        grad_inputs,
        low_in,
        low_rec,
        own(low_bias),
        up_in,
        up_rec,
        own(up_bias),
    )


def solution(mesh):
    return jax.shard_map(
        body,
        mesh=mesh,
        in_specs=(
            P("dp", None, None),
            P("dp", None),
            P("dp", None),
            P("dp", None),
            P("pipe", None),
            P("pipe", None),
            P("pipe"),
            P(),
            P("pipe", None),
            P("pipe", None),
            P("pipe"),
            P(),
            P("dp", None, None),
        ),
        out_specs=(
            P("dp", None, "pipe"),
            P("dp", None, "pipe"),
            P("pipe", None),
            P("pipe", None),
            P("pipe"),
            P("pipe", None),
            P("pipe", None),
            P("pipe"),
        ),
        check_vma=False,
    )
```

```python
import functools

import jax
import jax.numpy as jnp
from jax import lax
from jax.experimental import pallas as pl
from jax.experimental.pallas import tpu as pltpu
from jax.sharding import PartitionSpec as P

BF = jnp.bfloat16
F32 = jnp.float32
MESH = pl.DeviceIdType.MESH
ROWS = 16
VMEM_LIMIT = 62 * 2**20
TAIL_ROWS = 368
EARLY = 8
SUM_VMEM = 47 * 2**20
UNPACK_VMEM = 24 * 2**20


def ceil_to(value, multiple):
    return -(-value // multiple) * multiple


def split(value):
    high = value.astype(BF)
    low = (value - high.astype(F32)).astype(BF)
    return high, low


def fold(stacked):
    half = stacked.shape[0] // 2
    return stacked[:half] + stacked[half:]


def dot_nn(a, b):
    return jnp.dot(a, b, preferred_element_type=F32)


def dot_nt(a, b):
    return lax.dot_general(a, b, (((1,), (1,)), ((), ())), preferred_element_type=F32)


def torus():
    dp = lax.axis_index("dp")
    place = [lax.rem(dp, 4), lax.rem(lax.div(dp, 4), 4), lax.div(dp, 16)]
    stride = [1, 4, 16]

    def across(axis, distance):
        moved = lax.rem(place[axis] + (distance + 4), 4)
        return {"dp": dp + (moved - place[axis]) * stride[axis]}

    return place, across


def flags_at(words, column):
    column = lax.broadcasted_iota(jnp.int32, (1, 128), 1) + column
    index = (column * 52429) >> 20
    bit = column - index * 20
    index = jnp.broadcast_to(index & 127, words.shape)
    found = jnp.take_along_axis(words, index, axis=1, mode="promise_in_bounds")
    return (found >> bit) & 1


def recurrence_kernel(
    units,
    inputs,
    lower_lock,
    upper_lock,
    resets,
    grad_out,
    lower_drop,
    upper_drop,
    both_bias,
    wrec_in,
    win_in,
    uin_in,
    urec_in,
    hid_o,
    dx_o,
    da_o,
    du_o,
    xh_o,
    lr_o,
    left_o,
    right_o,
    rows_l_o,
    rows_u_o,
    wrec_raw,
    win_raw,
    uin_raw,
    urec_raw,
    words_l,
    words_u,
    slab,
    keep_ref,
    lock_low,
    lock_ref,
    gout_ref,
    blo,
    bup,
    wrec_t,
    uin_t,
    urec_t,
    wrec,
    uin,
    urec,
    da_all,
    du_all,
    xh,
    lr,
    x2,
    hk2,
    ux2,
    hku2,
    dal,
    dau,
    proj,
    send_l,
    recv_l,
    send_u,
    recv_u,
    act_l,
    act_u,
    save_l,
    save_u,
    cell_l,
    cell_u,
    da_l,
    da_u,
    dstate_l,
    dstate_u,
    dx_up,
    acc,
    acc_x,
    acc_h,
    dx,
    fs_l,
    fr_l,
    fs_u,
    fr_u,
    bs_l,
    br_l,
    bs_u,
    br_u,
    far_s,
    far_r,
    in_sem,
    out_sem,
):
    streams, steps = resets.shape
    me = lax.axis_index("pipe")
    other = 1 - me
    peer = {"pipe": other}
    wide_k = wrec.shape[1]
    wide = wrec.shape[2]
    up_wide = uin.shape[2]
    up_k = urec.shape[1]
    lane = act_l.shape[1] - wide + units

    barrier = pltpu.get_barrier_semaphore()
    pl.semaphore_signal(barrier, inc=1, device_id=peer, device_id_type=MESH)
    place, across = torus()
    for axis in range(3):
        for d in (1, 2, 3):
            pl.semaphore_signal(barrier, inc=1, device_id=across(axis, d), device_id_type=MESH)
    loads = [
        pltpu.make_async_copy(win_in, win_raw, in_sem.at[0]),
        pltpu.make_async_copy(wrec_in, wrec_raw, in_sem.at[1]),
        pltpu.make_async_copy(uin_in, uin_raw, in_sem.at[2]),
        pltpu.make_async_copy(urec_in, urec_raw, in_sem.at[3]),
    ]
    for load in loads:
        load.start()
    pl.semaphore_wait(barrier, 10)

    def remote(src, dst, send_sem, recv_sem):
        return pltpu.make_async_remote_copy(
            src_ref=src,
            dst_ref=dst,
            send_sem=send_sem,
            recv_sem=recv_sem,
            device_id=peer,
            device_id_type=MESH,
        )

    full = wrec_raw.shape[1]
    held = wrec_raw.shape[0]
    held_u = urec_raw.shape[0]
    full_u = urec_raw.shape[1]
    unit_u = full_u // 8
    gate_u = gout_ref.shape[2]
    rows_all = steps * ROWS

    def to_rows(value, lanes, filler=0.0):
        more = lanes - value.shape[1]
        if more:
            value = jnp.concatenate([value, jnp.full((streams, more), filler, F32)], axis=1)
        return jnp.concatenate([value, jnp.zeros((ROWS - streams, lanes), F32)], axis=0)

    keep_ref[...] = jnp.zeros_like(keep_ref)
    for t in range(steps):
        now = 1.0 - resets[:, t : t + 1].astype(F32)
        keep_ref[t] = to_rows(jnp.broadcast_to(now, (streams, 128)), 128)
    blo[...] = jnp.zeros_like(blo)
    bup[...] = jnp.zeros_like(bup)
    def place_words(target, packed):
        rows, lanes = packed.shape
        more = target.shape[1] - lanes
        packed = jnp.concatenate([packed, jnp.zeros((rows, more), jnp.int32)], axis=1)
        target[0:rows, :] = packed

    words_l[...] = jnp.zeros_like(words_l)
    words_u[...] = jnp.zeros_like(words_u)
    for half in range(2):

        @pl.when(me == half)
        def _(half=half):
            mine = slice(half * units, (half + 1) * units)
            lock_low[...] = to_rows(lower_lock[:, mine].astype(F32) * 1.25, lane)
            lock_ref[...] = to_rows(upper_lock[:, mine].astype(F32) * 1.25, lane)
            one = jnp.full((streams, 1), 1.0, F32)
            for t in range(steps):
                now = inputs[:, t, mine] * lock_low[0:streams, 0:units]
                now = to_rows(jnp.concatenate([now, one], axis=1), lane)
                high, low = split(now)
                x2[t * ROWS : (t + 1) * ROWS] = high
                x2[rows_all + t * ROWS : rows_all + (t + 1) * ROWS] = low
                out = grad_out[:, t, half * unit_u : (half + 1) * unit_u]
                gout_ref[t] = to_rows(out, gate_u)
            place_words(words_l, lower_drop[:, mine])
            place_words(words_u, upper_drop[:, half * held_u : (half + 1) * held_u])
            bias = both_bias[...].astype(F32)
            bias_u = bias[:, 4 * units :]
            for q in range(2):
                for i in range(2):
                    g = 2 * half + i
                    start = (2 * i + q) * units
                    blo[q, :, g * units : (g + 1) * units] = bias[:, start : start + units]
                    start = (2 * i + q) * unit_u
                    bup[q, :, g * unit_u : (g + 1) * unit_u] = bias_u[
                        :, start : start + unit_u
                    ]

    loads[0].wait()
    proj[:, :, :, wide - 128 :] = jnp.zeros((2, steps, ROWS, 128), F32)
    for q in range(2):
        for g in range(4):
            start, stop = (2 * g + q) * units, (2 * g + q + 1) * units
            first, last = start // 128 * 128, min(ceil_to(stop, 128), full)
            y = fold(dot_nn(x2[:, :held], win_raw[:, first:last]))
            y = y[:, start - first : stop - first] + blo[q, :, g * units : (g + 1) * units]
            proj[q, :, :, g * units : (g + 1) * units] = y.reshape(steps, ROWS, units)

    for load in loads[1:]:
        load.wait()
    sub = lax.broadcasted_iota(jnp.int32, (8, 128), 0)

    def flags_of(held, i):
        left, right = 8 * i // 20, (8 * i + 7) // 20
        now = jnp.broadcast_to(held[left : left + 1], (8, 128))
        if right != left:
            later = jnp.broadcast_to(held[right : right + 1], (8, 128))
            now = jnp.where(sub < 20 * right - 8 * i, now, later)
        bit = sub + 8 * i % 20
        bit = jnp.where(bit >= 20, bit - 20, bit)
        return (now >> bit) & 1

    def masked_columns(weight, words, first, lanes):
        rows, columns = weight.shape
        words = words[pl.ds(first, ceil_to(ceil_to(columns, 20) // 20, 8)), lanes]
        turned = jnp.transpose(weight.astype(F32))
        if rows < 128:
            turned = jnp.concatenate([turned, jnp.zeros((columns, 128 - rows), F32)], axis=1)
        out = []
        for i in range(columns // 8):
            now = turned[8 * i : 8 * i + 8]
            out.append(jnp.where(flags_of(words, i) != 0, now + now, 0.0))
        return jnp.concatenate(out, axis=0)

    block = 640
    row16 = lax.broadcasted_iota(jnp.int32, (ROWS, 128), 0)

    def lower_slab(rows, start):
        lanes = pl.ds(start, 128)
        many = min(128, wide_k - start) if isinstance(start, int) else 128

        def fill(index, carry):
            cols = pl.ds(pl.multiple_of(index * block, block), block)
            first = pl.multiple_of(index * (block // 20), block // 20)
            part = masked_columns(wrec_raw[rows, cols], words_l, first, lanes)
            slab[cols, :] = part
            return carry

        lax.fori_loop(0, full // block, fill, 0)
        last = full // block * block
        slab[last:full, :] = masked_columns(
            wrec_raw[rows, last:full], words_l, last // 20, lanes
        )
        target = pl.ds(start, many)
        tiles = units // ROWS
        for q in range(2):
            for g in range(4):
                shift = units * (g + q)
                base = (tiles + 1) * ROWS * g

                def move(index, carry, q=q, shift=shift, base=base):
                    for i in range(7):
                        row = pl.multiple_of(base + (index * 7 + i) * ROWS, ROWS)
                        now = slab[pl.ds(row + shift, ROWS), :]
                        wrec_t[q, pl.ds(row, ROWS), target] = now.astype(BF)[:, :many]
                    return carry

                lax.fori_loop(0, tiles // 7, move, 0)
                row = base + tiles * ROWS
                now = slab[row + shift : row + shift + ROWS, :]
                if g < 3:
                    later = slab[row + shift + units : row + shift + units + ROWS, :]
                else:
                    later = jnp.zeros((ROWS, 128), F32)
                now = jnp.where(row16 < units * (g + 1) - row, now, later)
                wrec_t[q, row : row + ROWS, target] = now.astype(BF)[:, :many]

    def lower_slab_step(index, carry):
        start = pl.multiple_of(index * 128, 128)
        lower_slab(pl.ds(start, 128), start)
        return carry

    lax.fori_loop(0, held // 128, lower_slab_step, 0)
    lower_slab(slice(held // 128 * 128, held), held // 128 * 128)

    def place_upper(target, turned, start, many):
        for q in range(2):
            gates = [turned[(2 * g + q) * unit_u : (2 * g + q + 1) * unit_u] for g in range(4)]
            gates.append(jnp.zeros((up_wide - 4 * unit_u, 128), F32))
            part = jnp.concatenate(gates, axis=0).astype(BF)
            target[q, :, pl.ds(start, many)] = part[:, :many]

    def upper_slab(index, carry):
        start = pl.multiple_of(index * 128, 128)
        turned = jnp.transpose(uin_raw[pl.ds(start, 128), :].astype(F32))
        place_upper(uin_t, turned, start, 128)
        return carry

    lax.fori_loop(0, held // 128, upper_slab, 0)
    start = held // 128 * 128
    turned = jnp.transpose(uin_raw[start:held, :].astype(F32))
    turned = jnp.concatenate([turned, jnp.zeros((full_u, 128 - held % 128), F32)], axis=1)
    place_upper(uin_t, turned, start, wide_k - start)
    for start in range(0, held_u, 128):
        stop = min(start + 128, held_u)
        lanes = pl.ds(start, 128)
        turned = [
            masked_columns(
                urec_raw[start:stop, i : min(i + block, full_u)], words_u, i // 20, lanes
            )
            for i in range(0, full_u, block)
        ]
        many = min(128, up_k - start)
        place_upper(urec_t, jnp.concatenate(turned, axis=0), start, many)
    for q in range(2):
        wrec[q] = jnp.transpose(wrec_t[q])
        uin[q] = jnp.transpose(uin_t[q])
        urec[q] = jnp.transpose(urec_t[q])
    rows_l_o[...] = jnp.transpose(words_l[...])
    rows_u_o[...] = jnp.transpose(words_u[...])

    early = EARLY * ROWS

    def place_left(target, row, count, high, low, first):
        steps_rows = high.shape[0]
        start = 2 * early if first else 0
        high, low = jnp.transpose(high)[:count], jnp.transpose(low)[:count]
        target[row : row + count, start : start + steps_rows] = high
        target[row : row + count, start + steps_rows : start + 2 * steps_rows] = low

    def place_steps(target, row, count, stack, first, last):
        width = stack.shape[2]
        high, low = [
            stack[first:last, i * ROWS : (i + 1) * ROWS, :].reshape((last - first) * ROWS, width)
            for i in (0, 1)
        ]
        place_left(target, row, count, high, low, first)

    place_left(xh, 0, wide_k, x2[0:early], x2[rows_all : rows_all + early], 0)
    place_left(xh, 0, wide_k, x2[early:rows_all], x2[rows_all + early :], EARLY)

    def far_copy(src, dst, number, axis, d):
        return pltpu.make_async_remote_copy(
            src_ref=src,
            dst_ref=dst,
            send_sem=far_s.at[number],
            recv_sem=far_r.at[number],
            device_id=across(axis, d),
            device_id_type=MESH,
        )

    lr_rows = lr.shape[0]

    def left_copy(k, d, kind, upper):
        lanes = slice(2 * early if kind == 2 else 0, 2 * early if kind == 1 else 2 * rows_all)
        if upper:
            src, rows = lr.at[:, lanes], slice(0, lr_rows)
        else:
            rows = slice(0, wide_k) if kind == 0 else slice(wide_k, 2 * wide_k)
            src = xh.at[rows, lanes]
        return far_copy(src, left_o.at[k, d - 1, rows, lanes], (k * 3 + d - 1) * 3 + kind, k, d)

    def for_left(kind, act, target):
        for k in range(3):
            for d in (1, 2, 3):
                lower_copy = left_copy(k, d, kind, False)
                if k < 2:
                    act(lower_copy)
                    continue
                is_lower = target(k, d) == 0

                @pl.when(is_lower)
                def _(copy=lower_copy):
                    act(copy)

                if kind > 0:
                    upper_copy = left_copy(k, d, kind, True)

                    @pl.when(jnp.logical_not(is_lower))
                    def _(copy=upper_copy):
                        act(copy)

    def at_peer(k, d):
        return lax.rem(place[k] + d, 4)

    def at_home(k, d):
        return place[k]

    for_left(0, lambda copy: copy.start(), at_peer)

    def right_copies(k, d, chunk, row, count, upper, target):
        rows = pl.ds(row, count)
        dst = right_o.at[k, d - 1, :, rows, 0:512]
        number = 27 + (k * 3 + d - 1) * 5 + chunk
        if not upper:
            col = (4 * k + (target if k < 2 else 0)) * 512
            src = da_all.at[:, rows, pl.ds(pl.multiple_of(col, 512), 512)]
            return [far_copy(src, dst, number, k, d)]
        col = pl.multiple_of(jnp.maximum(target - 1, 0) * 512, 512)
        tail_dst = right_o.at[k, d - 1, :, rows, 512:640]
        return [
            far_copy(du_all.at[:, rows, pl.ds(col, 512)], dst, number, k, d),
            far_copy(du_all.at[:, rows, 1536:1664], tail_dst, 72 + (d - 1) * 5 + chunk, k, d),
        ]

    def for_right(chunk, row, count, act, target):
        for k in range(3):
            for d in (1, 2, 3):
                goes = target(k, d)
                if k < 2:
                    for copy in right_copies(k, d, chunk, row, count, False, goes):
                        act(copy)
                    continue

                @pl.when(goes == 0)
                def _(k=k, d=d, goes=goes):
                    for copy in right_copies(k, d, chunk, row, count, False, goes):
                        act(copy)

                @pl.when(goes != 0)
                def _(k=k, d=d, goes=goes):
                    for copy in right_copies(k, d, chunk, row, count, True, goes):
                        act(copy)

    chunks = ((8, 4), (4, 4), (2, 2), (1, 1), (0, 1))

    act_l[...] = jnp.zeros_like(act_l)
    hk2[...] = jnp.zeros_like(hk2)
    ux2[...] = jnp.zeros_like(ux2)
    hku2[...] = jnp.zeros_like(hku2)
    cell_l[...] = jnp.zeros_like(cell_l)
    cell_u[...] = jnp.zeros_like(cell_u)

    def fcopy_l(t):
        return remote(send_l, recv_l.at[lax.rem(t, 2)], fs_l.at[t], fr_l.at[t])

    def fcopy_u(t):
        return remote(send_u, recv_u.at[lax.rem(t, 2)], fs_u.at[t], fr_u.at[t])

    def lower_send(t, first):
        if first:
            send_l[...] = proj[other, t]
        else:
            send_l[...] = fold(dot_nn(hk2[t, :, :wide_k], wrec[other])) + proj[other, t]
        fcopy_l(t).start()

    def lower_own(t, first):
        if first:
            act_l[:, :wide] = proj[me, t]
        else:
            act_l[:, :wide] = fold(dot_nn(hk2[t, :, :wide_k], wrec[me])) + proj[me, t]

    def upper_part(t, q):
        y = dot_nn(ux2[t, :, :wide_k], uin[q]) + dot_nn(hku2[t, :, :up_k], urec[q])
        return fold(y) + bup[q]

    def upper_send(t):
        send_u[...] = upper_part(t, other)
        fcopy_u(t).start()

    def upper_own(t):
        act_u[...] = upper_part(t, me)

    def keep_at(t, lanes):
        return jnp.concatenate([keep_ref[t]] * (ceil_to(lanes, 128) // 128), axis=1)[
            :, :lanes
        ]

    def cell_update(a_in, a_forget, a_cand, a_out, cell, keep_now, save, t):
        gate_in = jax.nn.sigmoid(a_in)
        forget = jax.nn.sigmoid(a_forget)
        cand = jnp.tanh(a_cand)
        gate_out = jax.nn.sigmoid(a_out)
        cell_keep = cell[...] * keep_now
        cell_new = forget * cell_keep + gate_in * cand
        squashed = jnp.tanh(cell_new)
        cell[...] = cell_new
        save[t, 0] = gate_in
        save[t, 1] = forget
        save[t, 2] = cand
        save[t, 3] = gate_out
        save[t, 4] = cell_keep
        save[t, 5] = squashed
        return gate_out * squashed

    def lower_cell(t):
        act_l[:, :wide] += recv_l[lax.rem(t, 2)]
        hidden = cell_update(
            act_l[:, 0:lane],
            act_l[:, units : units + lane],
            act_l[:, 2 * units : 2 * units + lane],
            act_l[:, 3 * units : 3 * units + lane],
            cell_l,
            keep_at(t, lane),
            save_l,
            t,
        )
        high, low = split(hidden * keep_at(t + 1, lane))
        hk2[t + 1, 0:ROWS] = high
        hk2[t + 1, ROWS:] = low
        ones_at = lax.broadcasted_iota(jnp.int32, (ROWS, lane), 1) == units
        high, low = split(jnp.where(ones_at, 1.0, hidden * lock_ref[...]))
        ux2[t, 0:ROWS] = high
        ux2[t, ROWS:] = low

    def upper_cell(t):
        a = act_u[...] + recv_u[lax.rem(t, 2)]
        hidden = cell_update(
            a[:, 0:gate_u],
            a[:, unit_u : unit_u + gate_u],
            a[:, 2 * unit_u : 2 * unit_u + gate_u],
            a[:, 3 * unit_u : 3 * unit_u + gate_u],
            cell_u,
            keep_at(t, gate_u),
            save_u,
            t,
        )
        hid_o[:, pl.ds(t, 1), :] = hidden[:streams, :unit_u].reshape(streams, 1, unit_u)
        high, low = split(hidden * keep_at(t + 1, gate_u))
        hku2[t + 1, 0:ROWS] = high
        hku2[t + 1, ROWS:] = low

    lower_send(0, True)
    lower_own(0, True)
    fcopy_l(0).wait()
    lower_cell(0)

    def forward_round(r, carry, with_cell=True):
        lower_send(r, False)
        if with_cell:
            fcopy_u(r - 2).wait()
            upper_cell(r - 2)
        lower_own(r, False)
        upper_send(r - 1)
        upper_own(r - 1)
        fcopy_l(r).wait()
        lower_cell(r)
        if with_cell:

            @pl.when(r == EARLY)
            def _():
                place_steps(xh, wide_k, wide_k, hk2, 0, EARLY)
                place_steps(lr, 0, wide_k, ux2, 0, EARLY)
                place_steps(lr, wide_k, up_k, hku2, 0, EARLY)
                for_left(1, lambda copy: copy.start(), at_peer)

        return carry

    forward_round(1, 0, False)
    lax.fori_loop(2, steps, forward_round, 0)
    fcopy_u(steps - 2).wait()
    upper_cell(steps - 2)
    upper_send(steps - 1)
    upper_own(steps - 1)
    fcopy_u(steps - 1).wait()
    upper_cell(steps - 1)

    place_steps(xh, wide_k, wide_k, hk2, EARLY, steps)
    place_steps(lr, 0, wide_k, ux2, EARLY, steps)
    place_steps(lr, wide_k, up_k, hku2, EARLY, steps)
    for_left(2, lambda copy: copy.start(), at_peer)

    da_all[...] = jnp.zeros_like(da_all)
    du_all[...] = jnp.zeros_like(du_all)

    def own_order(t, carry):
        to = pl.ds(pl.multiple_of(t * ROWS, ROWS), ROWS)
        for part in range(2):
            rows = slice(part * ROWS, (part + 1) * ROWS)
            for q in range(2):
                for g in range(4):
                    start = (2 * g + q) * units
                    da_all[part, to, start : start + units] = dal[
                        q, t, rows, g * units : (g + 1) * units
                    ]
                    start = (2 * g + q) * unit_u
                    du_all[part, to, start : start + unit_u] = dau[
                        q, t, rows, g * unit_u : (g + 1) * unit_u
                    ]
        return carry

    def send_right(chunk):
        first, count = chunks[chunk]
        lax.fori_loop(first, first + count, own_order, 0)
        for_right(chunk, first * ROWS, count * ROWS, lambda copy: copy.start(), at_peer)

    dstate_l[...] = jnp.zeros_like(dstate_l)
    dstate_u[...] = jnp.zeros_like(dstate_u)
    da_l[...] = jnp.zeros_like(da_l)
    da_u[...] = jnp.zeros_like(da_u)

    def bcopy_l(t):
        return remote(dal.at[me, t], dal.at[me, t], bs_l.at[t], br_l.at[t])

    def bcopy_u(t):
        return remote(dau.at[me, t], dau.at[me, t], bs_u.at[t], br_u.at[t])

    def gate_grads(dy, dstate, save, keep_now, t):
        gate_in, forget, cand, gate_out = save[t, 0], save[t, 1], save[t, 2], save[t, 3]
        cell_keep, squashed = save[t, 4], save[t, 5]
        dh = dstate[0] + dy
        dc = dstate[1] + dh * gate_out * (1.0 - squashed * squashed)
        dstate[1] = dc * forget * keep_now
        return (
            dc * cand * gate_in * (1.0 - gate_in),
            dc * cell_keep * forget * (1.0 - forget),
            dc * gate_in * (1.0 - cand * cand),
            dh * squashed * gate_out * (1.0 - gate_out),
        )

    def lower_back_start(t):
        grads = gate_grads(dx_up[...] * lock_ref[...], dstate_l, save_l, keep_at(t, lane), t)
        for g in range(4):
            da_l[:, g * units : (g + 1) * units] = grads[g][:, :units]
        high, low = split(da_l[...])
        dal[me, t, 0:ROWS] = high
        dal[me, t, ROWS:] = low
        bcopy_l(t).start()

    def upper_back_start(t):
        grads = gate_grads(gout_ref[t], dstate_u, save_u, keep_at(t, gate_u), t)
        for g in range(4):
            da_u[:, g * unit_u : (g + 1) * unit_u] = grads[g][:, :unit_u]
        high, low = split(da_u[...])
        dau[me, t, 0:ROWS] = high
        dau[me, t, ROWS:] = low
        bcopy_u(t).start()

    def lower_back_part(t, q):
        return fold(dot_nn(dal[q, t], wrec_t[q]))

    def upper_back_part(t, q):
        grad = dau[q, t]
        return fold(dot_nn(grad, uin_t[q])), fold(dot_nn(grad, urec_t[q]))

    def lower_back_own(t):
        acc[:, :wide_k] = lower_back_part(t, me)

    def lower_back_other(t):
        total = acc[:, :wide_k] + lower_back_part(t, other)
        dstate_l[0, :, :wide_k] = keep_at(t, wide_k) * total

    def upper_back_own(t):
        into_x, into_h = upper_back_part(t, me)
        acc_x[:, :wide_k] = into_x
        acc_h[:, :up_k] = into_h

    def upper_back_other(t):
        into_x, into_h = upper_back_part(t, other)
        dx_up[:, :wide_k] = acc_x[:, :wide_k] + into_x
        dstate_u[0, :, :up_k] = keep_at(t, up_k) * (acc_h[:, :up_k] + into_h)

    dx_up[...] = jnp.zeros_like(dx_up)
    upper_back_start(steps - 1)
    upper_back_own(steps - 1)
    bcopy_u(steps - 1).wait()
    upper_back_other(steps - 1)
    upper_back_start(steps - 2)

    def backward_round(r, carry, last=False):
        t = steps - r
        lower_back_start(t)
        lower_back_own(t)
        upper_back_own(t - 1)
        bcopy_u(t - 1).wait()
        upper_back_other(t - 1)
        bcopy_l(t).wait()
        lower_back_other(t)
        if last:
            send_right(3)
            return carry
        upper_back_start(t - 2)
        for chunk in range(3):

            @pl.when(t == chunks[chunk][0])
            def _(chunk=chunk):
                send_right(chunk)

        return carry

    lax.fori_loop(1, steps - 1, backward_round, 0)
    backward_round(steps - 1, 0, True)
    lower_back_start(0)
    bcopy_l(0).wait()

    send_right(4)

    copies = [
        pltpu.make_async_copy(da_all, da_o, out_sem.at[0]),
        pltpu.make_async_copy(du_all, du_o, out_sem.at[1]),
        pltpu.make_async_copy(xh, xh_o, out_sem.at[2]),
        pltpu.make_async_copy(lr, lr_o, out_sem.at[3]),
    ]
    for copy in copies:
        copy.start()

    chunk = 512

    def input_grad(cols, width):
        grad = da_all[:, :, cols].reshape(2 * rows_all, width)
        return fold(dot_nt(grad, win_raw[:, cols]))

    tail = full // chunk * chunk
    dx[:, :held] = input_grad(slice(tail, full), full % chunk) if full % chunk else 0.0

    def input_grad_step(index, carry):
        dx[:, :held] += input_grad(pl.ds(pl.multiple_of(index * chunk, chunk), chunk), chunk)
        return carry

    lax.fori_loop(0, full // chunk, input_grad_step, 0)
    for t in range(steps):
        now = dx[t * ROWS : t * ROWS + streams, :held] * lock_low[0:streams, :held]
        dx_o[:, t, :] = now
    for copy in copies:
        copy.wait()
    for kind in range(3):
        for_left(kind, lambda copy: copy.wait_send(), at_peer)
        for_left(kind, lambda copy: copy.wait_recv(), at_home)
    for chunk in range(5):
        row, count = chunks[chunk][0] * ROWS, chunks[chunk][1] * ROWS
        for_right(chunk, row, count, lambda copy: copy.wait_send(), at_peer)
        for_right(chunk, row, count, lambda copy: copy.wait_recv(), at_home)


def recurrence(
    inputs,
    lower_lock,
    upper_lock,
    resets,
    grad_out,
    lower_drop,
    upper_drop,
    bias,
    wrec,
    win,
    uin,
    urec,
):
    streams, steps = resets.shape
    units, full = wrec.shape
    outs, full_u = urec.shape
    wide_k = ceil_to(units, 16)
    wide = ceil_to(full // 2, 256)
    up_k = ceil_to(outs, 16)
    gate_u = ceil_to(outs, 128)
    up_wide = ceil_to(full_u // 2, 128)
    lane = ceil_to(units, 128)
    rows_all = steps * ROWS
    vm = pl.BlockSpec(memory_space=pltpu.VMEM)
    hbm = pl.BlockSpec(memory_space=pl.ANY)
    sds = jax.ShapeDtypeStruct
    i32 = jnp.int32
    shared = [
        ((2, rows_all, ceil_to(full, 512)), BF),
        ((2, rows_all, ceil_to(full_u, 128)), BF),
        ((2 * wide_k, 2 * rows_all), BF),
        ((wide_k + up_k, 2 * rows_all), BF),
    ]
    landed = [
        ((3, 3, 2 * wide_k, 2 * rows_all), BF),
        ((3, 3, 2, rows_all, 640), BF),
    ]
    raw = [(w.shape, BF) for w in (wrec, win, uin, urec)]
    dma = pltpu.SemaphoreType.DMA
    return pl.pallas_call(
        functools.partial(recurrence_kernel, units),
        out_shape=(sds((streams, steps, outs), F32), sds((streams, steps, units), F32))
        + tuple(sds(*s) for s in shared + landed)
        + (sds((lane, 256), i32), sds((ceil_to(outs, 128), 128), i32)),
        in_specs=[vm] * 8 + [hbm] * 4,
        out_specs=(vm, vm) + (hbm,) * len(shared + landed) + (vm, vm),
        scratch_shapes=[pltpu.VMEM(*s) for s in raw]
        + [
            pltpu.VMEM((256, lane), i32),
            pltpu.VMEM((128, ceil_to(outs, 128)), i32),
            pltpu.VMEM((ceil_to(full, 16), 128), F32),
            pltpu.VMEM((steps + 1, ROWS, 128), F32),
            pltpu.VMEM((ROWS, lane), F32),
            pltpu.VMEM((ROWS, lane), F32),
            pltpu.VMEM((steps, ROWS, gate_u), F32),
            pltpu.VMEM((2, 1, wide), F32),
            pltpu.VMEM((2, 1, up_wide), F32),
            pltpu.VMEM((2, wide, wide_k), BF),
            pltpu.VMEM((2, up_wide, wide_k), BF),
            pltpu.VMEM((2, up_wide, up_k), BF),
            pltpu.VMEM((2, wide_k, wide), BF),
            pltpu.VMEM((2, wide_k, up_wide), BF),
            pltpu.VMEM((2, up_k, up_wide), BF),
        ]
        + [pltpu.VMEM(*s) for s in shared]
        + [
            pltpu.VMEM((2 * rows_all, lane), BF),
            pltpu.VMEM((steps + 1, 2 * ROWS, lane), BF),
            pltpu.VMEM((steps, 2 * ROWS, lane), BF),
            pltpu.VMEM((steps + 1, 2 * ROWS, gate_u), BF),
            pltpu.VMEM((2, steps, 2 * ROWS, wide), BF),
            pltpu.VMEM((2, steps, 2 * ROWS, up_wide), BF),
            pltpu.VMEM((2, steps, ROWS, wide), F32),
            pltpu.VMEM((ROWS, wide), F32),
            pltpu.VMEM((2, ROWS, wide), F32),
            pltpu.VMEM((ROWS, up_wide), F32),
            pltpu.VMEM((2, ROWS, up_wide), F32),
            pltpu.VMEM((ROWS, wide + lane - units), F32),
            pltpu.VMEM((ROWS, up_wide), F32),
            pltpu.VMEM((steps, 6, ROWS, lane), F32),
            pltpu.VMEM((steps, 6, ROWS, gate_u), F32),
            pltpu.VMEM((ROWS, lane), F32),
            pltpu.VMEM((ROWS, gate_u), F32),
            pltpu.VMEM((ROWS, wide), F32),
            pltpu.VMEM((ROWS, up_wide), F32),
            pltpu.VMEM((2, ROWS, lane), F32),
            pltpu.VMEM((2, ROWS, gate_u), F32),
            pltpu.VMEM((ROWS, lane), F32),
            pltpu.VMEM((ROWS, lane), F32),
            pltpu.VMEM((ROWS, lane), F32),
            pltpu.VMEM((ROWS, gate_u), F32),
            pltpu.VMEM((rows_all, lane), F32),
        ]
        + [dma((steps,))] * 8
        + [dma((87,)), dma((87,)), dma((4,)), dma((4,))],
        compiler_params=pltpu.CompilerParams(
            vmem_limit_bytes=VMEM_LIMIT, collective_id=0, has_side_effects=True
        ),
    )(
        inputs,
        lower_lock,
        upper_lock,
        resets,
        grad_out,
        lower_drop,
        upper_drop,
        bias,
        wrec,
        win,
        uin,
        urec,
    )


PANEL = 576
STRIP = 288
GROUP = 72
HALF = 2 * GROUP
FULL = STRIP + 8
PAIRS = 24
LOWER_PAIRS = 18
SMALLEST = 2.0**-111
WIDTH = 4


def code(group):
    largest = jnp.maximum(jnp.max(jnp.abs(group), axis=0, keepdims=True), SMALLEST)
    step = jnp.floor(jnp.log2(largest) * 64.0).astype(jnp.int32) + 2
    return step, 32767.0 * jnp.exp2(step.astype(F32) * (-1.0 / 64.0))


def factor(step):
    return jnp.exp2(step.astype(F32) * (1.0 / 64.0)) * (1.0 / 32767.0)


def encode(a, b):
    step_a, up_a = code(a)
    step_b, up_b = code(b)
    word_a = jnp.round(a * up_a).astype(jnp.int32)
    word_b = jnp.round(b * up_b).astype(jnp.int32)
    return (word_a << 16) | (word_b & 0xFFFF), step_a, step_b


def decode(words, step_a, step_b):
    a = (words >> 16).astype(F32) * factor(step_a)
    b = ((words << 16) >> 16).astype(F32) * factor(step_b)
    return a, b


def sum_kernel(
    xh,
    lr,
    da,
    du,
    far_left,
    far_right,
    words,
    out,
    kept,
    lhs,
    rhs,
    mine,
    send2,
    recv2,
    send3,
    recv3,
    shard,
    scales,
    panel,
    send_sem,
    recv_sem,
    copy_sem,
    kept_sem,
    left_sem,
    right_sem,
):
    place, peer = torus()
    barrier = pltpu.get_barrier_semaphore()
    for axis in range(3):
        for distance in (1, 2, 3):
            pl.semaphore_signal(
                barrier, inc=1, device_id=peer(axis, distance), device_id_type=MESH
            )

    parts = tuple(range(6))

    def axes(m):
        return m % 3, (m + 1) % 3, (m + 2) % 3

    def kept_copy(m):
        first, second, third = axes(m)
        number = first * 16 + place[first] * 4 + place[second]
        start = pl.multiple_of(m // 3 * STRIP + place[third] * GROUP, 8)
        part = jnp.minimum(lax.div(number, 20), 1)
        lanes = pl.ds(pl.multiple_of(part * 128, 128), 128)
        src = words.at[pl.ds(start, GROUP), lanes]
        return number, pltpu.make_async_copy(src, kept.at[m], kept_sem.at[m])

    for m in parts:
        kept_copy(m)[1].start()

    def remote(src, dst, number, axis, distance):
        return pltpu.make_async_remote_copy(
            src_ref=src,
            dst_ref=dst,
            send_sem=send_sem.at[number],
            recv_sem=recv_sem.at[number],
            device_id=peer(axis, distance),
            device_id_type=MESH,
        )

    upper_here = place[2] != 0
    rows_all = da.shape[1]
    lr_rows = lr.shape[0]
    early = EARLY * ROWS

    def operand_copies(k, upper):
        copies = []
        for s in range(4):
            rows = slice(0, lr_rows if upper else 2 * PANEL)
            src = (lr if upper else xh) if s == 0 else far_left.at[k, s - 1]
            at = s * 640
            for i, (first, last) in enumerate(((0, 384), (0, 128), (256, 384))):
                to = lhs.at[k, rows, at : at + last - first]
                copies.append(
                    pltpu.make_async_copy(
                        src.at[rows, first:last], to, left_sem.at[(k * 4 + s) * 3 + i]
                    )
                )
                at += last - first
            sems = [right_sem.at[(k * 4 + s) * 2 + i] for i in (0, 1)]
            to = rhs.at[k, s, :, :, 0:512]
            if s > 0:
                src = far_right.at[k, s - 1, :, :, 0:512]
            elif upper:
                col = pl.multiple_of(jnp.maximum(place[k] - 1, 0) * 512, 512)
                src = du.at[:, :, pl.ds(col, 512)]
            else:
                col = pl.multiple_of((4 * k + (place[k] if k < 2 else 0)) * 512, 512)
                src = da.at[:, :, pl.ds(col, 512)]
            copies.append(pltpu.make_async_copy(src, to, sems[0]))
            if upper:
                src = far_right.at[k, s - 1, :, :, 512:640] if s > 0 else du.at[:, :, 1536:1664]
                copies.append(pltpu.make_async_copy(src, rhs.at[k, s, :, :, 512:640], sems[1]))
        return copies

    def for_operands(k, act):
        if k < 2:
            for copy in operand_copies(k, False):
                act(copy)
            return

        @pl.when(jnp.logical_not(upper_here))
        def _():
            for copy in operand_copies(k, False):
                act(copy)

        @pl.when(upper_here)
        def _():
            for copy in operand_copies(k, True):
                act(copy)

    def right(k, cols, width):
        parts = []
        for s in range(4):
            high, low = rhs[k, s, 0, :, cols], rhs[k, s, 1, :, cols]
            parts += [high[:early], high[:early], high[early:], high[early:]]
            parts += [low[:early], low[early:], jnp.zeros((640 - 3 * rows_all, width), BF)]
        return jnp.concatenate(parts, axis=0)

    def compute(m, half):
        k, row = m % 3, m // 3 * STRIP
        cols = pl.ds(pl.multiple_of(half * 256, 256), 256)

        def put(ab, n, rows, value):
            mine[m, ab, 2 * half + n, rows, :] = value[:, n * 128 : (n + 1) * 128]

        def lower():
            operand = right(k, cols, 256)
            for ab in range(2):
                y = dot_nn(lhs[k, ab * PANEL + row : ab * PANEL + row + STRIP], operand)
                for n in range(2):
                    put(ab, n, slice(0, STRIP), y)

        def upper():
            operand = right(k, cols, 256)
            y = dot_nn(lhs[k, row : row + STRIP], operand)
            top = PANEL - TAIL_ROWS if row == 0 else 0
            index = 2 * (place[k] - 1) + half
            start = jnp.clip(index, 0, 2) * TAIL_ROWS + (STRIP - PANEL + TAIL_ROWS if row else 0)
            rows = pl.ds(pl.multiple_of(start, 16), STRIP - top)
            bottom = dot_nn(lhs[k, rows], right(k, slice(512, 640), 128))
            bottom = jnp.where(index < 3, bottom, 0.0)
            for n in range(2):
                put(0, n, slice(0, STRIP), y)
            if top:
                y = dot_nn(lhs[k, PANEL : PANEL + top], operand)
                for n in range(2):
                    put(1, n, slice(0, top), y)
            mine[m, 1, 2 * half, top:, :] = bottom
            mine[m, 1, 2 * half + 1, top:, :] = jnp.zeros_like(bottom)

        if k < 2:
            lower()
        else:
            pl.when(jnp.logical_not(upper_here))(lower)
            pl.when(upper_here)(upper)

    def compute_part(m):
        def step(half, carry):
            compute(m, half)
            return carry

        lax.fori_loop(0, 2, step, 0)

    @pl.when(upper_here)
    def _():
        lhs[2, lr_rows:, :] = jnp.zeros((2 * PANEL - lr_rows, lhs.shape[2]), BF)

    def rows_of(group):
        return pl.ds(pl.multiple_of(group * GROUP, 8), GROUP)

    def steps_at(ref, base, group):
        return ref[pl.ds(base + 2 * group, 1), :], ref[pl.ds(base + 2 * group + 1, 1), :]

    def store_code(ref, base, group, words, step_a, step_b):
        ref[rows_of(group), :] = words
        ref[pl.ds(base + 2 * group, 1), :] = step_a
        ref[pl.ds(base + 2 * group + 1, 1), :] = step_b

    def arrived(ref, base, group):
        return decode(ref[rows_of(group), :], *steps_at(ref, base, group))

    ways = ((0, 1), (1, -1))

    def stage2(m, way, kind):
        number = (m * 2 + way) * 3 + kind
        return remote(
            send2.at[m, way, kind], recv2.at[m, way, kind], number, axes(m)[1], 1 - 2 * way
        )

    def pack_half(m, offset, half, target, added):
        block = lax.rem(place[axes(m)[1]] + (offset + 4), 4)
        for group in range(2):
            rows = slice(half * HALF + group * GROUP, half * HALF + (group + 1) * GROUP)
            a, b = mine[m, 0, block, rows, :], mine[m, 1, block, rows, :]
            if added is not None:
                more_a, more_b = arrived(added, HALF, group)
                a, b = a + more_a, b + more_b
            store_code(target, HALF, group, *encode(a, b))

    def reduce2_first(m):
        for way, sign in ways:
            pack_half(m, 2, way, send2.at[m, way, 0], None)
            stage2(m, way, 0).start()
        for way, sign in ways:
            pack_half(m, sign, 1 - way, send2.at[m, way, 1], None)
            stage2(m, way, 1).start()

    def reduce2_second(m):
        for way, sign in ways:
            stage2(m, way, 0).wait_recv()
            pack_half(m, sign, way, send2.at[m, way, 2], recv2.at[m, way, 0])
            stage2(m, way, 2).start()

    def stage3(m, d):
        number = 36 + m * 3 + d - 1
        return remote(send3.at[m, d - 1], recv3.at[m, d - 1], number, axes(m)[2], d)

    def reduce3(m):
        block = place[axes(m)[1]]
        for kind in (1, 2):
            for way in range(2):
                stage2(m, way, kind).wait_recv()
        for group in range(4):
            half, inner = group // 2, group % 2
            a1, b1 = arrived(recv2.at[m, 0, 2 - half], HALF, inner)
            a2, b2 = arrived(recv2.at[m, 1, 1 + half], HALF, inner)
            rows = slice(group * GROUP, (group + 1) * GROUP)
            mine[m, 0, block, rows, :] += a1 + a2
            mine[m, 1, block, rows, :] += b1 + b2
        for d in (1, 2, 3):
            group = lax.rem(place[axes(m)[2]] + d, 4)
            a, b = mine[m, 0, block, rows_of(group), :], mine[m, 1, block, rows_of(group), :]
            store_code(send3.at[m, d - 1], GROUP, 0, *encode(a, b))
            stage3(m, d).start()

    def spread3(m, d, group):
        number = 54 + (m * 3 + d - 1) * 2
        axis = axes(m)[2]
        data = remote(shard.at[m, 0:GROUP], panel.at[m, rows_of(group)], number, axis, d)
        scale = remote(
            shard.at[m, GROUP : GROUP + 8], scales.at[m, d - 1], number + 1, axis, d
        )
        return data, scale

    def finish(m):
        first, second, third = axes(m)
        block, own = place[second], place[third]
        a, b = mine[m, 0, block, rows_of(own), :], mine[m, 1, block, rows_of(own), :]
        for d in (1, 2, 3):
            stage3(m, d).wait_recv()
            more_a, more_b = arrived(recv3.at[m, d - 1], GROUP, 0)
            a, b = a + more_a, b + more_b
        number, copy = kept_copy(m)
        copy.wait()
        flags = jnp.where(number < 2 * LOWER_PAIRS, flags_at(kept[m], number * 128) * 2, 1)
        store_code(shard.at[m], GROUP, 0, *encode(a, b * flags.astype(F32)))
        for d in (1, 2, 3):
            for copy in spread3(m, d, own):
                copy.start()
        panel[m, rows_of(own), :] = shard[m, 0:GROUP, :]

    def at(m, first, second):
        return out.at[m * 16 + first * 4 + second]

    def turned(axis, distance):
        return lax.rem(place[axis] + (distance + 4), 4)

    def spread2(m, way, src, first, second):
        return remote(src, at(m, first, second), 90 + m * 4 + way, axes(m)[1], 1 - 2 * way)

    def pass2(m, way, first, second):
        rows = slice(0, HALF) if way == 0 else slice(HALF, FULL)
        ref = at(m, first, second).at[rows]
        return remote(ref, ref, 90 + m * 4 + 2 + way, axes(m)[1], 1 - 2 * way)

    def spread1(m, way, order, src, first, second):
        number = 114 + (m * 2 + way) * 6 + order
        return remote(src, at(m, first, second), number, axes(m)[0], 1 - 2 * way)

    offsets = (0, -1, 1, 2)

    def own_copy(m):
        first, second, third = axes(m)
        return pltpu.make_async_copy(
            panel.at[m], at(m, place[first], place[second]), copy_sem.at[m]
        )

    def gather_own(m):
        first, second, third = axes(m)
        row = lax.broadcasted_iota(jnp.int32, (8, 128), 0)
        total = jnp.zeros((8, 128), jnp.int32)
        for d in (0, 1, 2, 3):
            group = lax.rem(place[third] + (4 - d), 4)
            if d == 0:
                tile = shard[m, GROUP : GROUP + 8, :]
            else:
                for copy in spread3(m, d, group):
                    copy.wait_recv()
                tile = scales[m, d - 1]
            total = jnp.where(row == 2 * group, tile[0:1], total)
            total = jnp.where(row == 2 * group + 1, tile[1:2], total)
        panel[m, STRIP:FULL, :] = total
        for way in range(2):
            spread2(m, way, panel.at[m], place[first], place[second]).start()
        own_copy(m).start()
        for way in range(2):
            spread1(m, way, 0, panel.at[m], place[first], place[second]).start()

    def gather_near(m):
        first = place[axes(m)[0]]
        for way in range(2):
            second = turned(axes(m)[1], 2 * way - 1)
            spread2(m, way, panel.at[m], first, second).wait_recv()
            pass2(m, way, first, second).start()
            for way1 in range(2):
                spread1(m, way1, 1 + way, at(m, first, second), first, second).start()

    def gather_far(m):
        first, second = place[axes(m)[0]], turned(axes(m)[1], 2)
        for way in range(2):
            pass2(m, way, first, second).wait_recv()
        for way1 in range(2):
            spread1(m, way1, 3, at(m, first, second), first, second).start()

    passed = ((0, 0), (1, 2), (0, 1), (1, 3))

    def pass1(m, way, order, first):
        ref = at(m, first, turned(axes(m)[1], offsets[order]))
        number = 114 + (m * 2 + way) * 6 + 4 + order % 2
        return remote(ref, ref, number, axes(m)[0], 1 - 2 * way)

    def spread1_arrived(m, way, order):
        first = turned(axes(m)[0], 2 * way - 1)
        second = turned(axes(m)[1], offsets[order])
        spread1(m, way, order, panel.at[m], first, second).wait_recv()

    def pass_on(m, which):
        for way, order in passed[which]:
            spread1_arrived(m, way, order)
            pass1(m, way, order, turned(axes(m)[0], 2 * way - 1)).start()

    for_operands(0, lambda copy: copy.start())
    for_operands(1, lambda copy: copy.start())
    pl.semaphore_wait(barrier, 9)

    def begin(m):
        if m < 3:
            for_operands(m, lambda copy: copy.wait())
        if m == 0:
            for_operands(2, lambda copy: copy.start())
        compute_part(m)
        reduce2_first(m)

    def pass_early(m):
        pass_on(m, slice(0, 2))

    def pass_late(m):
        pass_on(m, slice(2, 4))

    for step, m in (
        (begin, 0),
        (begin, 1),
        (begin, 2),
        (reduce2_second, 0),
        (reduce2_second, 1),
        (begin, 3),
        (reduce2_second, 2),
        (reduce3, 0),
        (reduce3, 1),
        (begin, 4),
        (reduce3, 2),
        (finish, 0),
        (finish, 1),
        (begin, 5),
        (finish, 2),
        (gather_own, 0),
        (gather_own, 1),
        (reduce2_second, 3),
        (gather_own, 2),
        (reduce2_second, 4),
        (reduce2_second, 5),
        (gather_near, 0),
        (reduce3, 3),
        (gather_near, 1),
        (reduce3, 4),
        (gather_near, 2),
        (reduce3, 5),
        (finish, 3),
        (gather_far, 0),
        (finish, 4),
        (gather_far, 1),
        (finish, 5),
        (gather_far, 2),
        (gather_own, 3),
        (pass_early, 0),
        (gather_own, 4),
        (pass_early, 1),
        (gather_own, 5),
        (pass_early, 2),
        (gather_near, 3),
        (gather_near, 4),
        (gather_near, 5),
        (pass_late, 0),
        (pass_late, 1),
        (pass_late, 2),
        (gather_far, 3),
        (gather_far, 4),
        (gather_far, 5),
        (pass_early, 3),
        (pass_early, 4),
        (pass_early, 5),
        (pass_late, 3),
        (pass_late, 4),
        (pass_late, 5),
    ):
        step(m)
    for m in parts:
        for way in range(2):
            for order in range(4):
                if (way, order) not in passed:
                    spread1_arrived(m, way, order)
        for way, order in passed:
            pass1(m, way, order, turned(axes(m)[0], 2)).wait_recv()

    for m in parts:
        for way in range(2):
            for kind in range(3):
                stage2(m, way, kind).wait_send()
        for d in (1, 2, 3):
            stage3(m, d).wait_send()
            for copy in spread3(m, d, place[axes(m)[2]]):
                copy.wait_send()
        first, second = place[axes(m)[0]], place[axes(m)[1]]
        own_copy(m).wait()
        for way in range(2):
            spread2(m, way, panel.at[m], first, second).wait_send()
            pass2(m, way, first, turned(axes(m)[1], 2 * way - 1)).wait_send()
            for order in range(4):
                second_now = turned(axes(m)[1], offsets[order])
                src = panel.at[m] if order == 0 else at(m, first, second_now)
                spread1(m, way, order, src, first, second_now).wait_send()
        for way, order in passed:
            pass1(m, way, order, turned(axes(m)[0], 2 * way - 1)).wait_send()


def summed_panels(xh, lr, da, du, left, right, words):
    i32 = jnp.int32
    messages = 114 + 72
    rows_all = da.shape[1]
    dma = pltpu.SemaphoreType.DMA
    return pl.pallas_call(
        sum_kernel,
        out_shape=pltpu.VMEM((4 * PAIRS, FULL, 128), i32),
        in_specs=[pl.BlockSpec(memory_space=pl.ANY)] * 7,
        out_specs=pl.BlockSpec(memory_space=pl.ANY),
        scratch_shapes=[
            pltpu.VMEM((6, GROUP, 128), i32),
            pltpu.VMEM((3, 2 * PANEL, 4 * 640), BF),
            pltpu.VMEM((3, 4, 2, rows_all, 640), BF),
            pltpu.VMEM((6, 2, 4, STRIP, 128), F32),
            pltpu.VMEM((6, 2, 3, HALF + 8, 128), i32),
            pltpu.VMEM((6, 2, 3, HALF + 8, 128), i32),
            pltpu.VMEM((6, 3, GROUP + 8, 128), i32),
            pltpu.VMEM((6, 3, GROUP + 8, 128), i32),
            pltpu.VMEM((6, GROUP + 8, 128), i32),
            pltpu.VMEM((6, 3, 8, 128), i32),
            pltpu.VMEM((6, FULL, 128), i32),
            dma((messages,)),
            dma((messages,)),
            dma((6,)),
            dma((6,)),
            dma((36,)),
            dma((24,)),
        ],
        compiler_params=pltpu.CompilerParams(
            vmem_limit_bytes=SUM_VMEM, collective_id=1, has_side_effects=True
        ),
    )(xh, lr, da, du, left, right, words)


def unpack_kernel(panels, words_u, low_in, low_rec, low_bias, up_in, up_rec, up_bias, tail):
    step = pl.program_id(0)
    units, outs = low_in.shape[0], up_rec.shape[0]
    lower_steps, all_steps = 2 * LOWER_PAIRS // WIDTH, 2 * PAIRS // WIDTH

    def values(n, ab):
        parts = []
        n = jnp.minimum(step, all_steps - 1) * WIDTH + n
        for strip in range(2):
            at = strip * 2 * PAIRS + n
            for group in range(4):
                words = panels[at, group * GROUP : (group + 1) * GROUP, :]
                row = STRIP + 2 * group + ab
                scale = factor(panels[at, row : row + 1, :])
                half = (words >> 16) if ab == 0 else ((words << 16) >> 16)
                parts.append(half.astype(F32) * scale)
        return jnp.concatenate(parts, axis=0)

    for n in range(WIDTH):
        cols = slice(n * 128, (n + 1) * 128)

        @pl.when(step < lower_steps)
        def _():
            a = values(n, 0)
            low_in[:, cols] = a[:units]
            low_bias[:, cols] = a[units : units + 1]
            b = values(n, 1)[:units]
            low_rec[:, cols] = b

        @pl.when((step >= lower_steps) & (step < all_steps))
        def _():
            a = values(n, 0)
            up_in[:, cols] = a[:units]
            up_bias[:, cols] = a[units : units + 1]
            b = values(n, 1)
            flags = flags_at(words_u[...], (step - lower_steps) * WIDTH * 128 + n * 128)
            up_rec[:, cols] = b[:outs] * (flags * 2).astype(F32)[:outs]
            if n % 2 == 0:
                index = (step - lower_steps) * (WIDTH // 2) + n // 2
                rows = pl.ds(pl.multiple_of(index * TAIL_ROWS, 8), TAIL_ROWS)
                tail[rows, :] = b[PANEL - TAIL_ROWS :]

    @pl.when(step == all_steps)
    def _():
        up_in[:, :128] = tail[:units]
        up_bias[:, :128] = tail[units : units + 1]
        flags = flags_at(words_u[...], 2 * (PAIRS - LOWER_PAIRS) * 128)
        up_rec[:, :128] = tail[PANEL : PANEL + outs] * (flags * 2).astype(F32)[:outs]


def unpack(panels, words_u, units, full, outs, full_u):
    sds = jax.ShapeDtypeStruct
    lower_steps, all_steps = 2 * LOWER_PAIRS // WIDTH, 2 * PAIRS // WIDTH
    wide = 128 * WIDTH
    lower = lambda i: (0, jnp.minimum(i, lower_steps - 1))
    upper = lambda i: (0, jnp.maximum(i - lower_steps, 0))
    return pl.pallas_call(
        unpack_kernel,
        grid=(all_steps + 1,),
        out_shape=(
            sds((units, full), F32),
            sds((units, full), F32),
            sds((1, full), F32),
            sds((units, full_u), F32),
            sds((outs, full_u), F32),
            sds((1, full_u), F32),
        ),
        in_specs=[
            pl.BlockSpec(memory_space=pltpu.VMEM),
            pl.BlockSpec(memory_space=pltpu.VMEM),
        ],
        out_specs=(
            pl.BlockSpec((units, wide), lower),
            pl.BlockSpec((units, wide), lower),
            pl.BlockSpec((1, wide), lower),
            pl.BlockSpec((units, wide), upper),
            pl.BlockSpec((outs, wide), upper),
            pl.BlockSpec((1, wide), upper),
        ),
        scratch_shapes=[pltpu.VMEM((6 * TAIL_ROWS, 128), F32)],
        compiler_params=pltpu.CompilerParams(vmem_limit_bytes=UNPACK_VMEM),
    )(panels, words_u)


def body(
    inputs,
    lower_lock,
    upper_lock,
    resets,
    lower_input,
    lower_recur,
    lower_bias,
    lower_drop,
    upper_input,
    upper_recur,
    upper_bias,
    upper_drop,
    grad_out,
):
    me = lax.axis_index("pipe")
    streams, steps, width = inputs.shape
    hidden_out, grad_inputs, da, du, xh, lr, left, right, words_l, words_u = recurrence(
        inputs,
        lower_lock,
        upper_lock,
        resets,
        grad_out,
        lower_drop.T,
        upper_drop.T,
        jnp.concatenate([lower_bias, upper_bias])[None],
        lower_recur,
        lower_input,
        upper_input,
        upper_recur,
    )
    panels = summed_panels(xh, lr, da, du, left, right, words_l)
    low_in, low_rec, low_bias, up_in, up_rec, up_bias = unpack(
        panels, words_u, *lower_recur.shape, *upper_recur.shape
    )

    def own(row):
        half = row.shape[1] // 2
        return lax.dynamic_slice_in_dim(row[0], me * half, half, 0)

    return (
        hidden_out,
        grad_inputs,
        low_in,
        low_rec,
        own(low_bias),
        up_in,
        up_rec,
        own(up_bias),
    )


def solution(mesh):
    return jax.shard_map(
        body,
        mesh=mesh,
        in_specs=(
            P("dp", None, None),
            P("dp", None),
            P("dp", None),
            P("dp", None),
            P("pipe", None),
            P("pipe", None),
            P("pipe"),
            P(),
            P("pipe", None),
            P("pipe", None),
            P("pipe"),
            P(),
            P("dp", None, None),
        ),
        out_specs=(
            P("dp", None, "pipe"),
            P("dp", None, "pipe"),
            P("pipe", None),
            P("pipe", None),
            P("pipe"),
            P("pipe", None),
            P("pipe", None),
            P("pipe"),
        ),
        check_vma=False,
    )
```

```python
import functools

import jax
import jax.numpy as jnp
from jax import lax
from jax.experimental import pallas as pl
from jax.experimental.pallas import tpu as pltpu
from jax.sharding import PartitionSpec as P

BF = jnp.bfloat16
F32 = jnp.float32
MESH = pl.DeviceIdType.MESH
ROWS = 16
VMEM_LIMIT = 62 * 2**20
TAIL_ROWS = 368
EARLY = 8
SUM_VMEM = 47 * 2**20
UNPACK_VMEM = 24 * 2**20


def ceil_to(value, multiple):
    return -(-value // multiple) * multiple


def split(value):
    high = value.astype(BF)
    low = (value - high.astype(F32)).astype(BF)
    return high, low


def fold(stacked):
    half = stacked.shape[0] // 2
    return stacked[:half] + stacked[half:]


def dot_nn(a, b):
    return jnp.dot(a, b, preferred_element_type=F32)


def dot_nt(a, b):
    return lax.dot_general(a, b, (((1,), (1,)), ((), ())), preferred_element_type=F32)


def torus():
    dp = lax.axis_index("dp")
    place = [lax.rem(dp, 4), lax.rem(lax.div(dp, 4), 4), lax.div(dp, 16)]
    stride = [1, 4, 16]

    def across(axis, distance):
        moved = lax.rem(place[axis] + (distance + 4), 4)
        return {"dp": dp + (moved - place[axis]) * stride[axis]}

    return place, across


def flags_at(words, column):
    column = lax.broadcasted_iota(jnp.int32, (1, 128), 1) + column
    index = (column * 52429) >> 20
    bit = column - index * 20
    index = jnp.broadcast_to(index & 127, words.shape)
    found = jnp.take_along_axis(words, index, axis=1, mode="promise_in_bounds")
    return (found >> bit) & 1


def recurrence_kernel(
    units,
    inputs,
    lower_lock,
    upper_lock,
    resets,
    grad_out,
    lower_drop,
    upper_drop,
    both_bias,
    wrec_in,
    win_in,
    uin_in,
    urec_in,
    hid_o,
    dx_o,
    da_o,
    du_o,
    xh_o,
    lr_o,
    left_o,
    right_o,
    rows_l_o,
    rows_u_o,
    wrec_raw,
    win_raw,
    uin_raw,
    urec_raw,
    words_l,
    words_u,
    slab,
    keep_ref,
    lock_low,
    lock_ref,
    gout_ref,
    blo,
    bup,
    wrec_t,
    uin_t,
    urec_t,
    wrec,
    uin,
    urec,
    da_all,
    du_all,
    xh,
    lr,
    x2,
    hk2,
    ux2,
    hku2,
    dal,
    dau,
    proj,
    send_l,
    recv_l,
    send_u,
    recv_u,
    act_l,
    act_u,
    save_l,
    save_u,
    cell_l,
    cell_u,
    da_l,
    da_u,
    dstate_l,
    dstate_u,
    dx_up,
    acc,
    acc_x,
    acc_h,
    dx,
    fs_l,
    fr_l,
    fs_u,
    fr_u,
    bs_l,
    br_l,
    bs_u,
    br_u,
    far_s,
    far_r,
    in_sem,
    out_sem,
):
    streams, steps = resets.shape
    me = lax.axis_index("pipe")
    other = 1 - me
    peer = {"pipe": other}
    wide_k = wrec.shape[1]
    wide = wrec.shape[2]
    up_wide = uin.shape[2]
    up_k = urec.shape[1]
    lane = act_l.shape[1] - wide + units

    barrier = pltpu.get_barrier_semaphore()
    pl.semaphore_signal(barrier, inc=1, device_id=peer, device_id_type=MESH)
    place, across = torus()
    for axis in range(3):
        for d in (1, 2, 3):
            pl.semaphore_signal(barrier, inc=1, device_id=across(axis, d), device_id_type=MESH)
    loads = [
        pltpu.make_async_copy(wrec_in, wrec_raw, in_sem.at[1]),
        pltpu.make_async_copy(uin_in, uin_raw, in_sem.at[2]),
        pltpu.make_async_copy(urec_in, urec_raw, in_sem.at[3]),
        pltpu.make_async_copy(win_in, win_raw, in_sem.at[0]),
    ]
    for load in loads:
        load.start()
    pl.semaphore_wait(barrier, 10)

    def remote(src, dst, send_sem, recv_sem):
        return pltpu.make_async_remote_copy(
            src_ref=src,
            dst_ref=dst,
            send_sem=send_sem,
            recv_sem=recv_sem,
            device_id=peer,
            device_id_type=MESH,
        )

    full = wrec_raw.shape[1]
    held = wrec_raw.shape[0]
    held_u = urec_raw.shape[0]
    full_u = urec_raw.shape[1]
    unit_u = full_u // 8
    gate_u = gout_ref.shape[2]
    rows_all = steps * ROWS

    def to_rows(value, lanes, filler=0.0):
        more = lanes - value.shape[1]
        if more:
            value = jnp.concatenate([value, jnp.full((streams, more), filler, F32)], axis=1)
        return jnp.concatenate([value, jnp.zeros((ROWS - streams, lanes), F32)], axis=0)

    keep_ref[...] = jnp.zeros_like(keep_ref)
    for t in range(steps):
        now = 1.0 - resets[:, t : t + 1].astype(F32)
        keep_ref[t] = to_rows(jnp.broadcast_to(now, (streams, 128)), 128)
    blo[...] = jnp.zeros_like(blo)
    bup[...] = jnp.zeros_like(bup)
    def place_words(target, packed):
        rows, lanes = packed.shape
        more = target.shape[1] - lanes
        packed = jnp.concatenate([packed, jnp.zeros((rows, more), jnp.int32)], axis=1)
        target[0:rows, :] = packed

    words_l[...] = jnp.zeros_like(words_l)
    words_u[...] = jnp.zeros_like(words_u)
    for half in range(2):

        @pl.when(me == half)
        def _(half=half):
            mine = slice(half * units, (half + 1) * units)
            lock_low[...] = to_rows(lower_lock[:, mine].astype(F32) * 1.25, lane)
            lock_ref[...] = to_rows(upper_lock[:, mine].astype(F32) * 1.25, lane)
            one = jnp.full((streams, 1), 1.0, F32)
            for t in range(steps):
                now = inputs[:, t, mine] * lock_low[0:streams, 0:units]
                now = to_rows(jnp.concatenate([now, one], axis=1), lane)
                high, low = split(now)
                x2[t * ROWS : (t + 1) * ROWS] = high
                x2[rows_all + t * ROWS : rows_all + (t + 1) * ROWS] = low
                out = grad_out[:, t, half * unit_u : (half + 1) * unit_u]
                gout_ref[t] = to_rows(out, gate_u)
            place_words(words_l, lower_drop[:, mine])
            place_words(words_u, upper_drop[:, half * held_u : (half + 1) * held_u])
            bias = both_bias[...].astype(F32)
            bias_u = bias[:, 4 * units :]
            for q in range(2):
                for i in range(2):
                    g = 2 * half + i
                    start = (2 * i + q) * units
                    blo[q, :, g * units : (g + 1) * units] = bias[:, start : start + units]
                    start = (2 * i + q) * unit_u
                    bup[q, :, g * unit_u : (g + 1) * unit_u] = bias_u[
                        :, start : start + unit_u
                    ]

    loads[0].wait()
    sub = lax.broadcasted_iota(jnp.int32, (8, 128), 0)

    def flags_of(held, i):
        left, right = 8 * i // 20, (8 * i + 7) // 20
        now = jnp.broadcast_to(held[left : left + 1], (8, 128))
        if right != left:
            later = jnp.broadcast_to(held[right : right + 1], (8, 128))
            now = jnp.where(sub < 20 * right - 8 * i, now, later)
        bit = sub + 8 * i % 20
        bit = jnp.where(bit >= 20, bit - 20, bit)
        return (now >> bit) & 1

    def masked_columns(weight, words, first, lanes):
        rows, columns = weight.shape
        words = words[pl.ds(first, ceil_to(ceil_to(columns, 20) // 20, 8)), lanes]
        turned = jnp.transpose(weight.astype(F32))
        if rows < 128:
            turned = jnp.concatenate([turned, jnp.zeros((columns, 128 - rows), F32)], axis=1)
        out = []
        for i in range(columns // 8):
            now = turned[8 * i : 8 * i + 8]
            out.append(jnp.where(flags_of(words, i) != 0, now + now, 0.0))
        return jnp.concatenate(out, axis=0)

    block = 640
    row16 = lax.broadcasted_iota(jnp.int32, (ROWS, 128), 0)

    def lower_slab(rows, start):
        lanes = pl.ds(start, 128)
        many = min(128, wide_k - start) if isinstance(start, int) else 128

        def fill(index, carry):
            cols = pl.ds(pl.multiple_of(index * block, block), block)
            first = pl.multiple_of(index * (block // 20), block // 20)
            part = masked_columns(wrec_raw[rows, cols], words_l, first, lanes)
            slab[cols, :] = part
            return carry

        lax.fori_loop(0, full // block, fill, 0)
        last = full // block * block
        slab[last:full, :] = masked_columns(
            wrec_raw[rows, last:full], words_l, last // 20, lanes
        )
        target = pl.ds(start, many)
        tiles = units // ROWS
        for q in range(2):
            for g in range(4):
                shift = units * (g + q)
                base = (tiles + 1) * ROWS * g

                def move(index, carry, q=q, shift=shift, base=base):
                    for i in range(7):
                        row = pl.multiple_of(base + (index * 7 + i) * ROWS, ROWS)
                        now = slab[pl.ds(row + shift, ROWS), :]
                        wrec_t[q, pl.ds(row, ROWS), target] = now.astype(BF)[:, :many]
                    return carry

                lax.fori_loop(0, tiles // 7, move, 0)
                row = base + tiles * ROWS
                now = slab[row + shift : row + shift + ROWS, :]
                if g < 3:
                    later = slab[row + shift + units : row + shift + units + ROWS, :]
                else:
                    later = jnp.zeros((ROWS, 128), F32)
                now = jnp.where(row16 < units * (g + 1) - row, now, later)
                wrec_t[q, row : row + ROWS, target] = now.astype(BF)[:, :many]

    def lower_slab_step(index, carry):
        start = pl.multiple_of(index * 128, 128)
        lower_slab(pl.ds(start, 128), start)
        return carry

    lax.fori_loop(0, held // 128, lower_slab_step, 0)
    lower_slab(slice(held // 128 * 128, held), held // 128 * 128)

    def place_upper(target, turned, start, many):
        for q in range(2):
            gates = [turned[(2 * g + q) * unit_u : (2 * g + q + 1) * unit_u] for g in range(4)]
            gates.append(jnp.zeros((up_wide - 4 * unit_u, 128), F32))
            part = jnp.concatenate(gates, axis=0).astype(BF)
            target[q, :, pl.ds(start, many)] = part[:, :many]

    for load in loads[1:]:
        load.wait()

    def upper_slab(index, carry):
        start = pl.multiple_of(index * 128, 128)
        turned = jnp.transpose(uin_raw[pl.ds(start, 128), :].astype(F32))
        place_upper(uin_t, turned, start, 128)
        return carry

    lax.fori_loop(0, held // 128, upper_slab, 0)
    start = held // 128 * 128
    turned = jnp.transpose(uin_raw[start:held, :].astype(F32))
    turned = jnp.concatenate([turned, jnp.zeros((full_u, 128 - held % 128), F32)], axis=1)
    place_upper(uin_t, turned, start, wide_k - start)
    for start in range(0, held_u, 128):
        stop = min(start + 128, held_u)
        lanes = pl.ds(start, 128)
        turned = [
            masked_columns(
                urec_raw[start:stop, i : min(i + block, full_u)], words_u, i // 20, lanes
            )
            for i in range(0, full_u, block)
        ]
        many = min(128, up_k - start)
        place_upper(urec_t, jnp.concatenate(turned, axis=0), start, many)
    for q in range(2):
        wrec[q] = jnp.transpose(wrec_t[q])
        uin[q] = jnp.transpose(uin_t[q])
        urec[q] = jnp.transpose(urec_t[q])
    proj[:, :, :, wide - 128 :] = jnp.zeros((2, steps, ROWS, 128), F32)
    for q in range(2):
        for g in range(4):
            start, stop = (2 * g + q) * units, (2 * g + q + 1) * units
            first, last = start // 128 * 128, min(ceil_to(stop, 128), full)
            y = fold(dot_nn(x2[:, :held], win_raw[:, first:last]))
            y = y[:, start - first : stop - first] + blo[q, :, g * units : (g + 1) * units]
            proj[q, :, :, g * units : (g + 1) * units] = y.reshape(steps, ROWS, units)

    rows_l_o[...] = jnp.transpose(words_l[...])
    rows_u_o[...] = jnp.transpose(words_u[...])

    early = EARLY * ROWS

    def place_left(target, row, count, high, low, first):
        steps_rows = high.shape[0]
        start = 2 * early if first else 0
        high, low = jnp.transpose(high)[:count], jnp.transpose(low)[:count]
        target[row : row + count, start : start + steps_rows] = high
        target[row : row + count, start + steps_rows : start + 2 * steps_rows] = low

    def place_steps(target, row, count, stack, first, last):
        width = stack.shape[2]
        high, low = [
            stack[first:last, i * ROWS : (i + 1) * ROWS, :].reshape((last - first) * ROWS, width)
            for i in (0, 1)
        ]
        place_left(target, row, count, high, low, first)

    place_left(xh, 0, wide_k, x2[0:early], x2[rows_all : rows_all + early], 0)
    place_left(xh, 0, wide_k, x2[early:rows_all], x2[rows_all + early :], EARLY)

    def far_copy(src, dst, number, axis, d):
        return pltpu.make_async_remote_copy(
            src_ref=src,
            dst_ref=dst,
            send_sem=far_s.at[number],
            recv_sem=far_r.at[number],
            device_id=across(axis, d),
            device_id_type=MESH,
        )

    lr_rows = lr.shape[0]

    def left_copy(k, d, kind, upper):
        lanes = slice(2 * early if kind == 2 else 0, 2 * early if kind == 1 else 2 * rows_all)
        if upper:
            src, rows = lr.at[:, lanes], slice(0, lr_rows)
        else:
            rows = slice(0, wide_k) if kind == 0 else slice(wide_k, 2 * wide_k)
            src = xh.at[rows, lanes]
        return far_copy(src, left_o.at[k, d - 1, rows, lanes], (k * 3 + d - 1) * 3 + kind, k, d)

    def for_left(kind, act, target):
        for k in range(3):
            for d in (1, 2, 3):
                lower_copy = left_copy(k, d, kind, False)
                if k < 2:
                    act(lower_copy)
                    continue
                is_lower = target(k, d) == 0

                @pl.when(is_lower)
                def _(copy=lower_copy):
                    act(copy)

                if kind > 0:
                    upper_copy = left_copy(k, d, kind, True)

                    @pl.when(jnp.logical_not(is_lower))
                    def _(copy=upper_copy):
                        act(copy)

    def at_peer(k, d):
        return lax.rem(place[k] + d, 4)

    def at_home(k, d):
        return place[k]

    for_left(0, lambda copy: copy.start(), at_peer)

    def right_copies(k, d, chunk, row, count, upper, target):
        rows = pl.ds(row, count)
        dst = right_o.at[k, d - 1, :, rows, 0:512]
        number = 27 + (k * 3 + d - 1) * 5 + chunk
        if not upper:
            col = (4 * k + (target if k < 2 else 0)) * 512
            src = da_all.at[:, rows, pl.ds(pl.multiple_of(col, 512), 512)]
            return [far_copy(src, dst, number, k, d)]
        col = pl.multiple_of(jnp.maximum(target - 1, 0) * 512, 512)
        tail_dst = right_o.at[k, d - 1, :, rows, 512:640]
        return [
            far_copy(du_all.at[:, rows, pl.ds(col, 512)], dst, number, k, d),
            far_copy(du_all.at[:, rows, 1536:1664], tail_dst, 72 + (d - 1) * 5 + chunk, k, d),
        ]

    def for_right(chunk, row, count, act, target):
        for k in range(3):
            for d in (1, 2, 3):
                goes = target(k, d)
                if k < 2:
                    for copy in right_copies(k, d, chunk, row, count, False, goes):
                        act(copy)
                    continue

                @pl.when(goes == 0)
                def _(k=k, d=d, goes=goes):
                    for copy in right_copies(k, d, chunk, row, count, False, goes):
                        act(copy)

                @pl.when(goes != 0)
                def _(k=k, d=d, goes=goes):
                    for copy in right_copies(k, d, chunk, row, count, True, goes):
                        act(copy)

    chunks = ((8, 4), (4, 4), (2, 2), (1, 1), (0, 1))

    act_l[...] = jnp.zeros_like(act_l)
    hk2[...] = jnp.zeros_like(hk2)
    ux2[...] = jnp.zeros_like(ux2)
    hku2[...] = jnp.zeros_like(hku2)
    cell_l[...] = jnp.zeros_like(cell_l)
    cell_u[...] = jnp.zeros_like(cell_u)

    def fcopy_l(t):
        return remote(send_l, recv_l.at[lax.rem(t, 2)], fs_l.at[t], fr_l.at[t])

    def fcopy_u(t):
        return remote(send_u, recv_u.at[lax.rem(t, 2)], fs_u.at[t], fr_u.at[t])

    def lower_send(t, first):
        if first:
            send_l[...] = proj[other, t]
        else:
            send_l[...] = fold(dot_nn(hk2[t, :, :wide_k], wrec[other])) + proj[other, t]
        fcopy_l(t).start()

    def lower_own(t, first):
        if first:
            act_l[:, :wide] = proj[me, t]
        else:
            act_l[:, :wide] = fold(dot_nn(hk2[t, :, :wide_k], wrec[me])) + proj[me, t]

    def upper_part(t, q):
        y = dot_nn(ux2[t, :, :wide_k], uin[q]) + dot_nn(hku2[t, :, :up_k], urec[q])
        return fold(y) + bup[q]

    def upper_send(t):
        send_u[...] = upper_part(t, other)
        fcopy_u(t).start()

    def upper_own(t):
        act_u[...] = upper_part(t, me)

    def keep_at(t, lanes):
        return jnp.concatenate([keep_ref[t]] * (ceil_to(lanes, 128) // 128), axis=1)[
            :, :lanes
        ]

    def cell_update(a_in, a_forget, a_cand, a_out, cell, keep_now, save, t):
        gate_in = jax.nn.sigmoid(a_in)
        forget = jax.nn.sigmoid(a_forget)
        cand = jnp.tanh(a_cand)
        gate_out = jax.nn.sigmoid(a_out)
        cell_keep = cell[...] * keep_now
        cell_new = forget * cell_keep + gate_in * cand
        squashed = jnp.tanh(cell_new)
        cell[...] = cell_new
        save[t, 0] = gate_in
        save[t, 1] = forget
        save[t, 2] = cand
        save[t, 3] = gate_out
        save[t, 4] = cell_keep
        save[t, 5] = squashed
        return gate_out * squashed

    def lower_cell(t):
        act_l[:, :wide] += recv_l[lax.rem(t, 2)]
        hidden = cell_update(
            act_l[:, 0:lane],
            act_l[:, units : units + lane],
            act_l[:, 2 * units : 2 * units + lane],
            act_l[:, 3 * units : 3 * units + lane],
            cell_l,
            keep_at(t, lane),
            save_l,
            t,
        )
        high, low = split(hidden * keep_at(t + 1, lane))
        hk2[t + 1, 0:ROWS] = high
        hk2[t + 1, ROWS:] = low
        ones_at = lax.broadcasted_iota(jnp.int32, (ROWS, lane), 1) == units
        high, low = split(jnp.where(ones_at, 1.0, hidden * lock_ref[...]))
        ux2[t, 0:ROWS] = high
        ux2[t, ROWS:] = low

    def upper_cell(t):
        a = act_u[...] + recv_u[lax.rem(t, 2)]
        hidden = cell_update(
            a[:, 0:gate_u],
            a[:, unit_u : unit_u + gate_u],
            a[:, 2 * unit_u : 2 * unit_u + gate_u],
            a[:, 3 * unit_u : 3 * unit_u + gate_u],
            cell_u,
            keep_at(t, gate_u),
            save_u,
            t,
        )
        hid_o[:, pl.ds(t, 1), :] = hidden[:streams, :unit_u].reshape(streams, 1, unit_u)
        high, low = split(hidden * keep_at(t + 1, gate_u))
        hku2[t + 1, 0:ROWS] = high
        hku2[t + 1, ROWS:] = low

    lower_send(0, True)
    lower_own(0, True)
    fcopy_l(0).wait()
    lower_cell(0)

    def forward_round(r, carry, with_cell=True):
        lower_send(r, False)
        if with_cell:
            fcopy_u(r - 2).wait()
            upper_cell(r - 2)
        lower_own(r, False)
        upper_send(r - 1)
        upper_own(r - 1)
        fcopy_l(r).wait()
        lower_cell(r)
        if with_cell:

            @pl.when(r == EARLY)
            def _():
                place_steps(xh, wide_k, wide_k, hk2, 0, EARLY)
                place_steps(lr, 0, wide_k, ux2, 0, EARLY)
                place_steps(lr, wide_k, up_k, hku2, 0, EARLY)
                for_left(1, lambda copy: copy.start(), at_peer)

        return carry

    forward_round(1, 0, False)
    lax.fori_loop(2, steps, forward_round, 0)
    fcopy_u(steps - 2).wait()
    upper_cell(steps - 2)
    upper_send(steps - 1)
    upper_own(steps - 1)
    fcopy_u(steps - 1).wait()
    upper_cell(steps - 1)

    place_steps(xh, wide_k, wide_k, hk2, EARLY, steps)
    place_steps(lr, 0, wide_k, ux2, EARLY, steps)
    place_steps(lr, wide_k, up_k, hku2, EARLY, steps)
    for_left(2, lambda copy: copy.start(), at_peer)

    da_all[...] = jnp.zeros_like(da_all)
    du_all[...] = jnp.zeros_like(du_all)

    def own_order(t, carry):
        to = pl.ds(pl.multiple_of(t * ROWS, ROWS), ROWS)
        for part in range(2):
            rows = slice(part * ROWS, (part + 1) * ROWS)
            for q in range(2):
                for g in range(4):
                    start = (2 * g + q) * units
                    da_all[part, to, start : start + units] = dal[
                        q, t, rows, g * units : (g + 1) * units
                    ]
                    start = (2 * g + q) * unit_u
                    du_all[part, to, start : start + unit_u] = dau[
                        q, t, rows, g * unit_u : (g + 1) * unit_u
                    ]
        return carry

    def send_right(chunk):
        first, count = chunks[chunk]
        lax.fori_loop(first, first + count, own_order, 0)
        for_right(chunk, first * ROWS, count * ROWS, lambda copy: copy.start(), at_peer)

    dstate_l[...] = jnp.zeros_like(dstate_l)
    dstate_u[...] = jnp.zeros_like(dstate_u)
    da_l[...] = jnp.zeros_like(da_l)
    da_u[...] = jnp.zeros_like(da_u)

    def bcopy_l(t):
        return remote(dal.at[me, t], dal.at[me, t], bs_l.at[t], br_l.at[t])

    def bcopy_u(t):
        return remote(dau.at[me, t], dau.at[me, t], bs_u.at[t], br_u.at[t])

    def gate_grads(dy, dstate, save, keep_now, t):
        gate_in, forget, cand, gate_out = save[t, 0], save[t, 1], save[t, 2], save[t, 3]
        cell_keep, squashed = save[t, 4], save[t, 5]
        dh = dstate[0] + dy
        dc = dstate[1] + dh * gate_out * (1.0 - squashed * squashed)
        dstate[1] = dc * forget * keep_now
        return (
            dc * cand * gate_in * (1.0 - gate_in),
            dc * cell_keep * forget * (1.0 - forget),
            dc * gate_in * (1.0 - cand * cand),
            dh * squashed * gate_out * (1.0 - gate_out),
        )

    def lower_back_start(t):
        grads = gate_grads(dx_up[...] * lock_ref[...], dstate_l, save_l, keep_at(t, lane), t)
        for g in range(4):
            da_l[:, g * units : (g + 1) * units] = grads[g][:, :units]
        high, low = split(da_l[...])
        dal[me, t, 0:ROWS] = high
        dal[me, t, ROWS:] = low
        bcopy_l(t).start()

    def upper_back_start(t):
        grads = gate_grads(gout_ref[t], dstate_u, save_u, keep_at(t, gate_u), t)
        for g in range(4):
            da_u[:, g * unit_u : (g + 1) * unit_u] = grads[g][:, :unit_u]
        high, low = split(da_u[...])
        dau[me, t, 0:ROWS] = high
        dau[me, t, ROWS:] = low
        bcopy_u(t).start()

    def lower_back_part(t, q):
        return fold(dot_nn(dal[q, t], wrec_t[q]))

    def upper_back_part(t, q):
        grad = dau[q, t]
        return fold(dot_nn(grad, uin_t[q])), fold(dot_nn(grad, urec_t[q]))

    def lower_back_own(t):
        acc[:, :wide_k] = lower_back_part(t, me)

    def lower_back_other(t):
        total = acc[:, :wide_k] + lower_back_part(t, other)
        dstate_l[0, :, :wide_k] = keep_at(t, wide_k) * total

    def upper_back_own(t):
        into_x, into_h = upper_back_part(t, me)
        acc_x[:, :wide_k] = into_x
        acc_h[:, :up_k] = into_h

    def upper_back_other(t):
        into_x, into_h = upper_back_part(t, other)
        dx_up[:, :wide_k] = acc_x[:, :wide_k] + into_x
        dstate_u[0, :, :up_k] = keep_at(t, up_k) * (acc_h[:, :up_k] + into_h)

    dx_up[...] = jnp.zeros_like(dx_up)
    upper_back_start(steps - 1)
    upper_back_own(steps - 1)
    bcopy_u(steps - 1).wait()
    upper_back_other(steps - 1)
    upper_back_start(steps - 2)

    def backward_round(r, carry, last=False):
        t = steps - r
        lower_back_start(t)
        lower_back_own(t)
        upper_back_own(t - 1)
        bcopy_u(t - 1).wait()
        upper_back_other(t - 1)
        bcopy_l(t).wait()
        lower_back_other(t)
        if last:
            send_right(3)
            return carry
        upper_back_start(t - 2)
        for chunk in range(3):

            @pl.when(t == chunks[chunk][0])
            def _(chunk=chunk):
                send_right(chunk)

        return carry

    lax.fori_loop(1, steps - 1, backward_round, 0)
    backward_round(steps - 1, 0, True)
    lower_back_start(0)
    bcopy_l(0).wait()

    send_right(4)

    copies = [
        pltpu.make_async_copy(da_all, da_o, out_sem.at[0]),
        pltpu.make_async_copy(du_all, du_o, out_sem.at[1]),
        pltpu.make_async_copy(xh, xh_o, out_sem.at[2]),
        pltpu.make_async_copy(lr, lr_o, out_sem.at[3]),
    ]
    for copy in copies:
        copy.start()

    chunk = 512

    def input_grad(cols, width):
        grad = da_all[:, :, cols].reshape(2 * rows_all, width)
        return fold(dot_nt(grad, win_raw[:, cols]))

    tail = full // chunk * chunk
    dx[:, :held] = input_grad(slice(tail, full), full % chunk) if full % chunk else 0.0

    def input_grad_step(index, carry):
        dx[:, :held] += input_grad(pl.ds(pl.multiple_of(index * chunk, chunk), chunk), chunk)
        return carry

    lax.fori_loop(0, full // chunk, input_grad_step, 0)
    for t in range(steps):
        now = dx[t * ROWS : t * ROWS + streams, :held] * lock_low[0:streams, :held]
        dx_o[:, t, :] = now
    for copy in copies:
        copy.wait()
    for kind in range(3):
        for_left(kind, lambda copy: copy.wait_send(), at_peer)
        for_left(kind, lambda copy: copy.wait_recv(), at_home)
    for chunk in range(5):
        row, count = chunks[chunk][0] * ROWS, chunks[chunk][1] * ROWS
        for_right(chunk, row, count, lambda copy: copy.wait_send(), at_peer)
        for_right(chunk, row, count, lambda copy: copy.wait_recv(), at_home)


def recurrence(
    inputs,
    lower_lock,
    upper_lock,
    resets,
    grad_out,
    lower_drop,
    upper_drop,
    bias,
    wrec,
    win,
    uin,
    urec,
):
    streams, steps = resets.shape
    units, full = wrec.shape
    outs, full_u = urec.shape
    wide_k = ceil_to(units, 16)
    wide = ceil_to(full // 2, 256)
    up_k = ceil_to(outs, 16)
    gate_u = ceil_to(outs, 128)
    up_wide = ceil_to(full_u // 2, 128)
    lane = ceil_to(units, 128)
    rows_all = steps * ROWS
    vm = pl.BlockSpec(memory_space=pltpu.VMEM)
    hbm = pl.BlockSpec(memory_space=pl.ANY)
    sds = jax.ShapeDtypeStruct
    i32 = jnp.int32
    shared = [
        ((2, rows_all, ceil_to(full, 512)), BF),
        ((2, rows_all, ceil_to(full_u, 128)), BF),
        ((2 * wide_k, 2 * rows_all), BF),
        ((wide_k + up_k, 2 * rows_all), BF),
    ]
    landed = [
        ((3, 3, 2 * wide_k, 2 * rows_all), BF),
        ((3, 3, 2, rows_all, 640), BF),
    ]
    raw = [(w.shape, BF) for w in (wrec, win, uin, urec)]
    dma = pltpu.SemaphoreType.DMA
    return pl.pallas_call(
        functools.partial(recurrence_kernel, units),
        out_shape=(sds((streams, steps, outs), F32), sds((streams, steps, units), F32))
        + tuple(sds(*s) for s in shared + landed)
        + (sds((lane, 256), i32), sds((ceil_to(outs, 128), 128), i32)),
        in_specs=[vm] * 8 + [hbm] * 4,
        out_specs=(vm, vm) + (hbm,) * len(shared + landed) + (vm, vm),
        scratch_shapes=[pltpu.VMEM(*s) for s in raw]
        + [
            pltpu.VMEM((256, lane), i32),
            pltpu.VMEM((128, ceil_to(outs, 128)), i32),
            pltpu.VMEM((ceil_to(full, 16), 128), F32),
            pltpu.VMEM((steps + 1, ROWS, 128), F32),
            pltpu.VMEM((ROWS, lane), F32),
            pltpu.VMEM((ROWS, lane), F32),
            pltpu.VMEM((steps, ROWS, gate_u), F32),
            pltpu.VMEM((2, 1, wide), F32),
            pltpu.VMEM((2, 1, up_wide), F32),
            pltpu.VMEM((2, wide, wide_k), BF),
            pltpu.VMEM((2, up_wide, wide_k), BF),
            pltpu.VMEM((2, up_wide, up_k), BF),
            pltpu.VMEM((2, wide_k, wide), BF),
            pltpu.VMEM((2, wide_k, up_wide), BF),
            pltpu.VMEM((2, up_k, up_wide), BF),
        ]
        + [pltpu.VMEM(*s) for s in shared]
        + [
            pltpu.VMEM((2 * rows_all, lane), BF),
            pltpu.VMEM((steps + 1, 2 * ROWS, lane), BF),
            pltpu.VMEM((steps, 2 * ROWS, lane), BF),
            pltpu.VMEM((steps + 1, 2 * ROWS, gate_u), BF),
            pltpu.VMEM((2, steps, 2 * ROWS, wide), BF),
            pltpu.VMEM((2, steps, 2 * ROWS, up_wide), BF),
            pltpu.VMEM((2, steps, ROWS, wide), F32),
            pltpu.VMEM((ROWS, wide), F32),
            pltpu.VMEM((2, ROWS, wide), F32),
            pltpu.VMEM((ROWS, up_wide), F32),
            pltpu.VMEM((2, ROWS, up_wide), F32),
            pltpu.VMEM((ROWS, wide + lane - units), F32),
            pltpu.VMEM((ROWS, up_wide), F32),
            pltpu.VMEM((steps, 6, ROWS, lane), F32),
            pltpu.VMEM((steps, 6, ROWS, gate_u), F32),
            pltpu.VMEM((ROWS, lane), F32),
            pltpu.VMEM((ROWS, gate_u), F32),
            pltpu.VMEM((ROWS, wide), F32),
            pltpu.VMEM((ROWS, up_wide), F32),
            pltpu.VMEM((2, ROWS, lane), F32),
            pltpu.VMEM((2, ROWS, gate_u), F32),
            pltpu.VMEM((ROWS, lane), F32),
            pltpu.VMEM((ROWS, lane), F32),
            pltpu.VMEM((ROWS, lane), F32),
            pltpu.VMEM((ROWS, gate_u), F32),
            pltpu.VMEM((rows_all, lane), F32),
        ]
        + [dma((steps,))] * 8
        + [dma((87,)), dma((87,)), dma((4,)), dma((4,))],
        compiler_params=pltpu.CompilerParams(
            vmem_limit_bytes=VMEM_LIMIT, collective_id=0, has_side_effects=True
        ),
    )(
        inputs,
        lower_lock,
        upper_lock,
        resets,
        grad_out,
        lower_drop,
        upper_drop,
        bias,
        wrec,
        win,
        uin,
        urec,
    )


PANEL = 576
STRIP = 288
GROUP = 72
HALF = 2 * GROUP
FULL = STRIP + 8
PAIRS = 24
LOWER_PAIRS = 18
SMALLEST = 2.0**-111
WIDTH = 4


def code(group):
    largest = jnp.maximum(jnp.max(jnp.abs(group), axis=0, keepdims=True), SMALLEST)
    step = jnp.floor(jnp.log2(largest) * 64.0).astype(jnp.int32) + 2
    return step, 32767.0 * jnp.exp2(step.astype(F32) * (-1.0 / 64.0))


def factor(step):
    return jnp.exp2(step.astype(F32) * (1.0 / 64.0)) * (1.0 / 32767.0)


def encode(a, b):
    step_a, up_a = code(a)
    step_b, up_b = code(b)
    word_a = jnp.round(a * up_a).astype(jnp.int32)
    word_b = jnp.round(b * up_b).astype(jnp.int32)
    return (word_a << 16) | (word_b & 0xFFFF), step_a, step_b


def decode(words, step_a, step_b):
    a = (words >> 16).astype(F32) * factor(step_a)
    b = ((words << 16) >> 16).astype(F32) * factor(step_b)
    return a, b


def sum_kernel(
    xh,
    lr,
    da,
    du,
    far_left,
    far_right,
    words,
    out,
    kept,
    lhs,
    rhs,
    mine,
    send2,
    recv2,
    send3,
    recv3,
    shard,
    scales,
    panel,
    send_sem,
    recv_sem,
    copy_sem,
    kept_sem,
    left_sem,
    right_sem,
):
    place, peer = torus()
    barrier = pltpu.get_barrier_semaphore()
    for axis in range(3):
        for distance in (1, 2, 3):
            pl.semaphore_signal(
                barrier, inc=1, device_id=peer(axis, distance), device_id_type=MESH
            )

    parts = tuple(range(6))

    def axes(m):
        return m % 3, (m + 1) % 3, (m + 2) % 3

    def kept_copy(m):
        first, second, third = axes(m)
        number = first * 16 + place[first] * 4 + place[second]
        start = pl.multiple_of(m // 3 * STRIP + place[third] * GROUP, 8)
        part = jnp.minimum(lax.div(number, 20), 1)
        lanes = pl.ds(pl.multiple_of(part * 128, 128), 128)
        src = words.at[pl.ds(start, GROUP), lanes]
        return number, pltpu.make_async_copy(src, kept.at[m], kept_sem.at[m])

    for m in parts:
        kept_copy(m)[1].start()

    def remote(src, dst, number, axis, distance):
        return pltpu.make_async_remote_copy(
            src_ref=src,
            dst_ref=dst,
            send_sem=send_sem.at[number],
            recv_sem=recv_sem.at[number],
            device_id=peer(axis, distance),
            device_id_type=MESH,
        )

    upper_here = place[2] != 0
    rows_all = da.shape[1]
    lr_rows = lr.shape[0]
    early = EARLY * ROWS

    def operand_copies(k, upper):
        copies = []
        for s in range(4):
            rows = slice(0, lr_rows if upper else 2 * PANEL)
            src = (lr if upper else xh) if s == 0 else far_left.at[k, s - 1]
            at = s * 640
            for i, (first, last) in enumerate(((0, 384), (0, 128), (256, 384))):
                to = lhs.at[k, rows, at : at + last - first]
                copies.append(
                    pltpu.make_async_copy(
                        src.at[rows, first:last], to, left_sem.at[(k * 4 + s) * 3 + i]
                    )
                )
                at += last - first
            sems = [right_sem.at[(k * 4 + s) * 2 + i] for i in (0, 1)]
            to = rhs.at[k, s, :, :, 0:512]
            if s > 0:
                src = far_right.at[k, s - 1, :, :, 0:512]
            elif upper:
                col = pl.multiple_of(jnp.maximum(place[k] - 1, 0) * 512, 512)
                src = du.at[:, :, pl.ds(col, 512)]
            else:
                col = pl.multiple_of((4 * k + (place[k] if k < 2 else 0)) * 512, 512)
                src = da.at[:, :, pl.ds(col, 512)]
            copies.append(pltpu.make_async_copy(src, to, sems[0]))
            if upper:
                src = far_right.at[k, s - 1, :, :, 512:640] if s > 0 else du.at[:, :, 1536:1664]
                copies.append(pltpu.make_async_copy(src, rhs.at[k, s, :, :, 512:640], sems[1]))
        return copies

    def for_operands(k, act):
        if k < 2:
            for copy in operand_copies(k, False):
                act(copy)
            return

        @pl.when(jnp.logical_not(upper_here))
        def _():
            for copy in operand_copies(k, False):
                act(copy)

        @pl.when(upper_here)
        def _():
            for copy in operand_copies(k, True):
                act(copy)

    def right(k, cols, width):
        parts = []
        for s in range(4):
            high, low = rhs[k, s, 0, :, cols], rhs[k, s, 1, :, cols]
            parts += [high[:early], high[:early], high[early:], high[early:]]
            parts += [low[:early], low[early:], jnp.zeros((640 - 3 * rows_all, width), BF)]
        return jnp.concatenate(parts, axis=0)

    def compute(m, half):
        k, row = m % 3, m // 3 * STRIP
        cols = pl.ds(pl.multiple_of(half * 256, 256), 256)

        def put(ab, n, rows, value):
            mine[m, ab, 2 * half + n, rows, :] = value[:, n * 128 : (n + 1) * 128]

        def lower():
            operand = right(k, cols, 256)
            for ab in range(2):
                y = dot_nn(lhs[k, ab * PANEL + row : ab * PANEL + row + STRIP], operand)
                for n in range(2):
                    put(ab, n, slice(0, STRIP), y)

        def upper():
            operand = right(k, cols, 256)
            y = dot_nn(lhs[k, row : row + STRIP], operand)
            top = PANEL - TAIL_ROWS if row == 0 else 0
            index = 2 * (place[k] - 1) + half
            start = jnp.clip(index, 0, 2) * TAIL_ROWS + (STRIP - PANEL + TAIL_ROWS if row else 0)
            rows = pl.ds(pl.multiple_of(start, 16), STRIP - top)
            bottom = dot_nn(lhs[k, rows], right(k, slice(512, 640), 128))
            bottom = jnp.where(index < 3, bottom, 0.0)
            for n in range(2):
                put(0, n, slice(0, STRIP), y)
            if top:
                y = dot_nn(lhs[k, PANEL : PANEL + top], operand)
                for n in range(2):
                    put(1, n, slice(0, top), y)
            mine[m, 1, 2 * half, top:, :] = bottom
            mine[m, 1, 2 * half + 1, top:, :] = jnp.zeros_like(bottom)

        if k < 2:
            lower()
        else:
            pl.when(jnp.logical_not(upper_here))(lower)
            pl.when(upper_here)(upper)

    def compute_part(m):
        def step(half, carry):
            compute(m, half)
            return carry

        lax.fori_loop(0, 2, step, 0)

    @pl.when(upper_here)
    def _():
        lhs[2, lr_rows:, :] = jnp.zeros((2 * PANEL - lr_rows, lhs.shape[2]), BF)

    def rows_of(group):
        return pl.ds(pl.multiple_of(group * GROUP, 8), GROUP)

    def steps_at(ref, base, group):
        return ref[pl.ds(base + 2 * group, 1), :], ref[pl.ds(base + 2 * group + 1, 1), :]

    def store_code(ref, base, group, words, step_a, step_b):
        ref[rows_of(group), :] = words
        ref[pl.ds(base + 2 * group, 1), :] = step_a
        ref[pl.ds(base + 2 * group + 1, 1), :] = step_b

    def arrived(ref, base, group):
        return decode(ref[rows_of(group), :], *steps_at(ref, base, group))

    ways = ((0, 1), (1, -1))

    def stage2(m, way, kind):
        number = (m * 2 + way) * 3 + kind
        return remote(
            send2.at[m, way, kind], recv2.at[m, way, kind], number, axes(m)[1], 1 - 2 * way
        )

    def pack_half(m, offset, half, target, added):
        block = lax.rem(place[axes(m)[1]] + (offset + 4), 4)
        for group in range(2):
            rows = slice(half * HALF + group * GROUP, half * HALF + (group + 1) * GROUP)
            a, b = mine[m, 0, block, rows, :], mine[m, 1, block, rows, :]
            if added is not None:
                more_a, more_b = arrived(added, HALF, group)
                a, b = a + more_a, b + more_b
            store_code(target, HALF, group, *encode(a, b))

    def reduce2_first(m):
        for way, sign in ways:
            pack_half(m, 2, way, send2.at[m, way, 0], None)
            stage2(m, way, 0).start()
        for way, sign in ways:
            pack_half(m, sign, 1 - way, send2.at[m, way, 1], None)
            stage2(m, way, 1).start()

    def reduce2_second(m):
        for way, sign in ways:
            stage2(m, way, 0).wait_recv()
            pack_half(m, sign, way, send2.at[m, way, 2], recv2.at[m, way, 0])
            stage2(m, way, 2).start()

    def stage3(m, d):
        number = 36 + m * 3 + d - 1
        return remote(send3.at[m, d - 1], recv3.at[m, d - 1], number, axes(m)[2], d)

    def reduce3(m):
        block = place[axes(m)[1]]
        for kind in (1, 2):
            for way in range(2):
                stage2(m, way, kind).wait_recv()
        for group in range(4):
            half, inner = group // 2, group % 2
            a1, b1 = arrived(recv2.at[m, 0, 2 - half], HALF, inner)
            a2, b2 = arrived(recv2.at[m, 1, 1 + half], HALF, inner)
            rows = slice(group * GROUP, (group + 1) * GROUP)
            mine[m, 0, block, rows, :] += a1 + a2
            mine[m, 1, block, rows, :] += b1 + b2
        for d in (1, 2, 3):
            group = lax.rem(place[axes(m)[2]] + d, 4)
            a, b = mine[m, 0, block, rows_of(group), :], mine[m, 1, block, rows_of(group), :]
            store_code(send3.at[m, d - 1], GROUP, 0, *encode(a, b))
            stage3(m, d).start()

    def spread3(m, d, group):
        number = 54 + (m * 3 + d - 1) * 2
        axis = axes(m)[2]
        data = remote(shard.at[m, 0:GROUP], panel.at[m, rows_of(group)], number, axis, d)
        scale = remote(
            shard.at[m, GROUP : GROUP + 8], scales.at[m, d - 1], number + 1, axis, d
        )
        return data, scale

    def finish(m):
        first, second, third = axes(m)
        block, own = place[second], place[third]
        a, b = mine[m, 0, block, rows_of(own), :], mine[m, 1, block, rows_of(own), :]
        for d in (1, 2, 3):
            stage3(m, d).wait_recv()
            more_a, more_b = arrived(recv3.at[m, d - 1], GROUP, 0)
            a, b = a + more_a, b + more_b
        number, copy = kept_copy(m)
        copy.wait()
        flags = jnp.where(number < 2 * LOWER_PAIRS, flags_at(kept[m], number * 128) * 2, 1)
        store_code(shard.at[m], GROUP, 0, *encode(a, b * flags.astype(F32)))
        for d in (1, 2, 3):
            for copy in spread3(m, d, own):
                copy.start()
        panel[m, rows_of(own), :] = shard[m, 0:GROUP, :]

    def at(m, first, second):
        return out.at[m * 16 + first * 4 + second]

    def turned(axis, distance):
        return lax.rem(place[axis] + (distance + 4), 4)

    def spread2(m, way, src, first, second):
        return remote(src, at(m, first, second), 90 + m * 4 + way, axes(m)[1], 1 - 2 * way)

    def pass2(m, way, first, second):
        rows = slice(0, HALF) if way == 0 else slice(HALF, FULL)
        ref = at(m, first, second).at[rows]
        return remote(ref, ref, 90 + m * 4 + 2 + way, axes(m)[1], 1 - 2 * way)

    def spread1(m, way, order, src, first, second):
        number = 114 + (m * 2 + way) * 6 + order
        return remote(src, at(m, first, second), number, axes(m)[0], 1 - 2 * way)

    offsets = (0, -1, 1, 2)

    def own_copy(m):
        first, second, third = axes(m)
        return pltpu.make_async_copy(
            panel.at[m], at(m, place[first], place[second]), copy_sem.at[m]
        )

    def gather_own(m):
        first, second, third = axes(m)
        row = lax.broadcasted_iota(jnp.int32, (8, 128), 0)
        total = jnp.zeros((8, 128), jnp.int32)
        for d in (0, 1, 2, 3):
            group = lax.rem(place[third] + (4 - d), 4)
            if d == 0:
                tile = shard[m, GROUP : GROUP + 8, :]
            else:
                for copy in spread3(m, d, group):
                    copy.wait_recv()
                tile = scales[m, d - 1]
            total = jnp.where(row == 2 * group, tile[0:1], total)
            total = jnp.where(row == 2 * group + 1, tile[1:2], total)
        panel[m, STRIP:FULL, :] = total
        for way in range(2):
            spread2(m, way, panel.at[m], place[first], place[second]).start()
        own_copy(m).start()
        for way in range(2):
            spread1(m, way, 0, panel.at[m], place[first], place[second]).start()

    def gather_near(m):
        first = place[axes(m)[0]]
        for way in range(2):
            second = turned(axes(m)[1], 2 * way - 1)
            spread2(m, way, panel.at[m], first, second).wait_recv()
            pass2(m, way, first, second).start()
            for way1 in range(2):
                spread1(m, way1, 1 + way, at(m, first, second), first, second).start()

    def gather_far(m):
        first, second = place[axes(m)[0]], turned(axes(m)[1], 2)
        for way in range(2):
            pass2(m, way, first, second).wait_recv()
        for way1 in range(2):
            spread1(m, way1, 3, at(m, first, second), first, second).start()

    passed = ((0, 0), (1, 2), (0, 1), (1, 3))

    def pass1(m, way, order, first):
        ref = at(m, first, turned(axes(m)[1], offsets[order]))
        number = 114 + (m * 2 + way) * 6 + 4 + order % 2
        return remote(ref, ref, number, axes(m)[0], 1 - 2 * way)

    def spread1_arrived(m, way, order):
        first = turned(axes(m)[0], 2 * way - 1)
        second = turned(axes(m)[1], offsets[order])
        spread1(m, way, order, panel.at[m], first, second).wait_recv()

    def pass_on(m, which):
        for way, order in passed[which]:
            spread1_arrived(m, way, order)
            pass1(m, way, order, turned(axes(m)[0], 2 * way - 1)).start()

    for_operands(0, lambda copy: copy.start())

    def begin(m):
        if m < 3:
            for_operands(m, lambda copy: copy.wait())
        if m < 2:
            for_operands(m + 1, lambda copy: copy.start())
        compute_part(m)
        if m == 0:
            pl.semaphore_wait(barrier, 9)
        reduce2_first(m)

    def pass_early(m):
        pass_on(m, slice(0, 2))

    def pass_late(m):
        pass_on(m, slice(2, 4))

    def sent_sums(m):
        for way in range(2):
            for kind in range(3):
                stage2(m, way, kind).wait_send()
        for d in (1, 2, 3):
            stage3(m, d).wait_send()
            for copy in spread3(m, d, place[axes(m)[2]]):
                copy.wait_send()

    def sent_gather(m):
        first, second = place[axes(m)[0]], place[axes(m)[1]]
        own_copy(m).wait()
        for way in range(2):
            spread2(m, way, panel.at[m], first, second).wait_send()
            pass2(m, way, first, turned(axes(m)[1], 2 * way - 1)).wait_send()
            for order in range(4):
                second_now = turned(axes(m)[1], offsets[order])
                src = panel.at[m] if order == 0 else at(m, first, second_now)
                spread1(m, way, order, src, first, second_now).wait_send()
        for way, order in passed:
            pass1(m, way, order, turned(axes(m)[0], 2 * way - 1)).wait_send()

    for step, m in (
        (begin, 0),
        (begin, 1),
        (begin, 2),
        (reduce2_second, 0),
        (reduce2_second, 1),
        (begin, 3),
        (reduce2_second, 2),
        (reduce3, 0),
        (reduce3, 1),
        (begin, 4),
        (reduce3, 2),
        (finish, 0),
        (finish, 1),
        (begin, 5),
        (finish, 2),
        (gather_own, 0),
        (gather_own, 1),
        (reduce2_second, 3),
        (gather_own, 2),
        (reduce2_second, 4),
        (reduce2_second, 5),
        (gather_near, 0),
        (reduce3, 3),
        (gather_near, 1),
        (reduce3, 4),
        (gather_near, 2),
        (reduce3, 5),
        (finish, 3),
        (gather_far, 0),
        (finish, 4),
        (gather_far, 1),
        (finish, 5),
        (gather_far, 2),
        (gather_own, 3),
        (pass_early, 0),
        (gather_own, 4),
        (pass_early, 1),
        (gather_own, 5),
        (pass_early, 2),
        (gather_near, 3),
        (gather_near, 4),
        (gather_near, 5),
        (pass_late, 0),
        (pass_late, 1),
        (pass_late, 2),
        (gather_far, 3),
        (gather_far, 4),
        (gather_far, 5),
        (pass_early, 3),
        (pass_early, 4),
        (pass_early, 5),
        (pass_late, 3),
        (pass_late, 4),
        (pass_late, 5),
        (sent_sums, 0),
        (sent_sums, 1),
        (sent_sums, 2),
        (sent_sums, 3),
        (sent_sums, 4),
        (sent_sums, 5),
        (sent_gather, 0),
        (sent_gather, 1),
        (sent_gather, 2),
    ):
        step(m)
    for m in parts:
        for way in range(2):
            for order in range(4):
                if (way, order) not in passed:
                    spread1_arrived(m, way, order)
        for way, order in passed:
            pass1(m, way, order, turned(axes(m)[0], 2)).wait_recv()

    for m in parts[3:]:
        sent_gather(m)


def summed_panels(xh, lr, da, du, left, right, words):
    i32 = jnp.int32
    messages = 114 + 72
    rows_all = da.shape[1]
    dma = pltpu.SemaphoreType.DMA
    return pl.pallas_call(
        sum_kernel,
        out_shape=pltpu.VMEM((4 * PAIRS, FULL, 128), i32),
        in_specs=[pl.BlockSpec(memory_space=pl.ANY)] * 7,
        out_specs=pl.BlockSpec(memory_space=pl.ANY),
        scratch_shapes=[
            pltpu.VMEM((6, GROUP, 128), i32),
            pltpu.VMEM((3, 2 * PANEL, 4 * 640), BF),
            pltpu.VMEM((3, 4, 2, rows_all, 640), BF),
            pltpu.VMEM((6, 2, 4, STRIP, 128), F32),
            pltpu.VMEM((6, 2, 3, HALF + 8, 128), i32),
            pltpu.VMEM((6, 2, 3, HALF + 8, 128), i32),
            pltpu.VMEM((6, 3, GROUP + 8, 128), i32),
            pltpu.VMEM((6, 3, GROUP + 8, 128), i32),
            pltpu.VMEM((6, GROUP + 8, 128), i32),
            pltpu.VMEM((6, 3, 8, 128), i32),
            pltpu.VMEM((6, FULL, 128), i32),
            dma((messages,)),
            dma((messages,)),
            dma((6,)),
            dma((6,)),
            dma((36,)),
            dma((24,)),
        ],
        compiler_params=pltpu.CompilerParams(
            vmem_limit_bytes=SUM_VMEM, collective_id=1, has_side_effects=True
        ),
    )(xh, lr, da, du, left, right, words)


def unpack_kernel(
    panels,
    words_u,
    hidden,
    grads_in,
    low_in,
    low_rec,
    low_bias,
    up_in,
    up_rec,
    up_bias,
    hidden_o,
    grads_in_o,
    tail,
):
    step = pl.program_id(0)
    units, outs = low_in.shape[0], up_rec.shape[0]
    lower_steps, all_steps = 2 * LOWER_PAIRS // WIDTH, 2 * PAIRS // WIDTH

    @pl.when(step == 0)
    def _():
        hidden_o[...] = hidden[...]
        grads_in_o[...] = grads_in[...]

    def values(n, ab):
        parts = []
        n = jnp.minimum(step, all_steps - 1) * WIDTH + n
        for strip in range(2):
            at = strip * 2 * PAIRS + n
            for group in range(4):
                words = panels[at, group * GROUP : (group + 1) * GROUP, :]
                row = STRIP + 2 * group + ab
                scale = factor(panels[at, row : row + 1, :])
                half = (words >> 16) if ab == 0 else ((words << 16) >> 16)
                parts.append(half.astype(F32) * scale)
        return jnp.concatenate(parts, axis=0)

    for n in range(WIDTH):
        cols = slice(n * 128, (n + 1) * 128)

        @pl.when(step < lower_steps)
        def _():
            a = values(n, 0)
            low_in[:, cols] = a[:units]
            low_bias[:, cols] = a[units : units + 1]
            b = values(n, 1)[:units]
            low_rec[:, cols] = b

        @pl.when((step >= lower_steps) & (step < all_steps))
        def _():
            a = values(n, 0)
            up_in[:, cols] = a[:units]
            up_bias[:, cols] = a[units : units + 1]
            b = values(n, 1)
            flags = flags_at(words_u[...], (step - lower_steps) * WIDTH * 128 + n * 128)
            up_rec[:, cols] = b[:outs] * (flags * 2).astype(F32)[:outs]
            if n % 2 == 0:
                index = (step - lower_steps) * (WIDTH // 2) + n // 2
                rows = pl.ds(pl.multiple_of(index * TAIL_ROWS, 8), TAIL_ROWS)
                tail[rows, :] = b[PANEL - TAIL_ROWS :]

    @pl.when(step == all_steps)
    def _():
        up_in[:, :128] = tail[:units]
        up_bias[:, :128] = tail[units : units + 1]
        flags = flags_at(words_u[...], 2 * (PAIRS - LOWER_PAIRS) * 128)
        up_rec[:, :128] = tail[PANEL : PANEL + outs] * (flags * 2).astype(F32)[:outs]


def unpack(panels, words_u, hidden, grads_in, units, full, outs, full_u):
    sds = jax.ShapeDtypeStruct
    lower_steps, all_steps = 2 * LOWER_PAIRS // WIDTH, 2 * PAIRS // WIDTH
    wide = 128 * WIDTH
    lower = lambda i: (0, jnp.minimum(i, lower_steps - 1))
    upper = lambda i: (0, jnp.maximum(i - lower_steps, 0))
    return pl.pallas_call(
        unpack_kernel,
        grid=(all_steps + 1,),
        out_shape=(
            sds((units, full), F32),
            sds((units, full), F32),
            sds((1, full), F32),
            sds((units, full_u), F32),
            sds((outs, full_u), F32),
            sds((1, full_u), F32),
            sds(hidden.shape, F32),
            sds(grads_in.shape, F32),
        ),
        in_specs=[
            pl.BlockSpec(memory_space=pltpu.VMEM),
            pl.BlockSpec(memory_space=pltpu.VMEM),
            pl.BlockSpec(memory_space=pltpu.VMEM),
            pl.BlockSpec(memory_space=pltpu.VMEM),
        ],
        out_specs=(
            pl.BlockSpec((units, wide), lower),
            pl.BlockSpec((units, wide), lower),
            pl.BlockSpec((1, wide), lower),
            pl.BlockSpec((units, wide), upper),
            pl.BlockSpec((outs, wide), upper),
            pl.BlockSpec((1, wide), upper),
            pl.BlockSpec(hidden.shape, lambda i: (0, 0, 0)),
            pl.BlockSpec(grads_in.shape, lambda i: (0, 0, 0)),
        ),
        scratch_shapes=[pltpu.VMEM((6 * TAIL_ROWS, 128), F32)],
        compiler_params=pltpu.CompilerParams(vmem_limit_bytes=UNPACK_VMEM),
    )(panels, words_u, hidden, grads_in)


def body(
    inputs,
    lower_lock,
    upper_lock,
    resets,
    lower_input,
    lower_recur,
    lower_bias,
    lower_drop,
    upper_input,
    upper_recur,
    upper_bias,
    upper_drop,
    grad_out,
):
    me = lax.axis_index("pipe")
    streams, steps, width = inputs.shape
    hidden_out, grad_inputs, da, du, xh, lr, left, right, words_l, words_u = recurrence(
        inputs,
        lower_lock,
        upper_lock,
        resets,
        grad_out,
        lower_drop.T,
        upper_drop.T,
        jnp.concatenate([lower_bias, upper_bias])[None],
        lower_recur,
        lower_input,
        upper_input,
        upper_recur,
    )
    panels = summed_panels(xh, lr, da, du, left, right, words_l)
    low_in, low_rec, low_bias, up_in, up_rec, up_bias, hidden_out, grad_inputs = unpack(
        panels, words_u, hidden_out, grad_inputs, *lower_recur.shape, *upper_recur.shape
    )

    def own(row):
        half = row.shape[1] // 2
        return lax.dynamic_slice_in_dim(row[0], me * half, half, 0)

    return (
        hidden_out,
        grad_inputs,
        low_in,
        low_rec,
        own(low_bias),
        up_in,
        up_rec,
        own(up_bias),
    )


def solution(mesh):
    return jax.shard_map(
        body,
        mesh=mesh,
        in_specs=(
            P("dp", None, None),
            P("dp", None),
            P("dp", None),
            P("dp", None),
            P("pipe", None),
            P("pipe", None),
            P("pipe"),
            P(),
            P("pipe", None),
            P("pipe", None),
            P("pipe"),
            P(),
            P("dp", None, None),
        ),
        out_specs=(
            P("dp", None, "pipe"),
            P("dp", None, "pipe"),
            P("pipe", None),
            P("pipe", None),
            P("pipe"),
            P("pipe", None),
            P("pipe", None),
            P("pipe"),
        ),
        check_vma=False,
    )
```

```python
import functools

import jax
import jax.numpy as jnp
from jax import lax
from jax.experimental import pallas as pl
from jax.experimental.pallas import tpu as pltpu
from jax.sharding import PartitionSpec as P

BF = jnp.bfloat16
F32 = jnp.float32
MESH = pl.DeviceIdType.MESH
ROWS = 16
VMEM_LIMIT = 62 * 2**20
TAIL_ROWS = 368
SOME = 4
SUM_VMEM = 47 * 2**20
UNPACK_VMEM = 24 * 2**20


def ceil_to(value, multiple):
    return -(-value // multiple) * multiple


def split(value):
    high = value.astype(BF)
    low = (value - high.astype(F32)).astype(BF)
    return high, low


def fold(stacked):
    half = stacked.shape[0] // 2
    return stacked[:half] + stacked[half:]


def dot_nn(a, b):
    return jnp.dot(a, b, preferred_element_type=F32)


def dot_nt(a, b):
    return lax.dot_general(a, b, (((1,), (1,)), ((), ())), preferred_element_type=F32)


def torus():
    dp = lax.axis_index("dp")
    place = [lax.rem(dp, 4), lax.rem(lax.div(dp, 4), 4), lax.div(dp, 16)]
    stride = [1, 4, 16]

    def across(axis, distance):
        moved = lax.rem(place[axis] + (distance + 4), 4)
        return {"dp": dp + (moved - place[axis]) * stride[axis]}

    return place, across


def flags_at(words, column):
    column = lax.broadcasted_iota(jnp.int32, (1, 128), 1) + column
    index = (column * 52429) >> 20
    bit = column - index * 20
    index = jnp.broadcast_to(index & 127, words.shape)
    found = jnp.take_along_axis(words, index, axis=1, mode="promise_in_bounds")
    return (found >> bit) & 1


def recurrence_kernel(
    units,
    inputs,
    lower_lock,
    upper_lock,
    resets,
    grad_out,
    lower_drop,
    upper_drop,
    both_bias,
    wrec_in,
    win_in,
    uin_in,
    urec_in,
    hid_o,
    dx_o,
    da_o,
    du_o,
    xh_o,
    lr_o,
    left_o,
    right_o,
    rows_l_o,
    rows_u_o,
    wrec_raw,
    win_raw,
    uin_raw,
    urec_raw,
    words_l,
    words_u,
    slab,
    keep_ref,
    lock_low,
    lock_ref,
    gout_ref,
    blo,
    bup,
    wrec_t,
    uin_t,
    urec_t,
    wrec,
    uin,
    urec,
    da_all,
    du_all,
    xh,
    lr,
    x2,
    hk2,
    ux2,
    hku2,
    dal,
    dau,
    proj,
    send_l,
    recv_l,
    send_u,
    recv_u,
    act_l,
    act_u,
    save_l,
    save_u,
    cell_l,
    cell_u,
    da_l,
    da_u,
    dstate_l,
    dstate_u,
    dx_up,
    acc,
    acc_x,
    acc_h,
    dx,
    fs_l,
    fr_l,
    fs_u,
    fr_u,
    bs_l,
    br_l,
    bs_u,
    br_u,
    far_s,
    far_r,
    in_sem,
    out_sem,
):
    streams, steps = resets.shape
    me = lax.axis_index("pipe")
    other = 1 - me
    peer = {"pipe": other}
    wide_k = wrec.shape[1]
    wide = wrec.shape[2]
    up_wide = uin.shape[2]
    up_k = urec.shape[1]
    lane = act_l.shape[1] - wide + units

    barrier = pltpu.get_barrier_semaphore()
    pl.semaphore_signal(barrier, inc=1, device_id=peer, device_id_type=MESH)
    place, across = torus()
    for axis in range(3):
        for d in (1, 2, 3):
            pl.semaphore_signal(barrier, inc=1, device_id=across(axis, d), device_id_type=MESH)
    loads = [
        pltpu.make_async_copy(wrec_in, wrec_raw, in_sem.at[1]),
        pltpu.make_async_copy(uin_in, uin_raw, in_sem.at[2]),
        pltpu.make_async_copy(urec_in, urec_raw, in_sem.at[3]),
        pltpu.make_async_copy(win_in, win_raw, in_sem.at[0]),
    ]
    for load in loads:
        load.start()
    pl.semaphore_wait(barrier, 10)

    def remote(src, dst, send_sem, recv_sem):
        return pltpu.make_async_remote_copy(
            src_ref=src,
            dst_ref=dst,
            send_sem=send_sem,
            recv_sem=recv_sem,
            device_id=peer,
            device_id_type=MESH,
        )

    full = wrec_raw.shape[1]
    held = wrec_raw.shape[0]
    held_u = urec_raw.shape[0]
    full_u = urec_raw.shape[1]
    unit_u = full_u // 8
    gate_u = gout_ref.shape[2]
    rows_all = steps * ROWS

    def to_rows(value, lanes, filler=0.0):
        more = lanes - value.shape[1]
        if more:
            value = jnp.concatenate([value, jnp.full((streams, more), filler, F32)], axis=1)
        return jnp.concatenate([value, jnp.zeros((ROWS - streams, lanes), F32)], axis=0)

    keep_ref[...] = jnp.zeros_like(keep_ref)
    for t in range(steps):
        now = 1.0 - resets[:, t : t + 1].astype(F32)
        keep_ref[t] = to_rows(jnp.broadcast_to(now, (streams, 128)), 128)
    blo[...] = jnp.zeros_like(blo)
    bup[...] = jnp.zeros_like(bup)
    def place_words(target, packed):
        rows, lanes = packed.shape
        more = target.shape[1] - lanes
        packed = jnp.concatenate([packed, jnp.zeros((rows, more), jnp.int32)], axis=1)
        target[0:rows, :] = packed

    words_l[...] = jnp.zeros_like(words_l)
    words_u[...] = jnp.zeros_like(words_u)
    for half in range(2):

        @pl.when(me == half)
        def _(half=half):
            mine = slice(half * units, (half + 1) * units)
            lock_low[...] = to_rows(lower_lock[:, mine].astype(F32) * 1.25, lane)
            lock_ref[...] = to_rows(upper_lock[:, mine].astype(F32) * 1.25, lane)
            one = jnp.full((streams, 1), 1.0, F32)
            for t in range(steps):
                now = inputs[:, t, mine] * lock_low[0:streams, 0:units]
                now = to_rows(jnp.concatenate([now, one], axis=1), lane)
                high, low = split(now)
                x2[t * ROWS : (t + 1) * ROWS] = high
                x2[rows_all + t * ROWS : rows_all + (t + 1) * ROWS] = low
                out = grad_out[:, t, half * unit_u : (half + 1) * unit_u]
                gout_ref[t] = to_rows(out, gate_u)
            place_words(words_l, lower_drop[:, mine])
            place_words(words_u, upper_drop[:, half * held_u : (half + 1) * held_u])
            bias = both_bias[...].astype(F32)
            bias_u = bias[:, 4 * units :]
            for q in range(2):
                for i in range(2):
                    g = 2 * half + i
                    start = (2 * i + q) * units
                    blo[q, :, g * units : (g + 1) * units] = bias[:, start : start + units]
                    start = (2 * i + q) * unit_u
                    bup[q, :, g * unit_u : (g + 1) * unit_u] = bias_u[
                        :, start : start + unit_u
                    ]

    loads[0].wait()
    sub = lax.broadcasted_iota(jnp.int32, (8, 128), 0)

    def flags_of(held, i):
        left, right = 8 * i // 20, (8 * i + 7) // 20
        now = jnp.broadcast_to(held[left : left + 1], (8, 128))
        if right != left:
            later = jnp.broadcast_to(held[right : right + 1], (8, 128))
            now = jnp.where(sub < 20 * right - 8 * i, now, later)
        bit = sub + 8 * i % 20
        bit = jnp.where(bit >= 20, bit - 20, bit)
        return (now >> bit) & 1

    def masked_columns(weight, words, first, lanes):
        rows, columns = weight.shape
        words = words[pl.ds(first, ceil_to(ceil_to(columns, 20) // 20, 8)), lanes]
        turned = jnp.transpose(weight.astype(F32))
        if rows < 128:
            turned = jnp.concatenate([turned, jnp.zeros((columns, 128 - rows), F32)], axis=1)
        out = []
        for i in range(columns // 8):
            now = turned[8 * i : 8 * i + 8]
            out.append(jnp.where(flags_of(words, i) != 0, now + now, 0.0))
        return jnp.concatenate(out, axis=0)

    block = 640
    row16 = lax.broadcasted_iota(jnp.int32, (ROWS, 128), 0)

    def lower_slab(rows, start):
        lanes = pl.ds(start, 128)
        many = min(128, wide_k - start) if isinstance(start, int) else 128

        def fill(index, carry):
            cols = pl.ds(pl.multiple_of(index * block, block), block)
            first = pl.multiple_of(index * (block // 20), block // 20)
            part = masked_columns(wrec_raw[rows, cols], words_l, first, lanes)
            slab[cols, :] = part
            return carry

        lax.fori_loop(0, full // block, fill, 0)
        last = full // block * block
        slab[last:full, :] = masked_columns(
            wrec_raw[rows, last:full], words_l, last // 20, lanes
        )
        target = pl.ds(start, many)
        tiles = units // ROWS
        for q in range(2):
            for g in range(4):
                shift = units * (g + q)
                base = (tiles + 1) * ROWS * g

                def move(index, carry, q=q, shift=shift, base=base):
                    for i in range(7):
                        row = pl.multiple_of(base + (index * 7 + i) * ROWS, ROWS)
                        now = slab[pl.ds(row + shift, ROWS), :]
                        wrec_t[q, pl.ds(row, ROWS), target] = now.astype(BF)[:, :many]
                    return carry

                lax.fori_loop(0, tiles // 7, move, 0)
                row = base + tiles * ROWS
                now = slab[row + shift : row + shift + ROWS, :]
                if g < 3:
                    later = slab[row + shift + units : row + shift + units + ROWS, :]
                else:
                    later = jnp.zeros((ROWS, 128), F32)
                now = jnp.where(row16 < units * (g + 1) - row, now, later)
                wrec_t[q, row : row + ROWS, target] = now.astype(BF)[:, :many]

    def lower_slab_step(index, carry):
        start = pl.multiple_of(index * 128, 128)
        lower_slab(pl.ds(start, 128), start)
        return carry

    lax.fori_loop(0, held // 128, lower_slab_step, 0)
    lower_slab(slice(held // 128 * 128, held), held // 128 * 128)

    def place_upper(target, turned, start, many):
        for q in range(2):
            gates = [turned[(2 * g + q) * unit_u : (2 * g + q + 1) * unit_u] for g in range(4)]
            gates.append(jnp.zeros((up_wide - 4 * unit_u, 128), F32))
            part = jnp.concatenate(gates, axis=0).astype(BF)
            target[q, :, pl.ds(start, many)] = part[:, :many]

    for load in loads[1:]:
        load.wait()

    def upper_slab(index, carry):
        start = pl.multiple_of(index * 128, 128)
        turned = jnp.transpose(uin_raw[pl.ds(start, 128), :].astype(F32))
        place_upper(uin_t, turned, start, 128)
        return carry

    lax.fori_loop(0, held // 128, upper_slab, 0)
    start = held // 128 * 128
    turned = jnp.transpose(uin_raw[start:held, :].astype(F32))
    turned = jnp.concatenate([turned, jnp.zeros((full_u, 128 - held % 128), F32)], axis=1)
    place_upper(uin_t, turned, start, wide_k - start)
    for start in range(0, held_u, 128):
        stop = min(start + 128, held_u)
        lanes = pl.ds(start, 128)
        turned = [
            masked_columns(
                urec_raw[start:stop, i : min(i + block, full_u)], words_u, i // 20, lanes
            )
            for i in range(0, full_u, block)
        ]
        many = min(128, up_k - start)
        place_upper(urec_t, jnp.concatenate(turned, axis=0), start, many)
    for q in range(2):
        wrec[q] = jnp.transpose(wrec_t[q])
        uin[q] = jnp.transpose(uin_t[q])
        urec[q] = jnp.transpose(urec_t[q])
    proj[:, :, :, wide - 128 :] = jnp.zeros((2, steps, ROWS, 128), F32)
    for q in range(2):
        for g in range(4):
            start, stop = (2 * g + q) * units, (2 * g + q + 1) * units
            first, last = start // 128 * 128, min(ceil_to(stop, 128), full)
            y = fold(dot_nn(x2[:, :held], win_raw[:, first:last]))
            y = y[:, start - first : stop - first] + blo[q, :, g * units : (g + 1) * units]
            proj[q, :, :, g * units : (g + 1) * units] = y.reshape(steps, ROWS, units)

    rows_l_o[...] = jnp.transpose(words_l[...])
    rows_u_o[...] = jnp.transpose(words_u[...])

    some = SOME * ROWS
    pieces = steps // SOME

    def place_left(target, row, count, high, low, piece):
        start = 2 * some * piece
        target[row : row + count, start : start + some] = jnp.transpose(high)[:count]
        target[row : row + count, start + some : start + 2 * some] = jnp.transpose(low)[:count]

    def place_steps(target, row, count, stack, piece):
        width = stack.shape[2]
        now = slice(piece * SOME, (piece + 1) * SOME)
        high, low = [
            stack[now, i * ROWS : (i + 1) * ROWS, :].reshape(some, width) for i in (0, 1)
        ]
        place_left(target, row, count, high, low, piece)

    def send_piece(piece):
        place_steps(xh, wide_k, wide_k, hk2, piece)
        place_steps(lr, 0, wide_k, ux2, piece)
        place_steps(lr, wide_k, up_k, hku2, piece)
        for_left(1 + piece, lambda copy: copy.start(), at_peer)

    for piece in range(pieces):
        at = piece * some
        low = x2[rows_all + at : rows_all + at + some]
        place_left(xh, 0, wide_k, x2[at : at + some], low, piece)

    def far_copy(src, dst, number, axis, d):
        return pltpu.make_async_remote_copy(
            src_ref=src,
            dst_ref=dst,
            send_sem=far_s.at[number],
            recv_sem=far_r.at[number],
            device_id=across(axis, d),
            device_id_type=MESH,
        )

    lr_rows = lr.shape[0]

    def left_copy(k, d, kind, upper):
        lanes = slice(2 * some * (kind - 1), 2 * some * kind) if kind else slice(0, 2 * rows_all)
        if upper:
            src, rows = lr.at[:, lanes], slice(0, lr_rows)
        else:
            rows = slice(0, wide_k) if kind == 0 else slice(wide_k, 2 * wide_k)
            src = xh.at[rows, lanes]
        return far_copy(src, left_o.at[k, d - 1, rows, lanes], (k * 3 + d - 1) * 4 + kind, k, d)

    def for_left(kind, act, target):
        for k in range(3):
            for d in (1, 2, 3):
                lower_copy = left_copy(k, d, kind, False)
                if k < 2:
                    act(lower_copy)
                    continue
                is_lower = target(k, d) == 0

                @pl.when(is_lower)
                def _(copy=lower_copy):
                    act(copy)

                if kind > 0:
                    upper_copy = left_copy(k, d, kind, True)

                    @pl.when(jnp.logical_not(is_lower))
                    def _(copy=upper_copy):
                        act(copy)

    def at_peer(k, d):
        return lax.rem(place[k] + d, 4)

    def at_home(k, d):
        return place[k]

    for_left(0, lambda copy: copy.start(), at_peer)

    def right_copies(k, d, chunk, row, count, upper, target):
        rows = pl.ds(row, count)
        dst = right_o.at[k, d - 1, :, rows, 0:512]
        number = 36 + (k * 3 + d - 1) * 5 + chunk
        if not upper:
            col = (4 * k + (target if k < 2 else 0)) * 512
            src = da_all.at[:, rows, pl.ds(pl.multiple_of(col, 512), 512)]
            return [far_copy(src, dst, number, k, d)]
        col = pl.multiple_of(jnp.maximum(target - 1, 0) * 512, 512)
        tail_dst = right_o.at[k, d - 1, :, rows, 512:640]
        return [
            far_copy(du_all.at[:, rows, pl.ds(col, 512)], dst, number, k, d),
            far_copy(du_all.at[:, rows, 1536:1664], tail_dst, 81 + (d - 1) * 5 + chunk, k, d),
        ]

    def for_right(chunk, row, count, act, target):
        for k in range(3):
            for d in (1, 2, 3):
                goes = target(k, d)
                if k < 2:
                    for copy in right_copies(k, d, chunk, row, count, False, goes):
                        act(copy)
                    continue

                @pl.when(goes == 0)
                def _(k=k, d=d, goes=goes):
                    for copy in right_copies(k, d, chunk, row, count, False, goes):
                        act(copy)

                @pl.when(goes != 0)
                def _(k=k, d=d, goes=goes):
                    for copy in right_copies(k, d, chunk, row, count, True, goes):
                        act(copy)

    chunks = ((8, 4), (4, 4), (2, 2), (1, 1), (0, 1))

    act_l[...] = jnp.zeros_like(act_l)
    hk2[...] = jnp.zeros_like(hk2)
    ux2[...] = jnp.zeros_like(ux2)
    hku2[...] = jnp.zeros_like(hku2)
    cell_l[...] = jnp.zeros_like(cell_l)
    cell_u[...] = jnp.zeros_like(cell_u)

    def fcopy_l(t):
        return remote(send_l, recv_l.at[lax.rem(t, 2)], fs_l.at[t], fr_l.at[t])

    def fcopy_u(t):
        return remote(send_u, recv_u.at[lax.rem(t, 2)], fs_u.at[t], fr_u.at[t])

    def lower_send(t, first):
        if first:
            send_l[...] = proj[other, t]
        else:
            send_l[...] = fold(dot_nn(hk2[t, :, :wide_k], wrec[other])) + proj[other, t]
        fcopy_l(t).start()

    def lower_own(t, first):
        if first:
            act_l[:, :wide] = proj[me, t]
        else:
            act_l[:, :wide] = fold(dot_nn(hk2[t, :, :wide_k], wrec[me])) + proj[me, t]

    def upper_part(t, q):
        y = dot_nn(ux2[t, :, :wide_k], uin[q]) + dot_nn(hku2[t, :, :up_k], urec[q])
        return fold(y) + bup[q]

    def upper_send(t):
        send_u[...] = upper_part(t, other)
        fcopy_u(t).start()

    def upper_own(t):
        act_u[...] = upper_part(t, me)

    def keep_at(t, lanes):
        return jnp.concatenate([keep_ref[t]] * (ceil_to(lanes, 128) // 128), axis=1)[
            :, :lanes
        ]

    def cell_update(a_in, a_forget, a_cand, a_out, cell, keep_now, save, t):
        gate_in = jax.nn.sigmoid(a_in)
        forget = jax.nn.sigmoid(a_forget)
        cand = jnp.tanh(a_cand)
        gate_out = jax.nn.sigmoid(a_out)
        cell_keep = cell[...] * keep_now
        cell_new = forget * cell_keep + gate_in * cand
        squashed = jnp.tanh(cell_new)
        cell[...] = cell_new
        save[t, 0] = gate_in
        save[t, 1] = forget
        save[t, 2] = cand
        save[t, 3] = gate_out
        save[t, 4] = cell_keep
        save[t, 5] = squashed
        return gate_out * squashed

    def lower_cell(t):
        act_l[:, :wide] += recv_l[lax.rem(t, 2)]
        hidden = cell_update(
            act_l[:, 0:lane],
            act_l[:, units : units + lane],
            act_l[:, 2 * units : 2 * units + lane],
            act_l[:, 3 * units : 3 * units + lane],
            cell_l,
            keep_at(t, lane),
            save_l,
            t,
        )
        high, low = split(hidden * keep_at(t + 1, lane))
        hk2[t + 1, 0:ROWS] = high
        hk2[t + 1, ROWS:] = low
        ones_at = lax.broadcasted_iota(jnp.int32, (ROWS, lane), 1) == units
        high, low = split(jnp.where(ones_at, 1.0, hidden * lock_ref[...]))
        ux2[t, 0:ROWS] = high
        ux2[t, ROWS:] = low

    def upper_cell(t):
        a = act_u[...] + recv_u[lax.rem(t, 2)]
        hidden = cell_update(
            a[:, 0:gate_u],
            a[:, unit_u : unit_u + gate_u],
            a[:, 2 * unit_u : 2 * unit_u + gate_u],
            a[:, 3 * unit_u : 3 * unit_u + gate_u],
            cell_u,
            keep_at(t, gate_u),
            save_u,
            t,
        )
        hid_o[:, pl.ds(t, 1), :] = hidden[:streams, :unit_u].reshape(streams, 1, unit_u)
        high, low = split(hidden * keep_at(t + 1, gate_u))
        hku2[t + 1, 0:ROWS] = high
        hku2[t + 1, ROWS:] = low

    lower_send(0, True)
    lower_own(0, True)
    fcopy_l(0).wait()
    lower_cell(0)

    def forward_round(r, carry, with_cell=True):
        lower_send(r, False)
        if with_cell:
            fcopy_u(r - 2).wait()
            upper_cell(r - 2)
        lower_own(r, False)
        upper_send(r - 1)
        upper_own(r - 1)
        fcopy_l(r).wait()
        lower_cell(r)
        if with_cell:

            for piece in range(pieces - 1):

                @pl.when(r == SOME * (piece + 1))
                def _(piece=piece):
                    send_piece(piece)

        return carry

    forward_round(1, 0, False)
    lax.fori_loop(2, steps, forward_round, 0)
    fcopy_u(steps - 2).wait()
    upper_cell(steps - 2)
    upper_send(steps - 1)
    upper_own(steps - 1)
    fcopy_u(steps - 1).wait()
    upper_cell(steps - 1)

    send_piece(pieces - 1)

    da_all[...] = jnp.zeros_like(da_all)
    du_all[...] = jnp.zeros_like(du_all)

    def own_order(t, carry):
        to = pl.ds(pl.multiple_of(t * ROWS, ROWS), ROWS)
        for part in range(2):
            rows = slice(part * ROWS, (part + 1) * ROWS)
            for q in range(2):
                for g in range(4):
                    start = (2 * g + q) * units
                    da_all[part, to, start : start + units] = dal[
                        q, t, rows, g * units : (g + 1) * units
                    ]
                    start = (2 * g + q) * unit_u
                    du_all[part, to, start : start + unit_u] = dau[
                        q, t, rows, g * unit_u : (g + 1) * unit_u
                    ]
        return carry

    def send_right(chunk):
        first, count = chunks[chunk]
        lax.fori_loop(first, first + count, own_order, 0)
        for_right(chunk, first * ROWS, count * ROWS, lambda copy: copy.start(), at_peer)

    dstate_l[...] = jnp.zeros_like(dstate_l)
    dstate_u[...] = jnp.zeros_like(dstate_u)
    da_l[...] = jnp.zeros_like(da_l)
    da_u[...] = jnp.zeros_like(da_u)

    def bcopy_l(t):
        return remote(dal.at[me, t], dal.at[me, t], bs_l.at[t], br_l.at[t])

    def bcopy_u(t):
        return remote(dau.at[me, t], dau.at[me, t], bs_u.at[t], br_u.at[t])

    def gate_grads(dy, dstate, save, keep_now, t):
        gate_in, forget, cand, gate_out = save[t, 0], save[t, 1], save[t, 2], save[t, 3]
        cell_keep, squashed = save[t, 4], save[t, 5]
        dh = dstate[0] + dy
        dc = dstate[1] + dh * gate_out * (1.0 - squashed * squashed)
        dstate[1] = dc * forget * keep_now
        return (
            dc * cand * gate_in * (1.0 - gate_in),
            dc * cell_keep * forget * (1.0 - forget),
            dc * gate_in * (1.0 - cand * cand),
            dh * squashed * gate_out * (1.0 - gate_out),
        )

    def lower_back_start(t):
        grads = gate_grads(dx_up[...] * lock_ref[...], dstate_l, save_l, keep_at(t, lane), t)
        for g in range(4):
            da_l[:, g * units : (g + 1) * units] = grads[g][:, :units]
        high, low = split(da_l[...])
        dal[me, t, 0:ROWS] = high
        dal[me, t, ROWS:] = low
        bcopy_l(t).start()

    def upper_back_start(t):
        grads = gate_grads(gout_ref[t], dstate_u, save_u, keep_at(t, gate_u), t)
        for g in range(4):
            da_u[:, g * unit_u : (g + 1) * unit_u] = grads[g][:, :unit_u]
        high, low = split(da_u[...])
        dau[me, t, 0:ROWS] = high
        dau[me, t, ROWS:] = low
        bcopy_u(t).start()

    def lower_back_part(t, q):
        return fold(dot_nn(dal[q, t], wrec_t[q]))

    def upper_back_part(t, q):
        grad = dau[q, t]
        return fold(dot_nn(grad, uin_t[q])), fold(dot_nn(grad, urec_t[q]))

    def lower_back_own(t):
        acc[:, :wide_k] = lower_back_part(t, me)

    def lower_back_other(t):
        total = acc[:, :wide_k] + lower_back_part(t, other)
        dstate_l[0, :, :wide_k] = keep_at(t, wide_k) * total

    def upper_back_own(t):
        into_x, into_h = upper_back_part(t, me)
        acc_x[:, :wide_k] = into_x
        acc_h[:, :up_k] = into_h

    def upper_back_other(t):
        into_x, into_h = upper_back_part(t, other)
        dx_up[:, :wide_k] = acc_x[:, :wide_k] + into_x
        dstate_u[0, :, :up_k] = keep_at(t, up_k) * (acc_h[:, :up_k] + into_h)

    dx_up[...] = jnp.zeros_like(dx_up)
    upper_back_start(steps - 1)
    upper_back_own(steps - 1)
    bcopy_u(steps - 1).wait()
    upper_back_other(steps - 1)
    upper_back_start(steps - 2)

    def backward_round(r, carry, last=False):
        t = steps - r
        lower_back_start(t)
        lower_back_own(t)
        upper_back_own(t - 1)
        bcopy_u(t - 1).wait()
        upper_back_other(t - 1)
        bcopy_l(t).wait()
        lower_back_other(t)
        if last:
            send_right(3)
            return carry
        upper_back_start(t - 2)
        for chunk in range(3):

            @pl.when(t == chunks[chunk][0])
            def _(chunk=chunk):
                send_right(chunk)

        return carry

    lax.fori_loop(1, steps - 1, backward_round, 0)
    backward_round(steps - 1, 0, True)
    lower_back_start(0)
    bcopy_l(0).wait()

    send_right(4)

    copies = [
        pltpu.make_async_copy(da_all, da_o, out_sem.at[0]),
        pltpu.make_async_copy(du_all, du_o, out_sem.at[1]),
        pltpu.make_async_copy(xh, xh_o, out_sem.at[2]),
        pltpu.make_async_copy(lr, lr_o, out_sem.at[3]),
    ]
    for copy in copies:
        copy.start()

    chunk = 512

    def input_grad(cols, width):
        grad = da_all[:, :, cols].reshape(2 * rows_all, width)
        return fold(dot_nt(grad, win_raw[:, cols]))

    tail = full // chunk * chunk
    dx[:, :held] = input_grad(slice(tail, full), full % chunk) if full % chunk else 0.0

    def input_grad_step(index, carry):
        dx[:, :held] += input_grad(pl.ds(pl.multiple_of(index * chunk, chunk), chunk), chunk)
        return carry

    lax.fori_loop(0, full // chunk, input_grad_step, 0)
    for t in range(steps):
        now = dx[t * ROWS : t * ROWS + streams, :held] * lock_low[0:streams, :held]
        dx_o[:, t, :] = now
    for copy in copies:
        copy.wait()
    for kind in range(1 + pieces):
        for_left(kind, lambda copy: copy.wait_send(), at_peer)
        for_left(kind, lambda copy: copy.wait_recv(), at_home)
    for chunk in range(5):
        row, count = chunks[chunk][0] * ROWS, chunks[chunk][1] * ROWS
        for_right(chunk, row, count, lambda copy: copy.wait_send(), at_peer)
        for_right(chunk, row, count, lambda copy: copy.wait_recv(), at_home)


def recurrence(
    inputs,
    lower_lock,
    upper_lock,
    resets,
    grad_out,
    lower_drop,
    upper_drop,
    bias,
    wrec,
    win,
    uin,
    urec,
):
    streams, steps = resets.shape
    units, full = wrec.shape
    outs, full_u = urec.shape
    wide_k = ceil_to(units, 16)
    wide = ceil_to(full // 2, 256)
    up_k = ceil_to(outs, 16)
    gate_u = ceil_to(outs, 128)
    up_wide = ceil_to(full_u // 2, 128)
    lane = ceil_to(units, 128)
    rows_all = steps * ROWS
    vm = pl.BlockSpec(memory_space=pltpu.VMEM)
    hbm = pl.BlockSpec(memory_space=pl.ANY)
    sds = jax.ShapeDtypeStruct
    i32 = jnp.int32
    shared = [
        ((2, rows_all, ceil_to(full, 512)), BF),
        ((2, rows_all, ceil_to(full_u, 128)), BF),
        ((2 * wide_k, 2 * rows_all), BF),
        ((wide_k + up_k, 2 * rows_all), BF),
    ]
    landed = [
        ((3, 3, 2 * wide_k, 2 * rows_all), BF),
        ((3, 3, 2, rows_all, 640), BF),
    ]
    raw = [(w.shape, BF) for w in (wrec, win, uin, urec)]
    dma = pltpu.SemaphoreType.DMA
    return pl.pallas_call(
        functools.partial(recurrence_kernel, units),
        out_shape=(sds((streams, steps, outs), F32), sds((streams, steps, units), F32))
        + tuple(sds(*s) for s in shared + landed)
        + (sds((lane, 256), i32), sds((ceil_to(outs, 128), 128), i32)),
        in_specs=[vm] * 8 + [hbm] * 4,
        out_specs=(vm, vm) + (hbm,) * len(shared + landed) + (vm, vm),
        scratch_shapes=[pltpu.VMEM(*s) for s in raw]
        + [
            pltpu.VMEM((256, lane), i32),
            pltpu.VMEM((128, ceil_to(outs, 128)), i32),
            pltpu.VMEM((ceil_to(full, 16), 128), F32),
            pltpu.VMEM((steps + 1, ROWS, 128), F32),
            pltpu.VMEM((ROWS, lane), F32),
            pltpu.VMEM((ROWS, lane), F32),
            pltpu.VMEM((steps, ROWS, gate_u), F32),
            pltpu.VMEM((2, 1, wide), F32),
            pltpu.VMEM((2, 1, up_wide), F32),
            pltpu.VMEM((2, wide, wide_k), BF),
            pltpu.VMEM((2, up_wide, wide_k), BF),
            pltpu.VMEM((2, up_wide, up_k), BF),
            pltpu.VMEM((2, wide_k, wide), BF),
            pltpu.VMEM((2, wide_k, up_wide), BF),
            pltpu.VMEM((2, up_k, up_wide), BF),
        ]
        + [pltpu.VMEM(*s) for s in shared]
        + [
            pltpu.VMEM((2 * rows_all, lane), BF),
            pltpu.VMEM((steps + 1, 2 * ROWS, lane), BF),
            pltpu.VMEM((steps, 2 * ROWS, lane), BF),
            pltpu.VMEM((steps + 1, 2 * ROWS, gate_u), BF),
            pltpu.VMEM((2, steps, 2 * ROWS, wide), BF),
            pltpu.VMEM((2, steps, 2 * ROWS, up_wide), BF),
            pltpu.VMEM((2, steps, ROWS, wide), F32),
            pltpu.VMEM((ROWS, wide), F32),
            pltpu.VMEM((2, ROWS, wide), F32),
            pltpu.VMEM((ROWS, up_wide), F32),
            pltpu.VMEM((2, ROWS, up_wide), F32),
            pltpu.VMEM((ROWS, wide + lane - units), F32),
            pltpu.VMEM((ROWS, up_wide), F32),
            pltpu.VMEM((steps, 6, ROWS, lane), F32),
            pltpu.VMEM((steps, 6, ROWS, gate_u), F32),
            pltpu.VMEM((ROWS, lane), F32),
            pltpu.VMEM((ROWS, gate_u), F32),
            pltpu.VMEM((ROWS, wide), F32),
            pltpu.VMEM((ROWS, up_wide), F32),
            pltpu.VMEM((2, ROWS, lane), F32),
            pltpu.VMEM((2, ROWS, gate_u), F32),
            pltpu.VMEM((ROWS, lane), F32),
            pltpu.VMEM((ROWS, lane), F32),
            pltpu.VMEM((ROWS, lane), F32),
            pltpu.VMEM((ROWS, gate_u), F32),
            pltpu.VMEM((rows_all, lane), F32),
        ]
        + [dma((steps,))] * 8
        + [dma((96,)), dma((96,)), dma((4,)), dma((4,))],
        compiler_params=pltpu.CompilerParams(
            vmem_limit_bytes=VMEM_LIMIT, collective_id=0, has_side_effects=True
        ),
    )(
        inputs,
        lower_lock,
        upper_lock,
        resets,
        grad_out,
        lower_drop,
        upper_drop,
        bias,
        wrec,
        win,
        uin,
        urec,
    )


PANEL = 576
STRIP = 288
GROUP = 72
HALF = 2 * GROUP
FULL = STRIP + 8
PAIRS = 24
LOWER_PAIRS = 18
SMALLEST = 2.0**-111
WIDTH = 4


def code(group):
    largest = jnp.maximum(jnp.max(jnp.abs(group), axis=0, keepdims=True), SMALLEST)
    step = jnp.floor(jnp.log2(largest) * 64.0).astype(jnp.int32) + 2
    return step, 32767.0 * jnp.exp2(step.astype(F32) * (-1.0 / 64.0))


def factor(step):
    return jnp.exp2(step.astype(F32) * (1.0 / 64.0)) * (1.0 / 32767.0)


def encode(a, b):
    step_a, up_a = code(a)
    step_b, up_b = code(b)
    word_a = jnp.round(a * up_a).astype(jnp.int32)
    word_b = jnp.round(b * up_b).astype(jnp.int32)
    return (word_a << 16) | (word_b & 0xFFFF), step_a, step_b


def decode(words, step_a, step_b):
    a = (words >> 16).astype(F32) * factor(step_a)
    b = ((words << 16) >> 16).astype(F32) * factor(step_b)
    return a, b


def sum_kernel(
    xh,
    lr,
    da,
    du,
    far_left,
    far_right,
    words,
    out,
    kept,
    lhs,
    rhs,
    mine,
    send2,
    recv2,
    send3,
    recv3,
    shard,
    scales,
    panel,
    send_sem,
    recv_sem,
    copy_sem,
    kept_sem,
    left_sem,
    right_sem,
):
    place, peer = torus()
    barrier = pltpu.get_barrier_semaphore()
    for axis in range(3):
        for distance in (1, 2, 3):
            pl.semaphore_signal(
                barrier, inc=1, device_id=peer(axis, distance), device_id_type=MESH
            )

    parts = tuple(range(6))

    def axes(m):
        return m % 3, (m + 1) % 3, (m + 2) % 3

    def kept_copy(m):
        first, second, third = axes(m)
        number = first * 16 + place[first] * 4 + place[second]
        start = pl.multiple_of(m // 3 * STRIP + place[third] * GROUP, 8)
        part = jnp.minimum(lax.div(number, 20), 1)
        lanes = pl.ds(pl.multiple_of(part * 128, 128), 128)
        src = words.at[pl.ds(start, GROUP), lanes]
        return number, pltpu.make_async_copy(src, kept.at[m], kept_sem.at[m])

    for m in parts:
        kept_copy(m)[1].start()

    def remote(src, dst, number, axis, distance):
        return pltpu.make_async_remote_copy(
            src_ref=src,
            dst_ref=dst,
            send_sem=send_sem.at[number],
            recv_sem=recv_sem.at[number],
            device_id=peer(axis, distance),
            device_id_type=MESH,
        )

    upper_here = place[2] != 0
    rows_all = da.shape[1]
    lr_rows = lr.shape[0]
    some = SOME * ROWS
    depth = 4 * rows_all

    def operand_copies(k, upper):
        copies = []
        for s in range(4):
            rows = slice(0, lr_rows if upper else 2 * PANEL)
            src = (lr if upper else xh) if s == 0 else far_left.at[k, s - 1]
            for i in range(2):
                at = s * depth + i * 2 * rows_all
                to = lhs.at[k, rows, at : at + 2 * rows_all]
                sem = left_sem.at[(k * 4 + s) * 2 + i]
                copies.append(pltpu.make_async_copy(src.at[rows], to, sem))
            sems = [right_sem.at[(k * 4 + s) * 2 + i] for i in (0, 1)]
            to = rhs.at[k, s, :, :, 0:512]
            if s > 0:
                src = far_right.at[k, s - 1, :, :, 0:512]
            elif upper:
                col = pl.multiple_of(jnp.maximum(place[k] - 1, 0) * 512, 512)
                src = du.at[:, :, pl.ds(col, 512)]
            else:
                col = pl.multiple_of((4 * k + (place[k] if k < 2 else 0)) * 512, 512)
                src = da.at[:, :, pl.ds(col, 512)]
            copies.append(pltpu.make_async_copy(src, to, sems[0]))
            if upper:
                src = far_right.at[k, s - 1, :, :, 512:640] if s > 0 else du.at[:, :, 1536:1664]
                copies.append(pltpu.make_async_copy(src, rhs.at[k, s, :, :, 512:640], sems[1]))
        return copies

    def for_operands(k, act):
        if k < 2:
            for copy in operand_copies(k, False):
                act(copy)
            return

        @pl.when(jnp.logical_not(upper_here))
        def _():
            for copy in operand_copies(k, False):
                act(copy)

        @pl.when(upper_here)
        def _():
            for copy in operand_copies(k, True):
                act(copy)

    def right(k, cols, width):
        parts = []
        for s in range(4):
            high, low = rhs[k, s, 0, :, cols], rhs[k, s, 1, :, cols]
            for at in range(0, rows_all, some):
                parts += [high[at : at + some]] * 2
            for at in range(0, rows_all, some):
                parts += [low[at : at + some], jnp.zeros((some, width), BF)]
        return jnp.concatenate(parts, axis=0)

    def compute(m, half):
        k, row = m % 3, m // 3 * STRIP
        cols = pl.ds(pl.multiple_of(half * 256, 256), 256)

        def put(ab, n, rows, value):
            mine[m, ab, 2 * half + n, rows, :] = value[:, n * 128 : (n + 1) * 128]

        def lower():
            operand = right(k, cols, 256)
            for ab in range(2):
                y = dot_nn(lhs[k, ab * PANEL + row : ab * PANEL + row + STRIP], operand)
                for n in range(2):
                    put(ab, n, slice(0, STRIP), y)

        def upper():
            operand = right(k, cols, 256)
            y = dot_nn(lhs[k, row : row + STRIP], operand)
            top = PANEL - TAIL_ROWS if row == 0 else 0
            index = 2 * (place[k] - 1) + half
            start = jnp.clip(index, 0, 2) * TAIL_ROWS + (STRIP - PANEL + TAIL_ROWS if row else 0)
            rows = pl.ds(pl.multiple_of(start, 16), STRIP - top)
            bottom = dot_nn(lhs[k, rows], right(k, slice(512, 640), 128))
            bottom = jnp.where(index < 3, bottom, 0.0)
            for n in range(2):
                put(0, n, slice(0, STRIP), y)
            if top:
                y = dot_nn(lhs[k, PANEL : PANEL + top], operand)
                for n in range(2):
                    put(1, n, slice(0, top), y)
            mine[m, 1, 2 * half, top:, :] = bottom
            mine[m, 1, 2 * half + 1, top:, :] = jnp.zeros_like(bottom)

        if k < 2:
            lower()
        else:
            pl.when(jnp.logical_not(upper_here))(lower)
            pl.when(upper_here)(upper)

    def compute_part(m):
        def step(half, carry):
            compute(m, half)
            return carry

        lax.fori_loop(0, 2, step, 0)

    @pl.when(upper_here)
    def _():
        lhs[2, lr_rows:, :] = jnp.zeros((2 * PANEL - lr_rows, lhs.shape[2]), BF)

    def rows_of(group):
        return pl.ds(pl.multiple_of(group * GROUP, 8), GROUP)

    def steps_at(ref, base, group):
        return ref[pl.ds(base + 2 * group, 1), :], ref[pl.ds(base + 2 * group + 1, 1), :]

    def store_code(ref, base, group, words, step_a, step_b):
        ref[rows_of(group), :] = words
        ref[pl.ds(base + 2 * group, 1), :] = step_a
        ref[pl.ds(base + 2 * group + 1, 1), :] = step_b

    def arrived(ref, base, group):
        return decode(ref[rows_of(group), :], *steps_at(ref, base, group))

    ways = ((0, 1), (1, -1))

    def stage2(m, way, kind):
        number = (m * 2 + way) * 3 + kind
        return remote(
            send2.at[m, way, kind], recv2.at[m, way, kind], number, axes(m)[1], 1 - 2 * way
        )

    def pack_half(m, offset, half, target, added):
        block = lax.rem(place[axes(m)[1]] + (offset + 4), 4)
        for group in range(2):
            rows = slice(half * HALF + group * GROUP, half * HALF + (group + 1) * GROUP)
            a, b = mine[m, 0, block, rows, :], mine[m, 1, block, rows, :]
            if added is not None:
                more_a, more_b = arrived(added, HALF, group)
                a, b = a + more_a, b + more_b
            store_code(target, HALF, group, *encode(a, b))

    def reduce2_first(m):
        for way, sign in ways:
            pack_half(m, 2, way, send2.at[m, way, 0], None)
            stage2(m, way, 0).start()
        for way, sign in ways:
            pack_half(m, sign, 1 - way, send2.at[m, way, 1], None)
            stage2(m, way, 1).start()

    def reduce2_second(m):
        for way, sign in ways:
            stage2(m, way, 0).wait_recv()
            pack_half(m, sign, way, send2.at[m, way, 2], recv2.at[m, way, 0])
            stage2(m, way, 2).start()

    def stage3(m, d):
        number = 36 + m * 3 + d - 1
        return remote(send3.at[m, d - 1], recv3.at[m, d - 1], number, axes(m)[2], d)

    def reduce3(m):
        block = place[axes(m)[1]]
        for kind in (1, 2):
            for way in range(2):
                stage2(m, way, kind).wait_recv()
        for group in range(4):
            half, inner = group // 2, group % 2
            a1, b1 = arrived(recv2.at[m, 0, 2 - half], HALF, inner)
            a2, b2 = arrived(recv2.at[m, 1, 1 + half], HALF, inner)
            rows = slice(group * GROUP, (group + 1) * GROUP)
            mine[m, 0, block, rows, :] += a1 + a2
            mine[m, 1, block, rows, :] += b1 + b2
        for d in (1, 2, 3):
            group = lax.rem(place[axes(m)[2]] + d, 4)
            a, b = mine[m, 0, block, rows_of(group), :], mine[m, 1, block, rows_of(group), :]
            store_code(send3.at[m, d - 1], GROUP, 0, *encode(a, b))
            stage3(m, d).start()

    def spread3(m, d, group):
        number = 54 + (m * 3 + d - 1) * 2
        axis = axes(m)[2]
        data = remote(shard.at[m, 0:GROUP], panel.at[m, rows_of(group)], number, axis, d)
        scale = remote(
            shard.at[m, GROUP : GROUP + 8], scales.at[m, d - 1], number + 1, axis, d
        )
        return data, scale

    def finish(m):
        first, second, third = axes(m)
        block, own = place[second], place[third]
        a, b = mine[m, 0, block, rows_of(own), :], mine[m, 1, block, rows_of(own), :]
        for d in (1, 2, 3):
            stage3(m, d).wait_recv()
            more_a, more_b = arrived(recv3.at[m, d - 1], GROUP, 0)
            a, b = a + more_a, b + more_b
        number, copy = kept_copy(m)
        copy.wait()
        flags = jnp.where(number < 2 * LOWER_PAIRS, flags_at(kept[m], number * 128) * 2, 1)
        store_code(shard.at[m], GROUP, 0, *encode(a, b * flags.astype(F32)))
        for d in (1, 2, 3):
            for copy in spread3(m, d, own):
                copy.start()
        panel[m, rows_of(own), :] = shard[m, 0:GROUP, :]

    def at(m, first, second):
        return out.at[m * 16 + first * 4 + second]

    def turned(axis, distance):
        return lax.rem(place[axis] + (distance + 4), 4)

    def spread2(m, way, src, first, second):
        return remote(src, at(m, first, second), 90 + m * 4 + way, axes(m)[1], 1 - 2 * way)

    def pass2(m, way, first, second):
        rows = slice(0, HALF) if way == 0 else slice(HALF, FULL)
        ref = at(m, first, second).at[rows]
        return remote(ref, ref, 90 + m * 4 + 2 + way, axes(m)[1], 1 - 2 * way)

    def spread1(m, way, order, src, first, second):
        number = 114 + (m * 2 + way) * 6 + order
        return remote(src, at(m, first, second), number, axes(m)[0], 1 - 2 * way)

    offsets = (0, -1, 1, 2)

    def own_copy(m):
        first, second, third = axes(m)
        return pltpu.make_async_copy(
            panel.at[m], at(m, place[first], place[second]), copy_sem.at[m]
        )

    def gather_own(m):
        first, second, third = axes(m)
        row = lax.broadcasted_iota(jnp.int32, (8, 128), 0)
        total = jnp.zeros((8, 128), jnp.int32)
        for d in (0, 1, 2, 3):
            group = lax.rem(place[third] + (4 - d), 4)
            if d == 0:
                tile = shard[m, GROUP : GROUP + 8, :]
            else:
                for copy in spread3(m, d, group):
                    copy.wait_recv()
                tile = scales[m, d - 1]
            total = jnp.where(row == 2 * group, tile[0:1], total)
            total = jnp.where(row == 2 * group + 1, tile[1:2], total)
        panel[m, STRIP:FULL, :] = total
        for way in range(2):
            spread2(m, way, panel.at[m], place[first], place[second]).start()
        own_copy(m).start()
        for way in range(2):
            spread1(m, way, 0, panel.at[m], place[first], place[second]).start()

    def gather_near(m):
        first = place[axes(m)[0]]
        for way in range(2):
            second = turned(axes(m)[1], 2 * way - 1)
            spread2(m, way, panel.at[m], first, second).wait_recv()
            pass2(m, way, first, second).start()
            for way1 in range(2):
                spread1(m, way1, 1 + way, at(m, first, second), first, second).start()

    def gather_far(m):
        first, second = place[axes(m)[0]], turned(axes(m)[1], 2)
        for way in range(2):
            pass2(m, way, first, second).wait_recv()
        for way1 in range(2):
            spread1(m, way1, 3, at(m, first, second), first, second).start()

    passed = ((0, 0), (1, 2), (0, 1), (1, 3))

    def pass1(m, way, order, first):
        ref = at(m, first, turned(axes(m)[1], offsets[order]))
        number = 114 + (m * 2 + way) * 6 + 4 + order % 2
        return remote(ref, ref, number, axes(m)[0], 1 - 2 * way)

    def spread1_arrived(m, way, order):
        first = turned(axes(m)[0], 2 * way - 1)
        second = turned(axes(m)[1], offsets[order])
        spread1(m, way, order, panel.at[m], first, second).wait_recv()

    def pass_on(m, which):
        for way, order in passed[which]:
            spread1_arrived(m, way, order)
            pass1(m, way, order, turned(axes(m)[0], 2 * way - 1)).start()

    for_operands(0, lambda copy: copy.start())

    def begin(m):
        if m < 3:
            for_operands(m, lambda copy: copy.wait())
        if m < 2:
            for_operands(m + 1, lambda copy: copy.start())
        compute_part(m)
        if m == 0:
            pl.semaphore_wait(barrier, 9)
        reduce2_first(m)

    def pass_early(m):
        pass_on(m, slice(0, 2))

    def pass_late(m):
        pass_on(m, slice(2, 4))

    def sent_sums(m):
        for way in range(2):
            for kind in range(3):
                stage2(m, way, kind).wait_send()
        for d in (1, 2, 3):
            stage3(m, d).wait_send()
            for copy in spread3(m, d, place[axes(m)[2]]):
                copy.wait_send()

    def sent_gather(m):
        first, second = place[axes(m)[0]], place[axes(m)[1]]
        own_copy(m).wait()
        for way in range(2):
            spread2(m, way, panel.at[m], first, second).wait_send()
            pass2(m, way, first, turned(axes(m)[1], 2 * way - 1)).wait_send()
            for order in range(4):
                second_now = turned(axes(m)[1], offsets[order])
                src = panel.at[m] if order == 0 else at(m, first, second_now)
                spread1(m, way, order, src, first, second_now).wait_send()
        for way, order in passed:
            pass1(m, way, order, turned(axes(m)[0], 2 * way - 1)).wait_send()

    for step, m in (
        (begin, 0),
        (begin, 1),
        (begin, 2),
        (reduce2_second, 0),
        (reduce2_second, 1),
        (begin, 3),
        (reduce2_second, 2),
        (reduce3, 0),
        (reduce3, 1),
        (begin, 4),
        (reduce3, 2),
        (finish, 0),
        (finish, 1),
        (begin, 5),
        (finish, 2),
        (gather_own, 0),
        (gather_own, 1),
        (reduce2_second, 3),
        (gather_own, 2),
        (reduce2_second, 4),
        (reduce2_second, 5),
        (gather_near, 0),
        (reduce3, 3),
        (gather_near, 1),
        (reduce3, 4),
        (gather_near, 2),
        (reduce3, 5),
        (finish, 3),
        (gather_far, 0),
        (finish, 4),
        (gather_far, 1),
        (finish, 5),
        (gather_far, 2),
        (gather_own, 3),
        (pass_early, 0),
        (gather_own, 4),
        (pass_early, 1),
        (gather_own, 5),
        (pass_early, 2),
        (gather_near, 3),
        (gather_near, 4),
        (gather_near, 5),
        (pass_late, 0),
        (pass_late, 1),
        (pass_late, 2),
        (gather_far, 3),
        (gather_far, 4),
        (gather_far, 5),
        (pass_early, 3),
        (pass_early, 4),
        (pass_early, 5),
        (pass_late, 3),
        (pass_late, 4),
        (pass_late, 5),
        (sent_sums, 0),
        (sent_sums, 1),
        (sent_sums, 2),
        (sent_sums, 3),
        (sent_sums, 4),
        (sent_sums, 5),
        (sent_gather, 0),
        (sent_gather, 1),
        (sent_gather, 2),
    ):
        step(m)
    for m in parts:
        for way in range(2):
            for order in range(4):
                if (way, order) not in passed:
                    spread1_arrived(m, way, order)
        for way, order in passed:
            pass1(m, way, order, turned(axes(m)[0], 2)).wait_recv()

    for m in parts[3:]:
        sent_gather(m)


def summed_panels(xh, lr, da, du, left, right, words):
    i32 = jnp.int32
    messages = 114 + 72
    rows_all = da.shape[1]
    dma = pltpu.SemaphoreType.DMA
    return pl.pallas_call(
        sum_kernel,
        out_shape=pltpu.VMEM((4 * PAIRS, FULL, 128), i32),
        in_specs=[pl.BlockSpec(memory_space=pl.ANY)] * 7,
        out_specs=pl.BlockSpec(memory_space=pl.ANY),
        scratch_shapes=[
            pltpu.VMEM((6, GROUP, 128), i32),
            pltpu.VMEM((3, 2 * PANEL, 16 * rows_all), BF),
            pltpu.VMEM((3, 4, 2, rows_all, 640), BF),
            pltpu.VMEM((6, 2, 4, STRIP, 128), F32),
            pltpu.VMEM((6, 2, 3, HALF + 8, 128), i32),
            pltpu.VMEM((6, 2, 3, HALF + 8, 128), i32),
            pltpu.VMEM((6, 3, GROUP + 8, 128), i32),
            pltpu.VMEM((6, 3, GROUP + 8, 128), i32),
            pltpu.VMEM((6, GROUP + 8, 128), i32),
            pltpu.VMEM((6, 3, 8, 128), i32),
            pltpu.VMEM((6, FULL, 128), i32),
            dma((messages,)),
            dma((messages,)),
            dma((6,)),
            dma((6,)),
            dma((24,)),
            dma((24,)),
        ],
        compiler_params=pltpu.CompilerParams(
            vmem_limit_bytes=SUM_VMEM, collective_id=1, has_side_effects=True
        ),
    )(xh, lr, da, du, left, right, words)


def unpack_kernel(
    panels,
    words_u,
    hidden,
    grads_in,
    low_in,
    low_rec,
    low_bias,
    up_in,
    up_rec,
    up_bias,
    hidden_o,
    grads_in_o,
    tail,
):
    step = pl.program_id(0)
    units, outs = low_in.shape[0], up_rec.shape[0]
    lower_steps, all_steps = 2 * LOWER_PAIRS // WIDTH, 2 * PAIRS // WIDTH

    @pl.when(step == 0)
    def _():
        hidden_o[...] = hidden[...]
        grads_in_o[...] = grads_in[...]

    def values(n, ab):
        parts = []
        n = jnp.minimum(step, all_steps - 1) * WIDTH + n
        for strip in range(2):
            at = strip * 2 * PAIRS + n
            for group in range(4):
                words = panels[at, group * GROUP : (group + 1) * GROUP, :]
                row = STRIP + 2 * group + ab
                scale = factor(panels[at, row : row + 1, :])
                half = (words >> 16) if ab == 0 else ((words << 16) >> 16)
                parts.append(half.astype(F32) * scale)
        return jnp.concatenate(parts, axis=0)

    for n in range(WIDTH):
        cols = slice(n * 128, (n + 1) * 128)

        @pl.when(step < lower_steps)
        def _():
            a = values(n, 0)
            low_in[:, cols] = a[:units]
            low_bias[:, cols] = a[units : units + 1]
            b = values(n, 1)[:units]
            low_rec[:, cols] = b

        @pl.when((step >= lower_steps) & (step < all_steps))
        def _():
            a = values(n, 0)
            up_in[:, cols] = a[:units]
            up_bias[:, cols] = a[units : units + 1]
            b = values(n, 1)
            flags = flags_at(words_u[...], (step - lower_steps) * WIDTH * 128 + n * 128)
            up_rec[:, cols] = b[:outs] * (flags * 2).astype(F32)[:outs]
            if n % 2 == 0:
                index = (step - lower_steps) * (WIDTH // 2) + n // 2
                rows = pl.ds(pl.multiple_of(index * TAIL_ROWS, 8), TAIL_ROWS)
                tail[rows, :] = b[PANEL - TAIL_ROWS :]

    @pl.when(step == all_steps)
    def _():
        up_in[:, :128] = tail[:units]
        up_bias[:, :128] = tail[units : units + 1]
        flags = flags_at(words_u[...], 2 * (PAIRS - LOWER_PAIRS) * 128)
        up_rec[:, :128] = tail[PANEL : PANEL + outs] * (flags * 2).astype(F32)[:outs]


def unpack(panels, words_u, hidden, grads_in, units, full, outs, full_u):
    sds = jax.ShapeDtypeStruct
    lower_steps, all_steps = 2 * LOWER_PAIRS // WIDTH, 2 * PAIRS // WIDTH
    wide = 128 * WIDTH
    lower = lambda i: (0, jnp.minimum(i, lower_steps - 1))
    upper = lambda i: (0, jnp.maximum(i - lower_steps, 0))
    return pl.pallas_call(
        unpack_kernel,
        grid=(all_steps + 1,),
        out_shape=(
            sds((units, full), F32),
            sds((units, full), F32),
            sds((1, full), F32),
            sds((units, full_u), F32),
            sds((outs, full_u), F32),
            sds((1, full_u), F32),
            sds(hidden.shape, F32),
            sds(grads_in.shape, F32),
        ),
        in_specs=[
            pl.BlockSpec(memory_space=pltpu.VMEM),
            pl.BlockSpec(memory_space=pltpu.VMEM),
            pl.BlockSpec(memory_space=pltpu.VMEM),
            pl.BlockSpec(memory_space=pltpu.VMEM),
        ],
        out_specs=(
            pl.BlockSpec((units, wide), lower),
            pl.BlockSpec((units, wide), lower),
            pl.BlockSpec((1, wide), lower),
            pl.BlockSpec((units, wide), upper),
            pl.BlockSpec((outs, wide), upper),
            pl.BlockSpec((1, wide), upper),
            pl.BlockSpec(hidden.shape, lambda i: (0, 0, 0)),
            pl.BlockSpec(grads_in.shape, lambda i: (0, 0, 0)),
        ),
        scratch_shapes=[pltpu.VMEM((6 * TAIL_ROWS, 128), F32)],
        compiler_params=pltpu.CompilerParams(vmem_limit_bytes=UNPACK_VMEM),
    )(panels, words_u, hidden, grads_in)


def body(
    inputs,
    lower_lock,
    upper_lock,
    resets,
    lower_input,
    lower_recur,
    lower_bias,
    lower_drop,
    upper_input,
    upper_recur,
    upper_bias,
    upper_drop,
    grad_out,
):
    me = lax.axis_index("pipe")
    streams, steps, width = inputs.shape
    hidden_out, grad_inputs, da, du, xh, lr, left, right, words_l, words_u = recurrence(
        inputs,
        lower_lock,
        upper_lock,
        resets,
        grad_out,
        lower_drop.T,
        upper_drop.T,
        jnp.concatenate([lower_bias, upper_bias])[None],
        lower_recur,
        lower_input,
        upper_input,
        upper_recur,
    )
    panels = summed_panels(xh, lr, da, du, left, right, words_l)
    low_in, low_rec, low_bias, up_in, up_rec, up_bias, hidden_out, grad_inputs = unpack(
        panels, words_u, hidden_out, grad_inputs, *lower_recur.shape, *upper_recur.shape
    )

    def own(row):
        half = row.shape[1] // 2
        return lax.dynamic_slice_in_dim(row[0], me * half, half, 0)

    return (
        hidden_out,
        grad_inputs,
        low_in,
        low_rec,
        own(low_bias),
        up_in,
        up_rec,
        own(up_bias),
    )


def solution(mesh):
    return jax.shard_map(
        body,
        mesh=mesh,
        in_specs=(
            P("dp", None, None),
            P("dp", None),
            P("dp", None),
            P("dp", None),
            P("pipe", None),
            P("pipe", None),
            P("pipe"),
            P(),
            P("pipe", None),
            P("pipe", None),
            P("pipe"),
            P(),
            P("dp", None, None),
        ),
        out_specs=(
            P("dp", None, "pipe"),
            P("dp", None, "pipe"),
            P("pipe", None),
            P("pipe", None),
            P("pipe"),
            P("pipe", None),
            P("pipe", None),
            P("pipe"),
        ),
        check_vma=False,
    )
```

```python
import functools

import jax
import jax.numpy as jnp
from jax import lax
from jax.experimental import pallas as pl
from jax.experimental.pallas import tpu as pltpu
from jax.sharding import PartitionSpec as P

BF = jnp.bfloat16
F32 = jnp.float32
MESH = pl.DeviceIdType.MESH
ROWS = 16
VMEM_LIMIT = 62 * 2**20
TAIL_ROWS = 368
EARLY = 8
SUM_VMEM = 47 * 2**20
UNPACK_VMEM = 24 * 2**20


def ceil_to(value, multiple):
    return -(-value // multiple) * multiple


def split(value):
    high = value.astype(BF)
    low = (value - high.astype(F32)).astype(BF)
    return high, low


def fold(stacked):
    half = stacked.shape[0] // 2
    return stacked[:half] + stacked[half:]


def dot_nn(a, b):
    return jnp.dot(a, b, preferred_element_type=F32)


def dot_nt(a, b):
    return lax.dot_general(a, b, (((1,), (1,)), ((), ())), preferred_element_type=F32)


def torus():
    dp = lax.axis_index("dp")
    place = [lax.rem(dp, 4), lax.rem(lax.div(dp, 4), 4), lax.div(dp, 16)]
    stride = [1, 4, 16]

    def across(axis, distance):
        moved = lax.rem(place[axis] + (distance + 4), 4)
        return {"dp": dp + (moved - place[axis]) * stride[axis]}

    return place, across


def flags_at(words, column):
    column = lax.broadcasted_iota(jnp.int32, (1, 128), 1) + column
    index = (column * 52429) >> 20
    bit = column - index * 20
    index = jnp.broadcast_to(index & 127, words.shape)
    found = jnp.take_along_axis(words, index, axis=1, mode="promise_in_bounds")
    return (found >> bit) & 1


def recurrence_kernel(
    units,
    inputs,
    lower_lock,
    upper_lock,
    resets,
    grad_out,
    lower_drop,
    upper_drop,
    both_bias,
    wrec_in,
    win_in,
    uin_in,
    urec_in,
    hid_o,
    dx_o,
    da_o,
    du_o,
    xh_o,
    lr_o,
    left_o,
    right_o,
    rows_l_o,
    rows_u_o,
    wrec_raw,
    win_raw,
    uin_raw,
    urec_raw,
    words_l,
    words_u,
    slab,
    keep_ref,
    lock_low,
    lock_ref,
    gout_ref,
    blo,
    bup,
    wrec_t,
    uin_t,
    urec_t,
    wrec,
    uin,
    urec,
    da_all,
    du_all,
    xh,
    lr,
    x2,
    hk2,
    ux2,
    hku2,
    dal,
    dau,
    proj,
    send_l,
    recv_l,
    send_u,
    recv_u,
    act_l,
    act_u,
    save_l,
    save_u,
    cell_l,
    cell_u,
    da_l,
    da_u,
    dstate_l,
    dstate_u,
    dx_up,
    acc,
    acc_x,
    acc_h,
    dx,
    fs_l,
    fr_l,
    fs_u,
    fr_u,
    bs_l,
    br_l,
    bs_u,
    br_u,
    far_s,
    far_r,
    in_sem,
    out_sem,
):
    streams, steps = resets.shape
    me = lax.axis_index("pipe")
    other = 1 - me
    peer = {"pipe": other}
    wide_k = wrec.shape[1]
    wide = wrec.shape[2]
    up_wide = uin.shape[2]
    up_k = urec.shape[1]
    lane = act_l.shape[1] - wide + units

    barrier = pltpu.get_barrier_semaphore()
    pl.semaphore_signal(barrier, inc=1, device_id=peer, device_id_type=MESH)
    place, across = torus()
    for axis in range(3):
        for d in (1, 2, 3):
            pl.semaphore_signal(barrier, inc=1, device_id=across(axis, d), device_id_type=MESH)
    loads = [
        pltpu.make_async_copy(wrec_in, wrec_raw, in_sem.at[1]),
        pltpu.make_async_copy(uin_in, uin_raw, in_sem.at[2]),
        pltpu.make_async_copy(urec_in, urec_raw, in_sem.at[3]),
        pltpu.make_async_copy(win_in, win_raw, in_sem.at[0]),
    ]
    for load in loads:
        load.start()
    pl.semaphore_wait(barrier, 10)

    def remote(src, dst, send_sem, recv_sem):
        return pltpu.make_async_remote_copy(
            src_ref=src,
            dst_ref=dst,
            send_sem=send_sem,
            recv_sem=recv_sem,
            device_id=peer,
            device_id_type=MESH,
        )

    full = wrec_raw.shape[1]
    held = wrec_raw.shape[0]
    held_u = urec_raw.shape[0]
    full_u = urec_raw.shape[1]
    unit_u = full_u // 8
    gate_u = gout_ref.shape[2]
    rows_all = steps * ROWS

    def to_rows(value, lanes, filler=0.0):
        more = lanes - value.shape[1]
        if more:
            value = jnp.concatenate([value, jnp.full((streams, more), filler, F32)], axis=1)
        return jnp.concatenate([value, jnp.zeros((ROWS - streams, lanes), F32)], axis=0)

    keep_ref[...] = jnp.zeros_like(keep_ref)
    for t in range(steps):
        now = 1.0 - resets[:, t : t + 1].astype(F32)
        keep_ref[t] = to_rows(jnp.broadcast_to(now, (streams, 128)), 128)
    blo[...] = jnp.zeros_like(blo)
    bup[...] = jnp.zeros_like(bup)
    def place_words(target, packed):
        rows, lanes = packed.shape
        more = target.shape[1] - lanes
        packed = jnp.concatenate([packed, jnp.zeros((rows, more), jnp.int32)], axis=1)
        target[0:rows, :] = packed

    words_l[...] = jnp.zeros_like(words_l)
    words_u[...] = jnp.zeros_like(words_u)
    for half in range(2):

        @pl.when(me == half)
        def _(half=half):
            mine = slice(half * units, (half + 1) * units)
            lock_low[...] = to_rows(lower_lock[:, mine].astype(F32) * 1.25, lane)
            lock_ref[...] = to_rows(upper_lock[:, mine].astype(F32) * 1.25, lane)
            one = jnp.full((streams, 1), 1.0, F32)
            for t in range(steps):
                now = inputs[:, t, mine] * lock_low[0:streams, 0:units]
                now = to_rows(jnp.concatenate([now, one], axis=1), lane)
                high, low = split(now)
                x2[t * ROWS : (t + 1) * ROWS] = high
                x2[rows_all + t * ROWS : rows_all + (t + 1) * ROWS] = low
                out = grad_out[:, t, half * unit_u : (half + 1) * unit_u]
                gout_ref[t] = to_rows(out, gate_u)
            place_words(words_l, lower_drop[:, mine])
            place_words(words_u, upper_drop[:, half * held_u : (half + 1) * held_u])
            bias = both_bias[...].astype(F32)
            bias_u = bias[:, 4 * units :]
            for q in range(2):
                for i in range(2):
                    g = 2 * half + i
                    start = (2 * i + q) * units
                    blo[q, :, g * units : (g + 1) * units] = bias[:, start : start + units]
                    start = (2 * i + q) * unit_u
                    bup[q, :, g * unit_u : (g + 1) * unit_u] = bias_u[
                        :, start : start + unit_u
                    ]

    loads[0].wait()
    sub = lax.broadcasted_iota(jnp.int32, (8, 128), 0)

    def flags_of(held, i):
        left, right = 8 * i // 20, (8 * i + 7) // 20
        now = jnp.broadcast_to(held[left : left + 1], (8, 128))
        if right != left:
            later = jnp.broadcast_to(held[right : right + 1], (8, 128))
            now = jnp.where(sub < 20 * right - 8 * i, now, later)
        bit = sub + 8 * i % 20
        bit = jnp.where(bit >= 20, bit - 20, bit)
        return now & (1 << bit)

    def masked_columns(weight, words, first, lanes):
        rows, columns = weight.shape
        words = words[pl.ds(first, ceil_to(ceil_to(columns, 20) // 20, 8)), lanes]
        turned = jnp.transpose(weight).astype(F32)
        if rows < 128:
            turned = jnp.concatenate([turned, jnp.zeros((columns, 128 - rows), F32)], axis=1)
        out = []
        for i in range(columns // 8):
            now = turned[8 * i : 8 * i + 8]
            out.append(jnp.where(flags_of(words, i) != 0, now + now, 0.0))
        return jnp.concatenate(out, axis=0)

    block = 640
    row16 = lax.broadcasted_iota(jnp.int32, (ROWS, 128), 0)

    def lower_slab(rows, start):
        lanes = pl.ds(start, 128)
        many = min(128, wide_k - start) if isinstance(start, int) else 128

        def fill(index, carry):
            cols = pl.ds(pl.multiple_of(index * block, block), block)
            first = pl.multiple_of(index * (block // 20), block // 20)
            part = masked_columns(wrec_raw[rows, cols], words_l, first, lanes)
            slab[cols, :] = part
            return carry

        lax.fori_loop(0, full // block, fill, 0)
        last = full // block * block
        slab[last:full, :] = masked_columns(
            wrec_raw[rows, last:full], words_l, last // 20, lanes
        )
        target = pl.ds(start, many)
        tiles = units // ROWS
        for q in range(2):
            for g in range(4):
                shift = units * (g + q)
                base = (tiles + 1) * ROWS * g

                def move(index, carry, q=q, shift=shift, base=base):
                    for i in range(7):
                        row = pl.multiple_of(base + (index * 7 + i) * ROWS, ROWS)
                        now = slab[pl.ds(row + shift, ROWS), :]
                        wrec_t[q, pl.ds(row, ROWS), target] = now.astype(BF)[:, :many]
                    return carry

                lax.fori_loop(0, tiles // 7, move, 0)
                row = base + tiles * ROWS
                now = slab[row + shift : row + shift + ROWS, :]
                if g < 3:
                    later = slab[row + shift + units : row + shift + units + ROWS, :]
                else:
                    later = jnp.zeros((ROWS, 128), F32)
                now = jnp.where(row16 < units * (g + 1) - row, now, later)
                wrec_t[q, row : row + ROWS, target] = now.astype(BF)[:, :many]

    def lower_slab_step(index, carry):
        start = pl.multiple_of(index * 128, 128)
        lower_slab(pl.ds(start, 128), start)
        return carry

    lax.fori_loop(0, held // 128, lower_slab_step, 0)
    lower_slab(slice(held // 128 * 128, held), held // 128 * 128)

    def place_upper(target, turned, start, many):
        for q in range(2):
            gates = [turned[(2 * g + q) * unit_u : (2 * g + q + 1) * unit_u] for g in range(4)]
            gates.append(jnp.zeros((up_wide - 4 * unit_u, 128), F32))
            part = jnp.concatenate(gates, axis=0).astype(BF)
            target[q, :, pl.ds(start, many)] = part[:, :many]

    for load in loads[1:]:
        load.wait()

    def upper_slab(index, carry):
        start = pl.multiple_of(index * 128, 128)
        turned = jnp.transpose(uin_raw[pl.ds(start, 128), :].astype(F32))
        place_upper(uin_t, turned, start, 128)
        return carry

    lax.fori_loop(0, held // 128, upper_slab, 0)
    start = held // 128 * 128
    turned = jnp.transpose(uin_raw[start:held, :].astype(F32))
    turned = jnp.concatenate([turned, jnp.zeros((full_u, 128 - held % 128), F32)], axis=1)
    place_upper(uin_t, turned, start, wide_k - start)
    for start in range(0, held_u, 128):
        stop = min(start + 128, held_u)
        lanes = pl.ds(start, 128)
        turned = [
            masked_columns(
                urec_raw[start:stop, i : min(i + block, full_u)], words_u, i // 20, lanes
            )
            for i in range(0, full_u, block)
        ]
        many = min(128, up_k - start)
        place_upper(urec_t, jnp.concatenate(turned, axis=0), start, many)
    for q in range(2):
        wrec[q] = jnp.transpose(wrec_t[q])
        uin[q] = jnp.transpose(uin_t[q])
        urec[q] = jnp.transpose(urec_t[q])
    proj[:, :, :, wide - 128 :] = jnp.zeros((2, steps, ROWS, 128), F32)
    for q in range(2):
        for g in range(4):
            start, stop = (2 * g + q) * units, (2 * g + q + 1) * units
            first, last = start // 128 * 128, min(ceil_to(stop, 128), full)
            y = fold(dot_nn(x2[:, :held], win_raw[:, first:last]))
            y = y[:, start - first : stop - first] + blo[q, :, g * units : (g + 1) * units]
            proj[q, :, :, g * units : (g + 1) * units] = y.reshape(steps, ROWS, units)

    rows_l_o[...] = jnp.transpose(words_l[...])
    rows_u_o[...] = jnp.transpose(words_u[...])

    early = EARLY * ROWS

    def place_left(target, row, count, high, low, first):
        steps_rows = high.shape[0]
        start = 2 * early if first else 0
        high, low = jnp.transpose(high)[:count], jnp.transpose(low)[:count]
        target[row : row + count, start : start + steps_rows] = high
        target[row : row + count, start + steps_rows : start + 2 * steps_rows] = low

    def place_steps(target, row, count, stack, first, last):
        width = stack.shape[2]
        high, low = [
            stack[first:last, i * ROWS : (i + 1) * ROWS, :].reshape((last - first) * ROWS, width)
            for i in (0, 1)
        ]
        place_left(target, row, count, high, low, first)

    place_left(xh, 0, wide_k, x2[0:early], x2[rows_all : rows_all + early], 0)
    place_left(xh, 0, wide_k, x2[early:rows_all], x2[rows_all + early :], EARLY)

    def far_copy(src, dst, number, axis, d):
        return pltpu.make_async_remote_copy(
            src_ref=src,
            dst_ref=dst,
            send_sem=far_s.at[number],
            recv_sem=far_r.at[number],
            device_id=across(axis, d),
            device_id_type=MESH,
        )

    lr_rows = lr.shape[0]

    def left_copy(k, d, kind, upper):
        lanes = slice(2 * early if kind == 2 else 0, 2 * early if kind == 1 else 2 * rows_all)
        if upper:
            src, rows = lr.at[:, lanes], slice(0, lr_rows)
        else:
            rows = slice(0, wide_k) if kind == 0 else slice(wide_k, 2 * wide_k)
            src = xh.at[rows, lanes]
        return far_copy(src, left_o.at[k, d - 1, rows, lanes], (k * 3 + d - 1) * 3 + kind, k, d)

    def for_left(kind, act, target):
        for k in range(3):
            for d in (1, 2, 3):
                lower_copy = left_copy(k, d, kind, False)
                if k < 2:
                    act(lower_copy)
                    continue
                is_lower = target(k, d) == 0

                @pl.when(is_lower)
                def _(copy=lower_copy):
                    act(copy)

                if kind > 0:
                    upper_copy = left_copy(k, d, kind, True)

                    @pl.when(jnp.logical_not(is_lower))
                    def _(copy=upper_copy):
                        act(copy)

    def at_peer(k, d):
        return lax.rem(place[k] + d, 4)

    def at_home(k, d):
        return place[k]

    for_left(0, lambda copy: copy.start(), at_peer)

    def right_copies(k, d, chunk, row, count, upper, target):
        rows = pl.ds(row, count)
        dst = right_o.at[k, d - 1, :, rows, 0:512]
        number = 27 + (k * 3 + d - 1) * 5 + chunk
        if not upper:
            col = (4 * k + (target if k < 2 else 0)) * 512
            src = da_all.at[:, rows, pl.ds(pl.multiple_of(col, 512), 512)]
            return [far_copy(src, dst, number, k, d)]
        col = pl.multiple_of(jnp.maximum(target - 1, 0) * 512, 512)
        tail_dst = right_o.at[k, d - 1, :, rows, 512:640]
        return [
            far_copy(du_all.at[:, rows, pl.ds(col, 512)], dst, number, k, d),
            far_copy(du_all.at[:, rows, 1536:1664], tail_dst, 72 + (d - 1) * 5 + chunk, k, d),
        ]

    def for_right(chunk, row, count, act, target):
        for k in range(3):
            for d in (1, 2, 3):
                goes = target(k, d)
                if k < 2:
                    for copy in right_copies(k, d, chunk, row, count, False, goes):
                        act(copy)
                    continue

                @pl.when(goes == 0)
                def _(k=k, d=d, goes=goes):
                    for copy in right_copies(k, d, chunk, row, count, False, goes):
                        act(copy)

                @pl.when(goes != 0)
                def _(k=k, d=d, goes=goes):
                    for copy in right_copies(k, d, chunk, row, count, True, goes):
                        act(copy)

    chunks = ((8, 4), (4, 4), (2, 2), (1, 1), (0, 1))

    act_l[...] = jnp.zeros_like(act_l)
    hk2[...] = jnp.zeros_like(hk2)
    ux2[...] = jnp.zeros_like(ux2)
    hku2[...] = jnp.zeros_like(hku2)
    cell_l[...] = jnp.zeros_like(cell_l)
    cell_u[...] = jnp.zeros_like(cell_u)

    def fcopy_l(t):
        return remote(send_l, recv_l.at[lax.rem(t, 2)], fs_l.at[t], fr_l.at[t])

    def fcopy_u(t):
        return remote(send_u, recv_u.at[lax.rem(t, 2)], fs_u.at[t], fr_u.at[t])

    def lower_send(t, first):
        if first:
            send_l[...] = proj[other, t]
        else:
            send_l[...] = fold(dot_nn(hk2[t, :, :wide_k], wrec[other])) + proj[other, t]
        fcopy_l(t).start()

    def lower_own(t, first):
        if first:
            act_l[:, :wide] = proj[me, t]
        else:
            act_l[:, :wide] = fold(dot_nn(hk2[t, :, :wide_k], wrec[me])) + proj[me, t]

    def upper_part(t, q):
        y = dot_nn(ux2[t, :, :wide_k], uin[q]) + dot_nn(hku2[t, :, :up_k], urec[q])
        return fold(y) + bup[q]

    def upper_send(t):
        send_u[...] = upper_part(t, other)
        fcopy_u(t).start()

    def upper_own(t):
        act_u[...] = upper_part(t, me)

    def keep_at(t, lanes):
        return jnp.concatenate([keep_ref[t]] * (ceil_to(lanes, 128) // 128), axis=1)[
            :, :lanes
        ]

    def cell_update(a_in, a_forget, a_cand, a_out, cell, keep_now, save, t):
        gate_in = jax.nn.sigmoid(a_in)
        forget = jax.nn.sigmoid(a_forget)
        cand = jnp.tanh(a_cand)
        gate_out = jax.nn.sigmoid(a_out)
        cell_keep = cell[...] * keep_now
        cell_new = forget * cell_keep + gate_in * cand
        squashed = jnp.tanh(cell_new)
        cell[...] = cell_new
        save[t, 0] = gate_in
        save[t, 1] = forget
        save[t, 2] = cand
        save[t, 3] = gate_out
        save[t, 4] = cell_keep
        save[t, 5] = squashed
        return gate_out * squashed

    def lower_cell(t):
        act_l[:, :wide] += recv_l[lax.rem(t, 2)]
        hidden = cell_update(
            act_l[:, 0:lane],
            act_l[:, units : units + lane],
            act_l[:, 2 * units : 2 * units + lane],
            act_l[:, 3 * units : 3 * units + lane],
            cell_l,
            keep_at(t, lane),
            save_l,
            t,
        )
        high, low = split(hidden * keep_at(t + 1, lane))
        hk2[t + 1, 0:ROWS] = high
        hk2[t + 1, ROWS:] = low
        ones_at = lax.broadcasted_iota(jnp.int32, (ROWS, lane), 1) == units
        high, low = split(jnp.where(ones_at, 1.0, hidden * lock_ref[...]))
        ux2[t, 0:ROWS] = high
        ux2[t, ROWS:] = low

    def upper_cell(t):
        a = act_u[...] + recv_u[lax.rem(t, 2)]
        hidden = cell_update(
            a[:, 0:gate_u],
            a[:, unit_u : unit_u + gate_u],
            a[:, 2 * unit_u : 2 * unit_u + gate_u],
            a[:, 3 * unit_u : 3 * unit_u + gate_u],
            cell_u,
            keep_at(t, gate_u),
            save_u,
            t,
        )
        hid_o[:, pl.ds(t, 1), :] = hidden[:streams, :unit_u].reshape(streams, 1, unit_u)
        high, low = split(hidden * keep_at(t + 1, gate_u))
        hku2[t + 1, 0:ROWS] = high
        hku2[t + 1, ROWS:] = low

    lower_send(0, True)
    lower_own(0, True)
    fcopy_l(0).wait()
    lower_cell(0)

    def forward_round(r, carry, with_cell=True):
        lower_send(r, False)
        if with_cell:
            fcopy_u(r - 2).wait()
            upper_cell(r - 2)
        lower_own(r, False)
        upper_send(r - 1)
        upper_own(r - 1)
        fcopy_l(r).wait()
        lower_cell(r)
        if with_cell:

            @pl.when(r == EARLY)
            def _():
                place_steps(xh, wide_k, wide_k, hk2, 0, EARLY)
                place_steps(lr, 0, wide_k, ux2, 0, EARLY)
                place_steps(lr, wide_k, up_k, hku2, 0, EARLY)
                for_left(1, lambda copy: copy.start(), at_peer)

        return carry

    forward_round(1, 0, False)
    lax.fori_loop(2, steps, forward_round, 0)
    fcopy_u(steps - 2).wait()
    upper_cell(steps - 2)
    upper_send(steps - 1)
    upper_own(steps - 1)
    fcopy_u(steps - 1).wait()
    upper_cell(steps - 1)

    place_steps(xh, wide_k, wide_k, hk2, EARLY, steps)
    place_steps(lr, 0, wide_k, ux2, EARLY, steps)
    place_steps(lr, wide_k, up_k, hku2, EARLY, steps)
    for_left(2, lambda copy: copy.start(), at_peer)

    da_all[...] = jnp.zeros_like(da_all)
    du_all[...] = jnp.zeros_like(du_all)

    def own_order(t, carry):
        to = pl.ds(pl.multiple_of(t * ROWS, ROWS), ROWS)
        for part in range(2):
            rows = slice(part * ROWS, (part + 1) * ROWS)
            for q in range(2):
                for g in range(4):
                    start = (2 * g + q) * units
                    da_all[part, to, start : start + units] = dal[
                        q, t, rows, g * units : (g + 1) * units
                    ]
                    start = (2 * g + q) * unit_u
                    du_all[part, to, start : start + unit_u] = dau[
                        q, t, rows, g * unit_u : (g + 1) * unit_u
                    ]
        return carry

    def send_right(chunk):
        first, count = chunks[chunk]
        lax.fori_loop(first, first + count, own_order, 0)
        for_right(chunk, first * ROWS, count * ROWS, lambda copy: copy.start(), at_peer)

    dstate_l[...] = jnp.zeros_like(dstate_l)
    dstate_u[...] = jnp.zeros_like(dstate_u)
    da_l[...] = jnp.zeros_like(da_l)
    da_u[...] = jnp.zeros_like(da_u)

    def bcopy_l(t):
        return remote(dal.at[me, t], dal.at[me, t], bs_l.at[t], br_l.at[t])

    def bcopy_u(t):
        return remote(dau.at[me, t], dau.at[me, t], bs_u.at[t], br_u.at[t])

    def gate_grads(dy, dstate, save, keep_now, t):
        gate_in, forget, cand, gate_out = save[t, 0], save[t, 1], save[t, 2], save[t, 3]
        cell_keep, squashed = save[t, 4], save[t, 5]
        dh = dstate[0] + dy
        dc = dstate[1] + dh * gate_out * (1.0 - squashed * squashed)
        dstate[1] = dc * forget * keep_now
        return (
            dc * cand * gate_in * (1.0 - gate_in),
            dc * cell_keep * forget * (1.0 - forget),
            dc * gate_in * (1.0 - cand * cand),
            dh * squashed * gate_out * (1.0 - gate_out),
        )

    def lower_back_start(t):
        grads = gate_grads(dx_up[...] * lock_ref[...], dstate_l, save_l, keep_at(t, lane), t)
        for g in range(4):
            da_l[:, g * units : (g + 1) * units] = grads[g][:, :units]
        high, low = split(da_l[...])
        dal[me, t, 0:ROWS] = high
        dal[me, t, ROWS:] = low
        bcopy_l(t).start()

    def upper_back_start(t):
        grads = gate_grads(gout_ref[t], dstate_u, save_u, keep_at(t, gate_u), t)
        for g in range(4):
            da_u[:, g * unit_u : (g + 1) * unit_u] = grads[g][:, :unit_u]
        high, low = split(da_u[...])
        dau[me, t, 0:ROWS] = high
        dau[me, t, ROWS:] = low
        bcopy_u(t).start()

    def lower_back_part(t, q):
        return fold(dot_nn(dal[q, t], wrec_t[q]))

    def upper_back_part(t, q):
        grad = dau[q, t]
        return fold(dot_nn(grad, uin_t[q])), fold(dot_nn(grad, urec_t[q]))

    def lower_back_own(t):
        acc[:, :wide_k] = lower_back_part(t, me)

    def lower_back_other(t):
        total = acc[:, :wide_k] + lower_back_part(t, other)
        dstate_l[0, :, :wide_k] = keep_at(t, wide_k) * total

    def upper_back_own(t):
        into_x, into_h = upper_back_part(t, me)
        acc_x[:, :wide_k] = into_x
        acc_h[:, :up_k] = into_h

    def upper_back_other(t):
        into_x, into_h = upper_back_part(t, other)
        dx_up[:, :wide_k] = acc_x[:, :wide_k] + into_x
        dstate_u[0, :, :up_k] = keep_at(t, up_k) * (acc_h[:, :up_k] + into_h)

    dx_up[...] = jnp.zeros_like(dx_up)
    upper_back_start(steps - 1)
    upper_back_own(steps - 1)
    bcopy_u(steps - 1).wait()
    upper_back_other(steps - 1)
    upper_back_start(steps - 2)

    def backward_round(r, carry, last=False):
        t = steps - r
        lower_back_start(t)
        lower_back_own(t)
        upper_back_own(t - 1)
        bcopy_u(t - 1).wait()
        upper_back_other(t - 1)
        bcopy_l(t).wait()
        lower_back_other(t)
        if last:
            send_right(3)
            return carry
        upper_back_start(t - 2)
        for chunk in range(3):

            @pl.when(t == chunks[chunk][0])
            def _(chunk=chunk):
                send_right(chunk)

        return carry

    lax.fori_loop(1, steps - 1, backward_round, 0)
    backward_round(steps - 1, 0, True)
    lower_back_start(0)
    bcopy_l(0).wait()

    send_right(4)

    copies = [
        pltpu.make_async_copy(da_all, da_o, out_sem.at[0]),
        pltpu.make_async_copy(du_all, du_o, out_sem.at[1]),
        pltpu.make_async_copy(xh, xh_o, out_sem.at[2]),
        pltpu.make_async_copy(lr, lr_o, out_sem.at[3]),
    ]
    for copy in copies:
        copy.start()

    chunk = 512

    def input_grad(cols, width):
        grad = da_all[:, :, cols].reshape(2 * rows_all, width)
        return fold(dot_nt(grad, win_raw[:, cols]))

    tail = full // chunk * chunk
    dx[:, :held] = input_grad(slice(tail, full), full % chunk) if full % chunk else 0.0

    def input_grad_step(index, carry):
        dx[:, :held] += input_grad(pl.ds(pl.multiple_of(index * chunk, chunk), chunk), chunk)
        return carry

    lax.fori_loop(0, full // chunk, input_grad_step, 0)
    for t in range(steps):
        now = dx[t * ROWS : t * ROWS + streams, :held] * lock_low[0:streams, :held]
        dx_o[:, t, :] = now
    for copy in copies:
        copy.wait()
    for kind in range(3):
        for_left(kind, lambda copy: copy.wait_send(), at_peer)
        for_left(kind, lambda copy: copy.wait_recv(), at_home)
    for chunk in range(5):
        row, count = chunks[chunk][0] * ROWS, chunks[chunk][1] * ROWS
        for_right(chunk, row, count, lambda copy: copy.wait_send(), at_peer)
        for_right(chunk, row, count, lambda copy: copy.wait_recv(), at_home)


def recurrence(
    inputs,
    lower_lock,
    upper_lock,
    resets,
    grad_out,
    lower_drop,
    upper_drop,
    bias,
    wrec,
    win,
    uin,
    urec,
):
    streams, steps = resets.shape
    units, full = wrec.shape
    outs, full_u = urec.shape
    wide_k = ceil_to(units, 16)
    wide = ceil_to(full // 2, 256)
    up_k = ceil_to(outs, 16)
    gate_u = ceil_to(outs, 128)
    up_wide = ceil_to(full_u // 2, 128)
    lane = ceil_to(units, 128)
    rows_all = steps * ROWS
    vm = pl.BlockSpec(memory_space=pltpu.VMEM)
    hbm = pl.BlockSpec(memory_space=pl.ANY)
    sds = jax.ShapeDtypeStruct
    i32 = jnp.int32
    shared = [
        ((2, rows_all, ceil_to(full, 512)), BF),
        ((2, rows_all, ceil_to(full_u, 128)), BF),
        ((2 * wide_k, 2 * rows_all), BF),
        ((wide_k + up_k, 2 * rows_all), BF),
    ]
    landed = [
        ((3, 3, 2 * wide_k, 2 * rows_all), BF),
        ((3, 3, 2, rows_all, 640), BF),
    ]
    raw = [(w.shape, BF) for w in (wrec, win, uin, urec)]
    dma = pltpu.SemaphoreType.DMA
    return pl.pallas_call(
        functools.partial(recurrence_kernel, units),
        out_shape=(sds((streams, steps, outs), F32), sds((streams, steps, units), F32))
        + tuple(sds(*s) for s in shared + landed)
        + (sds((lane, 256), i32), sds((ceil_to(outs, 128), 128), i32)),
        in_specs=[vm] * 8 + [hbm] * 4,
        out_specs=(vm, vm) + (hbm,) * len(shared + landed) + (vm, vm),
        scratch_shapes=[pltpu.VMEM(*s) for s in raw]
        + [
            pltpu.VMEM((256, lane), i32),
            pltpu.VMEM((128, ceil_to(outs, 128)), i32),
            pltpu.VMEM((ceil_to(full, 16), 128), F32),
            pltpu.VMEM((steps + 1, ROWS, 128), F32),
            pltpu.VMEM((ROWS, lane), F32),
            pltpu.VMEM((ROWS, lane), F32),
            pltpu.VMEM((steps, ROWS, gate_u), F32),
            pltpu.VMEM((2, 1, wide), F32),
            pltpu.VMEM((2, 1, up_wide), F32),
            pltpu.VMEM((2, wide, wide_k), BF),
            pltpu.VMEM((2, up_wide, wide_k), BF),
            pltpu.VMEM((2, up_wide, up_k), BF),
            pltpu.VMEM((2, wide_k, wide), BF),
            pltpu.VMEM((2, wide_k, up_wide), BF),
            pltpu.VMEM((2, up_k, up_wide), BF),
        ]
        + [pltpu.VMEM(*s) for s in shared]
        + [
            pltpu.VMEM((2 * rows_all, lane), BF),
            pltpu.VMEM((steps + 1, 2 * ROWS, lane), BF),
            pltpu.VMEM((steps, 2 * ROWS, lane), BF),
            pltpu.VMEM((steps + 1, 2 * ROWS, gate_u), BF),
            pltpu.VMEM((2, steps, 2 * ROWS, wide), BF),
            pltpu.VMEM((2, steps, 2 * ROWS, up_wide), BF),
            pltpu.VMEM((2, steps, ROWS, wide), F32),
            pltpu.VMEM((ROWS, wide), F32),
            pltpu.VMEM((2, ROWS, wide), F32),
            pltpu.VMEM((ROWS, up_wide), F32),
            pltpu.VMEM((2, ROWS, up_wide), F32),
            pltpu.VMEM((ROWS, wide + lane - units), F32),
            pltpu.VMEM((ROWS, up_wide), F32),
            pltpu.VMEM((steps, 6, ROWS, lane), F32),
            pltpu.VMEM((steps, 6, ROWS, gate_u), F32),
            pltpu.VMEM((ROWS, lane), F32),
            pltpu.VMEM((ROWS, gate_u), F32),
            pltpu.VMEM((ROWS, wide), F32),
            pltpu.VMEM((ROWS, up_wide), F32),
            pltpu.VMEM((2, ROWS, lane), F32),
            pltpu.VMEM((2, ROWS, gate_u), F32),
            pltpu.VMEM((ROWS, lane), F32),
            pltpu.VMEM((ROWS, lane), F32),
            pltpu.VMEM((ROWS, lane), F32),
            pltpu.VMEM((ROWS, gate_u), F32),
            pltpu.VMEM((rows_all, lane), F32),
        ]
        + [dma((steps,))] * 8
        + [dma((87,)), dma((87,)), dma((4,)), dma((4,))],
        compiler_params=pltpu.CompilerParams(
            vmem_limit_bytes=VMEM_LIMIT, collective_id=0, has_side_effects=True
        ),
    )(
        inputs,
        lower_lock,
        upper_lock,
        resets,
        grad_out,
        lower_drop,
        upper_drop,
        bias,
        wrec,
        win,
        uin,
        urec,
    )


PANEL = 576
STRIP = 288
GROUP = 72
HALF = 2 * GROUP
FULL = STRIP + 8
PAIRS = 24
LOWER_PAIRS = 18
SMALLEST = 2.0**-111
WIDTH = 4


def code(group):
    largest = jnp.maximum(jnp.max(jnp.abs(group), axis=0, keepdims=True), SMALLEST)
    step = jnp.floor(jnp.log2(largest) * 64.0).astype(jnp.int32) + 2
    return step, 32767.0 * jnp.exp2(step.astype(F32) * (-1.0 / 64.0))


def factor(step):
    return jnp.exp2(step.astype(F32) * (1.0 / 64.0)) * (1.0 / 32767.0)


def encode(a, b):
    step_a, up_a = code(a)
    step_b, up_b = code(b)
    word_a = jnp.round(a * up_a).astype(jnp.int32)
    word_b = jnp.round(b * up_b).astype(jnp.int32)
    return (word_a << 16) | (word_b & 0xFFFF), step_a, step_b


def decode(words, step_a, step_b):
    a = (words >> 16).astype(F32) * factor(step_a)
    b = ((words << 16) >> 16).astype(F32) * factor(step_b)
    return a, b


def sum_kernel(
    xh,
    lr,
    da,
    du,
    far_left,
    far_right,
    words,
    out,
    kept,
    lhs,
    rhs,
    mine,
    send2,
    recv2,
    send3,
    recv3,
    shard,
    scales,
    panel,
    send_sem,
    recv_sem,
    copy_sem,
    kept_sem,
    left_sem,
    right_sem,
):
    place, peer = torus()
    barrier = pltpu.get_barrier_semaphore()
    for axis in range(3):
        for distance in (1, 2, 3):
            pl.semaphore_signal(
                barrier, inc=1, device_id=peer(axis, distance), device_id_type=MESH
            )

    parts = tuple(range(6))

    def axes(m):
        return m % 3, (m + 1) % 3, (m + 2) % 3

    def kept_copy(m):
        first, second, third = axes(m)
        number = first * 16 + place[first] * 4 + place[second]
        start = pl.multiple_of(m // 3 * STRIP + place[third] * GROUP, 8)
        part = jnp.minimum(lax.div(number, 20), 1)
        lanes = pl.ds(pl.multiple_of(part * 128, 128), 128)
        src = words.at[pl.ds(start, GROUP), lanes]
        return number, pltpu.make_async_copy(src, kept.at[m], kept_sem.at[m])

    for m in parts:
        kept_copy(m)[1].start()

    def remote(src, dst, number, axis, distance):
        return pltpu.make_async_remote_copy(
            src_ref=src,
            dst_ref=dst,
            send_sem=send_sem.at[number],
            recv_sem=recv_sem.at[number],
            device_id=peer(axis, distance),
            device_id_type=MESH,
        )

    upper_here = place[2] != 0
    rows_all = da.shape[1]
    lr_rows = lr.shape[0]
    early = EARLY * ROWS

    def operand_copies(k, upper):
        copies = []
        for s in range(4):
            rows = slice(0, lr_rows if upper else 2 * PANEL)
            src = (lr if upper else xh) if s == 0 else far_left.at[k, s - 1]
            at = s * 640
            for i, (first, last) in enumerate(((0, 384), (0, 128), (256, 384))):
                to = lhs.at[k, rows, at : at + last - first]
                copies.append(
                    pltpu.make_async_copy(
                        src.at[rows, first:last], to, left_sem.at[(k * 4 + s) * 3 + i]
                    )
                )
                at += last - first
            sems = [right_sem.at[(k * 4 + s) * 2 + i] for i in (0, 1)]
            to = rhs.at[k, s, :, :, 0:512]
            if s > 0:
                src = far_right.at[k, s - 1, :, :, 0:512]
            elif upper:
                col = pl.multiple_of(jnp.maximum(place[k] - 1, 0) * 512, 512)
                src = du.at[:, :, pl.ds(col, 512)]
            else:
                col = pl.multiple_of((4 * k + (place[k] if k < 2 else 0)) * 512, 512)
                src = da.at[:, :, pl.ds(col, 512)]
            copies.append(pltpu.make_async_copy(src, to, sems[0]))
            if upper:
                src = far_right.at[k, s - 1, :, :, 512:640] if s > 0 else du.at[:, :, 1536:1664]
                copies.append(pltpu.make_async_copy(src, rhs.at[k, s, :, :, 512:640], sems[1]))
        return copies

    def for_operands(k, act):
        if k < 2:
            for copy in operand_copies(k, False):
                act(copy)
            return

        @pl.when(jnp.logical_not(upper_here))
        def _():
            for copy in operand_copies(k, False):
                act(copy)

        @pl.when(upper_here)
        def _():
            for copy in operand_copies(k, True):
                act(copy)

    def right(k, cols, width):
        parts = []
        for s in range(4):
            high, low = rhs[k, s, 0, :, cols], rhs[k, s, 1, :, cols]
            parts += [high[:early], high[:early], high[early:], high[early:]]
            parts += [low[:early], low[early:], jnp.zeros((640 - 3 * rows_all, width), BF)]
        return jnp.concatenate(parts, axis=0)

    def compute(m, half):
        k, row = m % 3, m // 3 * STRIP
        cols = pl.ds(pl.multiple_of(half * 256, 256), 256)

        def put(ab, n, rows, value):
            mine[m, ab, 2 * half + n, rows, :] = value[:, n * 128 : (n + 1) * 128]

        def lower():
            operand = right(k, cols, 256)
            for ab in range(2):
                y = dot_nn(lhs[k, ab * PANEL + row : ab * PANEL + row + STRIP], operand)
                for n in range(2):
                    put(ab, n, slice(0, STRIP), y)

        def upper():
            operand = right(k, cols, 256)
            y = dot_nn(lhs[k, row : row + STRIP], operand)
            top = PANEL - TAIL_ROWS if row == 0 else 0
            index = 2 * (place[k] - 1) + half
            start = jnp.clip(index, 0, 2) * TAIL_ROWS + (STRIP - PANEL + TAIL_ROWS if row else 0)
            rows = pl.ds(pl.multiple_of(start, 16), STRIP - top)
            bottom = dot_nn(lhs[k, rows], right(k, slice(512, 640), 128))
            bottom = jnp.where(index < 3, bottom, 0.0)
            for n in range(2):
                put(0, n, slice(0, STRIP), y)
            if top:
                y = dot_nn(lhs[k, PANEL : PANEL + top], operand)
                for n in range(2):
                    put(1, n, slice(0, top), y)
            mine[m, 1, 2 * half, top:, :] = bottom
            mine[m, 1, 2 * half + 1, top:, :] = jnp.zeros_like(bottom)

        if k < 2:
            lower()
        else:
            pl.when(jnp.logical_not(upper_here))(lower)
            pl.when(upper_here)(upper)

    def compute_part(m):
        def step(half, carry):
            compute(m, half)
            return carry

        lax.fori_loop(0, 2, step, 0)

    @pl.when(upper_here)
    def _():
        lhs[2, lr_rows:, :] = jnp.zeros((2 * PANEL - lr_rows, lhs.shape[2]), BF)

    def rows_of(group):
        return pl.ds(pl.multiple_of(group * GROUP, 8), GROUP)

    def steps_at(ref, base, group):
        return ref[pl.ds(base + 2 * group, 1), :], ref[pl.ds(base + 2 * group + 1, 1), :]

    def store_code(ref, base, group, words, step_a, step_b):
        ref[rows_of(group), :] = words
        ref[pl.ds(base + 2 * group, 1), :] = step_a
        ref[pl.ds(base + 2 * group + 1, 1), :] = step_b

    def arrived(ref, base, group):
        return decode(ref[rows_of(group), :], *steps_at(ref, base, group))

    ways = ((0, 1), (1, -1))

    def stage2(m, way, kind):
        number = (m * 2 + way) * 3 + kind
        return remote(
            send2.at[m, way, kind], recv2.at[m, way, kind], number, axes(m)[1], 1 - 2 * way
        )

    def pack_half(m, offset, half, target, added):
        block = lax.rem(place[axes(m)[1]] + (offset + 4), 4)
        for group in range(2):
            rows = slice(half * HALF + group * GROUP, half * HALF + (group + 1) * GROUP)
            a, b = mine[m, 0, block, rows, :], mine[m, 1, block, rows, :]
            if added is not None:
                more_a, more_b = arrived(added, HALF, group)
                a, b = a + more_a, b + more_b
            store_code(target, HALF, group, *encode(a, b))

    def reduce2_first(m):
        for way, sign in ways:
            pack_half(m, 2, way, send2.at[m, way, 0], None)
            stage2(m, way, 0).start()
        for way, sign in ways:
            pack_half(m, sign, 1 - way, send2.at[m, way, 1], None)
            stage2(m, way, 1).start()

    def reduce2_second(m):
        for way, sign in ways:
            stage2(m, way, 0).wait_recv()
            pack_half(m, sign, way, send2.at[m, way, 2], recv2.at[m, way, 0])
            stage2(m, way, 2).start()

    def stage3(m, d):
        number = 36 + m * 3 + d - 1
        return remote(send3.at[m, d - 1], recv3.at[m, d - 1], number, axes(m)[2], d)

    def reduce3(m):
        block = place[axes(m)[1]]
        for kind in (1, 2):
            for way in range(2):
                stage2(m, way, kind).wait_recv()
        for group in range(4):
            half, inner = group // 2, group % 2
            a1, b1 = arrived(recv2.at[m, 0, 2 - half], HALF, inner)
            a2, b2 = arrived(recv2.at[m, 1, 1 + half], HALF, inner)
            rows = slice(group * GROUP, (group + 1) * GROUP)
            mine[m, 0, block, rows, :] += a1 + a2
            mine[m, 1, block, rows, :] += b1 + b2
        for d in (1, 2, 3):
            group = lax.rem(place[axes(m)[2]] + d, 4)
            a, b = mine[m, 0, block, rows_of(group), :], mine[m, 1, block, rows_of(group), :]
            store_code(send3.at[m, d - 1], GROUP, 0, *encode(a, b))
            stage3(m, d).start()

    def spread3(m, d, group):
        number = 54 + (m * 3 + d - 1) * 2
        axis = axes(m)[2]
        data = remote(shard.at[m, 0:GROUP], panel.at[m, rows_of(group)], number, axis, d)
        scale = remote(
            shard.at[m, GROUP : GROUP + 8], scales.at[m, d - 1], number + 1, axis, d
        )
        return data, scale

    def finish(m):
        first, second, third = axes(m)
        block, own = place[second], place[third]
        a, b = mine[m, 0, block, rows_of(own), :], mine[m, 1, block, rows_of(own), :]
        for d in (1, 2, 3):
            stage3(m, d).wait_recv()
            more_a, more_b = arrived(recv3.at[m, d - 1], GROUP, 0)
            a, b = a + more_a, b + more_b
        number, copy = kept_copy(m)
        copy.wait()
        flags = jnp.where(number < 2 * LOWER_PAIRS, flags_at(kept[m], number * 128) * 2, 1)
        store_code(shard.at[m], GROUP, 0, *encode(a, b * flags.astype(F32)))
        for d in (1, 2, 3):
            for copy in spread3(m, d, own):
                copy.start()
        panel[m, rows_of(own), :] = shard[m, 0:GROUP, :]

    def at(m, first, second):
        return out.at[m * 16 + first * 4 + second]

    def turned(axis, distance):
        return lax.rem(place[axis] + (distance + 4), 4)

    def spread2(m, way, src, first, second):
        return remote(src, at(m, first, second), 90 + m * 4 + way, axes(m)[1], 1 - 2 * way)

    def pass2(m, way, first, second):
        rows = slice(0, HALF) if way == 0 else slice(HALF, FULL)
        ref = at(m, first, second).at[rows]
        return remote(ref, ref, 90 + m * 4 + 2 + way, axes(m)[1], 1 - 2 * way)

    def spread1(m, way, order, src, first, second):
        number = 114 + (m * 2 + way) * 6 + order
        return remote(src, at(m, first, second), number, axes(m)[0], 1 - 2 * way)

    offsets = (0, -1, 1, 2)

    def own_copy(m):
        first, second, third = axes(m)
        return pltpu.make_async_copy(
            panel.at[m], at(m, place[first], place[second]), copy_sem.at[m]
        )

    def gather_own(m):
        first, second, third = axes(m)
        row = lax.broadcasted_iota(jnp.int32, (8, 128), 0)
        total = jnp.zeros((8, 128), jnp.int32)
        for d in (0, 1, 2, 3):
            group = lax.rem(place[third] + (4 - d), 4)
            if d == 0:
                tile = shard[m, GROUP : GROUP + 8, :]
            else:
                for copy in spread3(m, d, group):
                    copy.wait_recv()
                tile = scales[m, d - 1]
            total = jnp.where(row == 2 * group, tile[0:1], total)
            total = jnp.where(row == 2 * group + 1, tile[1:2], total)
        panel[m, STRIP:FULL, :] = total
        for way in range(2):
            spread2(m, way, panel.at[m], place[first], place[second]).start()
        own_copy(m).start()
        for way in range(2):
            spread1(m, way, 0, panel.at[m], place[first], place[second]).start()

    def gather_near(m):
        first = place[axes(m)[0]]
        for way in range(2):
            second = turned(axes(m)[1], 2 * way - 1)
            spread2(m, way, panel.at[m], first, second).wait_recv()
            pass2(m, way, first, second).start()
            for way1 in range(2):
                spread1(m, way1, 1 + way, at(m, first, second), first, second).start()

    def gather_far(m):
        first, second = place[axes(m)[0]], turned(axes(m)[1], 2)
        for way in range(2):
            pass2(m, way, first, second).wait_recv()
        for way1 in range(2):
            spread1(m, way1, 3, at(m, first, second), first, second).start()

    passed = ((0, 0), (1, 2), (0, 1), (1, 3))

    def pass1(m, way, order, first):
        ref = at(m, first, turned(axes(m)[1], offsets[order]))
        number = 114 + (m * 2 + way) * 6 + 4 + order % 2
        return remote(ref, ref, number, axes(m)[0], 1 - 2 * way)

    def spread1_arrived(m, way, order):
        first = turned(axes(m)[0], 2 * way - 1)
        second = turned(axes(m)[1], offsets[order])
        spread1(m, way, order, panel.at[m], first, second).wait_recv()

    def pass_on(m, which):
        for way, order in passed[which]:
            spread1_arrived(m, way, order)
            pass1(m, way, order, turned(axes(m)[0], 2 * way - 1)).start()

    for_operands(0, lambda copy: copy.start())

    def begin(m):
        if m < 3:
            for_operands(m, lambda copy: copy.wait())
        if m < 2:
            for_operands(m + 1, lambda copy: copy.start())
        compute_part(m)
        if m == 0:
            pl.semaphore_wait(barrier, 9)
        reduce2_first(m)

    def pass_early(m):
        pass_on(m, slice(0, 2))

    def pass_late(m):
        pass_on(m, slice(2, 4))

    def sent_sums(m):
        for way in range(2):
            for kind in range(3):
                stage2(m, way, kind).wait_send()
        for d in (1, 2, 3):
            stage3(m, d).wait_send()
            for copy in spread3(m, d, place[axes(m)[2]]):
                copy.wait_send()

    def sent_gather(m):
        first, second = place[axes(m)[0]], place[axes(m)[1]]
        own_copy(m).wait()
        for way in range(2):
            spread2(m, way, panel.at[m], first, second).wait_send()
            pass2(m, way, first, turned(axes(m)[1], 2 * way - 1)).wait_send()
            for order in range(4):
                second_now = turned(axes(m)[1], offsets[order])
                src = panel.at[m] if order == 0 else at(m, first, second_now)
                spread1(m, way, order, src, first, second_now).wait_send()
        for way, order in passed:
            pass1(m, way, order, turned(axes(m)[0], 2 * way - 1)).wait_send()

    for step, m in (
        (begin, 0),
        (begin, 1),
        (begin, 2),
        (reduce2_second, 0),
        (reduce2_second, 1),
        (begin, 3),
        (reduce2_second, 2),
        (reduce3, 0),
        (reduce3, 1),
        (begin, 4),
        (reduce3, 2),
        (finish, 0),
        (finish, 1),
        (begin, 5),
        (finish, 2),
        (gather_own, 0),
        (gather_own, 1),
        (reduce2_second, 3),
        (gather_own, 2),
        (reduce2_second, 4),
        (reduce2_second, 5),
        (gather_near, 0),
        (reduce3, 3),
        (gather_near, 1),
        (reduce3, 4),
        (gather_near, 2),
        (reduce3, 5),
        (finish, 3),
        (gather_far, 0),
        (finish, 4),
        (gather_far, 1),
        (finish, 5),
        (gather_far, 2),
        (gather_own, 3),
        (pass_early, 0),
        (gather_own, 4),
        (pass_early, 1),
        (gather_own, 5),
        (pass_early, 2),
        (gather_near, 3),
        (gather_near, 4),
        (gather_near, 5),
        (pass_late, 0),
        (pass_late, 1),
        (pass_late, 2),
        (gather_far, 3),
        (gather_far, 4),
        (gather_far, 5),
        (pass_early, 3),
        (pass_early, 4),
        (pass_early, 5),
        (pass_late, 3),
        (pass_late, 4),
        (pass_late, 5),
        (sent_sums, 0),
        (sent_sums, 1),
        (sent_sums, 2),
        (sent_sums, 3),
        (sent_sums, 4),
        (sent_sums, 5),
        (sent_gather, 0),
        (sent_gather, 1),
        (sent_gather, 2),
    ):
        step(m)
    for m in parts:
        for way in range(2):
            for order in range(4):
                if (way, order) not in passed:
                    spread1_arrived(m, way, order)
        for way, order in passed:
            pass1(m, way, order, turned(axes(m)[0], 2)).wait_recv()

    for m in parts[3:]:
        sent_gather(m)


def summed_panels(xh, lr, da, du, left, right, words):
    i32 = jnp.int32
    messages = 114 + 72
    rows_all = da.shape[1]
    dma = pltpu.SemaphoreType.DMA
    return pl.pallas_call(
        sum_kernel,
        out_shape=pltpu.VMEM((4 * PAIRS, FULL, 128), i32),
        in_specs=[pl.BlockSpec(memory_space=pl.ANY)] * 7,
        out_specs=pl.BlockSpec(memory_space=pl.ANY),
        scratch_shapes=[
            pltpu.VMEM((6, GROUP, 128), i32),
            pltpu.VMEM((3, 2 * PANEL, 4 * 640), BF),
            pltpu.VMEM((3, 4, 2, rows_all, 640), BF),
            pltpu.VMEM((6, 2, 4, STRIP, 128), F32),
            pltpu.VMEM((6, 2, 3, HALF + 8, 128), i32),
            pltpu.VMEM((6, 2, 3, HALF + 8, 128), i32),
            pltpu.VMEM((6, 3, GROUP + 8, 128), i32),
            pltpu.VMEM((6, 3, GROUP + 8, 128), i32),
            pltpu.VMEM((6, GROUP + 8, 128), i32),
            pltpu.VMEM((6, 3, 8, 128), i32),
            pltpu.VMEM((6, FULL, 128), i32),
            dma((messages,)),
            dma((messages,)),
            dma((6,)),
            dma((6,)),
            dma((36,)),
            dma((24,)),
        ],
        compiler_params=pltpu.CompilerParams(
            vmem_limit_bytes=SUM_VMEM, collective_id=1, has_side_effects=True
        ),
    )(xh, lr, da, du, left, right, words)


def unpack_kernel(
    panels,
    words_u,
    hidden,
    grads_in,
    low_in,
    low_rec,
    low_bias,
    up_in,
    up_rec,
    up_bias,
    hidden_o,
    grads_in_o,
    tail,
):
    step = pl.program_id(0)
    units, outs = low_in.shape[0], up_rec.shape[0]
    lower_steps, all_steps = 2 * LOWER_PAIRS // WIDTH, 2 * PAIRS // WIDTH

    @pl.when(step == 0)
    def _():
        hidden_o[...] = hidden[...]
        grads_in_o[...] = grads_in[...]

    def values(n, ab):
        parts = []
        n = jnp.minimum(step, all_steps - 1) * WIDTH + n
        for strip in range(2):
            at = strip * 2 * PAIRS + n
            for group in range(4):
                words = panels[at, group * GROUP : (group + 1) * GROUP, :]
                row = STRIP + 2 * group + ab
                scale = factor(panels[at, row : row + 1, :])
                half = (words >> 16) if ab == 0 else ((words << 16) >> 16)
                parts.append(half.astype(F32) * scale)
        return jnp.concatenate(parts, axis=0)

    for n in range(WIDTH):
        cols = slice(n * 128, (n + 1) * 128)

        @pl.when(step < lower_steps)
        def _():
            a = values(n, 0)
            low_in[:, cols] = a[:units]
            low_bias[:, cols] = a[units : units + 1]
            b = values(n, 1)[:units]
            low_rec[:, cols] = b

        @pl.when((step >= lower_steps) & (step < all_steps))
        def _():
            a = values(n, 0)
            up_in[:, cols] = a[:units]
            up_bias[:, cols] = a[units : units + 1]
            b = values(n, 1)
            flags = flags_at(words_u[...], (step - lower_steps) * WIDTH * 128 + n * 128)
            up_rec[:, cols] = b[:outs] * (flags * 2).astype(F32)[:outs]
            if n % 2 == 0:
                index = (step - lower_steps) * (WIDTH // 2) + n // 2
                rows = pl.ds(pl.multiple_of(index * TAIL_ROWS, 8), TAIL_ROWS)
                tail[rows, :] = b[PANEL - TAIL_ROWS :]

    @pl.when(step == all_steps)
    def _():
        up_in[:, :128] = tail[:units]
        up_bias[:, :128] = tail[units : units + 1]
        flags = flags_at(words_u[...], 2 * (PAIRS - LOWER_PAIRS) * 128)
        up_rec[:, :128] = tail[PANEL : PANEL + outs] * (flags * 2).astype(F32)[:outs]


def unpack(panels, words_u, hidden, grads_in, units, full, outs, full_u):
    sds = jax.ShapeDtypeStruct
    lower_steps, all_steps = 2 * LOWER_PAIRS // WIDTH, 2 * PAIRS // WIDTH
    wide = 128 * WIDTH
    lower = lambda i: (0, jnp.minimum(i, lower_steps - 1))
    upper = lambda i: (0, jnp.maximum(i - lower_steps, 0))
    return pl.pallas_call(
        unpack_kernel,
        grid=(all_steps + 1,),
        out_shape=(
            sds((units, full), F32),
            sds((units, full), F32),
            sds((1, full), F32),
            sds((units, full_u), F32),
            sds((outs, full_u), F32),
            sds((1, full_u), F32),
            sds(hidden.shape, F32),
            sds(grads_in.shape, F32),
        ),
        in_specs=[
            pl.BlockSpec(memory_space=pltpu.VMEM),
            pl.BlockSpec(memory_space=pltpu.VMEM),
            pl.BlockSpec(memory_space=pltpu.VMEM),
            pl.BlockSpec(memory_space=pltpu.VMEM),
        ],
        out_specs=(
            pl.BlockSpec((units, wide), lower),
            pl.BlockSpec((units, wide), lower),
            pl.BlockSpec((1, wide), lower),
            pl.BlockSpec((units, wide), upper),
            pl.BlockSpec((outs, wide), upper),
            pl.BlockSpec((1, wide), upper),
            pl.BlockSpec(hidden.shape, lambda i: (0, 0, 0)),
            pl.BlockSpec(grads_in.shape, lambda i: (0, 0, 0)),
        ),
        scratch_shapes=[pltpu.VMEM((6 * TAIL_ROWS, 128), F32)],
        compiler_params=pltpu.CompilerParams(vmem_limit_bytes=UNPACK_VMEM),
    )(panels, words_u, hidden, grads_in)


def body(
    inputs,
    lower_lock,
    upper_lock,
    resets,
    lower_input,
    lower_recur,
    lower_bias,
    lower_drop,
    upper_input,
    upper_recur,
    upper_bias,
    upper_drop,
    grad_out,
):
    me = lax.axis_index("pipe")
    streams, steps, width = inputs.shape
    hidden_out, grad_inputs, da, du, xh, lr, left, right, words_l, words_u = recurrence(
        inputs,
        lower_lock,
        upper_lock,
        resets,
        grad_out,
        lower_drop.T,
        upper_drop.T,
        jnp.concatenate([lower_bias, upper_bias])[None],
        lower_recur,
        lower_input,
        upper_input,
        upper_recur,
    )
    panels = summed_panels(xh, lr, da, du, left, right, words_l)
    low_in, low_rec, low_bias, up_in, up_rec, up_bias, hidden_out, grad_inputs = unpack(
        panels, words_u, hidden_out, grad_inputs, *lower_recur.shape, *upper_recur.shape
    )

    def own(row):
        half = row.shape[1] // 2
        return lax.dynamic_slice_in_dim(row[0], me * half, half, 0)

    return (
        hidden_out,
        grad_inputs,
        low_in,
        low_rec,
        own(low_bias),
        up_in,
        up_rec,
        own(up_bias),
    )


def solution(mesh):
    return jax.shard_map(
        body,
        mesh=mesh,
        in_specs=(
            P("dp", None, None),
            P("dp", None),
            P("dp", None),
            P("dp", None),
            P("pipe", None),
            P("pipe", None),
            P("pipe"),
            P(),
            P("pipe", None),
            P("pipe", None),
            P("pipe"),
            P(),
            P("dp", None, None),
        ),
        out_specs=(
            P("dp", None, "pipe"),
            P("dp", None, "pipe"),
            P("pipe", None),
            P("pipe", None),
            P("pipe"),
            P("pipe", None),
            P("pipe", None),
            P("pipe"),
        ),
        check_vma=False,
    )
```
